32 devices in a mesh: grp: 2 (over x), ex: 16 (over z, y, core).
Axes of the slice: x: 2, y: 2, z: 4, core: 2. Of those that a mesh axis runs over, the one named last changes fastest.
Arguments:
- features: bfloat16 [20480, 8192], P(('grp', 'ex')), parts along dimension 0, may hold values from -6 to 6
- labels: int32 [20480], P(('grp', 'ex')), parts along dimension 0, may hold values from 0 to 31
- pick_index: int32 [6, 32], P('grp'), parts along dimension 0, may hold values from 0 to 10239, as said below
Outputs:
- scores: float32 [3, 20480], P(None, ('grp', 'ex')), parts along dimension 1
- residual: float32 [64, 8192], P('grp'), parts along dimension 0
The draws below stay inside these ranges and needn't reach their ends.
There are 2 independent parts, one for each index of `grp`. The reference program is written for one: setup_inputs(seed, part) draws one part's arguments, and reference() takes and returns one part's arrays. A program takes and returns all parts, laid end to end along the dimension named above; each array names one. Nothing has to cross between parts.
Inputs may be any that keep to these rules, and one draw needn't show every extreme that they name: pick_index[s, c] is an example of class c; the picks of one class differ from step to step; at each step at most 2 picks lie among the 640 examples of one device, and some device holds exactly 2.
All inputs are finite; a program needn't handle non-finite values.
Results may differ from the reference program's by a relative error of at most 0.00105.
Values may be sent and summed in bfloat16 or wider, within the bound.
No kernel may reach another device: no remote copies, remote signals or barrier semaphores. Data moves between devices by JAX's collectives and lax.ppermute only.
A program may use at most 64 MiB of HBM per device.

```python
import math
import jax
import jax.numpy as jnp
from jax import lax

FEATURES = 8192
CLASSES = 32
ROWS_DEV = 640
STEPS = 3
PICK_MOST = 2
EXAMPLES = 10240
N_EX = 16


def draw_pairs(key):
    slot_width = ROWS_DEV // (STEPS * PICK_MOST)
    classes = jnp.arange(CLASSES, dtype=jnp.int32)
    owner_rows = []
    for section in range(STEPS):
        order_key = jax.random.fold_in(jax.random.fold_in(key, 101), section)
        shuffled = jax.random.permutation(order_key, N_EX).astype(jnp.int32)
        owner_rows.append(shuffled[classes // PICK_MOST])
    owners = jnp.stack(owner_rows)
    slot_number = jnp.arange(STEPS, dtype=jnp.int32)[:, None] * PICK_MOST + (classes % PICK_MOST)[None, :]
    offsets = jax.random.randint(jax.random.fold_in(key, 102), (STEPS, CLASSES), 0, slot_width, dtype=jnp.int32)
    pick_index = owners * ROWS_DEV + slot_number * slot_width + offsets
    device_of = jnp.arange(EXAMPLES, dtype=jnp.int32) // ROWS_DEV
    halves = jax.random.randint(jax.random.fold_in(key, 103), (EXAMPLES,), 0, CLASSES // 2, dtype=jnp.int32) * 2
    coins = jax.random.randint(jax.random.fold_in(key, 104), (EXAMPLES,), 0, 4 * N_EX, dtype=jnp.int32)
    parity = (coins < N_EX + 2 * device_of).astype(jnp.int32)
    labels = halves + parity
    labels = labels.at[pick_index.reshape(-1)].set(jnp.tile(classes, STEPS))
    return (labels, pick_index)


def draw_labels(key, part):
    labels, pick_index = draw_pairs(key)
    return labels


def draw_pick_index(key, part):
    labels, pick_index = draw_pairs(key)
    return pick_index


def block_scale(rng, dims, pieces, least, top_value):
    gain = 1.0
    for dim, shards_of in pieces:
        steps = jax.random.uniform(jax.random.fold_in(jax.random.fold_in(rng, 6), dim), (shards_of,), jnp.float32, least / len(pieces), top_value / len(pieces))
        gain = gain * jnp.repeat(jnp.exp(steps), dims[dim] // shards_of).reshape((-1,) + (1,) * (len(dims) - 1 - dim))
    return gain


def noise(rng, extent, scale, most, pieces=(), held_as=jnp.bfloat16):
    drawn = jax.random.normal(rng, extent, jnp.float32) * scale
    if len(pieces) > 0:
        drawn = block_scale(rng, extent, pieces, -0.22, 0.18) * drawn
    return jnp.clip(drawn, min=-most, max=most).astype(held_as)


def setup_inputs(seed: int = 0, part: int = 0) -> dict:
    key_list = jax.random.split(jax.random.key(seed), 4)
    part_splits = jax.random.split(jax.random.fold_in(key_list[3], part), 4)
    return {
        "features": noise(part_splits[0], (EXAMPLES, FEATURES), 1.0, 6.0, ((0, 16),)),
        "labels": draw_labels(jax.random.fold_in(jax.random.fold_in(key_list[3], part), 71), part),
        "pick_index": draw_pick_index(jax.random.fold_in(jax.random.fold_in(key_list[3], part), 71), part),
    }


ridge = 1.0

def solve_small(gram_matrix, right_side):
    factor = jnp.linalg.cholesky(gram_matrix)
    order_size = right_side.shape[1]
    forward = []
    for i in range(order_size):
        partial_value = right_side[:, i]
        for j in range(i):
            partial_value = partial_value - factor[:, i, j] * forward[j]
        forward.append(partial_value / factor[:, i, i])
    backward = [None] * order_size
    for i in reversed(range(order_size)):
        partial_value = forward[i]
        for j in range(i + 1, order_size):
            partial_value = partial_value - factor[:, j, i] * backward[j]
        backward[i] = partial_value / factor[:, i, i]
    return jnp.stack(backward, axis=1)

def project(picked, target, target_low):
    order_size = picked.shape[1]
    picked_float = picked.astype(jnp.float32)
    gram_matrix = jnp.einsum('ckf,cjf->ckj', picked_float, picked_float, precision=lax.Precision.HIGHEST)
    gram_matrix = gram_matrix + ridge * jnp.eye(order_size, dtype=jnp.float32)[None]
    right_side = jnp.einsum('ckf,cf->ck', picked_float, target_low.astype(jnp.float32), precision=lax.Precision.HIGHEST)
    weights = solve_small(gram_matrix, right_side)
    result = target
    for k in range(order_size):
        result = result - weights[:, k:k + 1] * picked_float[:, k, :]
    return result

def reference(features, labels, pick_index):
    classes = jnp.arange(CLASSES, dtype=jnp.int32)
    member = (classes[:, None] == labels[None, :]).astype(jnp.bfloat16)
    class_total = jnp.dot(member.astype(jnp.float32), features.astype(jnp.float32), preferred_element_type=jnp.float32)
    class_count = lax.optimization_barrier(jnp.sum(member.astype(jnp.float32), axis=1))
    target = class_total / jnp.sqrt(class_count)[:, None]
    target_low = target.astype(jnp.bfloat16)
    member_float = member.astype(jnp.float32)
    scale = 1.0 / math.sqrt(FEATURES)
    current = target
    chosen = []
    score_list = []
    for section in range(STEPS):
        product = lax.dot_general(current.astype(jnp.bfloat16).astype(jnp.float32), features.astype(jnp.float32), (((1,), (1,)), ((), ())), preferred_element_type=jnp.float32)
        score_list.append(lax.optimization_barrier(jnp.sum(product * member_float, axis=0)) * scale)
        chosen.append(features[pick_index[section]])
        current = project(jnp.stack(chosen, axis=1), target, target_low)
    return (jnp.stack(score_list), current)
```

```python
import functools
import math

import jax
import jax.numpy as jnp
from jax import lax
from jax.experimental import pallas as pl
from jax.experimental.pallas import tpu as pltpu
from jax.sharding import PartitionSpec as P

ridge = 1.0
slots = 2
f32 = jnp.float32
bf16 = jnp.bfloat16


def nt_dot(a, b):
    return lax.dot_general(a, b, (((1,), (1,)), ((), ())), preferred_element_type=f32)


def sums_kernel(place, labels_ref, pick_ref, feat_ref, send_ref, keep_ref, rows_ref, left, held, *, classes, steps):
    i = pl.program_id(0)
    half = pl.num_programs(0) // 2
    block = place[1 + i]
    width = feat_ref.shape[1]
    used = steps * slots

    @pl.when(i == 0)
    def _():
        lab = labels_ref[...]
        n = lab.shape[1]
        member = lax.broadcasted_iota(jnp.int32, (classes, n), 0) == lab
        spot = lax.broadcasted_iota(jnp.int32, (8, n), 1) == pick_ref[...]
        left[...] = jnp.concatenate(
            [jnp.where(member, 1.0, 0.0), jnp.where(spot, 1.0, 0.0), jnp.zeros((8, n), f32)], axis=0
        ).astype(bf16)

    both = jnp.dot(left[...], feat_ref[...], preferred_element_type=f32)

    @pl.when(i < half)
    def _():
        send_ref[0] = both[:classes]

    @pl.when(i >= half)
    def _():
        keep_ref[0] = both[:classes]

    held[:, pl.ds(pl.multiple_of(block * width, width), width)] = both[classes : classes + 8]

    @pl.when(i == pl.num_programs(0) - 1)
    def _():
        full = held.shape[1]
        main = full * used // 8
        tail = full - main
        per = main // tail
        lines = [held[0:used, :main]]
        for q in range(used // per):
            lines.append(jnp.concatenate([held[q * per + u : q * per + u + 1, main:] for u in range(per)], axis=1))
        count = jnp.sum(left[0:classes, :].astype(f32), axis=1, keepdims=True)
        high = jnp.floor(count * (1.0 / 128.0))
        low = count - 128.0 * high
        lane = lax.broadcasted_iota(jnp.int32, (8, 128), 1)
        extra = jnp.zeros((8, 128), f32)
        for q in range(classes // 8):
            extra = jnp.where(lane == 2 * q, high[8 * q : 8 * q + 8], extra)
            extra = jnp.where(lane == 2 * q + 1, low[8 * q : 8 * q + 8], extra)
        rows_ref[...] = jnp.concatenate([jnp.concatenate(lines, axis=0), extra], axis=1).astype(bf16)


def picked_kernel(index_ref, rows_ref, feat_ref, x_ref, cross_ref, gram_ref, *, steps):
    i = pl.program_id(0)
    width = feat_ref.shape[1]
    full = width * pl.num_programs(0)
    used = steps * slots
    main = full * used // 8
    per = main // (full - main)
    tail = full - main
    total = x_ref.shape[0]
    lines = rows_ref.shape[0]

    @pl.when(i == 0)
    def _():
        index = index_ref[...]
        line = lax.broadcasted_iota(jnp.int32, (total, lines), 1)
        one = jnp.where(line == index, 1.0, 0.0).astype(bf16)
        x_ref[:, :main] = jnp.dot(one, rows_ref[:, :main], preferred_element_type=f32).astype(bf16)
        slot = index % 8
        rest = jnp.zeros((total, tail), f32)
        home = index - slot + used + slot // per
        for u in range(per):
            here = jnp.where((line == home) & (slot % per == u), 1.0, 0.0).astype(bf16)
            rest = rest + jnp.dot(here, rows_ref[:, u * tail : (u + 1) * tail], preferred_element_type=f32)
        x_ref[:, main:] = rest.astype(bf16)
        cross_ref[...] = jnp.zeros_like(cross_ref)
        gram_ref[...] = jnp.zeros_like(gram_ref)

    x = x_ref[:, pl.ds(pl.multiple_of(i * width, width), width)]
    cross_ref[...] += nt_dot(x, feat_ref[...])
    gram_ref[...] += nt_dot(x, x)


def diagonal(block):
    n = block.shape[0]
    eye = lax.broadcasted_iota(jnp.int32, (n, n), 0) == lax.broadcasted_iota(jnp.int32, (n, n), 1)
    return jnp.sum(jnp.where(eye, block, 0.0), axis=1, keepdims=True)


def solve_all(gram, right):
    order = len(right)
    factor = [[None] * order for _ in range(order)]
    for j in range(order):
        value = gram[j][j]
        for k in range(j):
            value = value - factor[j][k] * factor[j][k]
        factor[j][j] = jnp.sqrt(value)
        for i in range(j + 1, order):
            value = gram[i][j]
            for k in range(j):
                value = value - factor[i][k] * factor[j][k]
            factor[i][j] = value / factor[j][j]
    forward = []
    for i in range(order):
        value = right[i]
        for j in range(i):
            value = value - factor[i][j] * forward[j]
        forward.append(value / factor[i][i])
    result = []
    for size in range(1, order + 1):
        back = [None] * size
        for i in reversed(range(size)):
            value = forward[i]
            for j in range(i + 1, size):
                value = value - factor[j][i] * back[j]
            back[i] = value / factor[i][i]
        result.append(back)
    return result


def final_kernel(
    place, labels_ref, extra_ref, x_ref, cross_ref, gram_ref, own_ref, twin_ref, feat_a, feat_b,
    scores_ref, resid_ref, inv, direct, right, *, steps, scale
):
    i = pl.program_id(0)
    width = feat_a.shape[1]
    classes = direct.shape[0]

    @pl.when(i == 0)
    def _():
        summed = jnp.sum(extra_ref[...].astype(f32), axis=0)
        parts = []
        for q in range(classes // 8):
            parts.append(128.0 * summed[:, 2 * q : 2 * q + 1] + summed[:, 2 * q + 1 : 2 * q + 2])
        inv[...] = jnp.broadcast_to(jnp.sqrt(jnp.concatenate(parts, axis=0)), inv.shape)
        direct[...] = jnp.zeros_like(direct)
        right[...] = jnp.zeros_like(right)

    for block, got, feat in ((place[1 + 2 * i], own_ref, feat_a), (place[2 + 2 * i], twin_ref, feat_b)):
        at = pl.ds(pl.multiple_of(block * width, width), width)
        target = got[0] / inv[:, 0:1]
        resid_ref[:, at] = target
        low = target.astype(bf16)
        direct[...] += nt_dot(low, feat[...])
        right[...] += nt_dot(low, x_ref[:, at])

    @pl.when(i == pl.num_programs(0) - 1)
    def _():
        gram = [
            [
                diagonal(gram_ref[a * classes : (a + 1) * classes, b * classes : (b + 1) * classes])
                + (ridge if a == b else 0.0)
                for b in range(steps)
            ]
            for a in range(steps)
        ]
        rhs = [diagonal(right[:, a * classes : (a + 1) * classes]) for a in range(steps)]
        weights = solve_all(gram, rhs)
        member = lax.broadcasted_iota(jnp.int32, direct.shape, 0) == labels_ref[...]
        for s in range(steps):
            value = direct[...]
            for k in range(s):
                value = value - weights[s - 1][k] * cross_ref[k * classes : (k + 1) * classes]
            scores_ref[s : s + 1, :] = jnp.sum(jnp.where(member, value, 0.0), axis=0, keepdims=True) * scale
        last = weights[steps - 1]
        value = resid_ref[...]
        for k in range(steps):
            value = value - last[k] * x_ref[k * classes : (k + 1) * classes].astype(f32)
        resid_ref[...] = value


def whole(shape):
    return pl.BlockSpec(shape, lambda i, *_: (0,) * len(shape))


def on_device(features, labels, pick_index, *, n_ex):
    rows, full = features.shape
    steps, classes = pick_index.shape
    groups = n_ex // 2
    width = full // n_ex
    device = lax.axis_index("ex")
    core = device % 2
    group = device // 2
    limit = pltpu.CompilerParams(vmem_limit_bytes=48 << 20)

    owner = pick_index // rows
    earlier = jnp.arange(classes)[:, None] > jnp.arange(classes)[None, :]
    rank = jnp.sum((owner[:, :, None] == owner[:, None, :]) & earlier[None], axis=2, dtype=jnp.int32)
    step_id = jnp.arange(steps, dtype=jnp.int32)[:, None]
    index = (owner * 8 + step_id * slots + rank).reshape(steps * classes, 1)
    mine = index - device * 8 == jnp.arange(8, dtype=jnp.int32)[None, :]
    local = (pick_index - device * rows).reshape(steps * classes, 1)
    spot = (jnp.sum(jnp.where(mine, local + 1, 0), axis=0, dtype=jnp.int32) - 1).reshape(8, 1)

    labels_row = labels.reshape(1, rows)
    ids = jnp.arange(groups, dtype=jnp.int32)
    order = jnp.concatenate([ids + (1 - core) * groups, ids + core * groups])
    place = jnp.concatenate([jnp.zeros((1,), jnp.int32), order])

    send, keep, packed = pl.pallas_call(
        functools.partial(sums_kernel, classes=classes, steps=steps),
        grid_spec=pltpu.PrefetchScalarGridSpec(
            num_scalar_prefetch=1,
            grid=(n_ex,),
            in_specs=[
                whole((1, rows)),
                whole((8, 1)),
                pl.BlockSpec((rows, width), lambda i, p: (0, p[1 + i])),
            ],
            out_specs=[
                pl.BlockSpec((1, classes, width), lambda i, p: (jnp.minimum(i, groups - 1), 0, 0)),
                pl.BlockSpec((1, classes, width), lambda i, p: (jnp.maximum(i - groups, 0), 0, 0)),
                whole((8, full * 6 // 8 + 128)),
            ],
            scratch_shapes=[pltpu.VMEM((classes + 16, rows), bf16), pltpu.VMEM((8, full), f32)],
        ),
        out_shape=[
            jax.ShapeDtypeStruct((groups, classes, width), f32),
            jax.ShapeDtypeStruct((groups, classes, width), f32),
            jax.ShapeDtypeStruct((8, full * 6 // 8 + 128), bf16),
        ],
        compiler_params=limit,
        name="class_sums",
    )(place, labels_row, spot, features)

    gathered = lax.all_gather(packed, "ex", axis=0, tiled=True)

    twin_pairs = [(d, d ^ 1) for d in range(n_ex)]
    summed = keep + lax.ppermute(send, "ex", twin_pairs)
    same_core = [[2 * g + c for g in range(groups)] for c in range(2)]
    pieces = lax.all_to_all(summed, "ex", 0, 0, axis_index_groups=same_core, tiled=True)
    mine_sum = jnp.sum(pieces, axis=0)
    own = [mine_sum]
    for k in range(1, groups):
        own.append(lax.ppermute(mine_sum, "ex", [(d, d ^ (2 * k)) for d in range(n_ex)]))
    own = jnp.stack(own)
    twin = lax.ppermute(own, "ex", twin_pairs)

    total = steps * classes
    x, cross, gram = pl.pallas_call(
        functools.partial(picked_kernel, steps=steps),
        grid=(n_ex,),
        in_specs=[
            whole((total, 1)),
            whole(gathered.shape),
            pl.BlockSpec((rows, width), lambda i: (0, i)),
        ],
        out_specs=[whole((total, full)), whole((total, rows)), whole((total, total))],
        out_shape=[
            jax.ShapeDtypeStruct((total, full), bf16),
            jax.ShapeDtypeStruct((total, rows), f32),
            jax.ShapeDtypeStruct((total, total), f32),
        ],
        compiler_params=limit,
        name="picked_products",
    )(index, gathered, features)

    peers = group ^ ids
    pairs = jnp.stack([core * groups + peers, (1 - core) * groups + peers], axis=1).reshape(-1)
    place = jnp.concatenate([jnp.zeros((1,), jnp.int32), pairs])
    extra = gathered[:, full * 6 // 8 :].reshape(n_ex, 8, 128)
    scores, resid = pl.pallas_call(
        functools.partial(final_kernel, steps=steps, scale=1.0 / math.sqrt(full)),
        grid_spec=pltpu.PrefetchScalarGridSpec(
            num_scalar_prefetch=1,
            grid=(groups,),
            in_specs=[
                whole((1, rows)),
                whole((n_ex, 8, 128)),
                whole((total, full)),
                whole((total, rows)),
                whole((total, total)),
                pl.BlockSpec((1, classes, width), lambda i, p: (i, 0, 0)),
                pl.BlockSpec((1, classes, width), lambda i, p: (i, 0, 0)),
                pl.BlockSpec((rows, width), lambda i, p: (0, p[1 + 2 * i])),
                pl.BlockSpec((rows, width), lambda i, p: (0, p[2 + 2 * i])),
            ],
            out_specs=[whole((steps, rows)), whole((classes, full))],
            scratch_shapes=[
                pltpu.VMEM((classes, 128), f32),
                pltpu.VMEM((classes, rows), f32),
                pltpu.VMEM((classes, total), f32),
            ],
        ),
        out_shape=[
            jax.ShapeDtypeStruct((steps, rows), f32),
            jax.ShapeDtypeStruct((classes, full), f32),
        ],
        compiler_params=limit,
        name="pursuit",
    )(place, labels_row, extra, x, cross, gram, own, twin, features, features)
    return scores, resid


def solution(mesh):
    return jax.shard_map(
        functools.partial(on_device, n_ex=mesh.shape["ex"]),
        mesh=mesh,
        in_specs=(P(("grp", "ex"), None), P(("grp", "ex")), P("grp", None)),
        out_specs=(P(None, ("grp", "ex")), P("grp", None)),
        check_vma=False,
    )
```

```python
import functools
import math

import jax
import jax.numpy as jnp
from jax import lax
from jax.experimental import pallas as pl
from jax.experimental.pallas import tpu as pltpu
from jax.sharding import PartitionSpec as P

ridge = 1.0
slots = 2
f32 = jnp.float32
bf16 = jnp.bfloat16


def nt_dot(a, b):
    return lax.dot_general(a, b, (((1,), (1,)), ((), ())), preferred_element_type=f32)


def encode(x):
    height, width = x.shape
    top = jnp.max(jnp.abs(x), axis=1, keepdims=True)
    power = jnp.ceil(jnp.log2(jnp.maximum(top, 1e-30)) + 0.01)
    whole_x = jnp.round(x * jnp.exp2(15.0 - power))
    lane = lax.broadcasted_iota(jnp.int32, (8, 128), 1)
    mark = jnp.zeros((8, 128), f32)
    for q in range(height // 8):
        mark = jnp.where(lane == q, power[8 * q : 8 * q + 8], mark)
    chunks = [whole_x[:, j * 128 : (j + 1) * 128] for j in range(width // 128)]
    return jnp.concatenate(chunks + [mark], axis=0).astype(jnp.int32).astype(jnp.int16)


def decode(code, height):
    value = code.astype(jnp.int32).astype(f32)
    count = value.shape[0] // height
    mark = value[count * height :]
    power = jnp.concatenate([mark[:, q : q + 1] for q in range(height // 8)], axis=0)
    x = jnp.concatenate([value[j * height : (j + 1) * height] for j in range(count)], axis=1)
    return x * jnp.exp2(power - 15.0)


def sums_kernel(labels_ref, pick_ref, feat_hbm, feat_ref, send_ref, keep_ref, rows_ref, left, held, sems, *, n_ex):
    rows, full = feat_ref.shape
    steps, classes = pick_ref.shape
    width = full // n_ex
    groups = n_ex // 2
    device = lax.axis_index("ex")
    core = device % 2
    columns = []
    copies = []
    for i in range(n_ex):
        block = (1 - core) * groups + i if i < groups else core * groups + i - groups
        at = pl.ds(pl.multiple_of(block * width, width), width)
        columns.append(at)
        copies.append(pltpu.make_async_copy(feat_hbm.at[:, at], feat_ref.at[:, at], sems.at[i]))
        copies[-1].start()

    local = pick_ref[...] - device * rows
    mine = (local >= 0) & (local < rows)
    lane = lax.broadcasted_iota(jnp.int32, local.shape, 1)
    first = jnp.min(jnp.where(mine, lane, classes), axis=1, keepdims=True)
    last = jnp.max(jnp.where(mine, lane, -1), axis=1, keepdims=True)
    spot0 = jnp.max(jnp.where(mine & (lane == first), local, -1), axis=1, keepdims=True)
    spot1 = jnp.max(jnp.where(mine & (lane == last) & (last > first), local, -1), axis=1, keepdims=True)
    member = lax.broadcasted_iota(jnp.int32, (classes, rows), 0) == labels_ref[...].reshape(1, rows)
    line = lax.broadcasted_iota(jnp.int32, (steps, rows), 1)
    left[...] = jnp.concatenate(
        [
            jnp.where(member, 1.0, 0.0),
            jnp.where(line == spot0, 1.0, 0.0),
            jnp.where(line == spot1, 1.0, 0.0),
            jnp.zeros((16 - 2 * steps, rows), f32),
        ],
        axis=0,
    ).astype(bf16)

    for i in range(n_ex):
        copies[i].wait()
        both = jnp.dot(left[...], feat_ref[:, columns[i]], preferred_element_type=f32)
        if i < groups:
            send_ref[i] = both[:classes]
        else:
            keep_ref[i - groups] = both[:classes]
        held[:, columns[i]] = both[classes : classes + 8]

    used = steps * slots
    main = full * used // 8
    tail = full - main
    per = main // tail
    lines = [held[0:used, :main]]
    for q in range(used // per):
        lines.append(jnp.concatenate([held[q * per + u : q * per + u + 1, main:] for u in range(per)], axis=1))
    count = jnp.sum(jnp.where(member, 1.0, 0.0), axis=1, keepdims=True)
    high = jnp.floor(count * (1.0 / 128.0))
    low = count - 128.0 * high
    lane = lax.broadcasted_iota(jnp.int32, (8, 128), 1)
    extra = jnp.zeros((8, 128), f32)
    for q in range(classes // 8):
        extra = jnp.where(lane == 2 * q, high[8 * q : 8 * q + 8], extra)
        extra = jnp.where(lane == 2 * q + 1, low[8 * q : 8 * q + 8], extra)
    rows_ref[...] = jnp.concatenate([jnp.concatenate(lines, axis=0), extra], axis=1).astype(bf16)


def pair_kernel(keep_ref, got_ref, own_ref, *code_refs):
    group = lax.axis_index("ex") // 2
    own_ref[...] = keep_ref[group] + got_ref[group]
    for k, code_ref in enumerate(code_refs):
        block = group ^ (k + 1)
        code_ref[...] = encode(keep_ref[block] + got_ref[block])


def total_kernel(own_ref, *refs):
    value = own_ref[...]
    for code_ref in refs[:-1]:
        value = value + decode(code_ref[...], value.shape[0])
    refs[-1][...] = encode(value)


def picked_kernel(index_ref, feat_ref, *refs, steps):
    parts, (x_ref, cross_ref, gram_ref, rows_ref) = refs[:-4], refs[-4:]
    full = feat_ref.shape[1]
    used = steps * slots
    main = full * used // 8
    per = main // (full - main)
    tail = full - main
    total = x_ref.shape[0]
    lines = rows_ref.shape[0]
    at = 0
    for part in parts:
        rows_ref[at : at + part.shape[0], :] = part[...]
        at += part.shape[0]

    index = index_ref[...]
    line = lax.broadcasted_iota(jnp.int32, (total, lines), 1)
    one = jnp.where(line == index, 1.0, 0.0).astype(bf16)
    x_ref[:, :main] = jnp.dot(one, rows_ref[:, :main], preferred_element_type=f32).astype(bf16)
    slot = index % 8
    rest = jnp.zeros((total, tail), f32)
    home = index - slot + used + slot // per
    for u in range(per):
        here = jnp.where((line == home) & (slot % per == u), 1.0, 0.0).astype(bf16)
        rest = rest + jnp.dot(here, rows_ref[:, u * tail : (u + 1) * tail], preferred_element_type=f32)
    x_ref[:, main:] = rest.astype(bf16)
    x = x_ref[...]
    cross_ref[...] = nt_dot(x, feat_ref[...])
    gram_ref[...] = nt_dot(x, x)


def diagonal(block):
    n = block.shape[0]
    eye = lax.broadcasted_iota(jnp.int32, (n, n), 0) == lax.broadcasted_iota(jnp.int32, (n, n), 1)
    return jnp.sum(jnp.where(eye, block, 0.0), axis=1, keepdims=True)


def solve_all(gram, right):
    order = len(right)
    factor = [[None] * order for _ in range(order)]
    for j in range(order):
        value = gram[j][j]
        for k in range(j):
            value = value - factor[j][k] * factor[j][k]
        factor[j][j] = jnp.sqrt(value)
        for i in range(j + 1, order):
            value = gram[i][j]
            for k in range(j):
                value = value - factor[i][k] * factor[j][k]
            factor[i][j] = value / factor[j][j]
    forward = []
    for i in range(order):
        value = right[i]
        for j in range(i):
            value = value - factor[i][j] * forward[j]
        forward.append(value / factor[i][i])
    result = []
    for size in range(1, order + 1):
        back = [None] * size
        for i in reversed(range(size)):
            value = forward[i]
            for j in range(i + 1, size):
                value = value - factor[j][i] * back[j]
            back[i] = value / factor[i][i]
        result.append(back)
    return result


def pursuit_kernel(
    labels_ref, extra_ref, x_ref, cross_ref, gram_ref, own_ref, twin_ref, feat_ref, scores_ref, resid_ref, low_ref,
    *, steps, scale
):
    classes, full = resid_ref.shape
    groups = own_ref.shape[0]
    width = full // (2 * groups)
    device = lax.axis_index("ex")
    group = device // 2
    core = device % 2

    summed = jnp.sum(extra_ref[...].astype(f32), axis=0)
    count = jnp.concatenate(
        [128.0 * summed[:, 2 * q : 2 * q + 1] + summed[:, 2 * q + 1 : 2 * q + 2] for q in range(classes // 8)], axis=0
    )
    root = jnp.sqrt(count)
    for k in range(groups):
        for side, code_ref in ((core, own_ref), (1 - core, twin_ref)):
            block = side * groups + (group ^ k)
            at = pl.ds(pl.multiple_of(block * width, width), width)
            target = decode(code_ref[k], classes) / root
            resid_ref[:, at] = target
            low_ref[:, at] = target.astype(bf16)

    low = low_ref[...]
    direct = nt_dot(low, feat_ref[...])
    right = nt_dot(low, x_ref[...])
    gram = [
        [
            diagonal(gram_ref[a * classes : (a + 1) * classes, b * classes : (b + 1) * classes])
            + (ridge if a == b else 0.0)
            for b in range(steps)
        ]
        for a in range(steps)
    ]
    rhs = [diagonal(right[:, a * classes : (a + 1) * classes]) for a in range(steps)]
    weights = solve_all(gram, rhs)
    member = lax.broadcasted_iota(jnp.int32, direct.shape, 0) == labels_ref[...].reshape(1, direct.shape[1])
    for s in range(steps):
        value = direct
        for k in range(s):
            value = value - weights[s - 1][k] * cross_ref[k * classes : (k + 1) * classes]
        scores_ref[s : s + 1, :] = jnp.sum(jnp.where(member, value, 0.0), axis=0, keepdims=True) * scale
    last = weights[steps - 1]
    value = resid_ref[...]
    for k in range(steps):
        value = value - last[k] * x_ref[k * classes : (k + 1) * classes].astype(f32)
    resid_ref[...] = value


def on_device(features, labels, pick_index, *, n_ex):
    rows, full = features.shape
    steps, classes = pick_index.shape
    groups = n_ex // 2
    deep = n_ex // 4
    width = full // n_ex
    total = steps * classes
    used = steps * slots
    main = full * used // 8
    device = lax.axis_index("ex")
    limit = pltpu.CompilerParams(vmem_limit_bytes=32 << 20)
    vmem = pl.BlockSpec(memory_space=pltpu.VMEM)
    half = jax.ShapeDtypeStruct((groups, classes, width), f32)
    code = jax.ShapeDtypeStruct((classes * (width // 128) + 8, 128), jnp.int16)

    def swap(x, mask):
        return lax.ppermute(x, "ex", [(d, d ^ mask) for d in range(n_ex)])

    feat, send, keep, packed = pl.pallas_call(
        functools.partial(sums_kernel, n_ex=n_ex),
        in_specs=[vmem, vmem, pl.BlockSpec(memory_space=pltpu.HBM)],
        out_specs=[vmem] * 4,
        out_shape=[
            jax.ShapeDtypeStruct((rows, full), bf16),
            half,
            half,
            jax.ShapeDtypeStruct((8, main + 128), bf16),
        ],
        scratch_shapes=[
            pltpu.VMEM((classes + 16, rows), bf16),
            pltpu.VMEM((8, full), f32),
            pltpu.SemaphoreType.DMA((n_ex,)),
        ],
        compiler_params=limit,
        name="class_sums",
    )(labels, pick_index, features)

    got = swap(send, 1)
    rows_z = jnp.concatenate([packed] + [swap(packed, 4 * k) for k in range(1, deep)], axis=0)

    own, *codes = pl.pallas_call(
        pair_kernel,
        in_specs=[vmem] * 2,
        out_specs=[vmem] * groups,
        out_shape=[jax.ShapeDtypeStruct((classes, width), f32)] + [code] * (groups - 1),
        compiler_params=limit,
        name="pair_sums",
    )(keep, got)
    codes = [swap(codes[k - 1], 2 * k) for k in range(1, groups)]
    summed = pl.pallas_call(
        total_kernel,
        in_specs=[vmem] * groups,
        out_specs=vmem,
        out_shape=code,
        compiler_params=limit,
        name="total_sums",
    )(own, *codes)
    own_half = jnp.stack([summed] + [swap(summed, 2 * k) for k in range(1, groups)])
    twin_half = swap(own_half, 1)

    rows_y = swap(rows_z, 2)
    parts = [rows_z, rows_y, swap(rows_z, 1), swap(rows_y, 1)]

    pick_late, _ = lax.optimization_barrier((pick_index, packed))
    owner = pick_late // rows
    earlier = jnp.arange(classes)[:, None] > jnp.arange(classes)[None, :]
    rank = jnp.sum((owner[:, :, None] == owner[:, None, :]) & earlier[None], axis=2, dtype=jnp.int32)
    step_id = jnp.arange(steps, dtype=jnp.int32)[:, None]
    away = owner ^ device
    spot = ((away & 1) * 2 + ((away >> 1) & 1)) * deep + (away >> 2)
    index = (spot * 8 + rank * steps + step_id).reshape(total, 1)

    x, cross, gram = pl.pallas_call(
        functools.partial(picked_kernel, steps=steps),
        in_specs=[vmem] * 6,
        out_specs=[vmem] * 3,
        out_shape=[
            jax.ShapeDtypeStruct((total, full), bf16),
            jax.ShapeDtypeStruct((total, rows), f32),
            jax.ShapeDtypeStruct((total, total), f32),
        ],
        scratch_shapes=[pltpu.VMEM((n_ex * 8, main + 128), bf16)],
        compiler_params=limit,
        name="picked_products",
    )(index, feat, *parts)

    extra = jnp.concatenate([p[:, main:].reshape(deep, 8, 128) for p in parts], axis=0)
    scores, resid = pl.pallas_call(
        functools.partial(pursuit_kernel, steps=steps, scale=1.0 / math.sqrt(full)),
        in_specs=[vmem] * 8,
        out_specs=[vmem] * 2,
        out_shape=[
            jax.ShapeDtypeStruct((steps, rows), f32),
            jax.ShapeDtypeStruct((classes, full), f32),
        ],
        scratch_shapes=[pltpu.VMEM((classes, full), bf16)],
        compiler_params=limit,
        name="pursuit",
    )(labels, extra, x, cross, gram, own_half, twin_half, feat)
    return scores, resid


def solution(mesh):
    return jax.shard_map(
        functools.partial(on_device, n_ex=mesh.shape["ex"]),
        mesh=mesh,
        in_specs=(P(("grp", "ex"), None), P(("grp", "ex")), P("grp", None)),
        out_specs=(P(None, ("grp", "ex")), P("grp", None)),
        check_vma=False,
    )
```

```python
import functools
import math

import jax
import jax.numpy as jnp
from jax import lax
from jax.experimental import pallas as pl
from jax.experimental.pallas import tpu as pltpu
from jax.sharding import PartitionSpec as P

ridge = 1.0
slots = 2
f32 = jnp.float32
bf16 = jnp.bfloat16


def nt_dot(a, b):
    return lax.dot_general(a, b, (((1,), (1,)), ((), ())), preferred_element_type=f32)


def encode(x):
    height, width = x.shape
    top = jnp.max(jnp.abs(x), axis=1, keepdims=True)
    power = jnp.ceil(jnp.log2(jnp.maximum(top, 1e-30)) + 0.01)
    whole_x = jnp.round(x * jnp.exp2(15.0 - power))
    lane = lax.broadcasted_iota(jnp.int32, (8, 128), 1)
    mark = jnp.zeros((8, 128), f32)
    for q in range(height // 8):
        mark = jnp.where(lane == q, power[8 * q : 8 * q + 8], mark)
    chunks = [whole_x[:, j * 128 : (j + 1) * 128] for j in range(width // 128)]
    return jnp.concatenate(chunks + [mark], axis=0).astype(jnp.int32).astype(jnp.int16)


def decode(code, height):
    value = code.astype(jnp.int32).astype(f32)
    count = value.shape[0] // height
    mark = value[count * height :]
    power = jnp.concatenate([mark[:, q : q + 1] for q in range(height // 8)], axis=0)
    x = jnp.concatenate([value[j * height : (j + 1) * height] for j in range(count)], axis=1)
    return x * jnp.exp2(power - 15.0)


def sums_kernel(
    labels_hbm, pick_hbm, feat_hbm, feat_ref, send_ref, keep_ref, rows_ref, labels_ref, pick_ref, left, held, sems, *, n_ex
):
    rows, full = feat_ref.shape
    steps, classes = pick_ref.shape
    width = full // n_ex
    groups = n_ex // 2
    device = lax.axis_index("ex")
    core = device % 2
    small = [
        pltpu.make_async_copy(pick_hbm, pick_ref, sems.at[n_ex]),
        pltpu.make_async_copy(labels_hbm, labels_ref, sems.at[n_ex + 1]),
    ]
    for copy in small:
        copy.start()
    columns = []
    copies = []
    for i in range(n_ex):
        block = (1 - core) * groups + i if i < groups else core * groups + i - groups
        at = pl.ds(pl.multiple_of(block * width, width), width)
        columns.append(at)
        copies.append(pltpu.make_async_copy(feat_hbm.at[:, at], feat_ref.at[:, at], sems.at[i]))
        copies[-1].start()

    for copy in small:
        copy.wait()
    local = pick_ref[...] - device * rows
    mine = (local >= 0) & (local < rows)
    lane = lax.broadcasted_iota(jnp.int32, local.shape, 1)
    first = jnp.min(jnp.where(mine, lane, classes), axis=1, keepdims=True)
    last = jnp.max(jnp.where(mine, lane, -1), axis=1, keepdims=True)
    spot0 = jnp.max(jnp.where(mine & (lane == first), local, -1), axis=1, keepdims=True)
    spot1 = jnp.max(jnp.where(mine & (lane == last) & (last > first), local, -1), axis=1, keepdims=True)
    member = lax.broadcasted_iota(jnp.int32, (classes, rows), 0) == labels_ref[...].reshape(1, rows)
    line = lax.broadcasted_iota(jnp.int32, (steps, rows), 1)
    left[...] = jnp.concatenate(
        [
            jnp.where(member, 1.0, 0.0),
            jnp.where(line == spot0, 1.0, 0.0),
            jnp.where(line == spot1, 1.0, 0.0),
            jnp.zeros((16 - 2 * steps, rows), f32),
        ],
        axis=0,
    ).astype(bf16)

    for i in range(n_ex):
        copies[i].wait()
        both = jnp.dot(left[...], feat_ref[:, columns[i]], preferred_element_type=f32)
        if i < groups:
            send_ref[i] = both[:classes]
        else:
            keep_ref[i - groups] = both[:classes]
        held[:, columns[i]] = both[classes : classes + 8]

    used = steps * slots
    main = full * used // 8
    tail = full - main
    per = main // tail
    lines = [held[0:used, :main]]
    for q in range(used // per):
        lines.append(jnp.concatenate([held[q * per + u : q * per + u + 1, main:] for u in range(per)], axis=1))
    count = jnp.sum(jnp.where(member, 1.0, 0.0), axis=1, keepdims=True)
    high = jnp.floor(count * (1.0 / 128.0))
    low = count - 128.0 * high
    lane = lax.broadcasted_iota(jnp.int32, (8, 128), 1)
    extra = jnp.zeros((8, 128), f32)
    for q in range(classes // 8):
        extra = jnp.where(lane == 2 * q, high[8 * q : 8 * q + 8], extra)
        extra = jnp.where(lane == 2 * q + 1, low[8 * q : 8 * q + 8], extra)
    rows_ref[...] = jnp.concatenate([jnp.concatenate(lines, axis=0), extra], axis=1).astype(bf16)


def pair_kernel(keep_ref, got_ref, code_ref):
    for k in range(keep_ref.shape[0]):
        code_ref[k] = encode(keep_ref[k] + got_ref[k])


def total_kernel(got_ref, code_ref, *, classes):
    value = decode(got_ref[0], classes)
    for k in range(1, got_ref.shape[0]):
        value = value + decode(got_ref[k], classes)
    code = encode(value)
    for k in range(code_ref.shape[0]):
        code_ref[k] = code


def picked_kernel(index_ref, feat_ref, *refs, steps):
    parts, (x_ref, cross_ref, gram_ref, rows_ref) = refs[:-4], refs[-4:]
    full = feat_ref.shape[1]
    used = steps * slots
    main = full * used // 8
    per = main // (full - main)
    tail = full - main
    total = x_ref.shape[0]
    lines = rows_ref.shape[0]
    at = 0
    for part in parts:
        rows_ref[at : at + part.shape[0], :] = part[...]
        at += part.shape[0]

    index = index_ref[...]
    line = lax.broadcasted_iota(jnp.int32, (total, lines), 1)
    one = jnp.where(line == index, 1.0, 0.0).astype(bf16)
    x_ref[:, :main] = jnp.dot(one, rows_ref[:, :main], preferred_element_type=f32).astype(bf16)
    slot = index % 8
    rest = jnp.zeros((total, tail), f32)
    home = index - slot + used + slot // per
    for u in range(per):
        here = jnp.where((line == home) & (slot % per == u), 1.0, 0.0).astype(bf16)
        rest = rest + jnp.dot(here, rows_ref[:, u * tail : (u + 1) * tail], preferred_element_type=f32)
    x_ref[:, main:] = rest.astype(bf16)
    x = x_ref[...]
    cross_ref[...] = nt_dot(x, feat_ref[...])
    gram_ref[...] = nt_dot(x, x)


def diagonal(block):
    n = block.shape[0]
    eye = lax.broadcasted_iota(jnp.int32, (n, n), 0) == lax.broadcasted_iota(jnp.int32, (n, n), 1)
    return jnp.sum(jnp.where(eye, block, 0.0), axis=1, keepdims=True)


def solve_all(gram, right):
    order = len(right)
    factor = [[None] * order for _ in range(order)]
    for j in range(order):
        value = gram[j][j]
        for k in range(j):
            value = value - factor[j][k] * factor[j][k]
        factor[j][j] = jnp.sqrt(value)
        for i in range(j + 1, order):
            value = gram[i][j]
            for k in range(j):
                value = value - factor[i][k] * factor[j][k]
            factor[i][j] = value / factor[j][j]
    forward = []
    for i in range(order):
        value = right[i]
        for j in range(i):
            value = value - factor[i][j] * forward[j]
        forward.append(value / factor[i][i])
    result = []
    for size in range(1, order + 1):
        back = [None] * size
        for i in reversed(range(size)):
            value = forward[i]
            for j in range(i + 1, size):
                value = value - factor[j][i] * back[j]
            back[i] = value / factor[i][i]
        result.append(back)
    return result


def pursuit_kernel(
    labels_ref, extra_ref, x_ref, cross_ref, gram_ref, own_ref, twin_ref, feat_ref, scores_ref, resid_ref, low_ref,
    *, steps, scale
):
    classes, full = resid_ref.shape
    groups = own_ref.shape[0]
    width = full // (2 * groups)
    device = lax.axis_index("ex")
    core = device % 2

    summed = jnp.sum(extra_ref[...].astype(f32), axis=0)
    count = jnp.concatenate(
        [128.0 * summed[:, 2 * q : 2 * q + 1] + summed[:, 2 * q + 1 : 2 * q + 2] for q in range(classes // 8)], axis=0
    )
    root = jnp.sqrt(count)
    for k in range(groups):
        for side, code_ref in ((core, own_ref), (1 - core, twin_ref)):
            block = side * groups + k
            at = pl.ds(pl.multiple_of(block * width, width), width)
            target = decode(code_ref[k], classes) / root
            resid_ref[:, at] = target
            low_ref[:, at] = target.astype(bf16)

    low = low_ref[...]
    direct = nt_dot(low, feat_ref[...])
    right = nt_dot(low, x_ref[...])
    gram = [
        [
            diagonal(gram_ref[a * classes : (a + 1) * classes, b * classes : (b + 1) * classes])
            + (ridge if a == b else 0.0)
            for b in range(steps)
        ]
        for a in range(steps)
    ]
    rhs = [diagonal(right[:, a * classes : (a + 1) * classes]) for a in range(steps)]
    weights = solve_all(gram, rhs)
    member = lax.broadcasted_iota(jnp.int32, direct.shape, 0) == labels_ref[...].reshape(1, direct.shape[1])
    for s in range(steps):
        value = direct
        for k in range(s):
            value = value - weights[s - 1][k] * cross_ref[k * classes : (k + 1) * classes]
        scores_ref[s : s + 1, :] = jnp.sum(jnp.where(member, value, 0.0), axis=0, keepdims=True) * scale
    last = weights[steps - 1]
    value = resid_ref[...]
    for k in range(steps):
        value = value - last[k] * x_ref[k * classes : (k + 1) * classes].astype(f32)
    resid_ref[...] = value


def on_device(features, labels, pick_index, *, n_ex):
    rows, full = features.shape
    steps, classes = pick_index.shape
    groups = n_ex // 2
    deep = n_ex // 4
    width = full // n_ex
    total = steps * classes
    used = steps * slots
    main = full * used // 8
    device = lax.axis_index("ex")
    limit = pltpu.CompilerParams(vmem_limit_bytes=12 << 20)
    vmem = pl.BlockSpec(memory_space=pltpu.VMEM)
    hbm = pl.BlockSpec(memory_space=pltpu.HBM)
    half = jax.ShapeDtypeStruct((groups, classes, width), f32)
    codes = jax.ShapeDtypeStruct((groups, classes * (width // 128) + 8, 128), jnp.int16)

    def swap(x, mask):
        return lax.ppermute(x, "ex", [(d, d ^ mask) for d in range(n_ex)])

    def trade(x, stride):
        teams = [[s + stride * k for k in range(n_ex // stride)] for s in range(stride)]
        return lax.all_to_all(x, "ex", 0, 0, axis_index_groups=teams, tiled=True)

    feat, send, keep, packed = pl.pallas_call(
        functools.partial(sums_kernel, n_ex=n_ex),
        in_specs=[hbm] * 3,
        out_specs=[vmem] * 4,
        out_shape=[
            pltpu.VMEM((rows, full), bf16),
            half,
            half,
            jax.ShapeDtypeStruct((8, main + 128), bf16),
        ],
        scratch_shapes=[
            pltpu.VMEM(labels.shape, jnp.int32),
            pltpu.VMEM(pick_index.shape, jnp.int32),
            pltpu.VMEM((classes + 16, rows), bf16),
            pltpu.VMEM((8, full), f32),
            pltpu.SemaphoreType.DMA((n_ex + 2,)),
        ],
        compiler_params=limit,
        name="class_sums",
    )(*[pltpu.with_memory_space_constraint(a, pltpu.HBM) for a in (labels, pick_index, features)])

    got = swap(send, 1)
    rows_z = trade(jnp.broadcast_to(packed[None], (deep,) + packed.shape), 4).reshape(deep * 8, main + 128)

    codes_out = pl.pallas_call(
        pair_kernel,
        in_specs=[vmem] * 2,
        out_specs=vmem,
        out_shape=codes,
        compiler_params=limit,
        name="pair_sums",
    )(keep, got)
    own_half = pl.pallas_call(
        functools.partial(total_kernel, classes=classes),
        in_specs=[vmem],
        out_specs=vmem,
        out_shape=codes,
        compiler_params=limit,
        name="total_sums",
    )(trade(codes_out, 2))
    own_half = trade(own_half, 2)
    twin_half = swap(own_half, 1)

    rows_y = swap(rows_z, 2)
    parts = [rows_z, rows_y, swap(rows_z, 1), swap(rows_y, 1)]

    pick_late, _ = lax.optimization_barrier((pick_index, packed))
    owner = pick_late // rows
    earlier = jnp.arange(classes)[:, None] > jnp.arange(classes)[None, :]
    rank = jnp.sum((owner[:, :, None] == owner[:, None, :]) & earlier[None], axis=2, dtype=jnp.int32)
    step_id = jnp.arange(steps, dtype=jnp.int32)[:, None]
    away = owner ^ device
    spot = ((away & 1) * 2 + ((away >> 1) & 1)) * deep + (owner >> 2)
    index = (spot * 8 + rank * steps + step_id).reshape(total, 1)

    x, cross, gram = pl.pallas_call(
        functools.partial(picked_kernel, steps=steps),
        in_specs=[vmem] * 6,
        out_specs=[vmem] * 3,
        out_shape=[
            jax.ShapeDtypeStruct((total, full), bf16),
            jax.ShapeDtypeStruct((total, rows), f32),
            jax.ShapeDtypeStruct((total, total), f32),
        ],
        scratch_shapes=[pltpu.VMEM((n_ex * 8, main + 128), bf16)],
        compiler_params=limit,
        name="picked_products",
    )(index, feat, *parts)

    extra = jnp.concatenate([p[:, main:].reshape(deep, 8, 128) for p in parts], axis=0)
    scores, resid = pl.pallas_call(
        functools.partial(pursuit_kernel, steps=steps, scale=1.0 / math.sqrt(full)),
        in_specs=[vmem] * 8,
        out_specs=[vmem] * 2,
        out_shape=[
            jax.ShapeDtypeStruct((steps, rows), f32),
            jax.ShapeDtypeStruct((classes, full), f32),
        ],
        scratch_shapes=[pltpu.VMEM((classes, full), bf16)],
        compiler_params=limit,
        name="pursuit",
    )(labels, extra, x, cross, gram, own_half, twin_half, feat)
    return scores, resid


def solution(mesh):
    return jax.shard_map(
        functools.partial(on_device, n_ex=mesh.shape["ex"]),
        mesh=mesh,
        in_specs=(P(("grp", "ex"), None), P(("grp", "ex")), P("grp", None)),
        out_specs=(P(None, ("grp", "ex")), P("grp", None)),
        check_vma=False,
    )
```

```python
import functools
import math

import jax
import jax.numpy as jnp
from jax import lax
from jax.experimental import pallas as pl
from jax.experimental.pallas import tpu as pltpu
from jax.sharding import PartitionSpec as P

ridge = 1.0
slots = 2
f32 = jnp.float32
bf16 = jnp.bfloat16


def nt_dot(a, b):
    return lax.dot_general(a, b, (((1,), (1,)), ((), ())), preferred_element_type=f32)


def column(tile, height, start=0):
    return jnp.concatenate([tile[:, start + q : start + q + 1] for q in range(height // 8)], axis=0)


def spread(values, start=0):
    lane = lax.broadcasted_iota(jnp.int32, (8, 128), 1)
    tile = jnp.zeros((8, 128), f32)
    for q in range(values.shape[0] // 8):
        tile = jnp.where(lane == start + q, values[8 * q : 8 * q + 8], tile)
    return tile


def encode(x, count_tile=None):
    height, width = x.shape
    top = jnp.max(jnp.abs(x), axis=1, keepdims=True)
    power = jnp.ceil(jnp.log2(jnp.maximum(top, 1e-30)) + 0.01)
    whole_x = jnp.round(x * jnp.exp2(15.0 - power))
    mark = spread(power)
    if count_tile is not None:
        mark = mark + count_tile
    chunks = [whole_x[:, j * 128 : (j + 1) * 128] for j in range(width // 128)]
    return jnp.concatenate(chunks + [mark], axis=0).astype(jnp.int32).astype(jnp.int16)


def decode(code, height):
    value = code.astype(jnp.int32).astype(f32)
    count = value.shape[0] // height
    mark = value[count * height :]
    x = jnp.concatenate([value[j * height : (j + 1) * height] for j in range(count)], axis=1)
    return x * jnp.exp2(column(mark, height) - 15.0), mark


def sums_kernel(
    labels_hbm, pick_hbm, feat_hbm, send_ref, keep_ref, rows_ref, labels_ref, pick_ref, feat_ref, left, held, sems, *, n_ex
):
    rows, full = feat_ref.shape
    steps, classes = pick_ref.shape
    width = full // n_ex
    groups = n_ex // 2
    device = lax.axis_index("ex")
    core = device % 2
    small = [
        pltpu.make_async_copy(pick_hbm, pick_ref, sems.at[n_ex]),
        pltpu.make_async_copy(labels_hbm, labels_ref, sems.at[n_ex + 1]),
    ]
    for copy in small:
        copy.start()
    columns = []
    copies = []
    for i in range(n_ex):
        block = (1 - core) * groups + i if i < groups else core * groups + i - groups
        at = pl.ds(pl.multiple_of(block * width, width), width)
        columns.append(at)
        copies.append(pltpu.make_async_copy(feat_hbm.at[:, at], feat_ref.at[:, at], sems.at[i]))
        copies[-1].start()

    for copy in small:
        copy.wait()
    local = pick_ref[...] - device * rows
    mine = (local >= 0) & (local < rows)
    lane = lax.broadcasted_iota(jnp.int32, local.shape, 1)
    first = jnp.min(jnp.where(mine, lane, classes), axis=1, keepdims=True)
    last = jnp.max(jnp.where(mine, lane, -1), axis=1, keepdims=True)
    spot0 = jnp.max(jnp.where(mine & (lane == first), local, -1), axis=1, keepdims=True)
    spot1 = jnp.max(jnp.where(mine & (lane == last) & (last > first), local, -1), axis=1, keepdims=True)
    member = lax.broadcasted_iota(jnp.int32, (classes, rows), 0) == labels_ref[...].reshape(1, rows)
    line = lax.broadcasted_iota(jnp.int32, (steps, rows), 1)
    left[...] = jnp.concatenate(
        [
            jnp.where(member, 1.0, 0.0),
            jnp.where(line == spot0, 1.0, 0.0),
            jnp.where(line == spot1, 1.0, 0.0),
            jnp.zeros((16 - 2 * steps, rows), f32),
        ],
        axis=0,
    ).astype(bf16)
    count = jnp.sum(jnp.where(member, 1.0, 0.0), axis=1, keepdims=True)
    tile = spread(count, classes // 8)
    for ref in (send_ref, keep_ref):
        ref[groups * classes :, :128] = tile
        if width > 128:
            ref[groups * classes :, 128:] = jnp.zeros((8, width - 128), f32)

    for i in range(n_ex):
        copies[i].wait()
        both = jnp.dot(left[...], feat_ref[:, columns[i]], preferred_element_type=f32)
        k = i % groups
        ref = send_ref if i < groups else keep_ref
        ref[k * classes : (k + 1) * classes, :] = both[:classes]
        held[:, columns[i]] = both[classes : classes + 8]

    used = steps * slots
    main = full * used // 8
    tail = full - main
    lines = [held[0:used, :main]]
    for q in range(slots):
        lines.append(jnp.concatenate([held[q * steps + u : q * steps + u + 1, main:] for u in range(steps)], axis=1))
    rows_ref[...] = jnp.concatenate(lines, axis=0).astype(bf16)


def pair_kernel(keep_ref, got_ref, code_ref, *, classes):
    groups = code_ref.shape[0]
    base = groups * classes
    tile = keep_ref[base : base + 8, :128] + got_ref[base : base + 8, :128]
    for k in range(groups):
        at = slice(k * classes, (k + 1) * classes)
        code_ref[k] = encode(keep_ref[at, :] + got_ref[at, :], tile)


def total_kernel(got_ref, code_ref, *, classes):
    value, mark = decode(got_ref[0], classes)
    for k in range(1, got_ref.shape[0]):
        more, more_mark = decode(got_ref[k], classes)
        value = value + more
        mark = mark + more_mark
    code = encode(value / jnp.sqrt(column(mark, classes, classes // 8)))
    for k in range(code_ref.shape[0]):
        code_ref[k] = code


def diagonal(block):
    n = block.shape[0]
    eye = lax.broadcasted_iota(jnp.int32, (n, n), 0) == lax.broadcasted_iota(jnp.int32, (n, n), 1)
    return jnp.sum(jnp.where(eye, block, 0.0), axis=1, keepdims=True)


def factor_all(gram):
    order = len(gram)
    factor = [[None] * order for _ in range(order)]
    for j in range(order):
        value = gram[j][j]
        for k in range(j):
            value = value - factor[j][k] * factor[j][k]
        root = jnp.sqrt(value)
        factor[j][j] = 1.0 / root
        for i in range(j + 1, order):
            value = gram[i][j]
            for k in range(j):
                value = value - factor[i][k] * factor[j][k]
            factor[i][j] = value * factor[j][j]
    return factor


def solve_all(factor, right):
    order = len(right)
    forward = []
    for i in range(order):
        value = right[i]
        for j in range(i):
            value = value - factor[i][j] * forward[j]
        forward.append(value * factor[i][i])
    result = []
    for size in range(1, order + 1):
        back = [None] * size
        for i in reversed(range(size)):
            value = forward[i]
            for j in range(i + 1, size):
                value = value - factor[j][i] * back[j]
            back[i] = value * factor[i][i]
        result.append(back)
    return result


def picked_kernel(pick_hbm, feat_hbm, *refs, n_ex):
    parts = refs[:-9]
    x_ref, cross_ref, factor_ref, pick_ref, rows_ref, feat_ref, feat_sems, part_sems, pick_sem = refs[-9:]
    rows, full = feat_ref.shape
    steps, classes = pick_ref.shape
    lines, main = rows_ref.shape
    tail = full - main
    width = full // n_ex
    device = lax.axis_index("ex")

    pick_copy = pltpu.make_async_copy(pick_hbm, pick_ref, pick_sem)
    pick_copy.start()
    part_copies = []
    at = 0
    for i, part in enumerate(parts):
        part_copies.append(pltpu.make_async_copy(part, rows_ref.at[at : at + part.shape[0]], part_sems.at[i]))
        part_copies[-1].start()
        at += part.shape[0]
    copies = []
    for i in range(n_ex):
        col = slice(i * width, (i + 1) * width)
        copies.append(pltpu.make_async_copy(feat_hbm.at[:, col], feat_ref.at[:, col], feat_sems.at[i]))
        copies[-1].start()

    pick_copy.wait()
    pick = pick_ref[...]
    lane = lax.broadcasted_iota(jnp.int32, pick.shape, 1)
    owner = jnp.zeros_like(pick)
    rank = jnp.zeros_like(pick)
    for d in range(n_ex):
        here = (pick >= d * rows) & (pick < (d + 1) * rows)
        first = jnp.min(jnp.where(here, lane, classes), axis=1, keepdims=True)
        owner = jnp.where(here, d, owner)
        rank = jnp.where(here & (lane > first), 1, rank)
    away = owner ^ device
    spot = jnp.zeros_like(pick)
    bits = n_ex.bit_length() - 1
    for b in range(1, bits):
        spot = spot + (((away >> b) & 1) << (bits - 1 - b))
    spot = spot + ((away & 1) << (bits - 1))
    step = lax.broadcasted_iota(jnp.int32, pick.shape, 0)
    index = spot * 8 + rank * steps + step
    home = spot * 8 + slots * steps + rank
    line = lax.broadcasted_iota(jnp.int32, (lines, classes), 0)

    def choose(where):
        hits = [jnp.where(line == where[s : s + 1, :], 1.0, 0.0) for s in range(steps)]
        pad = jnp.zeros((lines, 128 - steps * classes), f32)
        return jnp.transpose(jnp.concatenate(hits + [pad], axis=1))[: steps * classes].astype(bf16)

    one = choose(index)
    rest = choose(home)
    for copy in part_copies:
        copy.wait()
    x_ref[:, :main] = jnp.dot(one, rows_ref[...], preferred_element_type=f32).astype(bf16)
    for s in range(steps):
        at = slice(s * classes, (s + 1) * classes)
        x_ref[at, main:] = jnp.dot(rest[at], rows_ref[:, s * tail : (s + 1) * tail], preferred_element_type=f32).astype(bf16)

    x = x_ref[...]
    full_gram = nt_dot(x, x)
    gram = [
        [
            diagonal(full_gram[a * classes : (a + 1) * classes, b * classes : (b + 1) * classes])
            + (ridge if a == b else 0.0)
            for b in range(a + 1)
        ]
        for a in range(steps)
    ]
    factor = factor_all(gram)
    lane = lax.broadcasted_iota(jnp.int32, (classes, 128), 1)
    packed = jnp.zeros((classes, 128), f32)
    for i in range(steps):
        for j in range(i + 1):
            packed = jnp.where(lane == i * steps + j, factor[i][j], packed)
    factor_ref[...] = packed

    for i in range(n_ex):
        col = slice(i * width, (i + 1) * width)
        copies[i].wait()
        part = nt_dot(x_ref[:, col], feat_ref[:, col])
        cross_ref[...] = part if i == 0 else cross_ref[...] + part


def start_half(feat_hbm, feat_ref, sems, side, groups):
    half = feat_ref.shape[1]
    width = half // groups
    copies = []
    for k in range(groups):
        src = pl.ds(pl.multiple_of(side * half + k * width, width), width)
        dst = slice(k * width, (k + 1) * width)
        copies.append(pltpu.make_async_copy(feat_hbm.at[:, src], feat_ref.at[:, dst], sems.at[k]))
        copies[-1].start()
    return copies


def half_kernel(feat_hbm, code_ref, direct_ref, feat_ref, sems, *, classes):
    groups = code_ref.shape[0]
    width = feat_ref.shape[1] // groups
    copies = start_half(feat_hbm, feat_ref, sems, lax.axis_index("ex") % 2, groups)
    for k in range(groups):
        low = decode(code_ref[k], classes)[0].astype(bf16)
        copies[k].wait()
        part = nt_dot(low, feat_ref[:, k * width : (k + 1) * width])
        direct_ref[...] = part if k == 0 else direct_ref[...] + part


def pursuit_kernel(
    feat_hbm, labels_ref, x_ref, cross_ref, factor_ref, start_ref, own_ref, twin_ref,
    scores_ref, resid_ref, low_ref, feat_ref, sems, *, steps, scale
):
    classes, full = resid_ref.shape
    groups = own_ref.shape[0]
    half = full // 2
    width = half // groups
    core = lax.axis_index("ex") % 2
    copies = start_half(feat_hbm, feat_ref, sems, 1 - core, groups)
    direct = start_ref[...]
    for side, code_ref in ((core, own_ref), (1 - core, twin_ref)):
        for k in range(groups):
            at = pl.ds(pl.multiple_of(side * half + k * width, width), width)
            target = decode(code_ref[k], classes)[0]
            resid_ref[:, at] = target
            low = target.astype(bf16)
            low_ref[:, at] = low

    right = nt_dot(low_ref[...], x_ref[...])
    for k in range(groups):
        at = pl.ds(pl.multiple_of((1 - core) * half + k * width, width), width)
        copies[k].wait()
        direct = direct + nt_dot(low_ref[:, at], feat_ref[:, k * width : (k + 1) * width])

    rhs = [diagonal(right[:, a * classes : (a + 1) * classes]) for a in range(steps)]
    factor = [[factor_ref[:, i * steps + j : i * steps + j + 1] for j in range(i + 1)] for i in range(steps)]
    weights = solve_all(factor, rhs)
    member = lax.broadcasted_iota(jnp.int32, direct.shape, 0) == labels_ref[...].reshape(1, direct.shape[1])
    for s in range(steps):
        value = direct
        for k in range(s):
            value = value - weights[s - 1][k] * cross_ref[k * classes : (k + 1) * classes]
        scores_ref[s : s + 1, :] = jnp.sum(jnp.where(member, value, 0.0), axis=0, keepdims=True) * scale
    last = weights[steps - 1]
    value = resid_ref[...]
    for k in range(steps):
        value = value - last[k] * x_ref[k * classes : (k + 1) * classes].astype(f32)
    resid_ref[...] = value


def on_device(features, labels, pick_index, *, n_ex):
    rows, full = features.shape
    steps, classes = pick_index.shape
    groups = n_ex // 2
    width = full // n_ex
    total = steps * classes
    main = full * steps * slots // 8
    limit = pltpu.CompilerParams(vmem_limit_bytes=24 << 20)
    vmem = pl.BlockSpec(memory_space=pltpu.VMEM)
    hbm = pl.BlockSpec(memory_space=pltpu.HBM)
    anywhere = pl.BlockSpec(memory_space=pl.ANY)
    half = jax.ShapeDtypeStruct((groups * classes + 8, width), f32)
    codes = jax.ShapeDtypeStruct((groups, classes * (width // 128) + 8, 128), jnp.int16)
    features, picks, labels_in = [
        pltpu.with_memory_space_constraint(a, pltpu.HBM) for a in (features, pick_index, labels)
    ]

    def swap(x, mask):
        return lax.ppermute(x, "ex", [(d, d ^ mask) for d in range(n_ex)])

    def trade(x):
        teams = [[s + 2 * k for k in range(groups)] for s in range(2)]
        return lax.all_to_all(x, "ex", 0, 0, axis_index_groups=teams, tiled=True)

    send, keep, packed = pl.pallas_call(
        functools.partial(sums_kernel, n_ex=n_ex),
        in_specs=[hbm] * 3,
        out_specs=[vmem] * 3,
        out_shape=[half, half, jax.ShapeDtypeStruct((8, main), bf16)],
        scratch_shapes=[
            pltpu.VMEM(labels.shape, jnp.int32),
            pltpu.VMEM(pick_index.shape, jnp.int32),
            pltpu.VMEM((rows, full), bf16),
            pltpu.VMEM((classes + 16, rows), bf16),
            pltpu.VMEM((8, full), f32),
            pltpu.SemaphoreType.DMA((n_ex + 2,)),
        ],
        compiler_params=limit,
        name="class_sums",
    )(labels_in, picks, features)

    got = swap(send, 1)
    near = packed
    mask = n_ex // 2
    while mask > 4:
        near = jnp.concatenate([near, swap(near, mask)], axis=0)
        mask //= 2
    by_z = swap(near, 4)
    by_y = swap(near, 2)
    cut = near.shape[0] // 2
    last = jnp.concatenate([swap(by_y[:cut], 4), swap(by_z[cut:], 2)], axis=0)
    parts = [near, by_z, by_y, last]
    parts = parts + [swap(p, 1) for p in parts]

    codes_out = pl.pallas_call(
        functools.partial(pair_kernel, classes=classes),
        in_specs=[vmem] * 2,
        out_specs=vmem,
        out_shape=codes,
        compiler_params=limit,
        name="pair_sums",
    )(keep, got)
    own_half = trade(
        pl.pallas_call(
            functools.partial(total_kernel, classes=classes),
            in_specs=[vmem],
            out_specs=vmem,
            out_shape=codes,
            compiler_params=limit,
            name="total_sums",
        )(trade(codes_out))
    )
    twin_half = swap(own_half, 1)

    feat_half = pltpu.VMEM((rows, full // 2), bf16)
    direct = pl.pallas_call(
        functools.partial(half_kernel, classes=classes),
        in_specs=[hbm, vmem],
        out_specs=vmem,
        out_shape=jax.ShapeDtypeStruct((classes, rows), f32),
        scratch_shapes=[feat_half, pltpu.SemaphoreType.DMA((groups,))],
        compiler_params=limit,
        name="own_half_products",
    )(features, own_half)

    x, cross, factor = pl.pallas_call(
        functools.partial(picked_kernel, n_ex=n_ex),
        in_specs=[hbm, hbm] + [anywhere] * len(parts),
        out_specs=[vmem] * 3,
        out_shape=[
            jax.ShapeDtypeStruct((total, full), bf16),
            jax.ShapeDtypeStruct((total, rows), f32),
            jax.ShapeDtypeStruct((classes, 128), f32),
        ],
        scratch_shapes=[
            pltpu.VMEM(pick_index.shape, jnp.int32),
            pltpu.VMEM((n_ex * 8, main), bf16),
            pltpu.VMEM((rows, full), bf16),
            pltpu.SemaphoreType.DMA((n_ex,)),
            pltpu.SemaphoreType.DMA((len(parts),)),
            pltpu.SemaphoreType.DMA(()),
        ],
        compiler_params=limit,
        name="picked_products",
    )(picks, features, *parts)

    scores, resid = pl.pallas_call(
        functools.partial(pursuit_kernel, steps=steps, scale=1.0 / math.sqrt(full)),
        in_specs=[hbm] + [vmem] * 7,
        out_specs=[vmem] * 2,
        out_shape=[
            jax.ShapeDtypeStruct((steps, rows), f32),
            jax.ShapeDtypeStruct((classes, full), f32),
        ],
        scratch_shapes=[
            pltpu.VMEM((classes, full), bf16),
            feat_half,
            pltpu.SemaphoreType.DMA((groups,)),
        ],
        compiler_params=limit,
        name="pursuit",
    )(features, labels, x, cross, factor, direct, own_half, twin_half)
    return scores, resid


def solution(mesh):
    return jax.shard_map(
        functools.partial(on_device, n_ex=mesh.shape["ex"]),
        mesh=mesh,
        in_specs=(P(("grp", "ex"), None), P(("grp", "ex")), P("grp", None)),
        out_specs=(P(None, ("grp", "ex")), P("grp", None)),
        check_vma=False,
    )
```

```python
import functools
import math

import jax
import jax.numpy as jnp
from jax import lax
from jax.experimental import pallas as pl
from jax.experimental.pallas import tpu as pltpu
from jax.sharding import PartitionSpec as P

ridge = 1.0
slots = 2
f32 = jnp.float32
bf16 = jnp.bfloat16


def nt_dot(a, b):
    return lax.dot_general(a, b, (((1,), (1,)), ((), ())), preferred_element_type=f32)


def column(tile, height, start=0):
    return jnp.concatenate([tile[:, start + q : start + q + 1] for q in range(height // 8)], axis=0)


def spread(values, start=0):
    lane = lax.broadcasted_iota(jnp.int32, (8, 128), 1)
    tile = jnp.zeros((8, 128), f32)
    for q in range(values.shape[0] // 8):
        tile = jnp.where(lane == start + q, values[8 * q : 8 * q + 8], tile)
    return tile


def encode(x, count_tile=None):
    height, width = x.shape
    top = jnp.max(jnp.abs(x), axis=1, keepdims=True)
    power = jnp.ceil(jnp.log2(jnp.maximum(top, 1e-30)) + 0.01)
    whole_x = jnp.round(x * jnp.exp2(15.0 - power))
    mark = spread(power)
    if count_tile is not None:
        mark = mark + count_tile
    chunks = [whole_x[:, j * 128 : (j + 1) * 128] for j in range(width // 128)]
    return jnp.concatenate(chunks + [mark], axis=0).astype(jnp.int32).astype(jnp.int16)


def decode(code, height):
    value = code.astype(jnp.int32).astype(f32)
    count = value.shape[0] // height
    mark = value[count * height :]
    x = jnp.concatenate([value[j * height : (j + 1) * height] for j in range(count)], axis=1)
    return x * jnp.exp2(column(mark, height) - 15.0), mark


def sums_kernel(
    labels_hbm, pick_hbm, feat_hbm, send_ref, keep_ref, rows_ref, labels_ref, pick_ref, feat_ref, left, held, sems, *, n_ex
):
    rows, full = feat_ref.shape
    steps, classes = pick_ref.shape
    width = full // n_ex
    groups = n_ex // 2
    device = lax.axis_index("ex")
    core = device % 2
    small = [
        pltpu.make_async_copy(pick_hbm, pick_ref, sems.at[n_ex]),
        pltpu.make_async_copy(labels_hbm, labels_ref, sems.at[n_ex + 1]),
    ]
    for copy in small:
        copy.start()
    columns = []
    copies = []
    for i in range(n_ex):
        block = (1 - core) * groups + i if i < groups else core * groups + i - groups
        at = pl.ds(pl.multiple_of(block * width, width), width)
        columns.append(at)
        copies.append(pltpu.make_async_copy(feat_hbm.at[:, at], feat_ref.at[:, at], sems.at[i]))
        copies[-1].start()

    for copy in small:
        copy.wait()
    local = pick_ref[...] - device * rows
    mine = (local >= 0) & (local < rows)
    lane = lax.broadcasted_iota(jnp.int32, local.shape, 1)
    first = jnp.min(jnp.where(mine, lane, classes), axis=1, keepdims=True)
    last = jnp.max(jnp.where(mine, lane, -1), axis=1, keepdims=True)
    spot0 = jnp.max(jnp.where(mine & (lane == first), local, -1), axis=1, keepdims=True)
    spot1 = jnp.max(jnp.where(mine & (lane == last) & (last > first), local, -1), axis=1, keepdims=True)
    member = lax.broadcasted_iota(jnp.int32, (classes, rows), 0) == labels_ref[...].reshape(1, rows)
    line = lax.broadcasted_iota(jnp.int32, (steps, rows), 1)
    left[...] = jnp.concatenate(
        [
            jnp.where(member, 1.0, 0.0),
            jnp.where(line == spot0, 1.0, 0.0),
            jnp.where(line == spot1, 1.0, 0.0),
            jnp.zeros((16 - 2 * steps, rows), f32),
        ],
        axis=0,
    ).astype(bf16)
    count = jnp.sum(jnp.where(member, 1.0, 0.0), axis=1, keepdims=True)
    tile = spread(count, classes // 8)
    for ref in (send_ref, keep_ref):
        ref[groups * classes :, :128] = tile
        if width > 128:
            ref[groups * classes :, 128:] = jnp.zeros((8, width - 128), f32)

    for i in range(n_ex):
        copies[i].wait()
        both = jnp.dot(left[...], feat_ref[:, columns[i]], preferred_element_type=f32)
        k = i % groups
        ref = send_ref if i < groups else keep_ref
        ref[k * classes : (k + 1) * classes, :] = both[:classes]
        held[:, columns[i]] = both[classes : classes + 8]

    used = steps * slots
    main = full * used // 8
    tail = full - main
    lines = [held[0:used, :main]]
    for q in range(slots):
        lines.append(jnp.concatenate([held[q * steps + u : q * steps + u + 1, main:] for u in range(steps)], axis=1))
    rows_ref[...] = jnp.concatenate(lines, axis=0).astype(bf16)


def pair_kernel(keep_ref, got_ref, code_ref, *, classes):
    groups = code_ref.shape[0]
    base = groups * classes
    tile = keep_ref[base : base + 8, :128] + got_ref[base : base + 8, :128]
    for k in range(groups):
        at = slice(k * classes, (k + 1) * classes)
        code_ref[k] = encode(keep_ref[at, :] + got_ref[at, :], tile)


def total_kernel(got_ref, code_ref, *, classes):
    value, mark = decode(got_ref[0], classes)
    for k in range(1, got_ref.shape[0]):
        more, more_mark = decode(got_ref[k], classes)
        value = value + more
        mark = mark + more_mark
    code = encode(value / jnp.sqrt(column(mark, classes, classes // 8)))
    for k in range(code_ref.shape[0]):
        code_ref[k] = code


def diagonal(block):
    n = block.shape[0]
    eye = lax.broadcasted_iota(jnp.int32, (n, n), 0) == lax.broadcasted_iota(jnp.int32, (n, n), 1)
    return jnp.sum(jnp.where(eye, block, 0.0), axis=1, keepdims=True)


def factor_all(gram):
    order = len(gram)
    factor = [[None] * order for _ in range(order)]
    for j in range(order):
        value = gram[j][j]
        for k in range(j):
            value = value - factor[j][k] * factor[j][k]
        root = jnp.sqrt(value)
        factor[j][j] = 1.0 / root
        for i in range(j + 1, order):
            value = gram[i][j]
            for k in range(j):
                value = value - factor[i][k] * factor[j][k]
            factor[i][j] = value * factor[j][j]
    return factor


def solve_all(factor, right):
    order = len(right)
    forward = []
    for i in range(order):
        value = right[i]
        for j in range(i):
            value = value - factor[i][j] * forward[j]
        forward.append(value * factor[i][i])
    result = []
    for size in range(1, order + 1):
        back = [None] * size
        for i in reversed(range(size)):
            value = forward[i]
            for j in range(i + 1, size):
                value = value - factor[j][i] * back[j]
            back[i] = value * factor[i][i]
        result.append(back)
    return result


def picked_kernel(pick_hbm, feat_hbm, *refs, n_ex):
    parts = refs[:-9]
    x_ref, cross_ref, factor_ref, pick_ref, rows_ref, feat_ref, feat_sems, part_sems, pick_sem = refs[-9:]
    rows, full = feat_ref.shape
    steps, classes = pick_ref.shape
    lines, main = rows_ref.shape
    tail = full - main
    width = full // n_ex
    device = lax.axis_index("ex")

    pick_copy = pltpu.make_async_copy(pick_hbm, pick_ref, pick_sem)
    pick_copy.start()
    part_copies = []
    at = 0
    for i, part in enumerate(parts):
        part_copies.append(pltpu.make_async_copy(part, rows_ref.at[at : at + part.shape[0]], part_sems.at[i]))
        part_copies[-1].start()
        at += part.shape[0]
    copies = []
    for i in range(n_ex):
        col = slice(i * width, (i + 1) * width)
        copies.append(pltpu.make_async_copy(feat_hbm.at[:, col], feat_ref.at[:, col], feat_sems.at[i]))
        copies[-1].start()
    span = full // 4

    pick_copy.wait()
    pick = pick_ref[...]
    lane = lax.broadcasted_iota(jnp.int32, pick.shape, 1)
    owner = jnp.zeros_like(pick)
    rank = jnp.zeros_like(pick)
    for d in range(n_ex):
        here = (pick >= d * rows) & (pick < (d + 1) * rows)
        first = jnp.min(jnp.where(here, lane, classes), axis=1, keepdims=True)
        owner = jnp.where(here, d, owner)
        rank = jnp.where(here & (lane > first), 1, rank)
    away = owner ^ device
    spot = jnp.zeros_like(pick)
    bits = n_ex.bit_length() - 1
    for b in range(1, bits):
        spot = spot + (((away >> b) & 1) << (bits - 1 - b))
    spot = spot + ((away & 1) << (bits - 1))
    step = lax.broadcasted_iota(jnp.int32, pick.shape, 0)
    index = spot * 8 + rank * steps + step
    home = spot * 8 + slots * steps + rank
    line = lax.broadcasted_iota(jnp.int32, (lines, classes), 0)

    def choose(where):
        hits = [jnp.where(line == where[s : s + 1, :], 1.0, 0.0) for s in range(steps)]
        pad = jnp.zeros((lines, 128 - steps * classes), f32)
        return jnp.transpose(jnp.concatenate(hits + [pad], axis=1))[: steps * classes].astype(bf16)

    one = choose(index)
    rest = choose(home)
    for copy in part_copies:
        copy.wait()
    x_ref[:, :main] = jnp.dot(one, rows_ref[...], preferred_element_type=f32).astype(bf16)
    for s in range(steps):
        at = slice(s * classes, (s + 1) * classes)
        x_ref[at, main:] = jnp.dot(rest[at], rows_ref[:, s * tail : (s + 1) * tail], preferred_element_type=f32).astype(bf16)

    x = x_ref[...]
    full_gram = nt_dot(x, x)
    gram = [
        [
            diagonal(full_gram[a * classes : (a + 1) * classes, b * classes : (b + 1) * classes])
            + (ridge if a == b else 0.0)
            for b in range(a + 1)
        ]
        for a in range(steps)
    ]
    factor = factor_all(gram)
    lane = lax.broadcasted_iota(jnp.int32, (classes, 128), 1)
    packed = jnp.zeros((classes, 128), f32)
    for i in range(steps):
        for j in range(i + 1):
            packed = jnp.where(lane == i * steps + j, factor[i][j], packed)
    factor_ref[...] = packed

    for i in range(4):
        for copy in copies[i * n_ex // 4 : (i + 1) * n_ex // 4]:
            copy.wait()
        col = slice(i * span, (i + 1) * span)
        part = nt_dot(x_ref[: cross_ref.shape[0], col], feat_ref[:, col])
        cross_ref[...] = part if i == 0 else cross_ref[...] + part


def half_kernel(feat_hbm, code_ref, x_ref, direct_ref, right_ref, target_ref, other_ref, low_ref, feat_ref, sems, *, classes):
    groups = code_ref.shape[0]
    half = feat_ref.shape[1]
    width = half // groups
    core = lax.axis_index("ex") % 2
    copies = []
    for side, ref in ((core, feat_ref), (1 - core, other_ref)):
        for k in range(groups):
            src = pl.ds(pl.multiple_of(side * half + k * width, width), width)
            dst = slice(k * width, (k + 1) * width)
            copies.append(pltpu.make_async_copy(feat_hbm.at[:, src], ref.at[:, dst], sems.at[len(copies)]))
            copies[-1].start()
    for k in range(groups):
        target = decode(code_ref[k], classes)[0]
        target_ref[:, k * width : (k + 1) * width] = target
        low_ref[:, k * width : (k + 1) * width] = target.astype(bf16)
    right_ref[...] = nt_dot(low_ref[...], x_ref[:, pl.ds(pl.multiple_of(core * half, half), half)])
    for copy in copies[:groups]:
        copy.wait()
    direct_ref[...] = nt_dot(low_ref[...], feat_ref[...])
    for copy in copies[groups:]:
        copy.wait()


def pursuit_kernel(
    labels_ref, x_ref, cross_ref, factor_ref, direct_own, right_own, target_own, feat_ref, code_ref,
    scores_ref, resid_hbm, resid_ref, low_ref, sems, *, steps, scale
):
    classes, full = resid_ref.shape
    groups = code_ref.shape[0]
    half = full // 2
    width = half // groups
    core = lax.axis_index("ex") % 2
    mine = pl.ds(pl.multiple_of(core * half, half), half)
    rest = pl.ds(pl.multiple_of((1 - core) * half, half), half)
    for k in range(groups):
        at = pl.ds(pl.multiple_of((1 - core) * half + k * width, width), width)
        target = decode(code_ref[k], classes)[0]
        resid_ref[:, at] = target
        low_ref[:, k * width : (k + 1) * width] = target.astype(bf16)
    right = right_own[...] + nt_dot(low_ref[...], x_ref[:, rest])
    rhs = [diagonal(right[:, a * classes : (a + 1) * classes]) for a in range(steps)]
    factor = [[factor_ref[:, i * steps + j : i * steps + j + 1] for j in range(i + 1)] for i in range(steps)]
    weights = solve_all(factor, rhs)
    last = weights[steps - 1]
    copies = []
    for source, side, at in ((target_own, core, mine), (resid_ref, 1 - core, rest)):
        for q in range(2):
            span = half // 2
            here = pl.ds(pl.multiple_of(side * half + q * span, span), span)
            value = source[:, q * span : (q + 1) * span] if source is target_own else source[:, here]
            for k in range(steps):
                value = value - last[k] * x_ref[k * classes : (k + 1) * classes, here].astype(f32)
            resid_ref[:, here] = value
            copies.append(pltpu.make_async_copy(resid_ref.at[:, here], resid_hbm.at[:, here], sems.at[len(copies)]))
            copies[-1].start()

    direct = direct_own[...] + nt_dot(low_ref[...], feat_ref[...])
    member = lax.broadcasted_iota(jnp.int32, direct.shape, 0) == labels_ref[...].reshape(1, direct.shape[1])
    for s in range(steps):
        value = direct
        for k in range(s):
            value = value - weights[s - 1][k] * cross_ref[k * classes : (k + 1) * classes]
        scores_ref[s : s + 1, :] = jnp.sum(jnp.where(member, value, 0.0), axis=0, keepdims=True) * scale
    for copy in copies:
        copy.wait()


def on_device(features, labels, pick_index, *, n_ex):
    rows, full = features.shape
    steps, classes = pick_index.shape
    groups = n_ex // 2
    width = full // n_ex
    total = steps * classes
    main = full * steps * slots // 8
    limit = pltpu.CompilerParams(vmem_limit_bytes=24 << 20)
    vmem = pl.BlockSpec(memory_space=pltpu.VMEM)
    hbm = pl.BlockSpec(memory_space=pltpu.HBM)
    anywhere = pl.BlockSpec(memory_space=pl.ANY)
    half = jax.ShapeDtypeStruct((groups * classes + 8, width), f32)
    codes = jax.ShapeDtypeStruct((groups, classes * (width // 128) + 8, 128), jnp.int16)
    features, picks, labels_in = [
        pltpu.with_memory_space_constraint(a, pltpu.HBM) for a in (features, pick_index, labels)
    ]

    def swap(x, mask):
        return lax.ppermute(x, "ex", [(d, d ^ mask) for d in range(n_ex)])

    def trade(x):
        teams = [[s + 2 * k for k in range(groups)] for s in range(2)]
        return lax.all_to_all(x, "ex", 0, 0, axis_index_groups=teams, tiled=True)

    send, keep, packed = pl.pallas_call(
        functools.partial(sums_kernel, n_ex=n_ex),
        in_specs=[hbm] * 3,
        out_specs=[vmem] * 3,
        out_shape=[half, half, jax.ShapeDtypeStruct((8, main), bf16)],
        scratch_shapes=[
            pltpu.VMEM(labels.shape, jnp.int32),
            pltpu.VMEM(pick_index.shape, jnp.int32),
            pltpu.VMEM((rows, full), bf16),
            pltpu.VMEM((classes + 16, rows), bf16),
            pltpu.VMEM((8, full), f32),
            pltpu.SemaphoreType.DMA((n_ex + 2,)),
        ],
        compiler_params=limit,
        name="class_sums",
    )(labels_in, picks, features)

    got = swap(send, 1)
    near = packed
    mask = n_ex // 2
    while mask > 4:
        near = jnp.concatenate([near, swap(near, mask)], axis=0)
        mask //= 2
    parts = [near, swap(near, 4), swap(near, 2), swap(near, 6)]

    codes_out = pl.pallas_call(
        functools.partial(pair_kernel, classes=classes),
        in_specs=[vmem] * 2,
        out_specs=vmem,
        out_shape=codes,
        compiler_params=limit,
        name="pair_sums",
    )(keep, got)
    summed = pl.pallas_call(
        functools.partial(total_kernel, classes=classes),
        in_specs=[vmem],
        out_specs=vmem,
        out_shape=codes,
        compiler_params=limit,
        name="total_sums",
    )(trade(codes_out))
    parts, summed = lax.optimization_barrier((parts, summed))
    parts = parts + [swap(p, 1) for p in parts]
    own_half = trade(summed)

    x, cross, factor = pl.pallas_call(
        functools.partial(picked_kernel, n_ex=n_ex),
        in_specs=[hbm, hbm] + [anywhere] * len(parts),
        out_specs=[vmem] * 3,
        out_shape=[
            jax.ShapeDtypeStruct((total, full), bf16),
            jax.ShapeDtypeStruct((total - classes, rows), f32),
            jax.ShapeDtypeStruct((classes, 128), f32),
        ],
        scratch_shapes=[
            pltpu.VMEM(pick_index.shape, jnp.int32),
            pltpu.VMEM((n_ex * 8, main), bf16),
            pltpu.VMEM((rows, full), bf16),
            pltpu.SemaphoreType.DMA((n_ex,)),
            pltpu.SemaphoreType.DMA((len(parts),)),
            pltpu.SemaphoreType.DMA(()),
        ],
        compiler_params=limit,
        name="picked_products",
    )(picks, features, *parts)

    own_half, x = lax.optimization_barrier((own_half, x))
    twin_half = swap(own_half, 1)
    feat_half = pltpu.VMEM((rows, full // 2), bf16)
    direct, right, target, feat_rest = pl.pallas_call(
        functools.partial(half_kernel, classes=classes),
        in_specs=[hbm, vmem, vmem],
        out_specs=[vmem] * 4,
        out_shape=[
            jax.ShapeDtypeStruct((classes, rows), f32),
            jax.ShapeDtypeStruct((classes, total), f32),
            jax.ShapeDtypeStruct((classes, full // 2), f32),
            feat_half,
        ],
        scratch_shapes=[
            pltpu.VMEM((classes, full // 2), bf16),
            feat_half,
            pltpu.SemaphoreType.DMA((n_ex,)),
        ],
        compiler_params=limit,
        name="own_half_products",
    )(features, own_half, x)

    scores, resid = pl.pallas_call(
        functools.partial(pursuit_kernel, steps=steps, scale=1.0 / math.sqrt(full)),
        in_specs=[vmem] * 9,
        out_specs=[vmem, anywhere],
        out_shape=[
            jax.ShapeDtypeStruct((steps, rows), f32),
            jax.ShapeDtypeStruct((classes, full), f32),
        ],
        scratch_shapes=[
            pltpu.VMEM((classes, full), f32),
            pltpu.VMEM((classes, full // 2), bf16),
            pltpu.SemaphoreType.DMA((4,)),
        ],
        compiler_params=limit,
        name="pursuit",
    )(labels, x, cross, factor, direct, right, target, feat_rest, twin_half)
    return scores, resid


def solution(mesh):
    return jax.shard_map(
        functools.partial(on_device, n_ex=mesh.shape["ex"]),
        mesh=mesh,
        in_specs=(P(("grp", "ex"), None), P(("grp", "ex")), P("grp", None)),
        out_specs=(P(None, ("grp", "ex")), P("grp", None)),
        check_vma=False,
    )
```

```python
import functools
import math

import jax
import jax.numpy as jnp
from jax import lax
from jax.experimental import pallas as pl
from jax.experimental.pallas import tpu as pltpu
from jax.sharding import PartitionSpec as P

ridge = 1.0
slots = 2
f32 = jnp.float32
bf16 = jnp.bfloat16


def nt_dot(a, b):
    return lax.dot_general(a, b, (((1,), (1,)), ((), ())), preferred_element_type=f32)


def column(tile, height, start=0):
    return jnp.concatenate([tile[:, start + q : start + q + 1] for q in range(height // 8)], axis=0)


def spread(values, start=0):
    lane = lax.broadcasted_iota(jnp.int32, (8, 128), 1)
    tile = jnp.zeros((8, 128), f32)
    for q in range(values.shape[0] // 8):
        tile = jnp.where(lane == start + q, values[8 * q : 8 * q + 8], tile)
    return tile


def encode(x, count_tile=None):
    height, width = x.shape
    top = jnp.max(jnp.abs(x), axis=1, keepdims=True)
    power = jnp.ceil(jnp.log2(jnp.maximum(top, 1e-30)) + 0.01)
    whole_x = jnp.round(x * jnp.exp2(15.0 - power))
    mark = spread(power)
    if count_tile is not None:
        mark = mark + count_tile
    chunks = [whole_x[:, j * 128 : (j + 1) * 128] for j in range(width // 128)]
    return jnp.concatenate(chunks + [mark], axis=0).astype(jnp.int32).astype(jnp.int16)


def decode(code, height):
    value = code.astype(jnp.int32).astype(f32)
    count = value.shape[0] // height
    mark = value[count * height :]
    x = jnp.concatenate([value[j * height : (j + 1) * height] for j in range(count)], axis=1)
    return x * jnp.exp2(column(mark, height) - 15.0), mark


def sums_kernel(
    labels_hbm, pick_hbm, feat_hbm, send_ref, keep_ref, rows_ref, labels_ref, pick_ref, feat_ref, left, held, sems, *, n_ex
):
    rows, full = feat_ref.shape
    steps, classes = pick_ref.shape
    width = full // n_ex
    groups = n_ex // 2
    device = lax.axis_index("ex")
    core = device % 2
    small = [
        pltpu.make_async_copy(pick_hbm, pick_ref, sems.at[n_ex]),
        pltpu.make_async_copy(labels_hbm, labels_ref, sems.at[n_ex + 1]),
    ]
    for copy in small:
        copy.start()
    columns = []
    copies = []
    for i in range(n_ex):
        block = (1 - core) * groups + i if i < groups else core * groups + i - groups
        at = pl.ds(pl.multiple_of(block * width, width), width)
        columns.append(at)
        copies.append(pltpu.make_async_copy(feat_hbm.at[:, at], feat_ref.at[:, at], sems.at[i]))
        copies[-1].start()

    for copy in small:
        copy.wait()
    local = pick_ref[...] - device * rows
    mine = (local >= 0) & (local < rows)
    lane = lax.broadcasted_iota(jnp.int32, local.shape, 1)
    first = jnp.min(jnp.where(mine, lane, classes), axis=1, keepdims=True)
    last = jnp.max(jnp.where(mine, lane, -1), axis=1, keepdims=True)
    spot0 = jnp.max(jnp.where(mine & (lane == first), local, -1), axis=1, keepdims=True)
    spot1 = jnp.max(jnp.where(mine & (lane == last) & (last > first), local, -1), axis=1, keepdims=True)
    member = lax.broadcasted_iota(jnp.int32, (classes, rows), 0) == labels_ref[...].reshape(1, rows)
    line = lax.broadcasted_iota(jnp.int32, (steps, rows), 1)
    left[...] = jnp.concatenate(
        [
            jnp.where(member, 1.0, 0.0),
            jnp.where(line == spot0, 1.0, 0.0),
            jnp.where(line == spot1, 1.0, 0.0),
            jnp.zeros((16 - 2 * steps, rows), f32),
        ],
        axis=0,
    ).astype(bf16)
    count = jnp.sum(jnp.where(member, 1.0, 0.0), axis=1, keepdims=True)
    tile = spread(count, classes // 8)
    for ref in (send_ref, keep_ref):
        ref[groups * classes :, :128] = tile
        if width > 128:
            ref[groups * classes :, 128:] = jnp.zeros((8, width - 128), f32)

    for i in range(n_ex):
        copies[i].wait()
        both = jnp.dot(left[...], feat_ref[:, columns[i]], preferred_element_type=f32)
        k = i % groups
        ref = send_ref if i < groups else keep_ref
        ref[k * classes : (k + 1) * classes, :] = both[:classes]
        held[:, columns[i]] = both[classes : classes + 8]

    used = steps * slots
    main = full * used // 8
    tail = full - main
    lines = [held[0:used, :main]]
    for q in range(slots):
        lines.append(jnp.concatenate([held[q * steps + u : q * steps + u + 1, main:] for u in range(steps)], axis=1))
    rows_ref[...] = jnp.concatenate(lines, axis=0).astype(bf16)


def pair_kernel(keep_ref, got_ref, code_ref, *, classes):
    groups = code_ref.shape[0]
    base = groups * classes
    tile = keep_ref[base : base + 8, :128] + got_ref[base : base + 8, :128]
    for k in range(groups):
        at = slice(k * classes, (k + 1) * classes)
        code_ref[k] = encode(keep_ref[at, :] + got_ref[at, :], tile)


def total_kernel(got_ref, code_ref, *, classes):
    value, mark = decode(got_ref[0], classes)
    for k in range(1, got_ref.shape[0]):
        more, more_mark = decode(got_ref[k], classes)
        value = value + more
        mark = mark + more_mark
    code_ref[0] = encode(value / jnp.sqrt(column(mark, classes, classes // 8)))


def diagonal(block):
    n = block.shape[0]
    eye = lax.broadcasted_iota(jnp.int32, (n, n), 0) == lax.broadcasted_iota(jnp.int32, (n, n), 1)
    return jnp.sum(jnp.where(eye, block, 0.0), axis=1, keepdims=True)


def factor_all(gram):
    order = len(gram)
    factor = [[None] * order for _ in range(order)]
    for j in range(order):
        value = gram[j][j]
        for k in range(j):
            value = value - factor[j][k] * factor[j][k]
        root = jnp.sqrt(value)
        factor[j][j] = 1.0 / root
        for i in range(j + 1, order):
            value = gram[i][j]
            for k in range(j):
                value = value - factor[i][k] * factor[j][k]
            factor[i][j] = value * factor[j][j]
    return factor


def solve_all(factor, right):
    order = len(right)
    forward = []
    for i in range(order):
        value = right[i]
        for j in range(i):
            value = value - factor[i][j] * forward[j]
        forward.append(value * factor[i][i])
    result = []
    for size in range(1, order + 1):
        back = [None] * size
        for i in reversed(range(size)):
            value = forward[i]
            for j in range(i + 1, size):
                value = value - factor[j][i] * back[j]
            back[i] = value * factor[i][i]
        result.append(back)
    return result


def select_kernel(pick_ref, one_ref, rest_ref, *, n_ex, rows):
    steps, classes = pick_ref.shape
    lines = one_ref.shape[1]
    device = lax.axis_index("ex")
    pick = pick_ref[...]
    lane = lax.broadcasted_iota(jnp.int32, pick.shape, 1)
    owner = jnp.zeros_like(pick)
    rank = jnp.zeros_like(pick)
    for d in range(n_ex):
        here = (pick >= d * rows) & (pick < (d + 1) * rows)
        first = jnp.min(jnp.where(here, lane, classes), axis=1, keepdims=True)
        owner = jnp.where(here, d, owner)
        rank = jnp.where(here & (lane > first), 1, rank)
    away = owner ^ device
    spot = jnp.zeros_like(pick)
    bits = n_ex.bit_length() - 1
    for b in range(1, bits):
        spot = spot + (((away >> b) & 1) << (bits - 1 - b))
    spot = spot + ((away & 1) << (bits - 1))
    step = lax.broadcasted_iota(jnp.int32, pick.shape, 0)
    line = lax.broadcasted_iota(jnp.int32, (lines, classes), 0)
    for ref, where in ((one_ref, spot * 8 + rank * steps + step), (rest_ref, spot * 8 + slots * steps + rank)):
        hits = [jnp.where(line == where[s : s + 1, :], 1.0, 0.0) for s in range(steps)]
        pad = jnp.zeros((lines, 128 - steps * classes), f32)
        ref[...] = jnp.transpose(jnp.concatenate(hits + [pad], axis=1))[: steps * classes].astype(bf16)


def picked_kernel(feat_hbm, one_ref, rest_ref, *refs, steps):
    parts, (x_ref, factor_ref, feat_ref, rows_ref, sems, feat_sems) = refs[:-6], refs[-6:]
    total, full = x_ref.shape
    loads = feat_sems.shape[0]
    classes = total // steps
    main = rows_ref.shape[1]
    tail = full - main
    copies = []
    at = 0
    for i, part in enumerate(parts):
        copies.append(pltpu.make_async_copy(part, rows_ref.at[at : at + part.shape[0]], sems.at[i]))
        copies[-1].start()
        at += part.shape[0]
    feat_copies = []
    for i in range(loads):
        col = slice(i * full // loads, (i + 1) * full // loads)
        feat_copies.append(pltpu.make_async_copy(feat_hbm.at[:, col], feat_ref.at[:, col], feat_sems.at[i]))
        feat_copies[-1].start()
    for copy in copies:
        copy.wait()
    x_ref[:, :main] = jnp.dot(one_ref[...], rows_ref[...], preferred_element_type=f32).astype(bf16)
    for s in range(steps):
        at = slice(s * classes, (s + 1) * classes)
        rest = jnp.dot(rest_ref[at, :], rows_ref[:, s * tail : (s + 1) * tail], preferred_element_type=f32)
        x_ref[at, main:] = rest.astype(bf16)

    x = x_ref[...]
    full_gram = nt_dot(x, x)
    gram = [
        [
            diagonal(full_gram[a * classes : (a + 1) * classes, b * classes : (b + 1) * classes])
            + (ridge if a == b else 0.0)
            for b in range(a + 1)
        ]
        for a in range(steps)
    ]
    factor = factor_all(gram)
    lane = lax.broadcasted_iota(jnp.int32, (classes, 128), 1)
    packed = jnp.zeros((classes, 128), f32)
    for i in range(steps):
        for j in range(i + 1):
            packed = jnp.where(lane == i * steps + j, factor[i][j], packed)
    factor_ref[...] = packed
    for copy in feat_copies:
        copy.wait()


def masks_of(n_ex):
    masks = [0]
    mask = n_ex // 2
    while mask > 4:
        masks = masks + [m ^ mask for m in masks]
        mask //= 2
    return masks + [m ^ 4 for m in masks] + [m ^ 2 for m in masks] + [m ^ 6 for m in masks]


def half_products(side, code_ref, x_ref, feat_ref, target_ref, target_at, left_ref, *, n_ex, classes):
    half = left_ref.shape[1]
    width = half // code_ref.shape[0]
    used = left_ref.shape[0] - classes
    group = lax.axis_index("ex") // 2
    here = pl.ds(pl.multiple_of(side * half, half), half)
    for k, mask in enumerate(masks_of(n_ex)):
        block = group ^ (mask // 2)
        target = decode(code_ref[k], classes)[0]
        target_ref[:, pl.ds(pl.multiple_of(target_at + block * width, width), width)] = target
        left_ref[:classes, pl.ds(pl.multiple_of(block * width, width), width)] = target.astype(bf16)
    left_ref[classes:, :] = x_ref[:used, here]
    right = nt_dot(left_ref[:classes, :], x_ref[:, here])
    return right, nt_dot(left_ref[...], feat_ref[:, here])


def half_kernel(feat_ref, code_ref, x_ref, direct_ref, right_ref, target_ref, left_ref, *, n_ex, classes):
    core = lax.axis_index("ex") % 2
    right_ref[...], direct_ref[...] = half_products(
        core, code_ref, x_ref, feat_ref, target_ref, 0, left_ref, n_ex=n_ex, classes=classes
    )


def pursuit_kernel(
    labels_ref, feat_ref, x_ref, factor_ref, direct_own, right_own, target_own, code_ref,
    scores_ref, resid_hbm, resid_ref, left_ref, sems, *, n_ex, steps, scale
):
    classes, full = resid_ref.shape
    half = full // 2
    core = lax.axis_index("ex") % 2
    right, direct = half_products(
        1 - core, code_ref, x_ref, feat_ref, resid_ref, (1 - core) * half, left_ref, n_ex=n_ex, classes=classes
    )
    right = right + right_own[...]
    rhs = [diagonal(right[:, a * classes : (a + 1) * classes]) for a in range(steps)]
    factor = [[factor_ref[:, i * steps + j : i * steps + j + 1] for j in range(i + 1)] for i in range(steps)]
    weights = solve_all(factor, rhs)
    last = weights[steps - 1]
    copies = []
    span = half // 2
    for source, side in ((target_own, core), (resid_ref, 1 - core)):
        for q in range(2):
            here = pl.ds(pl.multiple_of(side * half + q * span, span), span)
            value = source[:, q * span : (q + 1) * span] if source is target_own else source[:, here]
            for k in range(steps):
                value = value - last[k] * x_ref[k * classes : (k + 1) * classes, here].astype(f32)
            resid_ref[:, here] = value
            copies.append(pltpu.make_async_copy(resid_ref.at[:, here], resid_hbm.at[:, here], sems.at[len(copies)]))
            copies[-1].start()

    direct = direct + direct_own[...]
    member = lax.broadcasted_iota(jnp.int32, (classes, direct.shape[1]), 0) == labels_ref[...].reshape(1, direct.shape[1])
    for s in range(steps):
        value = direct[:classes]
        for k in range(s):
            value = value - weights[s - 1][k] * direct[(k + 1) * classes : (k + 2) * classes]
        scores_ref[s : s + 1, :] = jnp.sum(jnp.where(member, value, 0.0), axis=0, keepdims=True) * scale
    for copy in copies:
        copy.wait()


def on_device(features, labels, pick_index, *, n_ex):
    rows, full = features.shape
    steps, classes = pick_index.shape
    groups = n_ex // 2
    width = full // n_ex
    total = steps * classes
    main = full * steps * slots // 8
    limit = pltpu.CompilerParams(vmem_limit_bytes=24 << 20)
    vmem = pl.BlockSpec(memory_space=pltpu.VMEM)
    hbm = pl.BlockSpec(memory_space=pltpu.HBM)
    anywhere = pl.BlockSpec(memory_space=pl.ANY)
    half = jax.ShapeDtypeStruct((groups * classes + 8, width), f32)
    codes = jax.ShapeDtypeStruct((groups, classes * (width // 128) + 8, 128), jnp.int16)
    features, picks, labels_in = [
        pltpu.with_memory_space_constraint(a, pltpu.HBM) for a in (features, pick_index, labels)
    ]

    def swap(x, mask):
        return lax.ppermute(x, "ex", [(d, d ^ mask) for d in range(n_ex)])

    def trade(x):
        teams = [[s + 2 * k for k in range(groups)] for s in range(2)]
        return lax.all_to_all(x, "ex", 0, 0, axis_index_groups=teams, tiled=True)

    send, keep, packed = pl.pallas_call(
        functools.partial(sums_kernel, n_ex=n_ex),
        in_specs=[hbm] * 3,
        out_specs=[vmem] * 3,
        out_shape=[half, half, jax.ShapeDtypeStruct((8, main), bf16)],
        scratch_shapes=[
            pltpu.VMEM(labels.shape, jnp.int32),
            pltpu.VMEM(pick_index.shape, jnp.int32),
            pltpu.VMEM((rows, full), bf16),
            pltpu.VMEM((classes + 16, rows), bf16),
            pltpu.VMEM((8, full), f32),
            pltpu.SemaphoreType.DMA((n_ex + 2,)),
        ],
        compiler_params=limit,
        name="class_sums",
    )(labels_in, picks, features)

    got = swap(send, 1)
    codes_out = pl.pallas_call(
        functools.partial(pair_kernel, classes=classes),
        in_specs=[vmem] * 2,
        out_specs=vmem,
        out_shape=codes,
        compiler_params=limit,
        name="pair_sums",
    )(keep, got)
    pick_late, packed, _ = lax.optimization_barrier((pick_index, packed, codes_out))

    def along_z(x):
        mask = n_ex // 2
        while mask > 4:
            x = jnp.concatenate([x, swap(x, mask)], axis=0)
            mask //= 2
        return x

    near = along_z(packed)
    parts = [near, swap(near, 4), swap(near, 2), swap(near, 6)]
    one, rest = pl.pallas_call(
        functools.partial(select_kernel, n_ex=n_ex, rows=rows),
        in_specs=[vmem],
        out_specs=[vmem] * 2,
        out_shape=[jax.ShapeDtypeStruct((total, n_ex * 8), bf16)] * 2,
        compiler_params=limit,
        name="selectors",
    )(pick_late)

    traded, _ = lax.optimization_barrier((trade(codes_out), parts[0]))
    summed = pl.pallas_call(
        functools.partial(total_kernel, classes=classes),
        in_specs=[vmem],
        out_specs=vmem,
        out_shape=jax.ShapeDtypeStruct((1,) + codes.shape[1:], codes.dtype),
        compiler_params=limit,
        name="total_sums",
    )(traded)
    near = along_z(summed)
    parts, _ = lax.optimization_barrier((parts, near))
    own_parts = [near, swap(near, 4), swap(near, 2), swap(near, 6)]
    parts = parts + [swap(p, 1) for p in parts]

    x, factor, features_in = pl.pallas_call(
        functools.partial(picked_kernel, steps=steps),
        in_specs=[hbm] + [vmem] * 2 + [anywhere] * len(parts),
        out_specs=[vmem] * 3,
        out_shape=[
            jax.ShapeDtypeStruct((total, full), bf16),
            jax.ShapeDtypeStruct((classes, 128), f32),
            pltpu.VMEM((rows, full), bf16),
        ],
        scratch_shapes=[
            pltpu.VMEM((n_ex * 8, main), bf16),
            pltpu.SemaphoreType.DMA((len(parts),)),
            pltpu.SemaphoreType.DMA((n_ex,)),
        ],
        compiler_params=limit,
        name="picked_rows",
    )(features, one, rest, *parts)

    own_parts, x = lax.optimization_barrier((own_parts, x))
    own_half = jnp.concatenate(own_parts, axis=0)
    twin_half = swap(own_half, 1)
    left = pltpu.VMEM((total, full // 2), bf16)
    direct, right, target = pl.pallas_call(
        functools.partial(half_kernel, n_ex=n_ex, classes=classes),
        in_specs=[vmem] * 3,
        out_specs=[vmem] * 3,
        out_shape=[
            jax.ShapeDtypeStruct((total, rows), f32),
            jax.ShapeDtypeStruct((classes, total), f32),
            jax.ShapeDtypeStruct((classes, full // 2), f32),
        ],
        scratch_shapes=[left],
        compiler_params=limit,
        name="own_half_products",
    )(features_in, own_half, x)

    scores, resid = pl.pallas_call(
        functools.partial(pursuit_kernel, n_ex=n_ex, steps=steps, scale=1.0 / math.sqrt(full)),
        in_specs=[vmem] * 8,
        out_specs=[vmem, anywhere],
        out_shape=[
            jax.ShapeDtypeStruct((steps, rows), f32),
            jax.ShapeDtypeStruct((classes, full), f32),
        ],
        scratch_shapes=[pltpu.VMEM((classes, full), f32), left, pltpu.SemaphoreType.DMA((4,))],
        compiler_params=limit,
        name="pursuit",
    )(labels, features_in, x, factor, direct, right, target, twin_half)
    return scores, resid


def solution(mesh):
    return jax.shard_map(
        functools.partial(on_device, n_ex=mesh.shape["ex"]),
        mesh=mesh,
        in_specs=(P(("grp", "ex"), None), P(("grp", "ex")), P("grp", None)),
        out_specs=(P(None, ("grp", "ex")), P("grp", None)),
        check_vma=False,
    )
```

```python
import functools
import math

import jax
import jax.numpy as jnp
from jax import lax
from jax.experimental import pallas as pl
from jax.experimental.pallas import tpu as pltpu
from jax.sharding import PartitionSpec as P

ridge = 1.0
slots = 2
f32 = jnp.float32
bf16 = jnp.bfloat16


def nt_dot(a, b):
    return lax.dot_general(a, b, (((1,), (1,)), ((), ())), preferred_element_type=f32)


def column(tile, height, start=0):
    return jnp.concatenate([tile[:, start + q : start + q + 1] for q in range(height // 8)], axis=0)


def spread(values, start=0):
    lane = lax.broadcasted_iota(jnp.int32, (8, 128), 1)
    tile = jnp.zeros((8, 128), f32)
    for q in range(values.shape[0] // 8):
        tile = jnp.where(lane == start + q, values[8 * q : 8 * q + 8], tile)
    return tile


def encode(x, count_tile=None):
    height, width = x.shape
    top = jnp.max(jnp.abs(x), axis=1, keepdims=True)
    power = jnp.ceil(jnp.log2(jnp.maximum(top, 1e-30)) + 0.01)
    whole_x = jnp.round(x * jnp.exp2(15.0 - power))
    mark = spread(power)
    if count_tile is not None:
        mark = mark + count_tile
    chunks = [whole_x[:, j * 128 : (j + 1) * 128] for j in range(width // 128)]
    return jnp.concatenate(chunks + [mark], axis=0).astype(jnp.int32).astype(jnp.int16)


def decode(code, height):
    value = code.astype(jnp.int32).astype(f32)
    count = value.shape[0] // height
    mark = value[count * height :]
    x = jnp.concatenate([value[j * height : (j + 1) * height] for j in range(count)], axis=1)
    return x * jnp.exp2(column(mark, height) - 15.0), mark


def sums_kernel(
    labels_hbm, pick_hbm, feat_hbm, feat_ref, send_ref, keep_ref, rows_ref, labels_ref, pick_ref, left, held, sems, *, n_ex
):
    rows, full = feat_ref.shape
    steps, classes = pick_ref.shape
    width = full // n_ex
    groups = n_ex // 2
    device = lax.axis_index("ex")
    core = device % 2
    small = [
        pltpu.make_async_copy(pick_hbm, pick_ref, sems.at[n_ex]),
        pltpu.make_async_copy(labels_hbm, labels_ref, sems.at[n_ex + 1]),
    ]
    for copy in small:
        copy.start()
    columns = []
    copies = []
    for i in range(n_ex):
        block = (1 - core) * groups + i if i < groups else core * groups + i - groups
        at = pl.ds(pl.multiple_of(block * width, width), width)
        columns.append(at)
        copies.append(pltpu.make_async_copy(feat_hbm.at[:, at], feat_ref.at[:, at], sems.at[i]))
        copies[-1].start()

    for copy in small:
        copy.wait()
    local = pick_ref[...] - device * rows
    mine = (local >= 0) & (local < rows)
    lane = lax.broadcasted_iota(jnp.int32, local.shape, 1)
    first = jnp.min(jnp.where(mine, lane, classes), axis=1, keepdims=True)
    last = jnp.max(jnp.where(mine, lane, -1), axis=1, keepdims=True)
    spot0 = jnp.max(jnp.where(mine & (lane == first), local, -1), axis=1, keepdims=True)
    spot1 = jnp.max(jnp.where(mine & (lane == last) & (last > first), local, -1), axis=1, keepdims=True)
    member = lax.broadcasted_iota(jnp.int32, (classes, rows), 0) == labels_ref[...].reshape(1, rows)
    line = lax.broadcasted_iota(jnp.int32, (steps, rows), 1)
    left[...] = jnp.concatenate(
        [
            jnp.where(member, 1.0, 0.0),
            jnp.where(line == spot0, 1.0, 0.0),
            jnp.where(line == spot1, 1.0, 0.0),
            jnp.zeros((16 - 2 * steps, rows), f32),
        ],
        axis=0,
    ).astype(bf16)
    count = jnp.sum(jnp.where(member, 1.0, 0.0), axis=1, keepdims=True)
    tile = spread(count, classes // 8)
    for ref in (send_ref, keep_ref):
        ref[groups * classes :, :128] = tile
        if width > 128:
            ref[groups * classes :, 128:] = jnp.zeros((8, width - 128), f32)

    for i in range(n_ex):
        copies[i].wait()
        both = jnp.dot(left[...], feat_ref[:, columns[i]], preferred_element_type=f32)
        k = i % groups
        ref = send_ref if i < groups else keep_ref
        ref[k * classes : (k + 1) * classes, :] = both[:classes]
        held[:, columns[i]] = both[classes : classes + 8]

    used = steps * slots
    main = full * used // 8
    tail = full - main
    lines = [held[0:used, :main]]
    for q in range(slots):
        lines.append(jnp.concatenate([held[q * steps + u : q * steps + u + 1, main:] for u in range(steps)], axis=1))
    rows_ref[...] = jnp.concatenate(lines, axis=0).astype(bf16)


def near_id(mask):
    return (lax.axis_index("ex") // 2 % 4) ^ (mask // 2)


def pair_kernel(keep_ref, got_ref, *code_refs, classes):
    far = code_refs[0].shape[0]
    base = 4 * far * classes
    tile = keep_ref[base : base + 8, :128] + got_ref[base : base + 8, :128]
    for mask, code_ref in zip((0, 4, 2, 6), code_refs):
        for j in range(far):
            at = pl.ds(pl.multiple_of((j * 4 + near_id(mask)) * classes, classes), classes)
            code_ref[j] = encode(keep_ref[at, :] + got_ref[at, :], tile)


def add_kernel(*refs, classes, last):
    code_ref = refs[-1]
    for j in range(code_ref.shape[0]):
        value, mark = decode(refs[0][j], classes)
        for ref in refs[1:-1]:
            more, more_mark = decode(ref[j], classes)
            value = value + more
            mark = mark + more_mark
        if last:
            code_ref[j] = encode(value / jnp.sqrt(column(mark, classes, classes // 8)))
        else:
            lane = lax.broadcasted_iota(jnp.int32, mark.shape, 1)
            code_ref[j] = encode(value, jnp.where(lane < classes // 8, 0.0, mark))


def diagonal(block):
    n = block.shape[0]
    eye = lax.broadcasted_iota(jnp.int32, (n, n), 0) == lax.broadcasted_iota(jnp.int32, (n, n), 1)
    return jnp.sum(jnp.where(eye, block, 0.0), axis=1, keepdims=True)


def factor_all(gram):
    order = len(gram)
    factor = [[None] * order for _ in range(order)]
    for j in range(order):
        value = gram[j][j]
        for k in range(j):
            value = value - factor[j][k] * factor[j][k]
        root = jnp.sqrt(value)
        factor[j][j] = 1.0 / root
        for i in range(j + 1, order):
            value = gram[i][j]
            for k in range(j):
                value = value - factor[i][k] * factor[j][k]
            factor[i][j] = value * factor[j][j]
    return factor


def solve_all(factor, right):
    order = len(right)
    forward = []
    for i in range(order):
        value = right[i]
        for j in range(i):
            value = value - factor[i][j] * forward[j]
        forward.append(value * factor[i][i])
    result = []
    for size in range(1, order + 1):
        back = [None] * size
        for i in reversed(range(size)):
            value = forward[i]
            for j in range(i + 1, size):
                value = value - factor[j][i] * back[j]
            back[i] = value * factor[i][i]
        result.append(back)
    return result


def select_kernel(pick_ref, one_ref, rest_ref, *, n_ex, rows):
    steps, classes = pick_ref.shape
    lines = one_ref.shape[1]
    device = lax.axis_index("ex")
    pick = pick_ref[...]
    lane = lax.broadcasted_iota(jnp.int32, pick.shape, 1)
    owner = jnp.zeros_like(pick)
    rank = jnp.zeros_like(pick)
    for d in range(n_ex):
        here = (pick >= d * rows) & (pick < (d + 1) * rows)
        first = jnp.min(jnp.where(here, lane, classes), axis=1, keepdims=True)
        owner = jnp.where(here, d, owner)
        rank = jnp.where(here & (lane > first), 1, rank)
    away = owner ^ device
    spot = jnp.zeros_like(pick)
    bits = n_ex.bit_length() - 1
    for b in range(1, bits):
        spot = spot + (((away >> b) & 1) << (bits - 1 - b))
    spot = spot + ((away & 1) << (bits - 1))
    step = lax.broadcasted_iota(jnp.int32, pick.shape, 0)
    line = lax.broadcasted_iota(jnp.int32, (lines, classes), 0)
    for ref, where in ((one_ref, spot * 8 + rank * steps + step), (rest_ref, spot * 8 + slots * steps + rank)):
        hits = [jnp.where(line == where[s : s + 1, :], 1.0, 0.0) for s in range(steps)]
        pad = jnp.zeros((lines, 128 - steps * classes), f32)
        ref[...] = jnp.transpose(jnp.concatenate(hits + [pad], axis=1))[: steps * classes].astype(bf16)


def picked_kernel(one_ref, rest_ref, *refs, steps):
    parts, (x_ref, factor_ref, rows_ref) = refs[:-3], refs[-3:]
    total, full = x_ref.shape
    classes = total // steps
    main = rows_ref.shape[1]
    tail = full - main
    at = 0
    for part in parts:
        rows_ref[at : at + part.shape[0], :] = part[...]
        at += part.shape[0]
    x_ref[:, :main] = jnp.dot(one_ref[...], rows_ref[...], preferred_element_type=f32).astype(bf16)
    for s in range(steps):
        at = slice(s * classes, (s + 1) * classes)
        rest = jnp.dot(rest_ref[at, :], rows_ref[:, s * tail : (s + 1) * tail], preferred_element_type=f32)
        x_ref[at, main:] = rest.astype(bf16)

    x = x_ref[...]
    full_gram = nt_dot(x, x)
    gram = [
        [
            diagonal(full_gram[a * classes : (a + 1) * classes, b * classes : (b + 1) * classes])
            + (ridge if a == b else 0.0)
            for b in range(a + 1)
        ]
        for a in range(steps)
    ]
    factor = factor_all(gram)
    lane = lax.broadcasted_iota(jnp.int32, (classes, 128), 1)
    packed = jnp.zeros((classes, 128), f32)
    for i in range(steps):
        for j in range(i + 1):
            packed = jnp.where(lane == i * steps + j, factor[i][j], packed)
    factor_ref[...] = packed


def half_products(side, code_ref, x_ref, feat_ref, target_ref, target_at, left_ref, *, classes):
    half = left_ref.shape[1]
    far = code_ref.shape[0] // 4
    width = half // code_ref.shape[0]
    used = left_ref.shape[0] - classes
    here = pl.ds(pl.multiple_of(side * half, half), half)
    for k in range(4 * far):
        block = k % far * 4 + near_id((0, 4, 2, 6)[k // far])
        target = decode(code_ref[k], classes)[0]
        target_ref[:, pl.ds(pl.multiple_of(target_at + block * width, width), width)] = target
        left_ref[:classes, pl.ds(pl.multiple_of(block * width, width), width)] = target.astype(bf16)
    left_ref[classes:, :] = x_ref[:used, here]
    right = nt_dot(left_ref[:classes, :], x_ref[:, here])
    return right, nt_dot(left_ref[...], feat_ref[:, here])


def half_kernel(feat_ref, code_ref, x_ref, direct_ref, right_ref, target_ref, left_ref, *, classes):
    core = lax.axis_index("ex") % 2
    right_ref[...], direct_ref[...] = half_products(
        core, code_ref, x_ref, feat_ref, target_ref, 0, left_ref, classes=classes
    )


def pursuit_kernel(
    labels_ref, feat_ref, x_ref, factor_ref, direct_own, right_own, target_own, code_ref,
    scores_ref, resid_hbm, resid_ref, left_ref, sems, *, steps, scale
):
    classes, full = resid_ref.shape
    half = full // 2
    core = lax.axis_index("ex") % 2
    right, direct = half_products(
        1 - core, code_ref, x_ref, feat_ref, resid_ref, (1 - core) * half, left_ref, classes=classes
    )
    right = right + right_own[...]
    rhs = [diagonal(right[:, a * classes : (a + 1) * classes]) for a in range(steps)]
    factor = [[factor_ref[:, i * steps + j : i * steps + j + 1] for j in range(i + 1)] for i in range(steps)]
    weights = solve_all(factor, rhs)
    last = weights[steps - 1]
    copies = []
    span = half // 2
    for source, side in ((target_own, core), (resid_ref, 1 - core)):
        for q in range(2):
            here = pl.ds(pl.multiple_of(side * half + q * span, span), span)
            value = source[:, q * span : (q + 1) * span] if source is target_own else source[:, here]
            for k in range(steps):
                value = value - last[k] * x_ref[k * classes : (k + 1) * classes, here].astype(f32)
            resid_ref[:, here] = value
            copies.append(pltpu.make_async_copy(resid_ref.at[:, here], resid_hbm.at[:, here], sems.at[len(copies)]))
            copies[-1].start()

    direct = direct + direct_own[...]
    member = lax.broadcasted_iota(jnp.int32, (classes, direct.shape[1]), 0) == labels_ref[...].reshape(1, direct.shape[1])
    for s in range(steps):
        value = direct[:classes]
        for k in range(s):
            value = value - weights[s - 1][k] * direct[(k + 1) * classes : (k + 2) * classes]
        scores_ref[s : s + 1, :] = jnp.sum(jnp.where(member, value, 0.0), axis=0, keepdims=True) * scale
    for copy in copies:
        copy.wait()


def on_device(features, labels, pick_index, *, n_ex):
    rows, full = features.shape
    steps, classes = pick_index.shape
    groups = n_ex // 2
    width = full // n_ex
    total = steps * classes
    main = full * steps * slots // 8
    limit = pltpu.CompilerParams(vmem_limit_bytes=16 << 20)
    vmem = pl.BlockSpec(memory_space=pltpu.VMEM)
    hbm = pl.BlockSpec(memory_space=pltpu.HBM)
    anywhere = pl.BlockSpec(memory_space=pl.ANY)
    half = jax.ShapeDtypeStruct((groups * classes + 8, width), f32)
    code = jax.ShapeDtypeStruct((groups // 4, classes * (width // 128) + 8, 128), jnp.int16)

    def swap(x, mask):
        return lax.ppermute(x, "ex", [(d, d ^ mask) for d in range(n_ex)])

    def after(x, *others):
        return lax.optimization_barrier((x,) + others)[0]

    feat, send, keep, packed = pl.pallas_call(
        functools.partial(sums_kernel, n_ex=n_ex),
        in_specs=[hbm] * 3,
        out_specs=[vmem] * 4,
        out_shape=[pltpu.VMEM((rows, full), bf16), half, half, jax.ShapeDtypeStruct((8, main), bf16)],
        scratch_shapes=[
            pltpu.VMEM(labels.shape, jnp.int32),
            pltpu.VMEM(pick_index.shape, jnp.int32),
            pltpu.VMEM((classes + 16, rows), bf16),
            pltpu.VMEM((8, full), f32),
            pltpu.SemaphoreType.DMA((n_ex + 2,)),
        ],
        compiler_params=limit,
        name="class_sums",
    )(*[pltpu.with_memory_space_constraint(a, pltpu.HBM) for a in (labels, pick_index, features)])

    def add(codes, last):
        return pl.pallas_call(
            functools.partial(add_kernel, classes=classes, last=last),
            in_specs=[vmem] * len(codes),
            out_specs=vmem,
            out_shape=code,
            compiler_params=limit,
            name="add_sums",
        )(*codes)

    far_masks = [8 << b for b in range(n_ex.bit_length() - 4)]
    codes = pl.pallas_call(
        functools.partial(pair_kernel, classes=classes),
        in_specs=[vmem] * 2,
        out_specs=[vmem] * 4,
        out_shape=[code] * 4,
        compiler_params=limit,
        name="pair_sums",
    )(keep, swap(send, 1))
    near = packed
    for mask in reversed(far_masks):
        near = jnp.concatenate([near, after(swap(near, mask), codes[0])], axis=0)
    parts = [near, swap(near, 4), swap(near, 2), swap(near, 6)]

    part_sum = add([codes[0], swap(codes[1], 4), swap(codes[2], 2), swap(codes[3], 6)], False)
    one, rest = pl.pallas_call(
        functools.partial(select_kernel, n_ex=n_ex, rows=rows),
        in_specs=[vmem],
        out_specs=[vmem] * 2,
        out_shape=[jax.ShapeDtypeStruct((total, n_ex * 8), bf16)] * 2,
        compiler_params=limit,
        name="selectors",
    )(after(pick_index, part_sum))
    for mask in far_masks:
        part_sum = add([part_sum, after(swap(part_sum, mask), one)], mask == far_masks[-1])
    own_parts = [part_sum, swap(part_sum, 4), swap(part_sum, 2), swap(part_sum, 6)]
    parts = [after(p, part_sum) for p in parts]
    parts = parts + [swap(p, 1) for p in parts]

    x, factor = pl.pallas_call(
        functools.partial(picked_kernel, steps=steps),
        in_specs=[vmem] * (2 + len(parts)),
        out_specs=[vmem] * 2,
        out_shape=[
            jax.ShapeDtypeStruct((total, full), bf16),
            jax.ShapeDtypeStruct((classes, 128), f32),
        ],
        scratch_shapes=[pltpu.VMEM((n_ex * 8, main), bf16)],
        compiler_params=limit,
        name="picked_rows",
    )(one, rest, *parts)

    own_parts, x = lax.optimization_barrier((own_parts, x))
    own_half = jnp.concatenate(own_parts, axis=0)
    twin_half = swap(own_half, 1)
    left = pltpu.VMEM((total, full // 2), bf16)
    direct, right, target = pl.pallas_call(
        functools.partial(half_kernel, classes=classes),
        in_specs=[vmem] * 3,
        out_specs=[vmem] * 3,
        out_shape=[
            jax.ShapeDtypeStruct((total, rows), f32),
            jax.ShapeDtypeStruct((classes, total), f32),
            jax.ShapeDtypeStruct((classes, full // 2), f32),
        ],
        scratch_shapes=[left],
        compiler_params=limit,
        name="own_half_products",
    )(feat, own_half, x)

    scores, resid = pl.pallas_call(
        functools.partial(pursuit_kernel, steps=steps, scale=1.0 / math.sqrt(full)),
        in_specs=[vmem] * 8,
        out_specs=[vmem, anywhere],
        out_shape=[
            jax.ShapeDtypeStruct((steps, rows), f32),
            jax.ShapeDtypeStruct((classes, full), f32),
        ],
        scratch_shapes=[pltpu.VMEM((classes, full), f32), left, pltpu.SemaphoreType.DMA((4,))],
        compiler_params=limit,
        name="pursuit",
    )(labels, feat, x, factor, direct, right, target, twin_half)
    return scores, resid


def solution(mesh):
    return jax.shard_map(
        functools.partial(on_device, n_ex=mesh.shape["ex"]),
        mesh=mesh,
        in_specs=(P(("grp", "ex"), None), P(("grp", "ex")), P("grp", None)),
        out_specs=(P(None, ("grp", "ex")), P("grp", None)),
        check_vma=False,
    )
```

```python
import functools
import math

import jax
import jax.numpy as jnp
from jax import lax
from jax.experimental import pallas as pl
from jax.experimental.pallas import tpu as pltpu
from jax.sharding import PartitionSpec as P

ridge = 1.0
slots = 2
f32 = jnp.float32
bf16 = jnp.bfloat16


def nt_dot(a, b):
    return lax.dot_general(a, b, (((1,), (1,)), ((), ())), preferred_element_type=f32)


def column(tile, height, start=0):
    return jnp.concatenate([tile[:, start + q : start + q + 1] for q in range(height // 8)], axis=0)


def spread(values, start=0):
    lane = lax.broadcasted_iota(jnp.int32, (8, 128), 1)
    tile = jnp.zeros((8, 128), f32)
    for q in range(values.shape[0] // 8):
        tile = jnp.where(lane == start + q, values[8 * q : 8 * q + 8], tile)
    return tile


def encode(x, count_tile=None):
    height, width = x.shape
    top = jnp.max(jnp.abs(x), axis=1, keepdims=True)
    power = jnp.ceil(jnp.log2(jnp.maximum(top, 1e-30)) + 0.01)
    whole_x = jnp.round(x * jnp.exp2(15.0 - power))
    mark = spread(power)
    if count_tile is not None:
        mark = mark + count_tile
    chunks = [whole_x[:, j * 128 : (j + 1) * 128] for j in range(width // 128)]
    return jnp.concatenate(chunks + [mark], axis=0).astype(jnp.int32).astype(jnp.int16)


def decode(code, height):
    value = code.astype(jnp.int32).astype(f32)
    count = value.shape[0] // height
    mark = value[count * height :]
    x = jnp.concatenate([value[j * height : (j + 1) * height] for j in range(count)], axis=1)
    return x * jnp.exp2(column(mark, height) - 15.0), mark


def sums_kernel(
    labels_hbm, pick_hbm, feat_hbm, feat_ref, send_ref, keep_ref, held, labels_ref, pick_ref, left, sems, *, n_ex
):
    rows, full = feat_ref.shape
    steps, classes = pick_ref.shape
    width = full // n_ex
    groups = n_ex // 2
    device = lax.axis_index("ex")
    core = device % 2
    small = [
        pltpu.make_async_copy(pick_hbm, pick_ref, sems.at[n_ex]),
        pltpu.make_async_copy(labels_hbm, labels_ref, sems.at[n_ex + 1]),
    ]
    for copy in small:
        copy.start()
    columns = []
    copies = []
    for i in range(n_ex):
        block = (1 - core) * groups + i if i < groups else core * groups + i - groups
        at = pl.ds(pl.multiple_of(block * width, width), width)
        columns.append(at)
        copies.append(pltpu.make_async_copy(feat_hbm.at[:, at], feat_ref.at[:, at], sems.at[i]))
        copies[-1].start()

    for copy in small:
        copy.wait()
    local = pick_ref[...] - device * rows
    mine = (local >= 0) & (local < rows)
    lane = lax.broadcasted_iota(jnp.int32, local.shape, 1)
    first = jnp.min(jnp.where(mine, lane, classes), axis=1, keepdims=True)
    last = jnp.max(jnp.where(mine, lane, -1), axis=1, keepdims=True)
    spot0 = jnp.max(jnp.where(mine & (lane == first), local, -1), axis=1, keepdims=True)
    spot1 = jnp.max(jnp.where(mine & (lane == last) & (last > first), local, -1), axis=1, keepdims=True)
    member = lax.broadcasted_iota(jnp.int32, (classes, rows), 0) == labels_ref[...].reshape(1, rows)
    line = lax.broadcasted_iota(jnp.int32, (steps, rows), 1)
    left[...] = jnp.concatenate(
        [
            jnp.where(member, 1.0, 0.0),
            jnp.where(line == spot0, 1.0, 0.0),
            jnp.where(line == spot1, 1.0, 0.0),
            jnp.zeros((16 - 2 * steps, rows), f32),
        ],
        axis=0,
    ).astype(bf16)
    count = jnp.sum(jnp.where(member, 1.0, 0.0), axis=1, keepdims=True)
    tile = spread(count, classes // 8)
    for ref in (send_ref, keep_ref):
        ref[groups * classes :, :128] = tile
        if width > 128:
            ref[groups * classes :, 128:] = jnp.zeros((8, width - 128), f32)

    for i in range(n_ex):
        copies[i].wait()
        both = jnp.dot(left[...], feat_ref[:, columns[i]], preferred_element_type=f32)
        k = i % groups
        ref = send_ref if i < groups else keep_ref
        ref[k * classes : (k + 1) * classes, :] = both[:classes]
        held[:, columns[i]] = both[classes : classes + 8]


def pack_kernel(held, rows_ref, *, steps):
    used = steps * slots
    main = rows_ref.shape[1]
    lines = [held[0:used, :main]]
    for q in range(slots):
        lines.append(jnp.concatenate([held[q * steps + u : q * steps + u + 1, main:] for u in range(steps)], axis=1))
    rows_ref[...] = jnp.concatenate(lines, axis=0).astype(bf16)


def near_id(mask):
    return (lax.axis_index("ex") // 2 % 4) ^ (mask // 2)


def pair_kernel(keep_ref, got_ref, *code_refs, classes):
    far = code_refs[0].shape[0]
    base = 4 * far * classes
    tile = keep_ref[base : base + 8, :128] + got_ref[base : base + 8, :128]
    for mask, code_ref in zip((0, 4, 2, 6), code_refs):
        for j in range(far):
            at = pl.ds(pl.multiple_of((j * 4 + near_id(mask)) * classes, classes), classes)
            code_ref[j] = encode(keep_ref[at, :] + got_ref[at, :], tile)


def add_kernel(*refs, classes, last):
    code_ref = refs[-1]
    for j in range(code_ref.shape[0]):
        value, mark = decode(refs[0][j], classes)
        for ref in refs[1:-1]:
            more, more_mark = decode(ref[j], classes)
            value = value + more
            mark = mark + more_mark
        if last:
            code_ref[j] = encode(value / jnp.sqrt(column(mark, classes, classes // 8)))
        else:
            lane = lax.broadcasted_iota(jnp.int32, mark.shape, 1)
            code_ref[j] = encode(value, jnp.where(lane < classes // 8, 0.0, mark))


def diagonal(block):
    n = block.shape[0]
    eye = lax.broadcasted_iota(jnp.int32, (n, n), 0) == lax.broadcasted_iota(jnp.int32, (n, n), 1)
    return jnp.sum(jnp.where(eye, block, 0.0), axis=1, keepdims=True)


def factor_all(gram):
    order = len(gram)
    factor = [[None] * order for _ in range(order)]
    for j in range(order):
        value = gram[j][j]
        for k in range(j):
            value = value - factor[j][k] * factor[j][k]
        root = jnp.sqrt(value)
        factor[j][j] = 1.0 / root
        for i in range(j + 1, order):
            value = gram[i][j]
            for k in range(j):
                value = value - factor[i][k] * factor[j][k]
            factor[i][j] = value * factor[j][j]
    return factor


def solve_all(factor, right):
    order = len(right)
    forward = []
    for i in range(order):
        value = right[i]
        for j in range(i):
            value = value - factor[i][j] * forward[j]
        forward.append(value * factor[i][i])
    result = []
    for size in range(1, order + 1):
        back = [None] * size
        for i in reversed(range(size)):
            value = forward[i]
            for j in range(i + 1, size):
                value = value - factor[j][i] * back[j]
            back[i] = value * factor[i][i]
        result.append(back)
    return result


def select_kernel(pick_ref, one_ref, *, n_ex, rows, tail):
    steps, classes = pick_ref.shape
    lines = one_ref.shape[1]
    device = lax.axis_index("ex")
    pick = pick_ref[...]
    lane = lax.broadcasted_iota(jnp.int32, pick.shape, 1)
    owner = jnp.zeros_like(pick)
    rank = jnp.zeros_like(pick)
    for d in range(n_ex):
        here = (pick >= d * rows) & (pick < (d + 1) * rows)
        first = jnp.min(jnp.where(here, lane, classes), axis=1, keepdims=True)
        owner = jnp.where(here, d, owner)
        rank = jnp.where(here & (lane > first), 1, rank)
    away = owner ^ device
    spot = jnp.zeros_like(pick)
    bits = n_ex.bit_length() - 1
    for b in range(1, bits):
        spot = spot + (((away >> b) & 1) << (bits - 1 - b))
    spot = spot + ((away & 1) << (bits - 1))
    step = lax.broadcasted_iota(jnp.int32, pick.shape, 0)
    line = lax.broadcasted_iota(jnp.int32, (lines, classes), 0)
    where = spot * 8 + (slots * steps + rank if tail else rank * steps + step)
    hits = [jnp.where(line == where[s : s + 1, :], 1.0, 0.0) for s in range(steps)]
    pad = jnp.zeros((lines, 128 - steps * classes), f32)
    one_ref[...] = jnp.transpose(jnp.concatenate(hits + [pad], axis=1))[: steps * classes].astype(bf16)


def picked_kernel(one_ref, rest_ref, *refs, steps):
    parts, (x_ref, factor_ref, rows_ref) = refs[:-3], refs[-3:]
    total, full = x_ref.shape
    classes = total // steps
    main = rows_ref.shape[1]
    tail = full - main
    at = 0
    for part in parts:
        rows_ref[at : at + part.shape[0], :] = part[...]
        at += part.shape[0]
    x_ref[:, :main] = jnp.dot(one_ref[...], rows_ref[...], preferred_element_type=f32).astype(bf16)
    for s in range(steps):
        at = slice(s * classes, (s + 1) * classes)
        rest = jnp.dot(rest_ref[at, :], rows_ref[:, s * tail : (s + 1) * tail], preferred_element_type=f32)
        x_ref[at, main:] = rest.astype(bf16)

    x = x_ref[...]
    full_gram = nt_dot(x, x)
    gram = [
        [
            diagonal(full_gram[a * classes : (a + 1) * classes, b * classes : (b + 1) * classes])
            + (ridge if a == b else 0.0)
            for b in range(a + 1)
        ]
        for a in range(steps)
    ]
    factor = factor_all(gram)
    lane = lax.broadcasted_iota(jnp.int32, (classes, 128), 1)
    packed = jnp.zeros((classes, 128), f32)
    for i in range(steps):
        for j in range(i + 1):
            packed = jnp.where(lane == i * steps + j, factor[i][j], packed)
    factor_ref[...] = packed


def half_target(side, code_ref, x_ref, target_ref, target_at, left_ref, *, classes):
    half = left_ref.shape[1]
    far = code_ref.shape[0] // 4
    width = half // code_ref.shape[0]
    used = left_ref.shape[0] - classes
    here = pl.ds(pl.multiple_of(side * half, half), half)
    for k in range(4 * far):
        block = k % far * 4 + near_id((0, 4, 2, 6)[k // far])
        target = decode(code_ref[k], classes)[0]
        target_ref[:, pl.ds(pl.multiple_of(target_at + block * width, width), width)] = target
        left_ref[:classes, pl.ds(pl.multiple_of(block * width, width), width)] = target.astype(bf16)
    left_ref[classes:, :] = x_ref[:used, here]
    return nt_dot(left_ref[:classes, :], x_ref[:, here]), here


def half_kernel(feat_ref, code_ref, x_ref, direct_ref, right_ref, target_ref, left_ref, *, classes):
    core = lax.axis_index("ex") % 2
    right_ref[...], here = half_target(core, code_ref, x_ref, target_ref, 0, left_ref, classes=classes)
    direct_ref[...] = nt_dot(left_ref[...], feat_ref[:, here])


def pursuit_kernel(
    labels_ref, feat_ref, x_ref, factor_ref, direct_own, right_own, target_own, code_ref,
    scores_ref, resid_hbm, resid_ref, left_ref, sems, *, steps, scale
):
    classes, full = resid_ref.shape
    half = full // 2
    core = lax.axis_index("ex") % 2
    right, other = half_target(1 - core, code_ref, x_ref, resid_ref, (1 - core) * half, left_ref, classes=classes)
    right = right + right_own[...]
    rhs = [diagonal(right[:, a * classes : (a + 1) * classes]) for a in range(steps)]
    factor = [[factor_ref[:, i * steps + j : i * steps + j + 1] for j in range(i + 1)] for i in range(steps)]
    weights = solve_all(factor, rhs)
    last = weights[steps - 1]
    copies = []
    span = half // 2
    for source, side in ((target_own, core), (resid_ref, 1 - core)):
        for q in range(2):
            here = pl.ds(pl.multiple_of(side * half + q * span, span), span)
            value = source[:, q * span : (q + 1) * span] if source is target_own else source[:, here]
            for k in range(steps):
                value = value - last[k] * x_ref[k * classes : (k + 1) * classes, here].astype(f32)
            resid_ref[:, here] = value
            copies.append(pltpu.make_async_copy(resid_ref.at[:, here], resid_hbm.at[:, here], sems.at[len(copies)]))
            copies[-1].start()

    direct = direct_own[...] + nt_dot(left_ref[...], feat_ref[:, other])
    member = lax.broadcasted_iota(jnp.int32, (classes, direct.shape[1]), 0) == labels_ref[...].reshape(1, direct.shape[1])
    for s in range(steps):
        value = direct[:classes]
        for k in range(s):
            value = value - weights[s - 1][k] * direct[(k + 1) * classes : (k + 2) * classes]
        scores_ref[s : s + 1, :] = jnp.sum(jnp.where(member, value, 0.0), axis=0, keepdims=True) * scale
    for copy in copies:
        copy.wait()


def on_device(features, labels, pick_index, *, n_ex):
    rows, full = features.shape
    steps, classes = pick_index.shape
    groups = n_ex // 2
    width = full // n_ex
    total = steps * classes
    main = full * steps * slots // 8
    limit = pltpu.CompilerParams(vmem_limit_bytes=16 << 20)
    vmem = pl.BlockSpec(memory_space=pltpu.VMEM)
    hbm = pl.BlockSpec(memory_space=pltpu.HBM)
    anywhere = pl.BlockSpec(memory_space=pl.ANY)
    half = jax.ShapeDtypeStruct((groups * classes + 8, width), f32)
    code = jax.ShapeDtypeStruct((groups // 4, classes * (width // 128) + 8, 128), jnp.int16)

    def swap(x, mask):
        return lax.ppermute(x, "ex", [(d, d ^ mask) for d in range(n_ex)])

    def after(x, *others):
        return lax.optimization_barrier((x,) + others)[0]

    feat, send, keep, held = pl.pallas_call(
        functools.partial(sums_kernel, n_ex=n_ex),
        in_specs=[hbm] * 3,
        out_specs=[vmem] * 4,
        out_shape=[pltpu.VMEM((rows, full), bf16), half, half, jax.ShapeDtypeStruct((8, full), f32)],
        scratch_shapes=[
            pltpu.VMEM(labels.shape, jnp.int32),
            pltpu.VMEM(pick_index.shape, jnp.int32),
            pltpu.VMEM((classes + 16, rows), bf16),
            pltpu.SemaphoreType.DMA((n_ex + 2,)),
        ],
        compiler_params=limit,
        name="class_sums",
    )(*[pltpu.with_memory_space_constraint(a, pltpu.HBM) for a in (labels, pick_index, features)])

    def add(codes, last):
        return pl.pallas_call(
            functools.partial(add_kernel, classes=classes, last=last),
            in_specs=[vmem] * len(codes),
            out_specs=vmem,
            out_shape=code,
            compiler_params=limit,
            name="add_sums",
        )(*codes)

    far_masks = [8 << b for b in range(n_ex.bit_length() - 4)]
    codes = pl.pallas_call(
        functools.partial(pair_kernel, classes=classes),
        in_specs=[vmem] * 2,
        out_specs=[vmem] * 4,
        out_shape=[code] * 4,
        compiler_params=limit,
        name="pair_sums",
    )(keep, swap(send, 1))
    near = pl.pallas_call(
        functools.partial(pack_kernel, steps=steps),
        in_specs=[vmem],
        out_specs=vmem,
        out_shape=jax.ShapeDtypeStruct((8, main), bf16),
        compiler_params=limit,
        name="pack_rows",
    )(held)
    for mask in reversed(far_masks):
        near = jnp.concatenate([near, swap(near, mask)], axis=0)
    got = [swap(codes[1], 4), swap(codes[2], 2), swap(codes[3], 6)]
    near = after(near, got[0])
    parts = [near, swap(near, 4), swap(near, 2), swap(near, 6)]
    part_sum = add([codes[0]] + got, False)


    def select(tail, *others):
        return pl.pallas_call(
            functools.partial(select_kernel, n_ex=n_ex, rows=rows, tail=tail),
            in_specs=[vmem],
            out_specs=vmem,
            out_shape=jax.ShapeDtypeStruct((total, n_ex * 8), bf16),
            compiler_params=limit,
            name="select_tails" if tail else "select_rows",
        )(after(pick_index, *others))

    one = select(False, part_sum)
    rest = select(True, part_sum)
    for mask in far_masks:
        part_sum = add([part_sum, after(swap(part_sum, mask), one, rest)], mask == far_masks[-1])
    own_parts = [part_sum, swap(part_sum, 4), swap(part_sum, 2), swap(part_sum, 6)]
    parts = [after(p, own_parts[2], own_parts[3]) for p in parts]
    parts = parts + [swap(p, 1) for p in parts]

    x, factor = pl.pallas_call(
        functools.partial(picked_kernel, steps=steps),
        in_specs=[vmem] * (2 + len(parts)),
        out_specs=[vmem] * 2,
        out_shape=[
            jax.ShapeDtypeStruct((total, full), bf16),
            jax.ShapeDtypeStruct((classes, 128), f32),
        ],
        scratch_shapes=[pltpu.VMEM((n_ex * 8, main), bf16)],
        compiler_params=limit,
        name="picked_rows",
    )(one, rest, *parts)

    own_parts, x = lax.optimization_barrier((own_parts, x))
    own_half = jnp.concatenate(own_parts, axis=0)
    twin_half = swap(own_half, 1)
    left = pltpu.VMEM((total, full // 2), bf16)
    direct, right, target = pl.pallas_call(
        functools.partial(half_kernel, classes=classes),
        in_specs=[vmem] * 3,
        out_specs=[vmem] * 3,
        out_shape=[
            jax.ShapeDtypeStruct((total, rows), f32),
            jax.ShapeDtypeStruct((classes, total), f32),
            jax.ShapeDtypeStruct((classes, full // 2), f32),
        ],
        scratch_shapes=[left],
        compiler_params=limit,
        name="own_half_products",
    )(feat, own_half, x)

    scores, resid = pl.pallas_call(
        functools.partial(pursuit_kernel, steps=steps, scale=1.0 / math.sqrt(full)),
        in_specs=[vmem] * 8,
        out_specs=[vmem, anywhere],
        out_shape=[
            jax.ShapeDtypeStruct((steps, rows), f32),
            jax.ShapeDtypeStruct((classes, full), f32),
        ],
        scratch_shapes=[pltpu.VMEM((classes, full), f32), left, pltpu.SemaphoreType.DMA((4,))],
        compiler_params=limit,
        name="pursuit",
    )(labels, feat, x, factor, direct, right, target, twin_half)
    return scores, resid


def solution(mesh):
    return jax.shard_map(
        functools.partial(on_device, n_ex=mesh.shape["ex"]),
        mesh=mesh,
        in_specs=(P(("grp", "ex"), None), P(("grp", "ex")), P("grp", None)),
        out_specs=(P(None, ("grp", "ex")), P("grp", None)),
        check_vma=False,
    )
```

```python
import functools
import math

import jax
import jax.numpy as jnp
from jax import lax
from jax.experimental import pallas as pl
from jax.experimental.pallas import tpu as pltpu
from jax.sharding import PartitionSpec as P

ridge = 1.0
slots = 2
near_masks = (0, 4, 2, 6)
f32 = jnp.float32
bf16 = jnp.bfloat16


def nt_dot(a, b):
    return lax.dot_general(a, b, (((1,), (1,)), ((), ())), preferred_element_type=f32)


def column(tile, height, start=0):
    return jnp.concatenate([tile[:, start + q : start + q + 1] for q in range(height // 8)], axis=0)


def spread(values, start=0):
    lane = lax.broadcasted_iota(jnp.int32, (8, 128), 1)
    tile = jnp.zeros((8, 128), f32)
    for q in range(values.shape[0] // 8):
        tile = jnp.where(lane == start + q, values[8 * q : 8 * q + 8], tile)
    return tile


def encode(x, count_tile=None):
    height, width = x.shape
    top = jnp.max(jnp.abs(x), axis=1, keepdims=True)
    power = jnp.ceil(jnp.log2(jnp.maximum(top, 1e-30)) + 0.01)
    whole_x = jnp.round(x * jnp.exp2(15.0 - power))
    mark = spread(power)
    if count_tile is not None:
        mark = mark + count_tile
    chunks = [whole_x[:, j * 128 : (j + 1) * 128] for j in range(width // 128)]
    return jnp.concatenate(chunks + [mark], axis=0).astype(jnp.int32).astype(jnp.int16)


def decode(code, height):
    value = code.astype(jnp.int32).astype(f32)
    count = value.shape[0] // height
    mark = value[count * height :]
    x = jnp.concatenate([value[j * height : (j + 1) * height] for j in range(count)], axis=1)
    return x * jnp.exp2(column(mark, height) - 15.0), mark


def sums_kernel(
    labels_hbm, pick_hbm, feat_hbm, feat_ref, sums_ref, tile_ref, code_ref, held, labels_ref, pick_ref, left, sems
):
    rows, full = feat_ref.shape
    steps, classes = pick_ref.shape
    blocks, _, width = sums_ref.shape
    device = lax.axis_index("ex")
    small = [
        pltpu.make_async_copy(pick_hbm, pick_ref, sems.at[blocks]),
        pltpu.make_async_copy(labels_hbm, labels_ref, sems.at[blocks + 1]),
    ]
    for copy in small:
        copy.start()
    copies = []
    for i in range(blocks):
        at = slice(i * width, (i + 1) * width)
        copies.append(pltpu.make_async_copy(feat_hbm.at[:, at], feat_ref.at[:, at], sems.at[i]))
        copies[-1].start()

    for copy in small:
        copy.wait()
    local = pick_ref[...] - device * rows
    mine = (local >= 0) & (local < rows)
    lane = lax.broadcasted_iota(jnp.int32, local.shape, 1)
    first = jnp.min(jnp.where(mine, lane, classes), axis=1, keepdims=True)
    last = jnp.max(jnp.where(mine, lane, -1), axis=1, keepdims=True)
    spot0 = jnp.max(jnp.where(mine & (lane == first), local, -1), axis=1, keepdims=True)
    spot1 = jnp.max(jnp.where(mine & (lane == last) & (last > first), local, -1), axis=1, keepdims=True)
    member = lax.broadcasted_iota(jnp.int32, (classes, rows), 0) == labels_ref[...].reshape(1, rows)
    line = lax.broadcasted_iota(jnp.int32, (steps, rows), 1)
    left[...] = jnp.concatenate(
        [
            jnp.where(member, 1.0, 0.0),
            jnp.where(line == spot0, 1.0, 0.0),
            jnp.where(line == spot1, 1.0, 0.0),
            jnp.zeros((16 - 2 * steps, rows), f32),
        ],
        axis=0,
    ).astype(bf16)
    count = jnp.sum(jnp.where(member, 1.0, 0.0), axis=1, keepdims=True)
    tile = spread(count, classes // 8)
    tile_ref[...] = tile

    for i in range(blocks):
        at = slice(i * width, (i + 1) * width)
        copies[i].wait()
        both = jnp.dot(left[...], feat_ref[:, at], preferred_element_type=f32)
        sums_ref[i] = both[:classes]
        code_ref[i] = encode(both[:classes], tile)
        held[:, at] = both[classes : classes + 8]


def pack_kernel(held, rows_ref, *, steps):
    used = steps * slots
    main = rows_ref.shape[1]
    lines = [held[0:used, :main]]
    for q in range(slots):
        lines.append(jnp.concatenate([held[q * steps + u : q * steps + u + 1, main:] for u in range(steps)], axis=1))
    rows_ref[...] = jnp.concatenate(lines, axis=0).astype(bf16)


def near_id(mask):
    return (lax.axis_index("ex") // 2 % 4) ^ (mask // 2)


def pair_kernel(sums_ref, tile_ref, got_ref, *code_refs, classes):
    lane = lax.broadcasted_iota(jnp.int32, (8, 128), 1)
    for mask, code_ref in zip(near_masks, code_refs):
        for j in range(code_ref.shape[0]):
            block = near_id(mask) * code_ref.shape[0] + j
            more, mark = decode(got_ref[block], classes)
            mark = jnp.where(lane < classes // 8, 0.0, mark) + tile_ref[...]
            code_ref[j] = encode(sums_ref[block] + more, mark)


def add_kernel(*refs, classes, last):
    code_ref = refs[-1]
    for j in range(code_ref.shape[0]):
        value, mark = decode(refs[0][j], classes)
        for ref in refs[1:-1]:
            more, more_mark = decode(ref[j], classes)
            value = value + more
            mark = mark + more_mark
        if last:
            code_ref[j] = encode(value / jnp.sqrt(column(mark, classes, classes // 8)))
        else:
            lane = lax.broadcasted_iota(jnp.int32, mark.shape, 1)
            code_ref[j] = encode(value, jnp.where(lane < classes // 8, 0.0, mark))


def diagonal(block):
    n = block.shape[0]
    eye = lax.broadcasted_iota(jnp.int32, (n, n), 0) == lax.broadcasted_iota(jnp.int32, (n, n), 1)
    return jnp.sum(jnp.where(eye, block, 0.0), axis=1, keepdims=True)


def factor_all(gram):
    order = len(gram)
    factor = [[None] * order for _ in range(order)]
    for j in range(order):
        value = gram[j][j]
        for k in range(j):
            value = value - factor[j][k] * factor[j][k]
        root = jnp.sqrt(value)
        factor[j][j] = 1.0 / root
        for i in range(j + 1, order):
            value = gram[i][j]
            for k in range(j):
                value = value - factor[i][k] * factor[j][k]
            factor[i][j] = value * factor[j][j]
    return factor


def solve_all(factor, right):
    order = len(right)
    forward = []
    for i in range(order):
        value = right[i]
        for j in range(i):
            value = value - factor[i][j] * forward[j]
        forward.append(value * factor[i][i])
    result = []
    for size in range(1, order + 1):
        back = [None] * size
        for i in reversed(range(size)):
            value = forward[i]
            for j in range(i + 1, size):
                value = value - factor[j][i] * back[j]
            back[i] = value * factor[i][i]
        result.append(back)
    return result


def select_kernel(pick_ref, one_ref, *, n_ex, rows, tail):
    steps, classes = pick_ref.shape
    lines = one_ref.shape[1]
    device = lax.axis_index("ex")
    pick = pick_ref[...]
    lane = lax.broadcasted_iota(jnp.int32, pick.shape, 1)
    owner = jnp.zeros_like(pick)
    rank = jnp.zeros_like(pick)
    for d in range(n_ex):
        here = (pick >= d * rows) & (pick < (d + 1) * rows)
        first = jnp.min(jnp.where(here, lane, classes), axis=1, keepdims=True)
        owner = jnp.where(here, d, owner)
        rank = jnp.where(here & (lane > first), 1, rank)
    away = owner ^ device
    spot = jnp.zeros_like(pick)
    bits = n_ex.bit_length() - 1
    for b in range(1, bits):
        spot = spot + (((away >> b) & 1) << (bits - 1 - b))
    spot = 2 * spot + 1 - (owner & 1)
    step = lax.broadcasted_iota(jnp.int32, pick.shape, 0)
    line = lax.broadcasted_iota(jnp.int32, (lines, classes), 0)
    where = spot * 8 + (slots * steps + rank if tail else rank * steps + step)
    hits = [jnp.where(line == where[s : s + 1, :], 1.0, 0.0) for s in range(steps)]
    pad = jnp.zeros((lines, 128 - steps * classes), f32)
    one_ref[...] = jnp.transpose(jnp.concatenate(hits + [pad], axis=1))[: steps * classes].astype(bf16)


def picked_kernel(one_ref, rest_ref, *refs, steps):
    (x_ref, factor_ref, rows_ref), count = refs[-3:], (len(refs) - 3) // 2
    odd = lax.axis_index("ex") % 2 == 1
    total, full = x_ref.shape
    classes = total // steps
    main = rows_ref.shape[1]
    tail = full - main
    at = 0
    for mine, got in zip(refs[:count], refs[count : 2 * count]):
        here = slice(at, at + mine.shape[0])

        @pl.when(odd)
        def _():
            rows_ref[here, :] = mine[...]

        @pl.when(jnp.logical_not(odd))
        def _():
            rows_ref[here, :] = got[...]

        at += mine.shape[0]
    x_ref[:, :main] = jnp.dot(one_ref[...], rows_ref[...], preferred_element_type=f32).astype(bf16)
    for s in range(steps):
        at = slice(s * classes, (s + 1) * classes)
        rest = jnp.dot(rest_ref[at, :], rows_ref[:, s * tail : (s + 1) * tail], preferred_element_type=f32)
        x_ref[at, main:] = rest.astype(bf16)

    x = x_ref[...]
    full_gram = nt_dot(x, x)
    gram = [
        [
            diagonal(full_gram[a * classes : (a + 1) * classes, b * classes : (b + 1) * classes])
            + (ridge if a == b else 0.0)
            for b in range(a + 1)
        ]
        for a in range(steps)
    ]
    factor = factor_all(gram)
    lane = lax.broadcasted_iota(jnp.int32, (classes, 128), 1)
    packed = jnp.zeros((classes, 128), f32)
    for i in range(steps):
        for j in range(i + 1):
            packed = jnp.where(lane == i * steps + j, factor[i][j], packed)
    factor_ref[...] = packed


def quarter_target(mask, own_ref, got_ref, x_ref, target_ref, left_ref, *, classes):
    count = own_ref.shape[0]
    span = left_ref.shape[1]
    width = span // count
    used = left_ref.shape[0] - classes
    even = lax.axis_index("ex") % 2 == 0
    quarter = near_id(mask)
    here = pl.ds(pl.multiple_of(quarter * span, span), span)
    for j in range(count):
        target = decode(jnp.where(even, own_ref[j].astype(jnp.int32), got_ref[j].astype(jnp.int32)), classes)[0]
        at = slice(j * width, (j + 1) * width)
        target_ref[:, at] = target
        left_ref[:classes, at] = target.astype(bf16)
    left_ref[classes:, :] = x_ref[:used, here]
    return nt_dot(left_ref[:classes, :], x_ref[:, here]), here


def first_kernel(feat_ref, own_ref, got_ref, x_ref, direct_ref, right_ref, target_ref, left_ref, *, classes):
    right_ref[...], here = quarter_target(0, own_ref, got_ref, x_ref, target_ref, left_ref, classes=classes)
    direct_ref[...] = nt_dot(left_ref[...], feat_ref[:, here])


def pursuit_kernel(
    labels_ref, feat_ref, x_ref, factor_ref, direct_first, right_first, target_first, *refs, steps, scale
):
    owns, gots, (scores_ref, resid_hbm, target_ref, left_ref, sems) = refs[:3], refs[3:6], refs[6:]
    classes = target_first.shape[0]
    right = right_first[...]
    places = []
    for k, mask in enumerate(near_masks[1:]):
        more, here = quarter_target(
            mask, owns[k], gots[k], x_ref, target_ref.at[k + 1], left_ref.at[k], classes=classes
        )
        right = right + more
        places.append(here)
    span = target_first.shape[1]
    target_ref[0] = target_first[...]
    places.insert(0, pl.ds(pl.multiple_of(near_id(0) * span, span), span))
    rhs = [diagonal(right[:, a * classes : (a + 1) * classes]) for a in range(steps)]
    factor = [[factor_ref[:, i * steps + j : i * steps + j + 1] for j in range(i + 1)] for i in range(steps)]
    weights = solve_all(factor, rhs)
    last = weights[steps - 1]
    copies = []
    for q, here in enumerate(places):
        value = target_ref[q]
        for k in range(steps):
            value = value - last[k] * x_ref[k * classes : (k + 1) * classes, here].astype(f32)
        target_ref[q] = value
        copies.append(pltpu.make_async_copy(target_ref.at[q], resid_hbm.at[:, here], sems.at[q]))
        copies[-1].start()

    direct = direct_first[...]
    for k, here in enumerate(places[1:]):
        direct = direct + nt_dot(left_ref[k], feat_ref[:, here])
    member = lax.broadcasted_iota(jnp.int32, (classes, direct.shape[1]), 0) == labels_ref[...].reshape(1, direct.shape[1])
    for s in range(steps):
        value = direct[:classes]
        for k in range(s):
            value = value - weights[s - 1][k] * direct[(k + 1) * classes : (k + 2) * classes]
        scores_ref[s : s + 1, :] = jnp.sum(jnp.where(member, value, 0.0), axis=0, keepdims=True) * scale
    for copy in copies:
        copy.wait()


def on_device(features, labels, pick_index, *, n_ex):
    rows, full = features.shape
    steps, classes = pick_index.shape
    total = steps * classes
    main = full * steps * slots // 8
    blocks = 16
    width = full // blocks
    limit = pltpu.CompilerParams(vmem_limit_bytes=16 << 20)
    vmem = pl.BlockSpec(memory_space=pltpu.VMEM)
    hbm = pl.BlockSpec(memory_space=pltpu.HBM)
    anywhere = pl.BlockSpec(memory_space=pl.ANY)
    code = jax.ShapeDtypeStruct((blocks // 4, classes * (width // 128) + 8, 128), jnp.int16)

    def after(x, *others):
        return lax.optimization_barrier((x,) + others)[0]

    def move(x, side, mask):
        return lax.ppermute(x, "ex", [(d, d ^ mask) for d in range(side, n_ex, 2)])

    feat, sums, tile, sum_codes, held = pl.pallas_call(
        sums_kernel,
        in_specs=[hbm] * 3,
        out_specs=[vmem] * 5,
        out_shape=[
            pltpu.VMEM((rows, full), bf16),
            jax.ShapeDtypeStruct((blocks, classes, width), f32),
            jax.ShapeDtypeStruct((8, 128), f32),
            jax.ShapeDtypeStruct((blocks,) + code.shape[1:], jnp.int16),
            jax.ShapeDtypeStruct((8, full), f32),
        ],
        scratch_shapes=[
            pltpu.VMEM(labels.shape, jnp.int32),
            pltpu.VMEM(pick_index.shape, jnp.int32),
            pltpu.VMEM((classes + 16, rows), bf16),
            pltpu.SemaphoreType.DMA((blocks + 2,)),
        ],
        compiler_params=limit,
        name="class_sums",
    )(*[pltpu.with_memory_space_constraint(a, pltpu.HBM) for a in (labels, pick_index, features)])

    packed = pl.pallas_call(
        functools.partial(pack_kernel, steps=steps),
        in_specs=[vmem],
        out_specs=vmem,
        out_shape=jax.ShapeDtypeStruct((8, main), bf16),
        compiler_params=limit,
        name="pack_rows",
    )(held)

    far_masks = [8 << b for b in range(n_ex.bit_length() - 4)]
    twin_codes = move(sum_codes, 1, 1)
    codes = pl.pallas_call(
        functools.partial(pair_kernel, classes=classes),
        in_specs=[vmem] * 3,
        out_specs=[vmem] * 4,
        out_shape=[code] * 4,
        compiler_params=limit,
        name="pair_sums",
    )(sums, tile, twin_codes)

    def add(parts, last):
        return pl.pallas_call(
            functools.partial(add_kernel, classes=classes, last=last),
            in_specs=[vmem] * len(parts),
            out_specs=vmem,
            out_shape=code,
            compiler_params=limit,
            name="add_sums",
        )(*parts)

    near_codes = [move(c, 0, m) for c, m in zip(codes[1:], near_masks[1:])]
    part_sum = add([codes[0]] + near_codes, False)
    for mask in far_masks:
        part_sum = add([part_sum, move(part_sum, 0, mask)], mask == far_masks[-1])

    near = after(jnp.concatenate([packed, move(packed, 0, 1)], axis=0), twin_codes)
    for mask in reversed(far_masks):
        near = jnp.concatenate([near, move(near, 1, mask)], axis=0)
    near = after(near, near_codes[0])
    own_rows = [near] + [move(near, 1, m) for m in near_masks[1:]]

    own = [part_sum] + [move(part_sum, 0, m) for m in near_masks[1:3]]
    own.append(move(after(part_sum, own_rows[1]), 0, near_masks[3]))
    got = [move(after(c, own[1]), 0, 1) for c in own]
    got_rows = [move(near, 1, 1)] + [move(after(p, *own[1:]), 1, 1) for p in own_rows[1:]]

    def select(tail):
        return pl.pallas_call(
            functools.partial(select_kernel, n_ex=n_ex, rows=rows, tail=tail),
            in_specs=[vmem],
            out_specs=vmem,
            out_shape=jax.ShapeDtypeStruct((total, n_ex * 8), bf16),
            compiler_params=limit,
            name="select_tails" if tail else "select_rows",
        )(after(pick_index, packed))

    x, factor = pl.pallas_call(
        functools.partial(picked_kernel, steps=steps),
        in_specs=[vmem] * 10,
        out_specs=[vmem] * 2,
        out_shape=[
            jax.ShapeDtypeStruct((total, full), bf16),
            jax.ShapeDtypeStruct((classes, 128), f32),
        ],
        scratch_shapes=[pltpu.VMEM((n_ex * 8, main), bf16)],
        compiler_params=limit,
        name="picked_rows",
    )(select(False), select(True), *own_rows, *got_rows)

    span = full // 4
    direct, right, target = pl.pallas_call(
        functools.partial(first_kernel, classes=classes),
        in_specs=[vmem] * 4,
        out_specs=[vmem] * 3,
        out_shape=[
            jax.ShapeDtypeStruct((total, rows), f32),
            jax.ShapeDtypeStruct((classes, total), f32),
            jax.ShapeDtypeStruct((classes, span), f32),
        ],
        scratch_shapes=[pltpu.VMEM((total, span), bf16)],
        compiler_params=limit,
        name="first_products",
    )(feat, own[0], got[0], x)

    scores, resid = pl.pallas_call(
        functools.partial(pursuit_kernel, steps=steps, scale=1.0 / math.sqrt(full)),
        in_specs=[vmem] * 13,
        out_specs=[vmem, anywhere],
        out_shape=[
            jax.ShapeDtypeStruct((steps, rows), f32),
            jax.ShapeDtypeStruct((classes, full), f32),
        ],
        scratch_shapes=[
            pltpu.VMEM((4, classes, span), f32),
            pltpu.VMEM((3, total, span), bf16),
            pltpu.SemaphoreType.DMA((4,)),
        ],
        compiler_params=limit,
        name="pursuit",
    )(labels, feat, x, factor, direct, right, target, *own[1:], *got[1:])
    return scores, resid


def solution(mesh):
    return jax.shard_map(
        functools.partial(on_device, n_ex=mesh.shape["ex"]),
        mesh=mesh,
        in_specs=(P(("grp", "ex"), None), P(("grp", "ex")), P("grp", None)),
        out_specs=(P(None, ("grp", "ex")), P("grp", None)),
        check_vma=False,
    )
```

```python
import functools
import math

import jax
import jax.numpy as jnp
from jax import lax
from jax.experimental import pallas as pl
from jax.experimental.pallas import tpu as pltpu
from jax.sharding import PartitionSpec as P

ridge = 1.0
slots = 2
near_masks = (0, 4, 2, 6)
f32 = jnp.float32
bf16 = jnp.bfloat16


def nt_dot(a, b):
    return lax.dot_general(a, b, (((1,), (1,)), ((), ())), preferred_element_type=f32)


def column(tile, height, start=0):
    return jnp.concatenate([tile[:, start + q : start + q + 1] for q in range(height // 8)], axis=0)


def spread(values, start=0):
    lane = lax.broadcasted_iota(jnp.int32, (8, 128), 1)
    tile = jnp.zeros((8, 128), f32)
    for q in range(values.shape[0] // 8):
        tile = jnp.where(lane == start + q, values[8 * q : 8 * q + 8], tile)
    return tile


def encode(x, count_tile=None):
    height, width = x.shape
    top = jnp.max(jnp.abs(x), axis=1, keepdims=True)
    power = jnp.ceil(jnp.log2(jnp.maximum(top, 1e-30)) + 0.01)
    whole_x = jnp.round(x * jnp.exp2(15.0 - power))
    mark = spread(power)
    if count_tile is not None:
        mark = mark + count_tile
    chunks = [whole_x[:, j * 128 : (j + 1) * 128] for j in range(width // 128)]
    return jnp.concatenate(chunks + [mark], axis=0).astype(jnp.int32).astype(jnp.int16)


def decode(code, height):
    value = code.astype(jnp.int32).astype(f32)
    count = value.shape[0] // height
    mark = value[count * height :]
    x = jnp.concatenate([value[j * height : (j + 1) * height] for j in range(count)], axis=1)
    return x * jnp.exp2(column(mark, height) - 15.0), mark


def sums_kernel(
    labels_hbm, pick_hbm, feat_hbm, feat_ref, send_ref, keep_ref, labels_ref, pick_ref, left, sems, *, n_ex
):
    rows, full = feat_ref.shape
    steps, classes = pick_ref.shape
    width = full // n_ex
    groups = n_ex // 2
    device = lax.axis_index("ex")
    core = device % 2
    small = [
        pltpu.make_async_copy(pick_hbm, pick_ref, sems.at[n_ex]),
        pltpu.make_async_copy(labels_hbm, labels_ref, sems.at[n_ex + 1]),
    ]
    for copy in small:
        copy.start()
    columns = []
    copies = []
    for i in range(n_ex):
        block = (1 - core) * groups + i if i < groups else core * groups + i - groups
        at = pl.ds(pl.multiple_of(block * width, width), width)
        columns.append(at)
        copies.append(pltpu.make_async_copy(feat_hbm.at[:, at], feat_ref.at[:, at], sems.at[i]))
        copies[-1].start()

    for copy in small:
        copy.wait()
    local = pick_ref[...] - device * rows
    mine = (local >= 0) & (local < rows)
    lane = lax.broadcasted_iota(jnp.int32, local.shape, 1)
    first = jnp.min(jnp.where(mine, lane, classes), axis=1, keepdims=True)
    last = jnp.max(jnp.where(mine, lane, -1), axis=1, keepdims=True)
    spot0 = jnp.max(jnp.where(mine & (lane == first), local, -1), axis=1, keepdims=True)
    spot1 = jnp.max(jnp.where(mine & (lane == last) & (last > first), local, -1), axis=1, keepdims=True)
    member = lax.broadcasted_iota(jnp.int32, (classes, rows), 0) == labels_ref[...].reshape(1, rows)
    line = lax.broadcasted_iota(jnp.int32, (steps, rows), 1)
    left[...] = jnp.concatenate(
        [
            jnp.where(member, 1.0, 0.0),
            jnp.where(line == spot0, 1.0, 0.0),
            jnp.where(line == spot1, 1.0, 0.0),
            jnp.zeros((16 - 2 * steps, rows), f32),
        ],
        axis=0,
    ).astype(bf16)
    count = jnp.sum(jnp.where(member, 1.0, 0.0), axis=1, keepdims=True)
    tile = spread(count, classes // 8)
    base = groups * classes
    for ref in (send_ref, keep_ref):
        ref[base : base + 8, :128] = tile
        if width > 128:
            ref[base : base + 8, 128:] = jnp.zeros((8, width - 128), f32)

    for i in range(n_ex):
        copies[i].wait()
        both = jnp.dot(left[...], feat_ref[:, columns[i]], preferred_element_type=f32)
        k = i % groups
        ref = send_ref if i < groups else keep_ref
        ref[k * classes : (k + 1) * classes, :] = both[:classes]
        ref[base + 8 + 8 * k : base + 16 + 8 * k, :] = both[classes : classes + 8]


def pack_kernel(keep_ref, got_ref, rows_ref, *, steps, start):
    lines, main = rows_ref.shape
    used = steps * slots
    count = (keep_ref.shape[0] - start) // 8
    halves = []
    for ref in (keep_ref, got_ref):
        halves.append(jnp.concatenate([ref[start + 8 * k : start + 8 * k + 8, :] for k in range(count)], axis=1))
    out = [h[:used, :main] for h in halves]
    for h in halves:
        for q in range(slots):
            out.append(jnp.concatenate([h[q * steps + u : q * steps + u + 1, main:] for u in range(steps)], axis=1))
    rows_ref[...] = jnp.concatenate(out, axis=0).astype(bf16)


def near_id(mask):
    return (lax.axis_index("ex") // 2 % 4) ^ (mask // 2)


def pair_kernel(keep_ref, got_ref, *code_refs, classes):
    far = code_refs[0].shape[0]
    base = 4 * far * classes
    tile = keep_ref[base : base + 8, :128] + got_ref[base : base + 8, :128]
    for mask, code_ref in zip(near_masks, code_refs):
        for j in range(far):
            at = pl.ds(pl.multiple_of((j * 4 + near_id(mask)) * classes, classes), classes)
            code_ref[j] = encode(keep_ref[at, :] + got_ref[at, :], tile)


def add_kernel(*refs, classes, last):
    code_ref = refs[-1]
    for j in range(code_ref.shape[0]):
        value, mark = decode(refs[0][j], classes)
        for ref in refs[1:-1]:
            more, more_mark = decode(ref[j], classes)
            value = value + more
            mark = mark + more_mark
        if last:
            code_ref[j] = encode(value / jnp.sqrt(column(mark, classes, classes // 8)))
        else:
            lane = lax.broadcasted_iota(jnp.int32, mark.shape, 1)
            code_ref[j] = encode(value, jnp.where(lane < classes // 8, 0.0, mark))


def diagonal(block):
    n = block.shape[0]
    eye = lax.broadcasted_iota(jnp.int32, (n, n), 0) == lax.broadcasted_iota(jnp.int32, (n, n), 1)
    return jnp.sum(jnp.where(eye, block, 0.0), axis=1, keepdims=True)


def factor_all(gram):
    order = len(gram)
    factor = [[None] * order for _ in range(order)]
    for j in range(order):
        value = gram[j][j]
        for k in range(j):
            value = value - factor[j][k] * factor[j][k]
        root = jnp.sqrt(value)
        factor[j][j] = 1.0 / root
        for i in range(j + 1, order):
            value = gram[i][j]
            for k in range(j):
                value = value - factor[i][k] * factor[j][k]
            factor[i][j] = value * factor[j][j]
    return factor


def solve_all(factor, right):
    order = len(right)
    forward = []
    for i in range(order):
        value = right[i]
        for j in range(i):
            value = value - factor[i][j] * forward[j]
        forward.append(value * factor[i][i])
    result = []
    for size in range(1, order + 1):
        back = [None] * size
        for i in reversed(range(size)):
            value = forward[i]
            for j in range(i + 1, size):
                value = value - factor[j][i] * back[j]
            back[i] = value * factor[i][i]
        result.append(back)
    return result


def select_kernel(pick_ref, one_ref, *, n_ex, rows, tail):
    steps, classes = pick_ref.shape
    lines = one_ref.shape[1]
    device = lax.axis_index("ex")
    pick = pick_ref[...]
    lane = lax.broadcasted_iota(jnp.int32, pick.shape, 1)
    owner = jnp.zeros_like(pick)
    rank = jnp.zeros_like(pick)
    for d in range(n_ex):
        here = (pick >= d * rows) & (pick < (d + 1) * rows)
        first = jnp.min(jnp.where(here, lane, classes), axis=1, keepdims=True)
        owner = jnp.where(here, d, owner)
        rank = jnp.where(here & (lane > first), 1, rank)
    away = owner ^ device
    spot = jnp.zeros_like(pick)
    bits = n_ex.bit_length() - 1
    for b in range(1, bits):
        spot = spot + (((away >> b) & 1) << (bits - 1 - b))
    other = away & 1
    used = steps * slots
    step = lax.broadcasted_iota(jnp.int32, pick.shape, 0)
    line = lax.broadcasted_iota(jnp.int32, (lines, classes), 0)
    if tail:
        where = spot * 16 + 2 * used + other * slots + rank
    else:
        where = spot * 16 + other * used + rank * steps + step
    hits = [jnp.where(line == where[s : s + 1, :], 1.0, 0.0) for s in range(steps)]
    pad = jnp.zeros((lines, 128 - steps * classes), f32)
    one_ref[...] = jnp.transpose(jnp.concatenate(hits + [pad], axis=1))[: steps * classes].astype(bf16)


def picked_kernel(one_ref, rest_ref, *refs, steps):
    parts, (x_ref, rows_ref) = refs[:-2], refs[-2:]
    total, half = x_ref.shape
    classes = total // steps
    main = rows_ref.shape[1]
    tail = half - main
    at = 0
    for part in parts:
        rows_ref[at : at + part.shape[0], :] = part[...]
        at += part.shape[0]
    x_ref[:, :main] = jnp.dot(one_ref[...], rows_ref[...], preferred_element_type=f32).astype(bf16)
    for s in range(steps):
        at = slice(s * classes, (s + 1) * classes)
        rest = jnp.dot(rest_ref[at, :], rows_ref[:, s * tail : (s + 1) * tail], preferred_element_type=f32)
        x_ref[at, main:] = rest.astype(bf16)


def half_target(side, code_ref, x_ref, target_ref, target_at, left_ref, *, classes):
    half = left_ref.shape[1]
    far = code_ref.shape[0] // 4
    width = half // code_ref.shape[0]
    here = pl.ds(pl.multiple_of(side * half, half), half)
    for k in range(4 * far):
        block = k % far * 4 + near_id(near_masks[k // far])
        target = decode(code_ref[k], classes)[0]
        target_ref[:, pl.ds(pl.multiple_of(target_at + block * width, width), width)] = target
        left_ref[:classes, pl.ds(pl.multiple_of(block * width, width), width)] = target.astype(bf16)
    left_ref[classes:, :] = x_ref[...]
    return nt_dot(left_ref[...], x_ref[...]), here


def half_kernel(feat_ref, code_ref, x_ref, direct_ref, gram_ref, target_ref, left_ref, *, classes):
    core = lax.axis_index("ex") % 2
    gram_ref[...], here = half_target(core, code_ref, x_ref, target_ref, 0, left_ref, classes=classes)
    direct_ref[...] = nt_dot(left_ref[: direct_ref.shape[0], :], feat_ref[:, here])


def pursuit_kernel(
    labels_ref, feat_ref, x_own, x_twin, direct_own, gram_own, target_own, code_ref,
    scores_ref, resid_hbm, resid_ref, left_ref, sems, *, steps, scale
):
    classes, full = resid_ref.shape
    half = full // 2
    core = lax.axis_index("ex") % 2
    gram, other = half_target(1 - core, code_ref, x_twin, resid_ref, (1 - core) * half, left_ref, classes=classes)
    gram = gram + gram_own[...]
    blocks = [
        [
            diagonal(gram[(a + 1) * classes : (a + 2) * classes, b * classes : (b + 1) * classes])
            + (ridge if a == b else 0.0)
            for b in range(a + 1)
        ]
        for a in range(steps)
    ]
    rhs = [diagonal(gram[:classes, a * classes : (a + 1) * classes]) for a in range(steps)]
    weights = solve_all(factor_all(blocks), rhs)
    last = weights[steps - 1]
    copies = []
    span = half // 2
    for x_ref, side in ((x_own, core), (x_twin, 1 - core)):
        for q in range(2):
            there = slice(q * span, (q + 1) * span)
            here = pl.ds(pl.multiple_of(side * half + q * span, span), span)
            value = target_own[:, there] if x_ref is x_own else resid_ref[:, here]
            for k in range(steps):
                value = value - last[k] * x_ref[k * classes : (k + 1) * classes, there].astype(f32)
            resid_ref[:, here] = value
            copies.append(pltpu.make_async_copy(resid_ref.at[:, here], resid_hbm.at[:, here], sems.at[len(copies)]))
            copies[-1].start()

    direct = direct_own[...] + nt_dot(left_ref[: direct_own.shape[0], :], feat_ref[:, other])
    member = lax.broadcasted_iota(jnp.int32, (classes, direct.shape[1]), 0) == labels_ref[...].reshape(1, direct.shape[1])
    for s in range(steps):
        value = direct[:classes]
        for k in range(s):
            value = value - weights[s - 1][k] * direct[(k + 1) * classes : (k + 2) * classes]
        scores_ref[s : s + 1, :] = jnp.sum(jnp.where(member, value, 0.0), axis=0, keepdims=True) * scale
    for copy in copies:
        copy.wait()


def on_device(features, labels, pick_index, *, n_ex):
    rows, full = features.shape
    steps, classes = pick_index.shape
    groups = n_ex // 2
    width = full // n_ex
    total = steps * classes
    main = full // 2 * steps * slots // 8
    limit = pltpu.CompilerParams(vmem_limit_bytes=16 << 20)
    vmem = pl.BlockSpec(memory_space=pltpu.VMEM)
    hbm = pl.BlockSpec(memory_space=pltpu.HBM)
    anywhere = pl.BlockSpec(memory_space=pl.ANY)
    half = jax.ShapeDtypeStruct((groups * (classes + 8) + 8, width), f32)
    code = jax.ShapeDtypeStruct((groups // 4, classes * (width // 128) + 8, 128), jnp.int16)

    def swap(x, mask):
        return lax.ppermute(x, "ex", [(d, d ^ mask) for d in range(n_ex)])

    def after(x, *others):
        return lax.optimization_barrier((x,) + others)[0]

    feat, send, keep = pl.pallas_call(
        functools.partial(sums_kernel, n_ex=n_ex),
        in_specs=[hbm] * 3,
        out_specs=[vmem] * 3,
        out_shape=[pltpu.VMEM((rows, full), bf16), half, half],
        scratch_shapes=[
            pltpu.VMEM(labels.shape, jnp.int32),
            pltpu.VMEM(pick_index.shape, jnp.int32),
            pltpu.VMEM((classes + 16, rows), bf16),
            pltpu.SemaphoreType.DMA((n_ex + 2,)),
        ],
        compiler_params=limit,
        name="class_sums",
    )(*[pltpu.with_memory_space_constraint(a, pltpu.HBM) for a in (labels, pick_index, features)])

    def add(codes, last):
        return pl.pallas_call(
            functools.partial(add_kernel, classes=classes, last=last),
            in_specs=[vmem] * len(codes),
            out_specs=vmem,
            out_shape=code,
            compiler_params=limit,
            name="add_sums",
        )(*codes)

    far_masks = [8 << b for b in range(n_ex.bit_length() - 4)]
    got = swap(send, 1)
    codes = pl.pallas_call(
        functools.partial(pair_kernel, classes=classes),
        in_specs=[vmem] * 2,
        out_specs=[vmem] * 4,
        out_shape=[code] * 4,
        compiler_params=limit,
        name="pair_sums",
    )(keep, got)
    near = pl.pallas_call(
        functools.partial(pack_kernel, steps=steps, start=groups * classes + 8),
        in_specs=[vmem] * 2,
        out_specs=vmem,
        out_shape=jax.ShapeDtypeStruct((16, main), bf16),
        compiler_params=limit,
        name="pack_rows",
    )(keep, got)
    for mask in reversed(far_masks):
        near = jnp.concatenate([near, swap(near, mask)], axis=0)

    near_codes = [swap(c, m) for c, m in zip(codes[1:], near_masks[1:])]
    near = after(near, near_codes[0])
    part_sum = add([codes[0]] + near_codes, False)
    parts = [near] + [swap(near, m) for m in near_masks[1:]]

    def select(tail, *others):
        return pl.pallas_call(
            functools.partial(select_kernel, n_ex=n_ex, rows=rows, tail=tail),
            in_specs=[vmem],
            out_specs=vmem,
            out_shape=jax.ShapeDtypeStruct((total, n_ex * 8), bf16),
            compiler_params=limit,
            name="select_tails" if tail else "select_rows",
        )(after(pick_index, *others))

    one = select(False, part_sum)
    rest = select(True, part_sum)
    for mask in far_masks:
        part_sum = add([part_sum, after(swap(part_sum, mask), one, rest)], mask == far_masks[-1])
    own_parts = [part_sum] + [swap(part_sum, m) for m in near_masks[1:3]]
    own_parts.append(swap(after(part_sum, parts[1]), near_masks[3]))

    x = pl.pallas_call(
        functools.partial(picked_kernel, steps=steps),
        in_specs=[vmem] * 6,
        out_specs=vmem,
        out_shape=jax.ShapeDtypeStruct((total, full // 2), bf16),
        scratch_shapes=[pltpu.VMEM((n_ex * 8, main), bf16)],
        compiler_params=limit,
        name="picked_rows",
    )(one, rest, *parts)

    x_twin = swap(x, 1)
    own_half = jnp.concatenate(after(own_parts, x), axis=0)
    twin_half = swap(own_half, 1)
    left = pltpu.VMEM((total + classes, full // 2), bf16)
    direct, gram, target = pl.pallas_call(
        functools.partial(half_kernel, classes=classes),
        in_specs=[vmem] * 3,
        out_specs=[vmem] * 3,
        out_shape=[
            jax.ShapeDtypeStruct((total, rows), f32),
            jax.ShapeDtypeStruct((total + classes, total), f32),
            jax.ShapeDtypeStruct((classes, full // 2), f32),
        ],
        scratch_shapes=[left],
        compiler_params=limit,
        name="own_half_products",
    )(feat, own_half, x)

    scores, resid = pl.pallas_call(
        functools.partial(pursuit_kernel, steps=steps, scale=1.0 / math.sqrt(full)),
        in_specs=[vmem] * 8,
        out_specs=[vmem, anywhere],
        out_shape=[
            jax.ShapeDtypeStruct((steps, rows), f32),
            jax.ShapeDtypeStruct((classes, full), f32),
        ],
        scratch_shapes=[pltpu.VMEM((classes, full), f32), left, pltpu.SemaphoreType.DMA((4,))],
        compiler_params=limit,
        name="pursuit",
    )(labels, feat, x, x_twin, direct, gram, target, twin_half)
    return scores, resid


def solution(mesh):
    return jax.shard_map(
        functools.partial(on_device, n_ex=mesh.shape["ex"]),
        mesh=mesh,
        in_specs=(P(("grp", "ex"), None), P(("grp", "ex")), P("grp", None)),
        out_specs=(P(None, ("grp", "ex")), P("grp", None)),
        check_vma=False,
    )
```

```python
import functools
import math

import jax
import jax.numpy as jnp
from jax import lax
from jax.experimental import pallas as pl
from jax.experimental.pallas import tpu as pltpu
from jax.sharding import PartitionSpec as P

ridge = 1.0
slots = 2
near_masks = (0, 4, 2, 6)
f32 = jnp.float32
bf16 = jnp.bfloat16


def nt_dot(a, b):
    return lax.dot_general(a, b, (((1,), (1,)), ((), ())), preferred_element_type=f32)


def column(tile, height, start=0):
    return jnp.concatenate([tile[:, start + q : start + q + 1] for q in range(height // 8)], axis=0)


def spread(values, start=0):
    lane = lax.broadcasted_iota(jnp.int32, (8, 128), 1)
    tile = jnp.zeros((8, 128), f32)
    for q in range(values.shape[0] // 8):
        tile = jnp.where(lane == start + q, values[8 * q : 8 * q + 8], tile)
    return tile


def encode(x, count_tile=None):
    height, width = x.shape
    top = jnp.max(jnp.abs(x), axis=1, keepdims=True)
    power = jnp.ceil(jnp.log2(jnp.maximum(top, 1e-30)) + 0.01)
    whole_x = jnp.round(x * jnp.exp2(15.0 - power))
    mark = spread(power)
    if count_tile is not None:
        mark = mark + count_tile
    chunks = [whole_x[:, j * 128 : (j + 1) * 128] for j in range(width // 128)]
    return jnp.concatenate(chunks + [mark], axis=0).astype(jnp.int32).astype(jnp.int16)


def decode(code, height):
    value = code.astype(jnp.int32).astype(f32)
    count = value.shape[0] // height
    mark = value[count * height :]
    x = jnp.concatenate([value[j * height : (j + 1) * height] for j in range(count)], axis=1)
    return x * jnp.exp2(column(mark, height) - 15.0), mark


def sums_kernel(
    labels_hbm, pick_hbm, feat_hbm, feat_ref, send_ref, keep_ref, labels_ref, pick_ref, left, sems, *, n_ex
):
    rows, full = feat_ref.shape
    steps, classes = pick_ref.shape
    width = full // n_ex
    groups = n_ex // 2
    device = lax.axis_index("ex")
    core = device % 2
    small = [
        pltpu.make_async_copy(pick_hbm, pick_ref, sems.at[n_ex]),
        pltpu.make_async_copy(labels_hbm, labels_ref, sems.at[n_ex + 1]),
    ]
    for copy in small:
        copy.start()
    columns = []
    copies = []
    for i in range(n_ex):
        block = (1 - core) * groups + i if i < groups else core * groups + i - groups
        at = pl.ds(pl.multiple_of(block * width, width), width)
        columns.append(at)
        copies.append(pltpu.make_async_copy(feat_hbm.at[:, at], feat_ref.at[:, at], sems.at[i]))
        copies[-1].start()

    for copy in small:
        copy.wait()
    local = pick_ref[...] - device * rows
    mine = (local >= 0) & (local < rows)
    lane = lax.broadcasted_iota(jnp.int32, local.shape, 1)
    first = jnp.min(jnp.where(mine, lane, classes), axis=1, keepdims=True)
    last = jnp.max(jnp.where(mine, lane, -1), axis=1, keepdims=True)
    spot0 = jnp.max(jnp.where(mine & (lane == first), local, -1), axis=1, keepdims=True)
    spot1 = jnp.max(jnp.where(mine & (lane == last) & (last > first), local, -1), axis=1, keepdims=True)
    member = lax.broadcasted_iota(jnp.int32, (classes, rows), 0) == labels_ref[...].reshape(1, rows)
    line = lax.broadcasted_iota(jnp.int32, (steps, rows), 1)
    left[...] = jnp.concatenate(
        [
            jnp.where(member, 1.0, 0.0),
            jnp.where(line == spot0, 1.0, 0.0),
            jnp.where(line == spot1, 1.0, 0.0),
            jnp.zeros((16 - 2 * steps, rows), f32),
        ],
        axis=0,
    ).astype(bf16)
    count = jnp.sum(jnp.where(member, 1.0, 0.0), axis=1, keepdims=True)
    tile = spread(count, classes // 8)
    base = groups * classes
    for ref in (send_ref, keep_ref):
        ref[base : base + 8, :128] = tile
        if width > 128:
            ref[base : base + 8, 128:] = jnp.zeros((8, width - 128), f32)

    for i in range(n_ex):
        copies[i].wait()
        both = jnp.dot(left[...], feat_ref[:, columns[i]], preferred_element_type=f32)
        k = i % groups
        ref = send_ref if i < groups else keep_ref
        ref[k * classes : (k + 1) * classes, :] = both[:classes]
        ref[base + 8 + 8 * k : base + 16 + 8 * k, :] = both[classes : classes + 8]


def pack_kernel(keep_ref, got_ref, rows_ref, *, steps, start):
    lines, main = rows_ref.shape
    used = steps * slots
    count = (keep_ref.shape[0] - start) // 8
    halves = []
    for ref in (keep_ref, got_ref):
        halves.append(jnp.concatenate([ref[start + 8 * k : start + 8 * k + 8, :] for k in range(count)], axis=1))
    out = [h[:used, :main] for h in halves]
    for h in halves:
        for q in range(slots):
            out.append(jnp.concatenate([h[q * steps + u : q * steps + u + 1, main:] for u in range(steps)], axis=1))
    rows_ref[...] = jnp.concatenate(out, axis=0).astype(bf16)


def near_id(mask):
    return (lax.axis_index("ex") // 2 % 4) ^ (mask // 2)


def pair_kernel(keep_ref, got_ref, *code_refs, classes):
    far = code_refs[0].shape[0]
    base = 4 * far * classes
    tile = keep_ref[base : base + 8, :128] + got_ref[base : base + 8, :128]
    for mask, code_ref in zip(near_masks, code_refs):
        for j in range(far):
            at = pl.ds(pl.multiple_of((j * 4 + near_id(mask)) * classes, classes), classes)
            code_ref[j] = encode(keep_ref[at, :] + got_ref[at, :], tile)


def add_kernel(*refs, classes, last):
    code_ref = refs[-1]
    for j in range(code_ref.shape[0]):
        value, mark = decode(refs[0][j], classes)
        for ref in refs[1:-1]:
            more, more_mark = decode(ref[j], classes)
            value = value + more
            mark = mark + more_mark
        if last:
            code_ref[j] = encode(value / jnp.sqrt(column(mark, classes, classes // 8)))
        else:
            lane = lax.broadcasted_iota(jnp.int32, mark.shape, 1)
            code_ref[j] = encode(value, jnp.where(lane < classes // 8, 0.0, mark))


def diagonal(block):
    n = block.shape[0]
    eye = lax.broadcasted_iota(jnp.int32, (n, n), 0) == lax.broadcasted_iota(jnp.int32, (n, n), 1)
    return jnp.sum(jnp.where(eye, block, 0.0), axis=1, keepdims=True)


def factor_all(gram):
    order = len(gram)
    factor = [[None] * order for _ in range(order)]
    for j in range(order):
        value = gram[j][j]
        for k in range(j):
            value = value - factor[j][k] * factor[j][k]
        root = jnp.sqrt(value)
        factor[j][j] = 1.0 / root
        for i in range(j + 1, order):
            value = gram[i][j]
            for k in range(j):
                value = value - factor[i][k] * factor[j][k]
            factor[i][j] = value * factor[j][j]
    return factor


def solve_all(factor, right):
    order = len(right)
    forward = []
    for i in range(order):
        value = right[i]
        for j in range(i):
            value = value - factor[i][j] * forward[j]
        forward.append(value * factor[i][i])
    result = []
    for size in range(1, order + 1):
        back = [None] * size
        for i in reversed(range(size)):
            value = forward[i]
            for j in range(i + 1, size):
                value = value - factor[j][i] * back[j]
            back[i] = value * factor[i][i]
        result.append(back)
    return result


def select_kernel(pick_ref, one_ref, *, n_ex, rows, tail):
    steps, classes = pick_ref.shape
    lines = one_ref.shape[1]
    device = lax.axis_index("ex")
    pick = pick_ref[...]
    lane = lax.broadcasted_iota(jnp.int32, pick.shape, 1)
    owner = jnp.zeros_like(pick)
    rank = jnp.zeros_like(pick)
    for d in range(n_ex):
        here = (pick >= d * rows) & (pick < (d + 1) * rows)
        first = jnp.min(jnp.where(here, lane, classes), axis=1, keepdims=True)
        owner = jnp.where(here, d, owner)
        rank = jnp.where(here & (lane > first), 1, rank)
    away = owner ^ device
    spot = jnp.zeros_like(pick)
    bits = n_ex.bit_length() - 1
    for b in range(1, bits):
        spot = spot + (((away >> b) & 1) << (bits - 1 - b))
    other = away & 1
    used = steps * slots
    step = lax.broadcasted_iota(jnp.int32, pick.shape, 0)
    line = lax.broadcasted_iota(jnp.int32, (lines, classes), 0)
    if tail:
        where = spot * 16 + 2 * used + other * slots + rank
    else:
        where = spot * 16 + other * used + rank * steps + step
    hits = [jnp.where(line == where[s : s + 1, :], 1.0, 0.0) for s in range(steps)]
    pad = jnp.zeros((lines, 128 - steps * classes), f32)
    one_ref[...] = jnp.transpose(jnp.concatenate(hits + [pad], axis=1))[: steps * classes].astype(bf16)


def picked_kernel(one_ref, rest_ref, *refs, steps):
    parts, (x_ref, rows_ref) = refs[:-2], refs[-2:]
    total, half = x_ref.shape
    classes = total // steps
    main = rows_ref.shape[1]
    tail = half - main
    at = 0
    for part in parts:
        rows_ref[at : at + part.shape[0], :] = part[...]
        at += part.shape[0]
    x_ref[:, :main] = jnp.dot(one_ref[...], rows_ref[...], preferred_element_type=f32).astype(bf16)
    for s in range(steps):
        at = slice(s * classes, (s + 1) * classes)
        rest = jnp.dot(rest_ref[at, :], rows_ref[:, s * tail : (s + 1) * tail], preferred_element_type=f32)
        x_ref[at, main:] = rest.astype(bf16)


def half_target(side, code_ref, x_ref, target_ref, target_at, left_ref, *, classes):
    half = left_ref.shape[1]
    far = code_ref.shape[0] // 4
    width = half // code_ref.shape[0]
    here = pl.ds(pl.multiple_of(side * half, half), half)
    for k in range(4 * far):
        block = k % far * 4 + near_id(near_masks[k // far])
        target = decode(code_ref[k], classes)[0]
        target_ref[:, pl.ds(pl.multiple_of(target_at + block * width, width), width)] = target
        left_ref[:classes, pl.ds(pl.multiple_of(block * width, width), width)] = target.astype(bf16)
    left_ref[classes:, :] = x_ref[...]
    return nt_dot(left_ref[...], x_ref[...]), here


def half_kernel(feat_ref, code_ref, x_ref, direct_ref, gram_ref, target_ref, left_ref, *, classes):
    core = lax.axis_index("ex") % 2
    gram_ref[...], here = half_target(core, code_ref, x_ref, target_ref, 0, left_ref, classes=classes)
    direct_ref[...] = nt_dot(left_ref[: direct_ref.shape[0], :], feat_ref[:, here])


def pursuit_kernel(
    labels_ref, feat_ref, x_own, x_twin, direct_own, gram_own, target_own, code_ref,
    scores_ref, resid_hbm, resid_ref, left_ref, sems, *, steps, scale
):
    classes, full = resid_ref.shape
    half = full // 2
    core = lax.axis_index("ex") % 2
    gram, other = half_target(1 - core, code_ref, x_twin, resid_ref, (1 - core) * half, left_ref, classes=classes)
    gram = gram + gram_own[...]
    blocks = [
        [
            diagonal(gram[(a + 1) * classes : (a + 2) * classes, b * classes : (b + 1) * classes])
            + (ridge if a == b else 0.0)
            for b in range(a + 1)
        ]
        for a in range(steps)
    ]
    rhs = [diagonal(gram[:classes, a * classes : (a + 1) * classes]) for a in range(steps)]
    weights = solve_all(factor_all(blocks), rhs)
    last = weights[steps - 1]
    copies = []
    span = half // 2
    for x_ref, side in ((x_own, core), (x_twin, 1 - core)):
        for q in range(2):
            there = slice(q * span, (q + 1) * span)
            here = pl.ds(pl.multiple_of(side * half + q * span, span), span)
            value = target_own[:, there] if x_ref is x_own else resid_ref[:, here]
            for k in range(steps):
                value = value - last[k] * x_ref[k * classes : (k + 1) * classes, there].astype(f32)
            resid_ref[:, here] = value
            copies.append(pltpu.make_async_copy(resid_ref.at[:, here], resid_hbm.at[:, here], sems.at[len(copies)]))
            copies[-1].start()

    direct = direct_own[...] + nt_dot(left_ref[: direct_own.shape[0], :], feat_ref[:, other])
    member = lax.broadcasted_iota(jnp.int32, (classes, direct.shape[1]), 0) == labels_ref[...].reshape(1, direct.shape[1])
    for s in range(steps):
        value = direct[:classes]
        for k in range(s):
            value = value - weights[s - 1][k] * direct[(k + 1) * classes : (k + 2) * classes]
        scores_ref[s : s + 1, :] = jnp.sum(jnp.where(member, value, 0.0), axis=0, keepdims=True) * scale
    for copy in copies:
        copy.wait()


def on_device(features, labels, pick_index, *, n_ex):
    rows, full = features.shape
    steps, classes = pick_index.shape
    groups = n_ex // 2
    width = full // n_ex
    total = steps * classes
    main = full // 2 * steps * slots // 8
    limit = pltpu.CompilerParams(vmem_limit_bytes=16 << 20)
    vmem = pl.BlockSpec(memory_space=pltpu.VMEM)
    hbm = pl.BlockSpec(memory_space=pltpu.HBM)
    anywhere = pl.BlockSpec(memory_space=pl.ANY)
    half = jax.ShapeDtypeStruct((groups * (classes + 8) + 8, width), f32)
    code = jax.ShapeDtypeStruct((groups // 4, classes * (width // 128) + 8, 128), jnp.int16)

    def swap(x, mask):
        return lax.ppermute(x, "ex", [(d, d ^ mask) for d in range(n_ex)])

    def after(x, *others):
        return lax.optimization_barrier((x,) + others)[0]

    feat, send, keep = pl.pallas_call(
        functools.partial(sums_kernel, n_ex=n_ex),
        in_specs=[hbm] * 3,
        out_specs=[vmem] * 3,
        out_shape=[pltpu.VMEM((rows, full), bf16), half, half],
        scratch_shapes=[
            pltpu.VMEM(labels.shape, jnp.int32),
            pltpu.VMEM(pick_index.shape, jnp.int32),
            pltpu.VMEM((classes + 16, rows), bf16),
            pltpu.SemaphoreType.DMA((n_ex + 2,)),
        ],
        compiler_params=limit,
        name="class_sums",
    )(*[pltpu.with_memory_space_constraint(a, pltpu.HBM) for a in (labels, pick_index, features)])

    def add(codes, last):
        return pl.pallas_call(
            functools.partial(add_kernel, classes=classes, last=last),
            in_specs=[vmem] * len(codes),
            out_specs=vmem,
            out_shape=code,
            compiler_params=limit,
            name="add_sums",
        )(*codes)

    far_masks = [8 << b for b in range(n_ex.bit_length() - 4)]
    got = swap(send, 1)
    codes = pl.pallas_call(
        functools.partial(pair_kernel, classes=classes),
        in_specs=[vmem] * 2,
        out_specs=[vmem] * 4,
        out_shape=[code] * 4,
        compiler_params=limit,
        name="pair_sums",
    )(keep, got)
    near = pl.pallas_call(
        functools.partial(pack_kernel, steps=steps, start=groups * classes + 8),
        in_specs=[vmem] * 2,
        out_specs=vmem,
        out_shape=jax.ShapeDtypeStruct((16, main), bf16),
        compiler_params=limit,
        name="pack_rows",
    )(keep, got)
    near_codes = [swap(c, m) for c, m in zip(codes[1:], near_masks[1:])]
    part_sum = add([codes[0]] + near_codes, False)
    def select(tail, *others):
        return pl.pallas_call(
            functools.partial(select_kernel, n_ex=n_ex, rows=rows, tail=tail),
            in_specs=[vmem],
            out_specs=vmem,
            out_shape=jax.ShapeDtypeStruct((total, n_ex * 8), bf16),
            compiler_params=limit,
            name="select_tails" if tail else "select_rows",
        )(after(pick_index, *others))

    one = select(False, codes[0])
    rest = select(True, codes[0])
    for far, mask in zip(reversed(far_masks), far_masks):
        far_rows = swap(near, far)
        more = swap(after(part_sum, far_rows, one, rest), mask)
        near = jnp.concatenate([after(near, more), far_rows], axis=0)
        part_sum = add([part_sum, more], mask == far_masks[-1])
    parts = [near] + [swap(near, m) for m in near_masks[1:]]
    own_parts = [part_sum] + [swap(part_sum, m) for m in near_masks[1:3]]
    own_parts.append(swap(after(part_sum, parts[1]), near_masks[3]))

    x = pl.pallas_call(
        functools.partial(picked_kernel, steps=steps),
        in_specs=[vmem] * 6,
        out_specs=vmem,
        out_shape=jax.ShapeDtypeStruct((total, full // 2), bf16),
        scratch_shapes=[pltpu.VMEM((n_ex * 8, main), bf16)],
        compiler_params=limit,
        name="picked_rows",
    )(one, rest, *parts)

    x_twin = swap(x, 1)
    own_half = jnp.concatenate(after(own_parts, x), axis=0)
    twin_half = swap(own_half, 1)
    left = pltpu.VMEM((total + classes, full // 2), bf16)
    direct, gram, target = pl.pallas_call(
        functools.partial(half_kernel, classes=classes),
        in_specs=[vmem] * 3,
        out_specs=[vmem] * 3,
        out_shape=[
            jax.ShapeDtypeStruct((total, rows), f32),
            jax.ShapeDtypeStruct((total + classes, total), f32),
            jax.ShapeDtypeStruct((classes, full // 2), f32),
        ],
        scratch_shapes=[left],
        compiler_params=limit,
        name="own_half_products",
    )(feat, own_half, x)

    scores, resid = pl.pallas_call(
        functools.partial(pursuit_kernel, steps=steps, scale=1.0 / math.sqrt(full)),
        in_specs=[vmem] * 8,
        out_specs=[vmem, anywhere],
        out_shape=[
            jax.ShapeDtypeStruct((steps, rows), f32),
            jax.ShapeDtypeStruct((classes, full), f32),
        ],
        scratch_shapes=[pltpu.VMEM((classes, full), f32), left, pltpu.SemaphoreType.DMA((4,))],
        compiler_params=limit,
        name="pursuit",
    )(labels, feat, x, x_twin, direct, gram, target, twin_half)
    return scores, resid


def solution(mesh):
    return jax.shard_map(
        functools.partial(on_device, n_ex=mesh.shape["ex"]),
        mesh=mesh,
        in_specs=(P(("grp", "ex"), None), P(("grp", "ex")), P("grp", None)),
        out_specs=(P(None, ("grp", "ex")), P("grp", None)),
        check_vma=False,
    )
```

```python
import functools
import math

import jax
import jax.numpy as jnp
from jax import lax
from jax.experimental import pallas as pl
from jax.experimental.pallas import tpu as pltpu
from jax.sharding import PartitionSpec as P

ridge = 1.0
slots = 2
near_masks = (0, 4, 2, 6)
f32 = jnp.float32
bf16 = jnp.bfloat16


def nt_dot(a, b):
    return lax.dot_general(a, b, (((1,), (1,)), ((), ())), preferred_element_type=f32)


def column(tile, height, start=0):
    return jnp.concatenate([tile[:, start + q : start + q + 1] for q in range(height // 8)], axis=0)


def spread(values, start=0):
    lane = lax.broadcasted_iota(jnp.int32, (8, 128), 1)
    tile = jnp.zeros((8, 128), f32)
    for q in range(values.shape[0] // 8):
        tile = jnp.where(lane == start + q, values[8 * q : 8 * q + 8], tile)
    return tile


def encode(x, count_tile=None):
    height, width = x.shape
    top = jnp.max(jnp.abs(x), axis=1, keepdims=True)
    power = jnp.ceil(jnp.log2(jnp.maximum(top, 1e-30)) + 0.01)
    whole_x = jnp.round(x * jnp.exp2(15.0 - power))
    mark = spread(power)
    if count_tile is not None:
        mark = mark + count_tile
    chunks = [whole_x[:, j * 128 : (j + 1) * 128] for j in range(width // 128)]
    return jnp.concatenate(chunks + [mark], axis=0).astype(jnp.int32).astype(jnp.int16)


def decode(code, height):
    value = code.astype(jnp.int32).astype(f32)
    count = value.shape[0] // height
    mark = value[count * height :]
    x = jnp.concatenate([value[j * height : (j + 1) * height] for j in range(count)], axis=1)
    return x * jnp.exp2(column(mark, height) - 15.0), mark


def sums_kernel(
    labels_hbm, pick_hbm, feat_hbm, feat_ref, send_ref, keep_ref, held, labels_ref, pick_ref, left, sems, *, n_ex
):
    rows, full = feat_ref.shape
    steps, classes = pick_ref.shape
    width = full // n_ex
    groups = n_ex // 2
    device = lax.axis_index("ex")
    core = device % 2
    small = [
        pltpu.make_async_copy(pick_hbm, pick_ref, sems.at[n_ex]),
        pltpu.make_async_copy(labels_hbm, labels_ref, sems.at[n_ex + 1]),
    ]
    for copy in small:
        copy.start()
    columns = []
    copies = []
    for i in range(n_ex):
        block = (1 - core) * groups + i if i < groups else core * groups + i - groups
        at = pl.ds(pl.multiple_of(block * width, width), width)
        columns.append(at)
        copies.append(pltpu.make_async_copy(feat_hbm.at[:, at], feat_ref.at[:, at], sems.at[i]))
        copies[-1].start()

    for copy in small:
        copy.wait()
    local = pick_ref[...] - device * rows
    mine = (local >= 0) & (local < rows)
    lane = lax.broadcasted_iota(jnp.int32, local.shape, 1)
    first = jnp.min(jnp.where(mine, lane, classes), axis=1, keepdims=True)
    last = jnp.max(jnp.where(mine, lane, -1), axis=1, keepdims=True)
    spot0 = jnp.max(jnp.where(mine & (lane == first), local, -1), axis=1, keepdims=True)
    spot1 = jnp.max(jnp.where(mine & (lane == last) & (last > first), local, -1), axis=1, keepdims=True)
    member = lax.broadcasted_iota(jnp.int32, (classes, rows), 0) == labels_ref[...].reshape(1, rows)
    line = lax.broadcasted_iota(jnp.int32, (steps, rows), 1)
    left[...] = jnp.concatenate(
        [
            jnp.where(member, 1.0, 0.0),
            jnp.where(line == spot0, 1.0, 0.0),
            jnp.where(line == spot1, 1.0, 0.0),
            jnp.zeros((16 - 2 * steps, rows), f32),
        ],
        axis=0,
    ).astype(bf16)
    count = jnp.sum(jnp.where(member, 1.0, 0.0), axis=1, keepdims=True)
    tile = spread(count, classes // 8)
    base = groups * classes
    for ref in (send_ref, keep_ref):
        ref[base : base + 8, :128] = tile
        if width > 128:
            ref[base : base + 8, 128:] = jnp.zeros((8, width - 128), f32)

    for i in range(n_ex):
        copies[i].wait()
        both = jnp.dot(left[...], feat_ref[:, columns[i]], preferred_element_type=f32)
        k = i % groups
        ref = send_ref if i < groups else keep_ref
        ref[k * classes : (k + 1) * classes, :] = both[:classes]
        held[:, columns[i]] = both[classes : classes + 8]


def pack_kernel(held, rows_ref, *, steps):
    half = held.shape[1] // 2
    used = steps * slots
    main = rows_ref.shape[2]
    core = lax.axis_index("ex") % 2
    for part, side in ((0, core), (1, 1 - core)):
        h = held[:, pl.ds(pl.multiple_of(side * half, half), half)]
        lines = [h[:used, :main]]
        for q in range(slots):
            lines.append(jnp.concatenate([h[q * steps + u : q * steps + u + 1, main:] for u in range(steps)], axis=1))
        rows_ref[part] = jnp.concatenate(lines, axis=0).astype(bf16)


def near_id(mask):
    return (lax.axis_index("ex") // 2 % 4) ^ (mask // 2)


def pair_kernel(keep_ref, got_ref, *code_refs, classes):
    far = code_refs[0].shape[0]
    base = 4 * far * classes
    tile = keep_ref[base : base + 8, :128] + got_ref[base : base + 8, :128]
    for mask, code_ref in zip(near_masks, code_refs):
        for j in range(far):
            at = pl.ds(pl.multiple_of((j * 4 + near_id(mask)) * classes, classes), classes)
            code_ref[j] = encode(keep_ref[at, :] + got_ref[at, :], tile)


def add_kernel(*refs, classes, last):
    code_ref = refs[-1]
    for j in range(code_ref.shape[0]):
        value, mark = decode(refs[0][j], classes)
        for ref in refs[1:-1]:
            more, more_mark = decode(ref[j], classes)
            value = value + more
            mark = mark + more_mark
        if last:
            code_ref[j] = encode(value / jnp.sqrt(column(mark, classes, classes // 8)))
        else:
            lane = lax.broadcasted_iota(jnp.int32, mark.shape, 1)
            code_ref[j] = encode(value, jnp.where(lane < classes // 8, 0.0, mark))


def diagonal(block):
    n = block.shape[0]
    eye = lax.broadcasted_iota(jnp.int32, (n, n), 0) == lax.broadcasted_iota(jnp.int32, (n, n), 1)
    return jnp.sum(jnp.where(eye, block, 0.0), axis=1, keepdims=True)


def factor_all(gram):
    order = len(gram)
    factor = [[None] * order for _ in range(order)]
    for j in range(order):
        value = gram[j][j]
        for k in range(j):
            value = value - factor[j][k] * factor[j][k]
        root = jnp.sqrt(value)
        factor[j][j] = 1.0 / root
        for i in range(j + 1, order):
            value = gram[i][j]
            for k in range(j):
                value = value - factor[i][k] * factor[j][k]
            factor[i][j] = value * factor[j][j]
    return factor


def solve_all(factor, right):
    order = len(right)
    forward = []
    for i in range(order):
        value = right[i]
        for j in range(i):
            value = value - factor[i][j] * forward[j]
        forward.append(value * factor[i][i])
    result = []
    for size in range(1, order + 1):
        back = [None] * size
        for i in reversed(range(size)):
            value = forward[i]
            for j in range(i + 1, size):
                value = value - factor[j][i] * back[j]
            back[i] = value * factor[i][i]
        result.append(back)
    return result


def select_kernel(pick_ref, one_ref, *, n_ex, rows, tail):
    steps, classes = pick_ref.shape
    lines = one_ref.shape[1]
    device = lax.axis_index("ex")
    pick = pick_ref[...]
    lane = lax.broadcasted_iota(jnp.int32, pick.shape, 1)
    owner = jnp.zeros_like(pick)
    rank = jnp.zeros_like(pick)
    for d in range(n_ex):
        here = (pick >= d * rows) & (pick < (d + 1) * rows)
        first = jnp.min(jnp.where(here, lane, classes), axis=1, keepdims=True)
        owner = jnp.where(here, d, owner)
        rank = jnp.where(here & (lane > first), 1, rank)
    away = owner ^ device
    bits = n_ex.bit_length() - 1
    far = jnp.zeros_like(pick)
    for b in range(3, bits):
        far = far + (((away >> b) & 1) << (bits - 1 - b))
    near = ((away >> 2) & 1) + 2 * ((away >> 1) & 1)
    spot = (2 * near + (away & 1)) * (n_ex // 8) + far
    step = lax.broadcasted_iota(jnp.int32, pick.shape, 0)
    line = lax.broadcasted_iota(jnp.int32, (lines, classes), 0)
    where = spot * 8 + (slots * steps + rank if tail else rank * steps + step)
    hits = [jnp.where(line == where[s : s + 1, :], 1.0, 0.0) for s in range(steps)]
    pad = jnp.zeros((lines, 128 - steps * classes), f32)
    one_ref[...] = jnp.transpose(jnp.concatenate(hits + [pad], axis=1))[: steps * classes].astype(bf16)


def picked_kernel(one_ref, rest_ref, *refs, steps):
    parts, (x_ref, rows_ref) = refs[:-2], refs[-2:]
    total, half = x_ref.shape
    classes = total // steps
    main = rows_ref.shape[1]
    tail = half - main
    at = 0
    for part in parts:
        rows_ref[at : at + part.shape[0], :] = part[...]
        at += part.shape[0]
    x_ref[:, :main] = jnp.dot(one_ref[...], rows_ref[...], preferred_element_type=f32).astype(bf16)
    for s in range(steps):
        at = slice(s * classes, (s + 1) * classes)
        rest = jnp.dot(rest_ref[at, :], rows_ref[:, s * tail : (s + 1) * tail], preferred_element_type=f32)
        x_ref[at, main:] = rest.astype(bf16)


def half_target(side, code_ref, x_ref, target_ref, target_at, left_ref, *, classes):
    half = left_ref.shape[1]
    far = code_ref.shape[0] // 4
    width = half // code_ref.shape[0]
    here = pl.ds(pl.multiple_of(side * half, half), half)
    for k in range(4 * far):
        block = k % far * 4 + near_id(near_masks[k // far])
        target = decode(code_ref[k], classes)[0]
        target_ref[:, pl.ds(pl.multiple_of(target_at + block * width, width), width)] = target
        left_ref[:classes, pl.ds(pl.multiple_of(block * width, width), width)] = target.astype(bf16)
    left_ref[classes:, :] = x_ref[...]
    return nt_dot(left_ref[...], x_ref[...]), here


def half_kernel(feat_ref, code_ref, x_ref, direct_ref, gram_ref, target_ref, left_ref, *, classes):
    core = lax.axis_index("ex") % 2
    gram_ref[...], here = half_target(core, code_ref, x_ref, target_ref, 0, left_ref, classes=classes)
    direct_ref[...] = nt_dot(left_ref[: direct_ref.shape[0], :], feat_ref[:, here])


def pursuit_kernel(
    labels_ref, feat_ref, x_own, x_twin, direct_own, gram_own, target_own, code_ref,
    scores_ref, resid_hbm, resid_ref, left_ref, sems, *, steps, scale
):
    classes, full = resid_ref.shape
    half = full // 2
    core = lax.axis_index("ex") % 2
    gram, other = half_target(1 - core, code_ref, x_twin, resid_ref, (1 - core) * half, left_ref, classes=classes)
    gram = gram + gram_own[...]
    blocks = [
        [
            diagonal(gram[(a + 1) * classes : (a + 2) * classes, b * classes : (b + 1) * classes])
            + (ridge if a == b else 0.0)
            for b in range(a + 1)
        ]
        for a in range(steps)
    ]
    rhs = [diagonal(gram[:classes, a * classes : (a + 1) * classes]) for a in range(steps)]
    weights = solve_all(factor_all(blocks), rhs)
    last = weights[steps - 1]
    copies = []
    span = half // 2
    for x_ref, side in ((x_own, core), (x_twin, 1 - core)):
        for q in range(2):
            there = slice(q * span, (q + 1) * span)
            here = pl.ds(pl.multiple_of(side * half + q * span, span), span)
            value = target_own[:, there] if x_ref is x_own else resid_ref[:, here]
            for k in range(steps):
                value = value - last[k] * x_ref[k * classes : (k + 1) * classes, there].astype(f32)
            resid_ref[:, here] = value
            copies.append(pltpu.make_async_copy(resid_ref.at[:, here], resid_hbm.at[:, here], sems.at[len(copies)]))
            copies[-1].start()

    direct = direct_own[...] + nt_dot(left_ref[: direct_own.shape[0], :], feat_ref[:, other])
    member = lax.broadcasted_iota(jnp.int32, (classes, direct.shape[1]), 0) == labels_ref[...].reshape(1, direct.shape[1])
    for s in range(steps):
        value = direct[:classes]
        for k in range(s):
            value = value - weights[s - 1][k] * direct[(k + 1) * classes : (k + 2) * classes]
        scores_ref[s : s + 1, :] = jnp.sum(jnp.where(member, value, 0.0), axis=0, keepdims=True) * scale
    for copy in copies:
        copy.wait()


def on_device(features, labels, pick_index, *, n_ex):
    rows, full = features.shape
    steps, classes = pick_index.shape
    groups = n_ex // 2
    width = full // n_ex
    total = steps * classes
    main = full // 2 * steps * slots // 8
    limit = pltpu.CompilerParams(vmem_limit_bytes=16 << 20)
    vmem = pl.BlockSpec(memory_space=pltpu.VMEM)
    hbm = pl.BlockSpec(memory_space=pltpu.HBM)
    anywhere = pl.BlockSpec(memory_space=pl.ANY)
    half = jax.ShapeDtypeStruct((groups * classes + 8, width), f32)
    code = jax.ShapeDtypeStruct((groups // 4, classes * (width // 128) + 8, 128), jnp.int16)

    def swap(x, mask):
        return lax.ppermute(x, "ex", [(d, d ^ mask) for d in range(n_ex)])

    def after(x, *others):
        return lax.optimization_barrier((x,) + others)[0]

    feat, send, keep, held = pl.pallas_call(
        functools.partial(sums_kernel, n_ex=n_ex),
        in_specs=[hbm] * 3,
        out_specs=[vmem] * 4,
        out_shape=[pltpu.VMEM((rows, full), bf16), half, half, jax.ShapeDtypeStruct((8, full), f32)],
        scratch_shapes=[
            pltpu.VMEM(labels.shape, jnp.int32),
            pltpu.VMEM(pick_index.shape, jnp.int32),
            pltpu.VMEM((classes + 16, rows), bf16),
            pltpu.SemaphoreType.DMA((n_ex + 2,)),
        ],
        compiler_params=limit,
        name="class_sums",
    )(*[pltpu.with_memory_space_constraint(a, pltpu.HBM) for a in (labels, pick_index, features)])

    def add(codes, last):
        return pl.pallas_call(
            functools.partial(add_kernel, classes=classes, last=last),
            in_specs=[vmem] * len(codes),
            out_specs=vmem,
            out_shape=code,
            compiler_params=limit,
            name="add_sums",
        )(*codes)

    far_masks = [8 << b for b in range(n_ex.bit_length() - 4)]
    got = swap(send, 1)
    codes = pl.pallas_call(
        functools.partial(pair_kernel, classes=classes),
        in_specs=[vmem] * 2,
        out_specs=[vmem] * 4,
        out_shape=[code] * 4,
        compiler_params=limit,
        name="pair_sums",
    )(keep, got)
    packed = pl.pallas_call(
        functools.partial(pack_kernel, steps=steps),
        in_specs=[vmem],
        out_specs=vmem,
        out_shape=jax.ShapeDtypeStruct((2, 8, main), bf16),
        compiler_params=limit,
        name="pack_rows",
    )(held)
    for mask in reversed(far_masks):
        packed = jnp.concatenate([packed, swap(packed, mask)], axis=1)

    near_codes = [swap(c, m) for c, m in zip(codes[1:], near_masks[1:])]
    part_sum = add([codes[0], after(near_codes[0], packed)] + near_codes[1:], False)

    def select(tail, *others):
        return pl.pallas_call(
            functools.partial(select_kernel, n_ex=n_ex, rows=rows, tail=tail),
            in_specs=[vmem],
            out_specs=vmem,
            out_shape=jax.ShapeDtypeStruct((total, n_ex * 8), bf16),
            compiler_params=limit,
            name="select_tails" if tail else "select_rows",
        )(after(pick_index, *others))

    one = select(False, codes[0])
    rest = select(True, codes[0])
    given = swap(after(packed[1], part_sum), 1)
    part_sum = after(part_sum, one, rest)
    for mask in far_masks:
        more = swap(part_sum, mask)
        part_sum = add([part_sum, more], mask == far_masks[-1])
    near = jnp.concatenate([after(packed[0], more), given], axis=0)
    parts = [near] + [swap(near, m) for m in near_masks[1:]]
    own_parts = [part_sum] + [swap(part_sum, m) for m in near_masks[1:3]]
    own_parts.append(swap(after(part_sum, parts[1]), near_masks[3]))

    x = pl.pallas_call(
        functools.partial(picked_kernel, steps=steps),
        in_specs=[vmem] * 6,
        out_specs=vmem,
        out_shape=jax.ShapeDtypeStruct((total, full // 2), bf16),
        scratch_shapes=[pltpu.VMEM((n_ex * 8, main), bf16)],
        compiler_params=limit,
        name="picked_rows",
    )(one, rest, *parts)

    x_twin = swap(x, 1)
    own_half = jnp.concatenate(after(own_parts, x), axis=0)
    twin_half = swap(own_half, 1)
    left = pltpu.VMEM((total + classes, full // 2), bf16)
    direct, gram, target = pl.pallas_call(
        functools.partial(half_kernel, classes=classes),
        in_specs=[vmem] * 3,
        out_specs=[vmem] * 3,
        out_shape=[
            jax.ShapeDtypeStruct((total, rows), f32),
            jax.ShapeDtypeStruct((total + classes, total), f32),
            jax.ShapeDtypeStruct((classes, full // 2), f32),
        ],
        scratch_shapes=[left],
        compiler_params=limit,
        name="own_half_products",
    )(feat, own_half, x)

    scores, resid = pl.pallas_call(
        functools.partial(pursuit_kernel, steps=steps, scale=1.0 / math.sqrt(full)),
        in_specs=[vmem] * 8,
        out_specs=[vmem, anywhere],
        out_shape=[
            jax.ShapeDtypeStruct((steps, rows), f32),
            jax.ShapeDtypeStruct((classes, full), f32),
        ],
        scratch_shapes=[pltpu.VMEM((classes, full), f32), left, pltpu.SemaphoreType.DMA((4,))],
        compiler_params=limit,
        name="pursuit",
    )(labels, feat, x, x_twin, direct, gram, target, twin_half)
    return scores, resid


def solution(mesh):
    return jax.shard_map(
        functools.partial(on_device, n_ex=mesh.shape["ex"]),
        mesh=mesh,
        in_specs=(P(("grp", "ex"), None), P(("grp", "ex")), P("grp", None)),
        out_specs=(P(None, ("grp", "ex")), P("grp", None)),
        check_vma=False,
    )
```

```python
import functools
import math

import jax
import jax.numpy as jnp
from jax import lax
from jax.experimental import pallas as pl
from jax.experimental.pallas import tpu as pltpu
from jax.sharding import PartitionSpec as P

ridge = 1.0
slots = 2
near_masks = (0, 4, 2, 6)
f32 = jnp.float32
bf16 = jnp.bfloat16


def nt_dot(a, b):
    return lax.dot_general(a, b, (((1,), (1,)), ((), ())), preferred_element_type=f32)


def column(tile, height, start=0):
    return jnp.concatenate([tile[:, start + q : start + q + 1] for q in range(height // 8)], axis=0)


def spread(values, start=0):
    lane = lax.broadcasted_iota(jnp.int32, (8, 128), 1)
    tile = jnp.zeros((8, 128), f32)
    for q in range(values.shape[0] // 8):
        tile = jnp.where(lane == start + q, values[8 * q : 8 * q + 8], tile)
    return tile


def encode(x, count_tile=None):
    height, width = x.shape
    top = jnp.max(jnp.abs(x), axis=1, keepdims=True)
    power = jnp.ceil(jnp.log2(jnp.maximum(top, 1e-30)) + 0.01)
    whole_x = jnp.round(x * jnp.exp2(15.0 - power))
    mark = spread(power)
    if count_tile is not None:
        mark = mark + count_tile
    chunks = [whole_x[:, j * 128 : (j + 1) * 128] for j in range(width // 128)]
    return jnp.concatenate(chunks + [mark], axis=0).astype(jnp.int32).astype(jnp.int16)


def decode(code, height):
    value = code.astype(jnp.int32).astype(f32)
    count = value.shape[0] // height
    mark = value[count * height :]
    x = jnp.concatenate([value[j * height : (j + 1) * height] for j in range(count)], axis=1)
    return x * jnp.exp2(column(mark, height) - 15.0), mark


def sums_kernel(
    labels_hbm, pick_hbm, feat_hbm, feat_ref, send_ref, keep_ref, held, labels_ref, pick_ref, left, sems, *, n_ex
):
    rows, full = feat_ref.shape
    steps, classes = pick_ref.shape
    width = full // n_ex
    groups = n_ex // 2
    device = lax.axis_index("ex")
    core = device % 2
    small = [
        pltpu.make_async_copy(pick_hbm, pick_ref, sems.at[n_ex]),
        pltpu.make_async_copy(labels_hbm, labels_ref, sems.at[n_ex + 1]),
    ]
    for copy in small:
        copy.start()
    columns = []
    copies = []
    for i in range(n_ex):
        block = (1 - core) * groups + i if i < groups else core * groups + i - groups
        at = pl.ds(pl.multiple_of(block * width, width), width)
        columns.append(at)
        copies.append(pltpu.make_async_copy(feat_hbm.at[:, at], feat_ref.at[:, at], sems.at[i]))
        copies[-1].start()

    for copy in small:
        copy.wait()
    local = pick_ref[...] - device * rows
    mine = (local >= 0) & (local < rows)
    lane = lax.broadcasted_iota(jnp.int32, local.shape, 1)
    first = jnp.min(jnp.where(mine, lane, classes), axis=1, keepdims=True)
    last = jnp.max(jnp.where(mine, lane, -1), axis=1, keepdims=True)
    spot0 = jnp.max(jnp.where(mine & (lane == first), local, -1), axis=1, keepdims=True)
    spot1 = jnp.max(jnp.where(mine & (lane == last) & (last > first), local, -1), axis=1, keepdims=True)
    member = lax.broadcasted_iota(jnp.int32, (classes, rows), 0) == labels_ref[...].reshape(1, rows)
    line = lax.broadcasted_iota(jnp.int32, (steps, rows), 1)
    left[...] = jnp.concatenate(
        [
            jnp.where(member, 1.0, 0.0),
            jnp.where(line == spot0, 1.0, 0.0),
            jnp.where(line == spot1, 1.0, 0.0),
            jnp.zeros((16 - 2 * steps, rows), f32),
        ],
        axis=0,
    ).astype(bf16)
    count = jnp.sum(jnp.where(member, 1.0, 0.0), axis=1, keepdims=True)
    tile = spread(count, classes // 8)
    base = groups * classes
    for ref in (send_ref, keep_ref):
        ref[base : base + 8, :128] = tile
        if width > 128:
            ref[base : base + 8, 128:] = jnp.zeros((8, width - 128), f32)

    for i in range(n_ex):
        copies[i].wait()
        both = jnp.dot(left[...], feat_ref[:, columns[i]], preferred_element_type=f32)
        k = i % groups
        ref = send_ref if i < groups else keep_ref
        ref[k * classes : (k + 1) * classes, :] = both[:classes]
        held[:, columns[i]] = both[classes : classes + 8]


def pack_kernel(held, rows_ref, *, steps):
    half = held.shape[1] // 2
    used = steps * slots
    main = rows_ref.shape[2]
    core = lax.axis_index("ex") % 2
    for part, side in ((0, core), (1, 1 - core)):
        h = held[:, pl.ds(pl.multiple_of(side * half, half), half)]
        lines = [h[:used, :main]]
        for q in range(slots):
            lines.append(jnp.concatenate([h[q * steps + u : q * steps + u + 1, main:] for u in range(steps)], axis=1))
        rows_ref[part] = jnp.concatenate(lines, axis=0).astype(bf16)


def near_id(mask):
    return (lax.axis_index("ex") // 2 % 4) ^ (mask // 2)


def pair_kernel(keep_ref, got_ref, *code_refs, classes):
    far = code_refs[0].shape[0]
    base = 4 * far * classes
    tile = keep_ref[base : base + 8, :128] + got_ref[base : base + 8, :128]
    for mask, code_ref in zip(near_masks, code_refs):
        for j in range(far):
            at = pl.ds(pl.multiple_of((j * 4 + near_id(mask)) * classes, classes), classes)
            code_ref[j] = encode(keep_ref[at, :] + got_ref[at, :], tile)


def add_kernel(*refs, classes, last):
    code_ref = refs[-1]
    for j in range(code_ref.shape[0]):
        value, mark = decode(refs[0][j], classes)
        for ref in refs[1:-1]:
            more, more_mark = decode(ref[j], classes)
            value = value + more
            mark = mark + more_mark
        if last:
            code_ref[j] = encode(value / jnp.sqrt(column(mark, classes, classes // 8)))
        else:
            lane = lax.broadcasted_iota(jnp.int32, mark.shape, 1)
            code_ref[j] = encode(value, jnp.where(lane < classes // 8, 0.0, mark))


def diagonal(block):
    n = block.shape[0]
    eye = lax.broadcasted_iota(jnp.int32, (n, n), 0) == lax.broadcasted_iota(jnp.int32, (n, n), 1)
    return jnp.sum(jnp.where(eye, block, 0.0), axis=1, keepdims=True)


def factor_all(gram):
    order = len(gram)
    factor = [[None] * order for _ in range(order)]
    for j in range(order):
        value = gram[j][j]
        for k in range(j):
            value = value - factor[j][k] * factor[j][k]
        root = jnp.sqrt(value)
        factor[j][j] = 1.0 / root
        for i in range(j + 1, order):
            value = gram[i][j]
            for k in range(j):
                value = value - factor[i][k] * factor[j][k]
            factor[i][j] = value * factor[j][j]
    return factor


def solve_all(factor, right):
    order = len(right)
    forward = []
    for i in range(order):
        value = right[i]
        for j in range(i):
            value = value - factor[i][j] * forward[j]
        forward.append(value * factor[i][i])
    result = []
    for size in range(1, order + 1):
        back = [None] * size
        for i in reversed(range(size)):
            value = forward[i]
            for j in range(i + 1, size):
                value = value - factor[j][i] * back[j]
            back[i] = value * factor[i][i]
        result.append(back)
    return result


def select_kernel(pick_ref, one_ref, *, n_ex, rows, tail):
    steps, classes = pick_ref.shape
    lines = one_ref.shape[1]
    device = lax.axis_index("ex")
    pick = pick_ref[...]
    lane = lax.broadcasted_iota(jnp.int32, pick.shape, 1)
    owner = jnp.zeros_like(pick)
    rank = jnp.zeros_like(pick)
    for d in range(n_ex):
        here = (pick >= d * rows) & (pick < (d + 1) * rows)
        first = jnp.min(jnp.where(here, lane, classes), axis=1, keepdims=True)
        owner = jnp.where(here, d, owner)
        rank = jnp.where(here & (lane > first), 1, rank)
    away = owner ^ device
    bits = n_ex.bit_length() - 1
    far = jnp.zeros_like(pick)
    for b in range(3, bits):
        far = far + (((away >> b) & 1) << (bits - 1 - b))
    near = ((away >> 2) & 1) + 2 * ((away >> 1) & 1)
    spot = (2 * near + (away & 1)) * (n_ex // 8) + far
    step = lax.broadcasted_iota(jnp.int32, pick.shape, 0)
    line = lax.broadcasted_iota(jnp.int32, (lines, classes), 0)
    where = spot * 8 + (slots * steps + rank if tail else rank * steps + step)
    hits = [jnp.where(line == where[s : s + 1, :], 1.0, 0.0) for s in range(steps)]
    pad = jnp.zeros((lines, 128 - steps * classes), f32)
    one_ref[...] = jnp.transpose(jnp.concatenate(hits + [pad], axis=1))[: steps * classes].astype(bf16)


def picked_kernel(one_ref, rest_ref, *refs, steps):
    parts, (x_ref, rows_ref) = refs[:-2], refs[-2:]
    total, half = x_ref.shape
    classes = total // steps
    main = rows_ref.shape[1]
    tail = half - main
    at = 0
    for part in parts:
        rows_ref[at : at + part.shape[0], :] = part[...]
        at += part.shape[0]
    x_ref[:, :main] = jnp.dot(one_ref[...], rows_ref[...], preferred_element_type=f32).astype(bf16)
    for s in range(steps):
        at = slice(s * classes, (s + 1) * classes)
        rest = jnp.dot(rest_ref[at, :], rows_ref[:, s * tail : (s + 1) * tail], preferred_element_type=f32)
        x_ref[at, main:] = rest.astype(bf16)


def half_target(side, code_ref, x_ref, target_ref, target_at, left_ref, *, classes):
    half = left_ref.shape[1]
    far = code_ref.shape[0] // 4
    width = half // code_ref.shape[0]
    here = pl.ds(pl.multiple_of(side * half, half), half)
    for k in range(4 * far):
        block = k % far * 4 + near_id(near_masks[k // far])
        target = decode(code_ref[k], classes)[0]
        target_ref[:, pl.ds(pl.multiple_of(target_at + block * width, width), width)] = target
        left_ref[:classes, pl.ds(pl.multiple_of(block * width, width), width)] = target.astype(bf16)
    left_ref[classes:, :] = x_ref[...]
    return nt_dot(left_ref[...], x_ref[...]), here


def half_kernel(feat_ref, code_ref, x_ref, direct_ref, gram_ref, target_ref, left_ref, *, classes):
    core = lax.axis_index("ex") % 2
    gram_ref[...], here = half_target(core, code_ref, x_ref, target_ref, 0, left_ref, classes=classes)
    direct_ref[...] = nt_dot(left_ref[: direct_ref.shape[0], :], feat_ref[:, here])


def pursuit_kernel(
    labels_ref, feat_ref, x_own, x_twin, direct_own, gram_own, target_own, code_ref,
    scores_ref, resid_hbm, resid_ref, left_ref, sems, *, steps, scale
):
    classes, full = resid_ref.shape
    half = full // 2
    core = lax.axis_index("ex") % 2
    gram, other = half_target(1 - core, code_ref, x_twin, resid_ref, (1 - core) * half, left_ref, classes=classes)
    gram = gram + gram_own[...]
    blocks = [
        [
            diagonal(gram[(a + 1) * classes : (a + 2) * classes, b * classes : (b + 1) * classes])
            + (ridge if a == b else 0.0)
            for b in range(a + 1)
        ]
        for a in range(steps)
    ]
    rhs = [diagonal(gram[:classes, a * classes : (a + 1) * classes]) for a in range(steps)]
    weights = solve_all(factor_all(blocks), rhs)
    last = weights[steps - 1]
    copies = []
    span = half // 2
    for x_ref, side in ((x_own, core), (x_twin, 1 - core)):
        for q in range(2):
            there = slice(q * span, (q + 1) * span)
            here = pl.ds(pl.multiple_of(side * half + q * span, span), span)
            value = target_own[:, there] if x_ref is x_own else resid_ref[:, here]
            for k in range(steps):
                value = value - last[k] * x_ref[k * classes : (k + 1) * classes, there].astype(f32)
            resid_ref[:, here] = value
            copies.append(pltpu.make_async_copy(resid_ref.at[:, here], resid_hbm.at[:, here], sems.at[len(copies)]))
            copies[-1].start()

    direct = direct_own[...] + nt_dot(left_ref[: direct_own.shape[0], :], feat_ref[:, other])
    member = lax.broadcasted_iota(jnp.int32, (classes, direct.shape[1]), 0) == labels_ref[...].reshape(1, direct.shape[1])
    for s in range(steps):
        value = direct[:classes]
        for k in range(s):
            value = value - weights[s - 1][k] * direct[(k + 1) * classes : (k + 2) * classes]
        scores_ref[s : s + 1, :] = jnp.sum(jnp.where(member, value, 0.0), axis=0, keepdims=True) * scale
    for copy in copies:
        copy.wait()


def on_device(features, labels, pick_index, *, n_ex):
    rows, full = features.shape
    steps, classes = pick_index.shape
    groups = n_ex // 2
    width = full // n_ex
    total = steps * classes
    main = full // 2 * steps * slots // 8
    limit = pltpu.CompilerParams(vmem_limit_bytes=16 << 20)
    vmem = pl.BlockSpec(memory_space=pltpu.VMEM)
    hbm = pl.BlockSpec(memory_space=pltpu.HBM)
    anywhere = pl.BlockSpec(memory_space=pl.ANY)
    half = jax.ShapeDtypeStruct((groups * classes + 8, width), f32)
    code = jax.ShapeDtypeStruct((groups // 4, classes * (width // 128) + 8, 128), jnp.int16)

    def swap(x, mask):
        return lax.ppermute(x, "ex", [(d, d ^ mask) for d in range(n_ex)])

    def after(x, *others):
        return lax.optimization_barrier((x,) + others)[0]

    feat, send, keep, held = pl.pallas_call(
        functools.partial(sums_kernel, n_ex=n_ex),
        in_specs=[hbm] * 3,
        out_specs=[vmem] * 4,
        out_shape=[pltpu.VMEM((rows, full), bf16), half, half, jax.ShapeDtypeStruct((8, full), f32)],
        scratch_shapes=[
            pltpu.VMEM(labels.shape, jnp.int32),
            pltpu.VMEM(pick_index.shape, jnp.int32),
            pltpu.VMEM((classes + 16, rows), bf16),
            pltpu.SemaphoreType.DMA((n_ex + 2,)),
        ],
        compiler_params=limit,
        name="class_sums",
    )(*[pltpu.with_memory_space_constraint(a, pltpu.HBM) for a in (labels, pick_index, features)])

    def add(codes, last):
        return pl.pallas_call(
            functools.partial(add_kernel, classes=classes, last=last),
            in_specs=[vmem] * len(codes),
            out_specs=vmem,
            out_shape=code,
            compiler_params=limit,
            cost_estimate=pl.CostEstimate(flops=0, bytes_accessed=10**8, transcendentals=0) if last else None,
            name="add_sums",
        )(*codes)

    far_masks = [8 << b for b in range(n_ex.bit_length() - 4)]
    got = swap(send, 1)
    codes = pl.pallas_call(
        functools.partial(pair_kernel, classes=classes),
        in_specs=[vmem] * 2,
        out_specs=[vmem] * 4,
        out_shape=[code] * 4,
        compiler_params=limit,
        name="pair_sums",
    )(keep, got)
    packed = pl.pallas_call(
        functools.partial(pack_kernel, steps=steps),
        in_specs=[vmem],
        out_specs=vmem,
        out_shape=jax.ShapeDtypeStruct((2, 8, main), bf16),
        compiler_params=limit,
        name="pack_rows",
    )(held)
    for mask in reversed(far_masks):
        packed = jnp.concatenate([packed, swap(packed, mask)], axis=1)

    near_codes = [swap(c, m) for c, m in zip(codes[1:], near_masks[1:])]
    part_sum = add([codes[0], after(near_codes[0], packed)] + near_codes[1:], False)

    def select(tail, *others):
        return pl.pallas_call(
            functools.partial(select_kernel, n_ex=n_ex, rows=rows, tail=tail),
            in_specs=[vmem],
            out_specs=vmem,
            out_shape=jax.ShapeDtypeStruct((total, n_ex * 8), bf16),
            compiler_params=limit,
            name="select_tails" if tail else "select_rows",
        )(after(pick_index, *others))

    rest = select(True, codes[0])
    near_sum = after(part_sum, rest)
    more = swap(near_sum, far_masks[0])
    one = select(False, near_sum)
    part_sum = add([near_sum, more], len(far_masks) == 1)
    for mask in far_masks[1:]:
        part_sum = add([part_sum, swap(part_sum, mask)], mask == far_masks[-1])
    given = swap(after(packed[1], one), 1)
    near = jnp.concatenate([packed[0], given], axis=0)
    parts = [near] + [swap(near, m) for m in near_masks[1:]]
    own_parts = [part_sum] + [swap(part_sum, m) for m in near_masks[1:3]]
    own_parts.append(swap(after(part_sum, parts[1]), near_masks[3]))

    x = pl.pallas_call(
        functools.partial(picked_kernel, steps=steps),
        in_specs=[vmem] * 6,
        out_specs=vmem,
        out_shape=jax.ShapeDtypeStruct((total, full // 2), bf16),
        scratch_shapes=[pltpu.VMEM((n_ex * 8, main), bf16)],
        compiler_params=limit,
        name="picked_rows",
    )(one, rest, *parts)

    x_twin = swap(x, 1)
    own_half = jnp.concatenate(after(own_parts, x), axis=0)
    twin_half = swap(own_half, 1)
    left = pltpu.VMEM((total + classes, full // 2), bf16)
    direct, gram, target = pl.pallas_call(
        functools.partial(half_kernel, classes=classes),
        in_specs=[vmem] * 3,
        out_specs=[vmem] * 3,
        out_shape=[
            jax.ShapeDtypeStruct((total, rows), f32),
            jax.ShapeDtypeStruct((total + classes, total), f32),
            jax.ShapeDtypeStruct((classes, full // 2), f32),
        ],
        scratch_shapes=[left],
        compiler_params=limit,
        name="own_half_products",
    )(feat, own_half, x)

    scores, resid = pl.pallas_call(
        functools.partial(pursuit_kernel, steps=steps, scale=1.0 / math.sqrt(full)),
        in_specs=[vmem] * 8,
        out_specs=[vmem, anywhere],
        out_shape=[
            jax.ShapeDtypeStruct((steps, rows), f32),
            jax.ShapeDtypeStruct((classes, full), f32),
        ],
        scratch_shapes=[pltpu.VMEM((classes, full), f32), left, pltpu.SemaphoreType.DMA((4,))],
        compiler_params=limit,
        name="pursuit",
    )(labels, feat, x, x_twin, direct, gram, target, twin_half)
    return scores, resid


def solution(mesh):
    return jax.shard_map(
        functools.partial(on_device, n_ex=mesh.shape["ex"]),
        mesh=mesh,
        in_specs=(P(("grp", "ex"), None), P(("grp", "ex")), P("grp", None)),
        out_specs=(P(None, ("grp", "ex")), P("grp", None)),
        check_vma=False,
    )
```

```python
import functools
import math

import jax
import jax.numpy as jnp
from jax import lax
from jax.experimental import pallas as pl
from jax.experimental.pallas import tpu as pltpu
from jax.sharding import PartitionSpec as P

ridge = 1.0
slots = 2
near_masks = (0, 4, 2, 6)
f32 = jnp.float32
bf16 = jnp.bfloat16


def nt_dot(a, b):
    return lax.dot_general(a, b, (((1,), (1,)), ((), ())), preferred_element_type=f32)


def column(tile, height, start=0):
    return jnp.concatenate([tile[:, start + q : start + q + 1] for q in range(height // 8)], axis=0)


def spread(values, start=0):
    lane = lax.broadcasted_iota(jnp.int32, (8, 128), 1)
    tile = jnp.zeros((8, 128), f32)
    for q in range(values.shape[0] // 8):
        tile = jnp.where(lane == start + q, values[8 * q : 8 * q + 8], tile)
    return tile


def encode(x, count_tile=None):
    height, width = x.shape
    top = jnp.max(jnp.abs(x), axis=1, keepdims=True)
    power = jnp.ceil(jnp.log2(jnp.maximum(top, 1e-30)) + 0.01)
    whole_x = jnp.round(x * jnp.exp2(15.0 - power))
    mark = spread(power)
    if count_tile is not None:
        mark = mark + count_tile
    chunks = [whole_x[:, j * 128 : (j + 1) * 128] for j in range(width // 128)]
    return jnp.concatenate(chunks + [mark], axis=0).astype(jnp.int32).astype(jnp.int16)


def decode(code, height):
    value = code.astype(jnp.int32).astype(f32)
    count = value.shape[0] // height
    mark = value[count * height :]
    x = jnp.concatenate([value[j * height : (j + 1) * height] for j in range(count)], axis=1)
    return x * jnp.exp2(column(mark, height) - 15.0), mark


def sums_kernel(
    labels_hbm, pick_hbm, feat_hbm, feat_ref, send_ref, keep_ref, held, labels_ref, pick_ref, left, sems, *, n_ex
):
    rows, full = feat_ref.shape
    steps, classes = pick_ref.shape
    width = full // n_ex
    groups = n_ex // 2
    device = lax.axis_index("ex")
    core = device % 2
    small = [
        pltpu.make_async_copy(pick_hbm, pick_ref, sems.at[n_ex]),
        pltpu.make_async_copy(labels_hbm, labels_ref, sems.at[n_ex + 1]),
    ]
    for copy in small:
        copy.start()
    columns = []
    copies = []
    for i in range(n_ex):
        block = (1 - core) * groups + i if i < groups else core * groups + i - groups
        at = pl.ds(pl.multiple_of(block * width, width), width)
        columns.append(at)
        copies.append(pltpu.make_async_copy(feat_hbm.at[:, at], feat_ref.at[:, at], sems.at[i]))
        copies[-1].start()

    for copy in small:
        copy.wait()
    local = pick_ref[...] - device * rows
    mine = (local >= 0) & (local < rows)
    lane = lax.broadcasted_iota(jnp.int32, local.shape, 1)
    first = jnp.min(jnp.where(mine, lane, classes), axis=1, keepdims=True)
    last = jnp.max(jnp.where(mine, lane, -1), axis=1, keepdims=True)
    spot0 = jnp.max(jnp.where(mine & (lane == first), local, -1), axis=1, keepdims=True)
    spot1 = jnp.max(jnp.where(mine & (lane == last) & (last > first), local, -1), axis=1, keepdims=True)
    member = lax.broadcasted_iota(jnp.int32, (classes, rows), 0) == labels_ref[...].reshape(1, rows)
    line = lax.broadcasted_iota(jnp.int32, (steps, rows), 1)
    left[...] = jnp.concatenate(
        [
            jnp.where(member, 1.0, 0.0),
            jnp.where(line == spot0, 1.0, 0.0),
            jnp.where(line == spot1, 1.0, 0.0),
            jnp.zeros((16 - 2 * steps, rows), f32),
        ],
        axis=0,
    ).astype(bf16)
    count = jnp.sum(jnp.where(member, 1.0, 0.0), axis=1, keepdims=True)
    tile = spread(count, classes // 8)
    base = groups * classes
    for ref in (send_ref, keep_ref):
        ref[base : base + 8, :128] = tile
        if width > 128:
            ref[base : base + 8, 128:] = jnp.zeros((8, width - 128), f32)

    for i in range(n_ex):
        copies[i].wait()
        both = jnp.dot(left[...], feat_ref[:, columns[i]], preferred_element_type=f32)
        k = i % groups
        ref = send_ref if i < groups else keep_ref
        ref[k * classes : (k + 1) * classes, :] = both[:classes]
        held[:, columns[i]] = both[classes : classes + 8]


def pack_kernel(held, rows_ref, *, steps):
    half = held.shape[1] // 2
    used = steps * slots
    main = rows_ref.shape[2]
    core = lax.axis_index("ex") % 2
    for part, side in ((0, core), (1, 1 - core)):
        h = held[:, pl.ds(pl.multiple_of(side * half, half), half)]
        lines = [h[:used, :main]]
        for q in range(slots):
            lines.append(jnp.concatenate([h[q * steps + u : q * steps + u + 1, main:] for u in range(steps)], axis=1))
        rows_ref[part] = jnp.concatenate(lines, axis=0).astype(bf16)


def near_id(mask):
    return (lax.axis_index("ex") // 2 % 4) ^ (mask // 2)


def pair_kernel(keep_ref, got_ref, *code_refs, classes):
    far = code_refs[0].shape[0]
    base = 4 * far * classes
    tile = keep_ref[base : base + 8, :128] + got_ref[base : base + 8, :128]
    for mask, code_ref in zip(near_masks, code_refs):
        for j in range(far):
            at = pl.ds(pl.multiple_of((j * 4 + near_id(mask)) * classes, classes), classes)
            code_ref[j] = encode(keep_ref[at, :] + got_ref[at, :], tile)


def add_kernel(*refs, classes, last):
    code_ref = refs[-1]
    for j in range(code_ref.shape[0]):
        value, mark = decode(refs[0][j], classes)
        for ref in refs[1:-1]:
            more, more_mark = decode(ref[j], classes)
            value = value + more
            mark = mark + more_mark
        if last:
            code_ref[j] = encode(value / jnp.sqrt(column(mark, classes, classes // 8)))
        else:
            lane = lax.broadcasted_iota(jnp.int32, mark.shape, 1)
            code_ref[j] = encode(value, jnp.where(lane < classes // 8, 0.0, mark))


def diagonal(block):
    n = block.shape[0]
    eye = lax.broadcasted_iota(jnp.int32, (n, n), 0) == lax.broadcasted_iota(jnp.int32, (n, n), 1)
    return jnp.sum(jnp.where(eye, block, 0.0), axis=1, keepdims=True)


def factor_all(gram):
    order = len(gram)
    factor = [[None] * order for _ in range(order)]
    for j in range(order):
        value = gram[j][j]
        for k in range(j):
            value = value - factor[j][k] * factor[j][k]
        root = jnp.sqrt(value)
        factor[j][j] = 1.0 / root
        for i in range(j + 1, order):
            value = gram[i][j]
            for k in range(j):
                value = value - factor[i][k] * factor[j][k]
            factor[i][j] = value * factor[j][j]
    return factor


def solve_all(factor, right):
    order = len(right)
    forward = []
    for i in range(order):
        value = right[i]
        for j in range(i):
            value = value - factor[i][j] * forward[j]
        forward.append(value * factor[i][i])
    result = []
    for size in range(1, order + 1):
        back = [None] * size
        for i in reversed(range(size)):
            value = forward[i]
            for j in range(i + 1, size):
                value = value - factor[j][i] * back[j]
            back[i] = value * factor[i][i]
        result.append(back)
    return result


def select_kernel(pick_ref, one_ref, *, n_ex, rows, tail):
    steps, classes = pick_ref.shape
    lines = one_ref.shape[1]
    device = lax.axis_index("ex")
    pick = pick_ref[...]
    lane = lax.broadcasted_iota(jnp.int32, pick.shape, 1)
    owner = jnp.zeros_like(pick)
    rank = jnp.zeros_like(pick)
    for d in range(n_ex):
        here = (pick >= d * rows) & (pick < (d + 1) * rows)
        first = jnp.min(jnp.where(here, lane, classes), axis=1, keepdims=True)
        owner = jnp.where(here, d, owner)
        rank = jnp.where(here & (lane > first), 1, rank)
    away = owner ^ device
    bits = n_ex.bit_length() - 1
    far = jnp.zeros_like(pick)
    for b in range(3, bits):
        far = far + (((away >> b) & 1) << (bits - 1 - b))
    near = ((away >> 2) & 1) + 2 * ((away >> 1) & 1)
    spot = (2 * near + (away & 1)) * (n_ex // 8) + far
    step = lax.broadcasted_iota(jnp.int32, pick.shape, 0)
    line = lax.broadcasted_iota(jnp.int32, (lines, classes), 0)
    where = spot * 8 + (slots * steps + rank if tail else rank * steps + step)
    hits = [jnp.where(line == where[s : s + 1, :], 1.0, 0.0) for s in range(steps)]
    pad = jnp.zeros((lines, 128 - steps * classes), f32)
    one_ref[...] = jnp.transpose(jnp.concatenate(hits + [pad], axis=1))[: steps * classes].astype(bf16)


def picked_kernel(one_ref, rest_ref, *refs, steps):
    parts, (x_ref, rows_ref) = refs[:-2], refs[-2:]
    total, half = x_ref.shape
    classes = total // steps
    main = rows_ref.shape[1]
    tail = half - main
    at = 0
    for part in parts:
        rows_ref[at : at + part.shape[0], :] = part[...]
        at += part.shape[0]
    x_ref[:, :main] = jnp.dot(one_ref[...], rows_ref[...], preferred_element_type=f32).astype(bf16)
    for s in range(steps):
        at = slice(s * classes, (s + 1) * classes)
        rest = jnp.dot(rest_ref[at, :], rows_ref[:, s * tail : (s + 1) * tail], preferred_element_type=f32)
        x_ref[at, main:] = rest.astype(bf16)


def half_target(side, code_ref, x_ref, target_ref, target_at, left_ref, *, classes):
    half = left_ref.shape[1]
    far = code_ref.shape[0] // 4
    width = half // code_ref.shape[0]
    here = pl.ds(pl.multiple_of(side * half, half), half)
    for k in range(4 * far):
        block = k % far * 4 + near_id(near_masks[k // far])
        target = decode(code_ref[k], classes)[0]
        target_ref[:, pl.ds(pl.multiple_of(target_at + block * width, width), width)] = target
        left_ref[:classes, pl.ds(pl.multiple_of(block * width, width), width)] = target.astype(bf16)
    left_ref[classes:, :] = x_ref[...]
    return nt_dot(left_ref[...], x_ref[...]), here


def half_kernel(feat_ref, code_ref, x_ref, direct_ref, gram_ref, target_ref, left_ref, *, classes):
    core = lax.axis_index("ex") % 2
    gram_ref[...], here = half_target(core, code_ref, x_ref, target_ref, 0, left_ref, classes=classes)
    direct_ref[...] = nt_dot(left_ref[: direct_ref.shape[0], :], feat_ref[:, here])


def pursuit_kernel(
    labels_ref, feat_ref, x_own, x_twin, direct_own, gram_own, target_own, code_ref,
    scores_ref, resid_hbm, resid_ref, left_ref, sems, *, steps, scale
):
    classes, full = resid_ref.shape
    half = full // 2
    core = lax.axis_index("ex") % 2
    gram, other = half_target(1 - core, code_ref, x_twin, resid_ref, (1 - core) * half, left_ref, classes=classes)
    gram = gram + gram_own[...]
    blocks = [
        [
            diagonal(gram[(a + 1) * classes : (a + 2) * classes, b * classes : (b + 1) * classes])
            + (ridge if a == b else 0.0)
            for b in range(a + 1)
        ]
        for a in range(steps)
    ]
    rhs = [diagonal(gram[:classes, a * classes : (a + 1) * classes]) for a in range(steps)]
    weights = solve_all(factor_all(blocks), rhs)
    last = weights[steps - 1]
    copies = []
    span = half // 2
    for x_ref, side in ((x_own, core), (x_twin, 1 - core)):
        for q in range(2):
            there = slice(q * span, (q + 1) * span)
            here = pl.ds(pl.multiple_of(side * half + q * span, span), span)
            value = target_own[:, there] if x_ref is x_own else resid_ref[:, here]
            for k in range(steps):
                value = value - last[k] * x_ref[k * classes : (k + 1) * classes, there].astype(f32)
            resid_ref[:, here] = value
            copies.append(pltpu.make_async_copy(resid_ref.at[:, here], resid_hbm.at[:, here], sems.at[len(copies)]))
            copies[-1].start()

    direct = direct_own[...] + nt_dot(left_ref[: direct_own.shape[0], :], feat_ref[:, other])
    member = lax.broadcasted_iota(jnp.int32, (classes, direct.shape[1]), 0) == labels_ref[...].reshape(1, direct.shape[1])
    for s in range(steps):
        value = direct[:classes]
        for k in range(s):
            value = value - weights[s - 1][k] * direct[(k + 1) * classes : (k + 2) * classes]
        scores_ref[s : s + 1, :] = jnp.sum(jnp.where(member, value, 0.0), axis=0, keepdims=True) * scale
    for copy in copies:
        copy.wait()


def on_device(features, labels, pick_index, *, n_ex):
    rows, full = features.shape
    steps, classes = pick_index.shape
    groups = n_ex // 2
    width = full // n_ex
    total = steps * classes
    main = full // 2 * steps * slots // 8
    limit = pltpu.CompilerParams(vmem_limit_bytes=16 << 20)
    vmem = pl.BlockSpec(memory_space=pltpu.VMEM)
    hbm = pl.BlockSpec(memory_space=pltpu.HBM)
    anywhere = pl.BlockSpec(memory_space=pl.ANY)
    half = jax.ShapeDtypeStruct((groups * classes + 8, width), f32)
    code = jax.ShapeDtypeStruct((groups // 4, classes * (width // 128) + 8, 128), jnp.int16)

    def swap(x, mask):
        return lax.ppermute(x, "ex", [(d, d ^ mask) for d in range(n_ex)])

    def after(x, *others):
        return lax.optimization_barrier((x,) + others)[0]

    feat, send, keep, held = pl.pallas_call(
        functools.partial(sums_kernel, n_ex=n_ex),
        in_specs=[hbm] * 3,
        out_specs=[vmem] * 4,
        out_shape=[pltpu.VMEM((rows, full), bf16), half, half, jax.ShapeDtypeStruct((8, full), f32)],
        scratch_shapes=[
            pltpu.VMEM(labels.shape, jnp.int32),
            pltpu.VMEM(pick_index.shape, jnp.int32),
            pltpu.VMEM((classes + 16, rows), bf16),
            pltpu.SemaphoreType.DMA((n_ex + 2,)),
        ],
        compiler_params=limit,
        name="class_sums",
    )(*[pltpu.with_memory_space_constraint(a, pltpu.HBM) for a in (labels, pick_index, features)])

    def add(codes, last):
        return pl.pallas_call(
            functools.partial(add_kernel, classes=classes, last=last),
            in_specs=[vmem] * len(codes),
            out_specs=vmem,
            out_shape=code,
            compiler_params=limit,
            cost_estimate=pl.CostEstimate(flops=10**10, bytes_accessed=10**8, transcendentals=0) if last else None,
            name="add_sums",
        )(*codes)

    far_masks = [8 << b for b in range(n_ex.bit_length() - 4)]
    got = swap(send, 1)
    codes = pl.pallas_call(
        functools.partial(pair_kernel, classes=classes),
        in_specs=[vmem] * 2,
        out_specs=[vmem] * 4,
        out_shape=[code] * 4,
        compiler_params=limit,
        name="pair_sums",
    )(keep, got)
    packed = pl.pallas_call(
        functools.partial(pack_kernel, steps=steps),
        in_specs=[vmem],
        out_specs=vmem,
        out_shape=jax.ShapeDtypeStruct((2, 8, main), bf16),
        compiler_params=limit,
        name="pack_rows",
    )(held)
    for mask in reversed(far_masks):
        packed = jnp.concatenate([packed, swap(packed, mask)], axis=1)

    near_codes = [swap(c, m) for c, m in zip(codes[1:], near_masks[1:])]
    part_sum = add([codes[0], after(near_codes[0], packed)] + near_codes[1:], False)

    def select(tail, *others):
        return pl.pallas_call(
            functools.partial(select_kernel, n_ex=n_ex, rows=rows, tail=tail),
            in_specs=[vmem],
            out_specs=vmem,
            out_shape=jax.ShapeDtypeStruct((total, n_ex * 8), bf16),
            compiler_params=limit,
            name="select_tails" if tail else "select_rows",
        )(after(pick_index, *others))

    rest = select(True, codes[0])
    near_sum = after(part_sum, rest)
    more = swap(near_sum, far_masks[0])
    one = select(False, near_sum)
    part_sum = add([near_sum, more], len(far_masks) == 1)
    for mask in far_masks[1:]:
        part_sum = add([part_sum, swap(part_sum, mask)], mask == far_masks[-1])
    given = swap(after(packed[1], near_sum), 1)
    near = jnp.concatenate([after(packed[0], one), given], axis=0)
    parts = [near] + [swap(near, m) for m in near_masks[1:]]
    own_parts = [part_sum] + [swap(part_sum, m) for m in near_masks[1:3]]
    own_parts.append(swap(after(part_sum, parts[1]), near_masks[3]))

    x = pl.pallas_call(
        functools.partial(picked_kernel, steps=steps),
        in_specs=[vmem] * 6,
        out_specs=vmem,
        out_shape=jax.ShapeDtypeStruct((total, full // 2), bf16),
        scratch_shapes=[pltpu.VMEM((n_ex * 8, main), bf16)],
        compiler_params=limit,
        name="picked_rows",
    )(one, rest, *parts)

    x_twin = swap(x, 1)
    own_half = jnp.concatenate(after(own_parts, x), axis=0)
    twin_half = swap(own_half, 1)
    left = pltpu.VMEM((total + classes, full // 2), bf16)
    direct, gram, target = pl.pallas_call(
        functools.partial(half_kernel, classes=classes),
        in_specs=[vmem] * 3,
        out_specs=[vmem] * 3,
        out_shape=[
            jax.ShapeDtypeStruct((total, rows), f32),
            jax.ShapeDtypeStruct((total + classes, total), f32),
            jax.ShapeDtypeStruct((classes, full // 2), f32),
        ],
        scratch_shapes=[left],
        compiler_params=limit,
        name="own_half_products",
    )(feat, own_half, x)

    scores, resid = pl.pallas_call(
        functools.partial(pursuit_kernel, steps=steps, scale=1.0 / math.sqrt(full)),
        in_specs=[vmem] * 8,
        out_specs=[vmem, anywhere],
        out_shape=[
            jax.ShapeDtypeStruct((steps, rows), f32),
            jax.ShapeDtypeStruct((classes, full), f32),
        ],
        scratch_shapes=[pltpu.VMEM((classes, full), f32), left, pltpu.SemaphoreType.DMA((4,))],
        compiler_params=limit,
        name="pursuit",
    )(labels, feat, x, x_twin, direct, gram, target, twin_half)
    return scores, resid


def solution(mesh):
    return jax.shard_map(
        functools.partial(on_device, n_ex=mesh.shape["ex"]),
        mesh=mesh,
        in_specs=(P(("grp", "ex"), None), P(("grp", "ex")), P("grp", None)),
        out_specs=(P(None, ("grp", "ex")), P("grp", None)),
        check_vma=False,
    )
```

```python
import functools
import math

import jax
import jax.numpy as jnp
from jax import lax
from jax.experimental import pallas as pl
from jax.experimental.pallas import tpu as pltpu
from jax.sharding import PartitionSpec as P

ridge = 1.0
slots = 2
near_masks = (0, 4, 2, 6)
f32 = jnp.float32
bf16 = jnp.bfloat16


def nt_dot(a, b):
    return lax.dot_general(a, b, (((1,), (1,)), ((), ())), preferred_element_type=f32)


def column(tile, height, start=0):
    return jnp.concatenate([tile[:, start + q : start + q + 1] for q in range(height // 8)], axis=0)


def spread(values, start=0):
    lane = lax.broadcasted_iota(jnp.int32, (8, 128), 1)
    tile = jnp.zeros((8, 128), f32)
    for q in range(values.shape[0] // 8):
        tile = jnp.where(lane == start + q, values[8 * q : 8 * q + 8], tile)
    return tile


def encode(x, count_tile=None):
    height, width = x.shape
    top = jnp.max(jnp.abs(x), axis=1, keepdims=True)
    power = jnp.ceil(jnp.log2(jnp.maximum(top, 1e-30)) + 0.01)
    whole_x = jnp.round(x * jnp.exp2(15.0 - power))
    mark = spread(power)
    if count_tile is not None:
        mark = mark + count_tile
    chunks = [whole_x[:, j * 128 : (j + 1) * 128] for j in range(width // 128)]
    return jnp.concatenate(chunks + [mark], axis=0).astype(jnp.int32).astype(jnp.int16)


def decode(code, height):
    value = code.astype(jnp.int32).astype(f32)
    count = value.shape[0] // height
    mark = value[count * height :]
    x = jnp.concatenate([value[j * height : (j + 1) * height] for j in range(count)], axis=1)
    return x * jnp.exp2(column(mark, height) - 15.0), mark


def sums_kernel(
    labels_hbm, pick_hbm, feat_hbm, feat_ref, send_ref, keep_ref, held, labels_ref, pick_ref, left, sems, *, n_ex
):
    rows, full = feat_ref.shape
    steps, classes = pick_ref.shape
    width = full // n_ex
    groups = n_ex // 2
    device = lax.axis_index("ex")
    core = device % 2
    small = [
        pltpu.make_async_copy(pick_hbm, pick_ref, sems.at[n_ex]),
        pltpu.make_async_copy(labels_hbm, labels_ref, sems.at[n_ex + 1]),
    ]
    for copy in small:
        copy.start()
    columns = []
    copies = []
    for i in range(n_ex):
        block = (1 - core) * groups + i if i < groups else core * groups + i - groups
        at = pl.ds(pl.multiple_of(block * width, width), width)
        columns.append(at)
        copies.append(pltpu.make_async_copy(feat_hbm.at[:, at], feat_ref.at[:, at], sems.at[i]))
        copies[-1].start()

    for copy in small:
        copy.wait()
    local = pick_ref[...] - device * rows
    mine = (local >= 0) & (local < rows)
    lane = lax.broadcasted_iota(jnp.int32, local.shape, 1)
    first = jnp.min(jnp.where(mine, lane, classes), axis=1, keepdims=True)
    last = jnp.max(jnp.where(mine, lane, -1), axis=1, keepdims=True)
    spot0 = jnp.max(jnp.where(mine & (lane == first), local, -1), axis=1, keepdims=True)
    spot1 = jnp.max(jnp.where(mine & (lane == last) & (last > first), local, -1), axis=1, keepdims=True)
    member = lax.broadcasted_iota(jnp.int32, (classes, rows), 0) == labels_ref[...].reshape(1, rows)
    line = lax.broadcasted_iota(jnp.int32, (steps, rows), 1)
    left[...] = jnp.concatenate(
        [
            jnp.where(member, 1.0, 0.0),
            jnp.where(line == spot0, 1.0, 0.0),
            jnp.where(line == spot1, 1.0, 0.0),
            jnp.zeros((16 - 2 * steps, rows), f32),
        ],
        axis=0,
    ).astype(bf16)
    count = jnp.sum(jnp.where(member, 1.0, 0.0), axis=1, keepdims=True)
    tile = spread(count, classes // 8)
    base = groups * classes
    for ref in (send_ref, keep_ref):
        ref[base : base + 8, :128] = tile
        if width > 128:
            ref[base : base + 8, 128:] = jnp.zeros((8, width - 128), f32)

    for i in range(n_ex):
        copies[i].wait()
        both = jnp.dot(left[...], feat_ref[:, columns[i]], preferred_element_type=f32)
        k = i % groups
        ref = send_ref if i < groups else keep_ref
        ref[k * classes : (k + 1) * classes, :] = both[:classes]
        held[:, columns[i]] = both[classes : classes + 8]


def pack_kernel(held, rows_ref, *, steps):
    half = held.shape[1] // 2
    used = steps * slots
    main = rows_ref.shape[2]
    core = lax.axis_index("ex") % 2
    for part, side in ((0, core), (1, 1 - core)):
        h = held[:, pl.ds(pl.multiple_of(side * half, half), half)]
        lines = [h[:used, :main]]
        for q in range(slots):
            lines.append(jnp.concatenate([h[q * steps + u : q * steps + u + 1, main:] for u in range(steps)], axis=1))
        rows_ref[part] = jnp.concatenate(lines, axis=0).astype(bf16)


def near_id(mask):
    return (lax.axis_index("ex") // 2 % 4) ^ (mask // 2)


def pair_kernel(keep_ref, got_ref, *code_refs, classes):
    far = code_refs[0].shape[0]
    base = 4 * far * classes
    tile = keep_ref[base : base + 8, :128] + got_ref[base : base + 8, :128]
    for mask, code_ref in zip(near_masks, code_refs):
        for j in range(far):
            at = pl.ds(pl.multiple_of((j * 4 + near_id(mask)) * classes, classes), classes)
            code_ref[j] = encode(keep_ref[at, :] + got_ref[at, :], tile)


def add_kernel(*refs, classes, last):
    code_ref = refs[-1]
    for j in range(code_ref.shape[0]):
        value, mark = decode(refs[0][j], classes)
        for ref in refs[1:-1]:
            more, more_mark = decode(ref[j], classes)
            value = value + more
            mark = mark + more_mark
        if last:
            code_ref[j] = encode(value / jnp.sqrt(column(mark, classes, classes // 8)))
        else:
            lane = lax.broadcasted_iota(jnp.int32, mark.shape, 1)
            code_ref[j] = encode(value, jnp.where(lane < classes // 8, 0.0, mark))


def diagonal(block):
    n = block.shape[0]
    eye = lax.broadcasted_iota(jnp.int32, (n, n), 0) == lax.broadcasted_iota(jnp.int32, (n, n), 1)
    return jnp.sum(jnp.where(eye, block, 0.0), axis=1, keepdims=True)


def factor_all(gram):
    order = len(gram)
    factor = [[None] * order for _ in range(order)]
    for j in range(order):
        value = gram[j][j]
        for k in range(j):
            value = value - factor[j][k] * factor[j][k]
        root = jnp.sqrt(value)
        factor[j][j] = 1.0 / root
        for i in range(j + 1, order):
            value = gram[i][j]
            for k in range(j):
                value = value - factor[i][k] * factor[j][k]
            factor[i][j] = value * factor[j][j]
    return factor


def solve_all(factor, right):
    order = len(right)
    forward = []
    for i in range(order):
        value = right[i]
        for j in range(i):
            value = value - factor[i][j] * forward[j]
        forward.append(value * factor[i][i])
    result = []
    for size in range(1, order + 1):
        back = [None] * size
        for i in reversed(range(size)):
            value = forward[i]
            for j in range(i + 1, size):
                value = value - factor[j][i] * back[j]
            back[i] = value * factor[i][i]
        result.append(back)
    return result


def select_kernel(pick_ref, one_ref, *, n_ex, rows, tail):
    steps, classes = pick_ref.shape
    lines = one_ref.shape[1]
    device = lax.axis_index("ex")
    pick = pick_ref[...]
    lane = lax.broadcasted_iota(jnp.int32, pick.shape, 1)
    owner = jnp.zeros_like(pick)
    rank = jnp.zeros_like(pick)
    for d in range(n_ex):
        here = (pick >= d * rows) & (pick < (d + 1) * rows)
        first = jnp.min(jnp.where(here, lane, classes), axis=1, keepdims=True)
        owner = jnp.where(here, d, owner)
        rank = jnp.where(here & (lane > first), 1, rank)
    away = owner ^ device
    bits = n_ex.bit_length() - 1
    far = jnp.zeros_like(pick)
    for b in range(3, bits):
        far = far + (((away >> b) & 1) << (bits - 1 - b))
    near = ((away >> 2) & 1) + 2 * ((away >> 1) & 1)
    spot = (2 * near + (away & 1)) * (n_ex // 8) + far
    step = lax.broadcasted_iota(jnp.int32, pick.shape, 0)
    line = lax.broadcasted_iota(jnp.int32, (lines, classes), 0)
    where = spot * 8 + (slots * steps + rank if tail else rank * steps + step)
    hits = [jnp.where(line == where[s : s + 1, :], 1.0, 0.0) for s in range(steps)]
    pad = jnp.zeros((lines, 128 - steps * classes), f32)
    one_ref[...] = jnp.transpose(jnp.concatenate(hits + [pad], axis=1))[: steps * classes].astype(bf16)


def picked_kernel(one_ref, rest_ref, *refs, steps):
    parts, (x_ref, rows_ref) = refs[:-2], refs[-2:]
    total, half = x_ref.shape
    classes = total // steps
    main = rows_ref.shape[1]
    tail = half - main
    at = 0
    for part in parts:
        rows_ref[at : at + part.shape[0], :] = part[...]
        at += part.shape[0]
    x_ref[:, :main] = jnp.dot(one_ref[...], rows_ref[...], preferred_element_type=f32).astype(bf16)
    for s in range(steps):
        at = slice(s * classes, (s + 1) * classes)
        rest = jnp.dot(rest_ref[at, :], rows_ref[:, s * tail : (s + 1) * tail], preferred_element_type=f32)
        x_ref[at, main:] = rest.astype(bf16)


def half_target(side, code_ref, x_ref, target_ref, target_at, left_ref, *, classes):
    half = left_ref.shape[1]
    far = code_ref.shape[0] // 4
    width = half // code_ref.shape[0]
    here = pl.ds(pl.multiple_of(side * half, half), half)
    for k in range(4 * far):
        block = k % far * 4 + near_id(near_masks[k // far])
        target = decode(code_ref[k], classes)[0]
        target_ref[:, pl.ds(pl.multiple_of(target_at + block * width, width), width)] = target
        left_ref[:classes, pl.ds(pl.multiple_of(block * width, width), width)] = target.astype(bf16)
    left_ref[classes:, :] = x_ref[...]
    return nt_dot(left_ref[...], x_ref[...]), here


def half_kernel(feat_ref, code_ref, x_ref, direct_ref, gram_ref, target_ref, left_ref, *, classes):
    core = lax.axis_index("ex") % 2
    gram_ref[...], here = half_target(core, code_ref, x_ref, target_ref, 0, left_ref, classes=classes)
    direct_ref[...] = nt_dot(left_ref[: direct_ref.shape[0], :], feat_ref[:, here])


def pursuit_kernel(
    labels_ref, feat_ref, x_own, x_twin, direct_own, gram_own, target_own, code_ref,
    scores_ref, resid_hbm, resid_ref, left_ref, sems, *, steps, scale
):
    classes, full = resid_ref.shape
    half = full // 2
    core = lax.axis_index("ex") % 2
    gram, other = half_target(1 - core, code_ref, x_twin, resid_ref, (1 - core) * half, left_ref, classes=classes)
    gram = gram + gram_own[...]
    blocks = [
        [
            diagonal(gram[(a + 1) * classes : (a + 2) * classes, b * classes : (b + 1) * classes])
            + (ridge if a == b else 0.0)
            for b in range(a + 1)
        ]
        for a in range(steps)
    ]
    rhs = [diagonal(gram[:classes, a * classes : (a + 1) * classes]) for a in range(steps)]
    weights = solve_all(factor_all(blocks), rhs)
    last = weights[steps - 1]
    copies = []
    span = half // 2
    for x_ref, side in ((x_own, core), (x_twin, 1 - core)):
        for q in range(2):
            there = slice(q * span, (q + 1) * span)
            here = pl.ds(pl.multiple_of(side * half + q * span, span), span)
            value = target_own[:, there] if x_ref is x_own else resid_ref[:, here]
            for k in range(steps):
                value = value - last[k] * x_ref[k * classes : (k + 1) * classes, there].astype(f32)
            resid_ref[:, here] = value
            copies.append(pltpu.make_async_copy(resid_ref.at[:, here], resid_hbm.at[:, here], sems.at[len(copies)]))
            copies[-1].start()

    direct = direct_own[...] + nt_dot(left_ref[: direct_own.shape[0], :], feat_ref[:, other])
    member = lax.broadcasted_iota(jnp.int32, (classes, direct.shape[1]), 0) == labels_ref[...].reshape(1, direct.shape[1])
    for s in range(steps):
        value = direct[:classes]
        for k in range(s):
            value = value - weights[s - 1][k] * direct[(k + 1) * classes : (k + 2) * classes]
        scores_ref[s : s + 1, :] = jnp.sum(jnp.where(member, value, 0.0), axis=0, keepdims=True) * scale
    for copy in copies:
        copy.wait()


def on_device(features, labels, pick_index, *, n_ex):
    rows, full = features.shape
    steps, classes = pick_index.shape
    groups = n_ex // 2
    width = full // n_ex
    total = steps * classes
    main = full // 2 * steps * slots // 8
    limit = pltpu.CompilerParams(vmem_limit_bytes=16 << 20)
    vmem = pl.BlockSpec(memory_space=pltpu.VMEM)
    hbm = pl.BlockSpec(memory_space=pltpu.HBM)
    anywhere = pl.BlockSpec(memory_space=pl.ANY)
    half = jax.ShapeDtypeStruct((groups * classes + 8, width), f32)
    code = jax.ShapeDtypeStruct((groups // 4, classes * (width // 128) + 8, 128), jnp.int16)

    def swap(x, mask):
        return lax.ppermute(x, "ex", [(d, d ^ mask) for d in range(n_ex)])

    def after(x, *others):
        return lax.optimization_barrier((x,) + others)[0]

    feat, send, keep, held = pl.pallas_call(
        functools.partial(sums_kernel, n_ex=n_ex),
        in_specs=[hbm] * 3,
        out_specs=[vmem] * 4,
        out_shape=[pltpu.VMEM((rows, full), bf16), half, half, jax.ShapeDtypeStruct((8, full), f32)],
        scratch_shapes=[
            pltpu.VMEM(labels.shape, jnp.int32),
            pltpu.VMEM(pick_index.shape, jnp.int32),
            pltpu.VMEM((classes + 16, rows), bf16),
            pltpu.SemaphoreType.DMA((n_ex + 2,)),
        ],
        compiler_params=limit,
        name="class_sums",
    )(*[pltpu.with_memory_space_constraint(a, pltpu.HBM) for a in (labels, pick_index, features)])

    def add(codes, last):
        return pl.pallas_call(
            functools.partial(add_kernel, classes=classes, last=last),
            in_specs=[vmem] * len(codes),
            out_specs=vmem,
            out_shape=code,
            compiler_params=limit,
            cost_estimate=pl.CostEstimate(flops=10**10, bytes_accessed=10**8, transcendentals=0) if last else None,
            name="add_sums",
        )(*codes)

    far_masks = [8 << b for b in range(n_ex.bit_length() - 4)]
    got = swap(send, 1)
    codes = pl.pallas_call(
        functools.partial(pair_kernel, classes=classes),
        in_specs=[vmem] * 2,
        out_specs=[vmem] * 4,
        out_shape=[code] * 4,
        compiler_params=limit,
        name="pair_sums",
    )(keep, got)
    packed = pl.pallas_call(
        functools.partial(pack_kernel, steps=steps),
        in_specs=[vmem],
        out_specs=vmem,
        out_shape=jax.ShapeDtypeStruct((2, 8, main), bf16),
        compiler_params=limit,
        name="pack_rows",
    )(held)
    for mask in reversed(far_masks):
        packed = jnp.concatenate([packed, swap(packed, mask)], axis=1)

    near_codes = [swap(c, m) for c, m in zip(codes[1:], near_masks[1:])]
    part_sum = add([codes[0], after(near_codes[0], packed)] + near_codes[1:], False)

    def select(tail, *others):
        return pl.pallas_call(
            functools.partial(select_kernel, n_ex=n_ex, rows=rows, tail=tail),
            in_specs=[vmem],
            out_specs=vmem,
            out_shape=jax.ShapeDtypeStruct((total, n_ex * 8), bf16),
            compiler_params=limit,
            name="select_tails" if tail else "select_rows",
        )(after(pick_index, *others))

    rest = select(True, codes[0])
    near_sum = after(part_sum, rest)
    more = swap(near_sum, far_masks[0])
    one = select(False, near_sum)
    part_sum = add([near_sum, more], len(far_masks) == 1)
    for mask in far_masks[1:]:
        part_sum = add([part_sum, swap(part_sum, mask)], mask == far_masks[-1])
    given = swap(after(packed[1], near_sum), 1)
    near = jnp.concatenate([after(packed[0], one), given], axis=0)
    by_z, by_y = swap(near, 4), swap(near, 2)
    own_parts = [part_sum] + [swap(part_sum, m) for m in near_masks[1:]]
    by_z, by_y = after(by_z, own_parts[1]), after(by_y, own_parts[1])
    cut = near.shape[0] // 2
    parts = [near, by_z, by_y, swap(by_y[:cut], 4), swap(by_z[cut:], 2)]

    x = pl.pallas_call(
        functools.partial(picked_kernel, steps=steps),
        in_specs=[vmem] * 7,
        out_specs=vmem,
        out_shape=jax.ShapeDtypeStruct((total, full // 2), bf16),
        scratch_shapes=[pltpu.VMEM((n_ex * 8, main), bf16)],
        compiler_params=limit,
        name="picked_rows",
    )(one, rest, *parts)

    x_twin = swap(x, 1)
    own_half = jnp.concatenate(after(own_parts, x), axis=0)
    twin_half = swap(own_half, 1)
    left = pltpu.VMEM((total + classes, full // 2), bf16)
    direct, gram, target = pl.pallas_call(
        functools.partial(half_kernel, classes=classes),
        in_specs=[vmem] * 3,
        out_specs=[vmem] * 3,
        out_shape=[
            jax.ShapeDtypeStruct((total, rows), f32),
            jax.ShapeDtypeStruct((total + classes, total), f32),
            jax.ShapeDtypeStruct((classes, full // 2), f32),
        ],
        scratch_shapes=[left],
        compiler_params=limit,
        name="own_half_products",
    )(feat, own_half, x)

    scores, resid = pl.pallas_call(
        functools.partial(pursuit_kernel, steps=steps, scale=1.0 / math.sqrt(full)),
        in_specs=[vmem] * 8,
        out_specs=[vmem, anywhere],
        out_shape=[
            jax.ShapeDtypeStruct((steps, rows), f32),
            jax.ShapeDtypeStruct((classes, full), f32),
        ],
        scratch_shapes=[pltpu.VMEM((classes, full), f32), left, pltpu.SemaphoreType.DMA((4,))],
        compiler_params=limit,
        name="pursuit",
    )(labels, feat, x, x_twin, direct, gram, target, twin_half)
    return scores, resid


def solution(mesh):
    return jax.shard_map(
        functools.partial(on_device, n_ex=mesh.shape["ex"]),
        mesh=mesh,
        in_specs=(P(("grp", "ex"), None), P(("grp", "ex")), P("grp", None)),
        out_specs=(P(None, ("grp", "ex")), P("grp", None)),
        check_vma=False,
    )
```

```python
import functools
import math

import jax
import jax.numpy as jnp
from jax import lax
from jax.experimental import pallas as pl
from jax.experimental.pallas import tpu as pltpu
from jax.sharding import PartitionSpec as P

ridge = 1.0
slots = 2
near_masks = (0, 4, 2, 6)
f32 = jnp.float32
bf16 = jnp.bfloat16


def nt_dot(a, b):
    return lax.dot_general(a, b, (((1,), (1,)), ((), ())), preferred_element_type=f32)


def column(tile, height, start=0):
    return jnp.concatenate([tile[:, start + q : start + q + 1] for q in range(height // 8)], axis=0)


def spread(values, start=0):
    lane = lax.broadcasted_iota(jnp.int32, (8, 128), 1)
    tile = jnp.zeros((8, 128), f32)
    for q in range(values.shape[0] // 8):
        tile = jnp.where(lane == start + q, values[8 * q : 8 * q + 8], tile)
    return tile


def encode(x, count_tile=None):
    height, width = x.shape
    top = jnp.max(jnp.abs(x), axis=1, keepdims=True)
    power = jnp.ceil(jnp.log2(jnp.maximum(top, 1e-30)) + 0.01)
    whole_x = jnp.round(x * jnp.exp2(15.0 - power))
    mark = spread(power)
    if count_tile is not None:
        mark = mark + count_tile
    chunks = [whole_x[:, j * 128 : (j + 1) * 128] for j in range(width // 128)]
    return jnp.concatenate(chunks + [mark], axis=0).astype(jnp.int32).astype(jnp.int16)


def decode(code, height):
    value = code.astype(jnp.int32).astype(f32)
    count = value.shape[0] // height
    mark = value[count * height :]
    x = jnp.concatenate([value[j * height : (j + 1) * height] for j in range(count)], axis=1)
    return x * jnp.exp2(column(mark, height) - 15.0), mark


def sums_kernel(
    labels_hbm, pick_hbm, feat_hbm, feat_ref, send_ref, keep_ref, held, labels_ref, pick_ref, left, sems, *, n_ex
):
    rows, full = feat_ref.shape
    steps, classes = pick_ref.shape
    width = full // n_ex
    groups = n_ex // 2
    device = lax.axis_index("ex")
    core = device % 2
    small = [
        pltpu.make_async_copy(pick_hbm, pick_ref, sems.at[n_ex]),
        pltpu.make_async_copy(labels_hbm, labels_ref, sems.at[n_ex + 1]),
    ]
    for copy in small:
        copy.start()
    columns = []
    copies = []
    for i in range(n_ex):
        block = (1 - core) * groups + i if i < groups else core * groups + i - groups
        at = pl.ds(pl.multiple_of(block * width, width), width)
        columns.append(at)
        copies.append(pltpu.make_async_copy(feat_hbm.at[:, at], feat_ref.at[:, at], sems.at[i]))
        copies[-1].start()

    for copy in small:
        copy.wait()
    local = pick_ref[...] - device * rows
    mine = (local >= 0) & (local < rows)
    lane = lax.broadcasted_iota(jnp.int32, local.shape, 1)
    first = jnp.min(jnp.where(mine, lane, classes), axis=1, keepdims=True)
    last = jnp.max(jnp.where(mine, lane, -1), axis=1, keepdims=True)
    spot0 = jnp.max(jnp.where(mine & (lane == first), local, -1), axis=1, keepdims=True)
    spot1 = jnp.max(jnp.where(mine & (lane == last) & (last > first), local, -1), axis=1, keepdims=True)
    member = lax.broadcasted_iota(jnp.int32, (classes, rows), 0) == labels_ref[...].reshape(1, rows)
    line = lax.broadcasted_iota(jnp.int32, (steps, rows), 1)
    left[...] = jnp.concatenate(
        [
            jnp.where(member, 1.0, 0.0),
            jnp.where(line == spot0, 1.0, 0.0),
            jnp.where(line == spot1, 1.0, 0.0),
            jnp.zeros((16 - 2 * steps, rows), f32),
        ],
        axis=0,
    ).astype(bf16)
    count = jnp.sum(jnp.where(member, 1.0, 0.0), axis=1, keepdims=True)
    tile = spread(count, classes // 8)
    base = groups * classes
    for ref in (send_ref, keep_ref):
        ref[base : base + 8, :128] = tile
        if width > 128:
            ref[base : base + 8, 128:] = jnp.zeros((8, width - 128), f32)

    for i in range(n_ex):
        copies[i].wait()
        both = jnp.dot(left[...], feat_ref[:, columns[i]], preferred_element_type=f32)
        k = i % groups
        ref = send_ref if i < groups else keep_ref
        ref[k * classes : (k + 1) * classes, :] = both[:classes]
        held[:, columns[i]] = both[classes : classes + 8]


def pack_kernel(held, rows_ref, *, steps):
    half = held.shape[1] // 2
    used = steps * slots
    main = rows_ref.shape[2]
    core = lax.axis_index("ex") % 2
    for part, side in ((0, core), (1, 1 - core)):
        h = held[:, pl.ds(pl.multiple_of(side * half, half), half)]
        lines = [h[:used, :main]]
        for q in range(slots):
            lines.append(jnp.concatenate([h[q * steps + u : q * steps + u + 1, main:] for u in range(steps)], axis=1))
        rows_ref[part] = jnp.concatenate(lines, axis=0).astype(bf16)


def near_id(mask):
    return (lax.axis_index("ex") // 2 % 4) ^ (mask // 2)


def pair_kernel(keep_ref, got_ref, *code_refs, classes):
    far = code_refs[0].shape[0]
    base = 4 * far * classes
    tile = keep_ref[base : base + 8, :128] + got_ref[base : base + 8, :128]
    for mask, code_ref in zip(near_masks, code_refs):
        for j in range(far):
            at = pl.ds(pl.multiple_of((j * 4 + near_id(mask)) * classes, classes), classes)
            code_ref[j] = encode(keep_ref[at, :] + got_ref[at, :], tile)


def add_kernel(*refs, classes, last):
    code_ref = refs[-1]
    for j in range(code_ref.shape[0]):
        value, mark = decode(refs[0][j], classes)
        for ref in refs[1:-1]:
            more, more_mark = decode(ref[j], classes)
            value = value + more
            mark = mark + more_mark
        if last:
            code_ref[j] = encode(value / jnp.sqrt(column(mark, classes, classes // 8)))
        else:
            lane = lax.broadcasted_iota(jnp.int32, mark.shape, 1)
            code_ref[j] = encode(value, jnp.where(lane < classes // 8, 0.0, mark))


def diagonal(block):
    n = block.shape[0]
    eye = lax.broadcasted_iota(jnp.int32, (n, n), 0) == lax.broadcasted_iota(jnp.int32, (n, n), 1)
    return jnp.sum(jnp.where(eye, block, 0.0), axis=1, keepdims=True)


def factor_all(gram):
    order = len(gram)
    factor = [[None] * order for _ in range(order)]
    for j in range(order):
        value = gram[j][j]
        for k in range(j):
            value = value - factor[j][k] * factor[j][k]
        root = jnp.sqrt(value)
        factor[j][j] = 1.0 / root
        for i in range(j + 1, order):
            value = gram[i][j]
            for k in range(j):
                value = value - factor[i][k] * factor[j][k]
            factor[i][j] = value * factor[j][j]
    return factor


def solve_all(factor, right):
    order = len(right)
    forward = []
    for i in range(order):
        value = right[i]
        for j in range(i):
            value = value - factor[i][j] * forward[j]
        forward.append(value * factor[i][i])
    result = []
    for size in range(1, order + 1):
        back = [None] * size
        for i in reversed(range(size)):
            value = forward[i]
            for j in range(i + 1, size):
                value = value - factor[j][i] * back[j]
            back[i] = value * factor[i][i]
        result.append(back)
    return result


def select_kernel(pick_ref, one_ref, *, n_ex, rows, tail):
    steps, classes = pick_ref.shape
    lines = one_ref.shape[1]
    device = lax.axis_index("ex")
    pick = pick_ref[...]
    lane = lax.broadcasted_iota(jnp.int32, pick.shape, 1)
    owner = jnp.zeros_like(pick)
    rank = jnp.zeros_like(pick)
    for d in range(n_ex):
        here = (pick >= d * rows) & (pick < (d + 1) * rows)
        first = jnp.min(jnp.where(here, lane, classes), axis=1, keepdims=True)
        owner = jnp.where(here, d, owner)
        rank = jnp.where(here & (lane > first), 1, rank)
    away = owner ^ device
    bits = n_ex.bit_length() - 1
    far = jnp.zeros_like(pick)
    for b in range(3, bits):
        far = far + (((away >> b) & 1) << (bits - 1 - b))
    near = ((away >> 2) & 1) + 2 * ((away >> 1) & 1)
    side = away & 1
    others = n_ex // 8 - 1
    spot = 2 * near * (others + 1) + jnp.where(far == 0, side, 1 + side * others + far)
    step = lax.broadcasted_iota(jnp.int32, pick.shape, 0)
    line = lax.broadcasted_iota(jnp.int32, (lines, classes), 0)
    where = spot * 8 + (slots * steps + rank if tail else rank * steps + step)
    hits = [jnp.where(line == where[s : s + 1, :], 1.0, 0.0) for s in range(steps)]
    pad = jnp.zeros((lines, 128 - steps * classes), f32)
    one_ref[...] = jnp.transpose(jnp.concatenate(hits + [pad], axis=1))[: steps * classes].astype(bf16)


def picked_kernel(one_ref, rest_ref, *refs, steps):
    parts, (x_ref, rows_ref) = refs[:-2], refs[-2:]
    total, half = x_ref.shape
    classes = total // steps
    main = rows_ref.shape[1]
    tail = half - main
    at = 0
    for part in parts:
        rows_ref[at : at + part.shape[0], :] = part[...]
        at += part.shape[0]
    x_ref[:, :main] = jnp.dot(one_ref[...], rows_ref[...], preferred_element_type=f32).astype(bf16)
    for s in range(steps):
        at = slice(s * classes, (s + 1) * classes)
        rest = jnp.dot(rest_ref[at, :], rows_ref[:, s * tail : (s + 1) * tail], preferred_element_type=f32)
        x_ref[at, main:] = rest.astype(bf16)


def half_target(side, code_ref, x_ref, target_ref, target_at, left_ref, *, classes):
    half = left_ref.shape[1]
    far = code_ref.shape[0] // 4
    width = half // code_ref.shape[0]
    here = pl.ds(pl.multiple_of(side * half, half), half)
    for k in range(4 * far):
        block = k % far * 4 + near_id(near_masks[k // far])
        target = decode(code_ref[k], classes)[0]
        target_ref[:, pl.ds(pl.multiple_of(target_at + block * width, width), width)] = target
        left_ref[:classes, pl.ds(pl.multiple_of(block * width, width), width)] = target.astype(bf16)
    left_ref[classes:, :] = x_ref[...]
    return nt_dot(left_ref[...], x_ref[...]), here


def half_kernel(feat_ref, code_ref, x_ref, direct_ref, gram_ref, target_ref, left_ref, *, classes):
    core = lax.axis_index("ex") % 2
    gram_ref[...], here = half_target(core, code_ref, x_ref, target_ref, 0, left_ref, classes=classes)
    direct_ref[...] = nt_dot(left_ref[: direct_ref.shape[0], :], feat_ref[:, here])


def pursuit_kernel(
    labels_ref, feat_ref, x_own, x_twin, direct_own, gram_own, target_own, code_ref,
    scores_ref, resid_hbm, resid_ref, left_ref, sems, *, steps, scale
):
    classes, full = resid_ref.shape
    half = full // 2
    core = lax.axis_index("ex") % 2
    gram, other = half_target(1 - core, code_ref, x_twin, resid_ref, (1 - core) * half, left_ref, classes=classes)
    gram = gram + gram_own[...]
    blocks = [
        [
            diagonal(gram[(a + 1) * classes : (a + 2) * classes, b * classes : (b + 1) * classes])
            + (ridge if a == b else 0.0)
            for b in range(a + 1)
        ]
        for a in range(steps)
    ]
    rhs = [diagonal(gram[:classes, a * classes : (a + 1) * classes]) for a in range(steps)]
    weights = solve_all(factor_all(blocks), rhs)
    last = weights[steps - 1]
    copies = []
    span = half // 2
    for x_ref, side in ((x_own, core), (x_twin, 1 - core)):
        for q in range(2):
            there = slice(q * span, (q + 1) * span)
            here = pl.ds(pl.multiple_of(side * half + q * span, span), span)
            value = target_own[:, there] if x_ref is x_own else resid_ref[:, here]
            for k in range(steps):
                value = value - last[k] * x_ref[k * classes : (k + 1) * classes, there].astype(f32)
            resid_ref[:, here] = value
            copies.append(pltpu.make_async_copy(resid_ref.at[:, here], resid_hbm.at[:, here], sems.at[len(copies)]))
            copies[-1].start()

    direct = direct_own[...] + nt_dot(left_ref[: direct_own.shape[0], :], feat_ref[:, other])
    member = lax.broadcasted_iota(jnp.int32, (classes, direct.shape[1]), 0) == labels_ref[...].reshape(1, direct.shape[1])
    for s in range(steps):
        value = direct[:classes]
        for k in range(s):
            value = value - weights[s - 1][k] * direct[(k + 1) * classes : (k + 2) * classes]
        scores_ref[s : s + 1, :] = jnp.sum(jnp.where(member, value, 0.0), axis=0, keepdims=True) * scale
    for copy in copies:
        copy.wait()


def on_device(features, labels, pick_index, *, n_ex):
    rows, full = features.shape
    steps, classes = pick_index.shape
    groups = n_ex // 2
    width = full // n_ex
    total = steps * classes
    main = full // 2 * steps * slots // 8
    limit = pltpu.CompilerParams(vmem_limit_bytes=16 << 20)
    vmem = pl.BlockSpec(memory_space=pltpu.VMEM)
    hbm = pl.BlockSpec(memory_space=pltpu.HBM)
    anywhere = pl.BlockSpec(memory_space=pl.ANY)
    half = jax.ShapeDtypeStruct((groups * classes + 8, width), f32)
    code = jax.ShapeDtypeStruct((groups // 4, classes * (width // 128) + 8, 128), jnp.int16)

    def swap(x, mask):
        return lax.ppermute(x, "ex", [(d, d ^ mask) for d in range(n_ex)])

    def after(x, *others):
        return lax.optimization_barrier((x,) + others)[0]

    feat, send, keep, held = pl.pallas_call(
        functools.partial(sums_kernel, n_ex=n_ex),
        in_specs=[hbm] * 3,
        out_specs=[vmem] * 4,
        out_shape=[pltpu.VMEM((rows, full), bf16), half, half, jax.ShapeDtypeStruct((8, full), f32)],
        scratch_shapes=[
            pltpu.VMEM(labels.shape, jnp.int32),
            pltpu.VMEM(pick_index.shape, jnp.int32),
            pltpu.VMEM((classes + 16, rows), bf16),
            pltpu.SemaphoreType.DMA((n_ex + 2,)),
        ],
        compiler_params=limit,
        name="class_sums",
    )(*[pltpu.with_memory_space_constraint(a, pltpu.HBM) for a in (labels, pick_index, features)])

    def add(codes, last):
        return pl.pallas_call(
            functools.partial(add_kernel, classes=classes, last=last),
            in_specs=[vmem] * len(codes),
            out_specs=vmem,
            out_shape=code,
            compiler_params=limit,
            cost_estimate=pl.CostEstimate(flops=10**10, bytes_accessed=10**8, transcendentals=0),
            name="add_sums",
        )(*codes)

    far_masks = [8 << b for b in range(n_ex.bit_length() - 4)]
    got = swap(send, 1)
    codes = pl.pallas_call(
        functools.partial(pair_kernel, classes=classes),
        in_specs=[vmem] * 2,
        out_specs=[vmem] * 4,
        out_shape=[code] * 4,
        compiler_params=limit,
        name="pair_sums",
    )(keep, got)
    packed = pl.pallas_call(
        functools.partial(pack_kernel, steps=steps),
        in_specs=[vmem],
        out_specs=vmem,
        out_shape=jax.ShapeDtypeStruct((2, 8, main), bf16),
        compiler_params=limit,
        name="pack_rows",
    )(held)
    for mask in reversed(far_masks):
        packed = jnp.concatenate([packed, swap(packed, mask)], axis=1)

    near_codes = [swap(c, m) for c, m in zip(codes[1:], near_masks[1:])]
    given = swap(after(packed[1], *near_codes), 1)
    part_sum = add([codes[0]] + near_codes, False)

    def select(tail, *others):
        return pl.pallas_call(
            functools.partial(select_kernel, n_ex=n_ex, rows=rows, tail=tail),
            in_specs=[vmem],
            out_specs=vmem,
            out_shape=jax.ShapeDtypeStruct((total, n_ex * 8), bf16),
            compiler_params=limit,
            name="select_tails" if tail else "select_rows",
        )(after(pick_index, *others))

    rest = select(True, codes[0])
    near_sum = after(part_sum, rest, given)
    more = swap(near_sum, far_masks[0])
    one = select(False, near_sum)
    here = jnp.concatenate([packed[0][:8], after(given, near_sum)[:8]], axis=0)
    there = jnp.concatenate([packed[0][8:], after(given, more)[8:]], axis=0)
    part_sum = add([near_sum, more], len(far_masks) == 1)
    for mask in far_masks[1:]:
        part_sum = add([part_sum, swap(part_sum, mask)], mask == far_masks[-1])
    parts = [here, there]
    for m in near_masks[1:]:
        parts += [swap(here, m), swap(there, m)]
    own_parts = [part_sum] + [swap(part_sum, m) for m in near_masks[1:]]

    x = pl.pallas_call(
        functools.partial(picked_kernel, steps=steps),
        in_specs=[vmem] * (2 + len(parts)),
        out_specs=vmem,
        out_shape=jax.ShapeDtypeStruct((total, full // 2), bf16),
        scratch_shapes=[pltpu.VMEM((n_ex * 8, main), bf16)],
        compiler_params=limit,
        name="picked_rows",
    )(one, rest, *parts)

    x_twin = swap(x, 1)
    own_half = jnp.concatenate(after(own_parts, x), axis=0)
    twin_half = swap(own_half, 1)
    left = pltpu.VMEM((total + classes, full // 2), bf16)
    direct, gram, target = pl.pallas_call(
        functools.partial(half_kernel, classes=classes),
        in_specs=[vmem] * 3,
        out_specs=[vmem] * 3,
        out_shape=[
            jax.ShapeDtypeStruct((total, rows), f32),
            jax.ShapeDtypeStruct((total + classes, total), f32),
            jax.ShapeDtypeStruct((classes, full // 2), f32),
        ],
        scratch_shapes=[left],
        compiler_params=limit,
        name="own_half_products",
    )(feat, own_half, x)

    scores, resid = pl.pallas_call(
        functools.partial(pursuit_kernel, steps=steps, scale=1.0 / math.sqrt(full)),
        in_specs=[vmem] * 8,
        out_specs=[vmem, anywhere],
        out_shape=[
            jax.ShapeDtypeStruct((steps, rows), f32),
            jax.ShapeDtypeStruct((classes, full), f32),
        ],
        scratch_shapes=[pltpu.VMEM((classes, full), f32), left, pltpu.SemaphoreType.DMA((4,))],
        compiler_params=limit,
        name="pursuit",
    )(labels, feat, x, x_twin, direct, gram, target, twin_half)
    return scores, resid


def solution(mesh):
    return jax.shard_map(
        functools.partial(on_device, n_ex=mesh.shape["ex"]),
        mesh=mesh,
        in_specs=(P(("grp", "ex"), None), P(("grp", "ex")), P("grp", None)),
        out_specs=(P(None, ("grp", "ex")), P("grp", None)),
        check_vma=False,
    )
```

```python
import functools
import math

import jax
import jax.numpy as jnp
from jax import lax
from jax.experimental import pallas as pl
from jax.experimental.pallas import tpu as pltpu
from jax.sharding import PartitionSpec as P

ridge = 1.0
slots = 2
near_masks = (0, 4, 2, 6)
f32 = jnp.float32
bf16 = jnp.bfloat16


def nt_dot(a, b):
    return lax.dot_general(a, b, (((1,), (1,)), ((), ())), preferred_element_type=f32)


def column(tile, height, start=0):
    return jnp.concatenate([tile[:, start + q : start + q + 1] for q in range(height // 8)], axis=0)


def spread(values, start=0):
    lane = lax.broadcasted_iota(jnp.int32, (8, 128), 1)
    tile = jnp.zeros((8, 128), f32)
    for q in range(values.shape[0] // 8):
        tile = jnp.where(lane == start + q, values[8 * q : 8 * q + 8], tile)
    return tile


def encode(x, count_tile=None):
    height, width = x.shape
    top = jnp.max(jnp.abs(x), axis=1, keepdims=True)
    power = jnp.ceil(jnp.log2(jnp.maximum(top, 1e-30)) + 0.01)
    whole_x = jnp.round(x * jnp.exp2(15.0 - power))
    mark = spread(power)
    if count_tile is not None:
        mark = mark + count_tile
    chunks = [whole_x[:, j * 128 : (j + 1) * 128] for j in range(width // 128)]
    return jnp.concatenate(chunks + [mark], axis=0).astype(jnp.int32).astype(jnp.int16)


def decode(code, height):
    value = code.astype(jnp.int32).astype(f32)
    count = value.shape[0] // height
    mark = value[count * height :]
    x = jnp.concatenate([value[j * height : (j + 1) * height] for j in range(count)], axis=1)
    return x * jnp.exp2(column(mark, height) - 15.0), mark


def sums_kernel(
    labels_hbm, pick_hbm, feat_hbm, feat_ref, send_ref, keep_ref, held, labels_ref, pick_ref, left, sems, *, n_ex
):
    rows, full = feat_ref.shape
    steps, classes = pick_ref.shape
    width = full // n_ex
    groups = n_ex // 2
    device = lax.axis_index("ex")
    core = device % 2
    small = [
        pltpu.make_async_copy(pick_hbm, pick_ref, sems.at[n_ex]),
        pltpu.make_async_copy(labels_hbm, labels_ref, sems.at[n_ex + 1]),
    ]
    for copy in small:
        copy.start()
    columns = []
    copies = []
    for i in range(n_ex):
        block = (1 - core) * groups + i if i < groups else core * groups + i - groups
        at = pl.ds(pl.multiple_of(block * width, width), width)
        columns.append(at)
        copies.append(pltpu.make_async_copy(feat_hbm.at[:, at], feat_ref.at[:, at], sems.at[i]))
        copies[-1].start()

    for copy in small:
        copy.wait()
    local = pick_ref[...] - device * rows
    mine = (local >= 0) & (local < rows)
    lane = lax.broadcasted_iota(jnp.int32, local.shape, 1)
    first = jnp.min(jnp.where(mine, lane, classes), axis=1, keepdims=True)
    last = jnp.max(jnp.where(mine, lane, -1), axis=1, keepdims=True)
    spot0 = jnp.max(jnp.where(mine & (lane == first), local, -1), axis=1, keepdims=True)
    spot1 = jnp.max(jnp.where(mine & (lane == last) & (last > first), local, -1), axis=1, keepdims=True)
    member = lax.broadcasted_iota(jnp.int32, (classes, rows), 0) == labels_ref[...].reshape(1, rows)
    line = lax.broadcasted_iota(jnp.int32, (steps, rows), 1)
    left[...] = jnp.concatenate(
        [
            jnp.where(member, 1.0, 0.0),
            jnp.where(line == spot0, 1.0, 0.0),
            jnp.where(line == spot1, 1.0, 0.0),
            jnp.zeros((16 - 2 * steps, rows), f32),
        ],
        axis=0,
    ).astype(bf16)
    count = jnp.sum(jnp.where(member, 1.0, 0.0), axis=1, keepdims=True)
    tile = spread(count, classes // 8)
    base = groups * classes
    for ref in (send_ref, keep_ref):
        ref[base : base + 8, :128] = tile
        if width > 128:
            ref[base : base + 8, 128:] = jnp.zeros((8, width - 128), f32)

    for i in range(n_ex):
        copies[i].wait()
        both = jnp.dot(left[...], feat_ref[:, columns[i]], preferred_element_type=f32)
        k = i % groups
        ref = send_ref if i < groups else keep_ref
        ref[k * classes : (k + 1) * classes, :] = both[:classes]
        held[:, columns[i]] = both[classes : classes + 8]


def pack_kernel(held, rows_ref, *, steps):
    half = held.shape[1] // 2
    used = steps * slots
    main = rows_ref.shape[2]
    core = lax.axis_index("ex") % 2
    for part, side in ((0, core), (1, 1 - core)):
        h = held[:, pl.ds(pl.multiple_of(side * half, half), half)]
        lines = [h[:used, :main]]
        for q in range(slots):
            lines.append(jnp.concatenate([h[q * steps + u : q * steps + u + 1, main:] for u in range(steps)], axis=1))
        rows_ref[part] = jnp.concatenate(lines, axis=0).astype(bf16)


def near_id(mask):
    return (lax.axis_index("ex") // 2 % 4) ^ (mask // 2)


def pair_kernel(keep_ref, got_ref, *code_refs, classes):
    far = code_refs[0].shape[0]
    base = 4 * far * classes
    tile = keep_ref[base : base + 8, :128] + got_ref[base : base + 8, :128]
    for mask, code_ref in zip(near_masks, code_refs):
        for j in range(far):
            at = pl.ds(pl.multiple_of((j * 4 + near_id(mask)) * classes, classes), classes)
            code_ref[j] = encode(keep_ref[at, :] + got_ref[at, :], tile)


def add_kernel(*refs, classes, last):
    code_ref = refs[-1]
    for j in range(code_ref.shape[0]):
        value, mark = decode(refs[0][j], classes)
        for ref in refs[1:-1]:
            more, more_mark = decode(ref[j], classes)
            value = value + more
            mark = mark + more_mark
        if last:
            code_ref[j] = encode(value / jnp.sqrt(column(mark, classes, classes // 8)))
        else:
            lane = lax.broadcasted_iota(jnp.int32, mark.shape, 1)
            code_ref[j] = encode(value, jnp.where(lane < classes // 8, 0.0, mark))


def diagonal(block):
    n = block.shape[0]
    eye = lax.broadcasted_iota(jnp.int32, (n, n), 0) == lax.broadcasted_iota(jnp.int32, (n, n), 1)
    return jnp.sum(jnp.where(eye, block, 0.0), axis=1, keepdims=True)


def factor_all(gram):
    order = len(gram)
    factor = [[None] * order for _ in range(order)]
    for j in range(order):
        value = gram[j][j]
        for k in range(j):
            value = value - factor[j][k] * factor[j][k]
        root = jnp.sqrt(value)
        factor[j][j] = 1.0 / root
        for i in range(j + 1, order):
            value = gram[i][j]
            for k in range(j):
                value = value - factor[i][k] * factor[j][k]
            factor[i][j] = value * factor[j][j]
    return factor


def solve_all(factor, right):
    order = len(right)
    forward = []
    for i in range(order):
        value = right[i]
        for j in range(i):
            value = value - factor[i][j] * forward[j]
        forward.append(value * factor[i][i])
    result = []
    for size in range(1, order + 1):
        back = [None] * size
        for i in reversed(range(size)):
            value = forward[i]
            for j in range(i + 1, size):
                value = value - factor[j][i] * back[j]
            back[i] = value * factor[i][i]
        result.append(back)
    return result


def select_kernel(pick_ref, one_ref, *, n_ex, rows, tail):
    steps, classes = pick_ref.shape
    lines = one_ref.shape[1]
    device = lax.axis_index("ex")
    pick = pick_ref[...]
    lane = lax.broadcasted_iota(jnp.int32, pick.shape, 1)
    owner = jnp.zeros_like(pick)
    rank = jnp.zeros_like(pick)
    for d in range(n_ex):
        here = (pick >= d * rows) & (pick < (d + 1) * rows)
        first = jnp.min(jnp.where(here, lane, classes), axis=1, keepdims=True)
        owner = jnp.where(here, d, owner)
        rank = jnp.where(here & (lane > first), 1, rank)
    away = owner ^ device
    bits = n_ex.bit_length() - 1
    far = jnp.zeros_like(pick)
    for b in range(3, bits):
        far = far + (((away >> b) & 1) << (bits - 1 - b))
    near = ((away >> 2) & 1) + 2 * ((away >> 1) & 1)
    spot = (2 * near + (away & 1)) * (n_ex // 8) + far
    step = lax.broadcasted_iota(jnp.int32, pick.shape, 0)
    line = lax.broadcasted_iota(jnp.int32, (lines, classes), 0)
    where = spot * 8 + (slots * steps + rank if tail else rank * steps + step)
    hits = [jnp.where(line == where[s : s + 1, :], 1.0, 0.0) for s in range(steps)]
    pad = jnp.zeros((lines, 128 - steps * classes), f32)
    one_ref[...] = jnp.transpose(jnp.concatenate(hits + [pad], axis=1))[: steps * classes].astype(bf16)


def picked_kernel(one_ref, rest_ref, *refs, steps):
    parts, (x_ref, rows_ref) = refs[:-2], refs[-2:]
    total, half = x_ref.shape
    classes = total // steps
    main = rows_ref.shape[1]
    tail = half - main
    at = 0
    for part in parts:
        rows_ref[at : at + part.shape[0], :] = part[...]
        at += part.shape[0]
    x_ref[:, :main] = jnp.dot(one_ref[...], rows_ref[...], preferred_element_type=f32).astype(bf16)
    for s in range(steps):
        at = slice(s * classes, (s + 1) * classes)
        rest = jnp.dot(rest_ref[at, :], rows_ref[:, s * tail : (s + 1) * tail], preferred_element_type=f32)
        x_ref[at, main:] = rest.astype(bf16)


def half_target(side, code_ref, x_ref, target_ref, target_at, left_ref, *, classes):
    half = left_ref.shape[1]
    far = code_ref.shape[0] // 4
    width = half // code_ref.shape[0]
    here = pl.ds(pl.multiple_of(side * half, half), half)
    for k in range(4 * far):
        block = k % far * 4 + near_id(near_masks[k // far])
        target = decode(code_ref[k], classes)[0]
        target_ref[:, pl.ds(pl.multiple_of(target_at + block * width, width), width)] = target
        left_ref[:classes, pl.ds(pl.multiple_of(block * width, width), width)] = target.astype(bf16)
    left_ref[classes:, :] = x_ref[...]
    return nt_dot(left_ref[...], x_ref[...]), here


def half_kernel(feat_ref, code_ref, x_ref, direct_ref, gram_ref, target_ref, left_ref, *, classes):
    core = lax.axis_index("ex") % 2
    gram_ref[...], here = half_target(core, code_ref, x_ref, target_ref, 0, left_ref, classes=classes)
    direct_ref[...] = nt_dot(left_ref[: direct_ref.shape[0], :], feat_ref[:, here])


def pursuit_kernel(
    labels_ref, feat_ref, x_own, x_twin, direct_own, gram_own, target_own, code_ref,
    scores_ref, resid_hbm, resid_ref, left_ref, sems, *, steps, scale
):
    classes, full = resid_ref.shape
    half = full // 2
    core = lax.axis_index("ex") % 2
    gram, other = half_target(1 - core, code_ref, x_twin, resid_ref, (1 - core) * half, left_ref, classes=classes)
    gram = gram + gram_own[...]
    blocks = [
        [
            diagonal(gram[(a + 1) * classes : (a + 2) * classes, b * classes : (b + 1) * classes])
            + (ridge if a == b else 0.0)
            for b in range(a + 1)
        ]
        for a in range(steps)
    ]
    rhs = [diagonal(gram[:classes, a * classes : (a + 1) * classes]) for a in range(steps)]
    weights = solve_all(factor_all(blocks), rhs)
    last = weights[steps - 1]
    copies = []
    span = half // 2
    for x_ref, side in ((x_own, core), (x_twin, 1 - core)):
        for q in range(2):
            there = slice(q * span, (q + 1) * span)
            here = pl.ds(pl.multiple_of(side * half + q * span, span), span)
            value = target_own[:, there] if x_ref is x_own else resid_ref[:, here]
            for k in range(steps):
                value = value - last[k] * x_ref[k * classes : (k + 1) * classes, there].astype(f32)
            resid_ref[:, here] = value
            copies.append(pltpu.make_async_copy(resid_ref.at[:, here], resid_hbm.at[:, here], sems.at[len(copies)]))
            copies[-1].start()

    direct = direct_own[...] + nt_dot(left_ref[: direct_own.shape[0], :], feat_ref[:, other])
    member = lax.broadcasted_iota(jnp.int32, (classes, direct.shape[1]), 0) == labels_ref[...].reshape(1, direct.shape[1])
    for s in range(steps):
        value = direct[:classes]
        for k in range(s):
            value = value - weights[s - 1][k] * direct[(k + 1) * classes : (k + 2) * classes]
        scores_ref[s : s + 1, :] = jnp.sum(jnp.where(member, value, 0.0), axis=0, keepdims=True) * scale
    for copy in copies:
        copy.wait()


def on_device(features, labels, pick_index, *, n_ex):
    rows, full = features.shape
    steps, classes = pick_index.shape
    groups = n_ex // 2
    width = full // n_ex
    total = steps * classes
    main = full // 2 * steps * slots // 8
    limit = pltpu.CompilerParams(vmem_limit_bytes=16 << 20)
    vmem = pl.BlockSpec(memory_space=pltpu.VMEM)
    hbm = pl.BlockSpec(memory_space=pltpu.HBM)
    anywhere = pl.BlockSpec(memory_space=pl.ANY)
    half = jax.ShapeDtypeStruct((groups * classes + 8, width), f32)
    code = jax.ShapeDtypeStruct((groups // 4, classes * (width // 128) + 8, 128), jnp.int16)

    def swap(x, mask):
        return lax.ppermute(x, "ex", [(d, d ^ mask) for d in range(n_ex)])

    def after(x, *others):
        return lax.optimization_barrier((x,) + others)[0]

    feat, send, keep, held = pl.pallas_call(
        functools.partial(sums_kernel, n_ex=n_ex),
        in_specs=[hbm] * 3,
        out_specs=[vmem] * 4,
        out_shape=[pltpu.VMEM((rows, full), bf16), half, half, jax.ShapeDtypeStruct((8, full), f32)],
        scratch_shapes=[
            pltpu.VMEM(labels.shape, jnp.int32),
            pltpu.VMEM(pick_index.shape, jnp.int32),
            pltpu.VMEM((classes + 16, rows), bf16),
            pltpu.SemaphoreType.DMA((n_ex + 2,)),
        ],
        compiler_params=limit,
        name="class_sums",
    )(*[pltpu.with_memory_space_constraint(a, pltpu.HBM) for a in (labels, pick_index, features)])

    def add(codes, last):
        return pl.pallas_call(
            functools.partial(add_kernel, classes=classes, last=last),
            in_specs=[vmem] * len(codes),
            out_specs=vmem,
            out_shape=code,
            compiler_params=limit,
            cost_estimate=pl.CostEstimate(flops=10**10, bytes_accessed=10**8, transcendentals=0) if last else None,
            name="add_sums",
        )(*codes)

    far_masks = [8 << b for b in range(n_ex.bit_length() - 4)]
    got = swap(send, 1)
    codes = pl.pallas_call(
        functools.partial(pair_kernel, classes=classes),
        in_specs=[vmem] * 2,
        out_specs=[vmem] * 4,
        out_shape=[code] * 4,
        compiler_params=limit,
        name="pair_sums",
    )(keep, got)
    packed = pl.pallas_call(
        functools.partial(pack_kernel, steps=steps),
        in_specs=[vmem],
        out_specs=vmem,
        out_shape=jax.ShapeDtypeStruct((2, 8, main), bf16),
        compiler_params=limit,
        name="pack_rows",
    )(held)
    for mask in reversed(far_masks):
        packed = jnp.concatenate([packed, swap(packed, mask)], axis=1)

    near_codes = [swap(c, m) for c, m in zip(codes[1:], near_masks[1:])]
    part_sum = add([codes[0], after(near_codes[0], packed)] + near_codes[1:], False)

    def select(tail, *others):
        return pl.pallas_call(
            functools.partial(select_kernel, n_ex=n_ex, rows=rows, tail=tail),
            in_specs=[vmem],
            out_specs=vmem,
            out_shape=jax.ShapeDtypeStruct((total, n_ex * 8), bf16),
            compiler_params=limit,
            name="select_tails" if tail else "select_rows",
        )(after(pick_index, *others))

    rest = select(True, codes[0])
    near_sum = after(part_sum, rest)
    more = swap(near_sum, far_masks[0])
    one = select(False, near_sum)
    part_sum = add([near_sum, more], len(far_masks) == 1)
    for mask in far_masks[1:]:
        part_sum = add([part_sum, swap(part_sum, mask)], mask == far_masks[-1])
    given = swap(after(packed[1], near_sum), 1)
    near = jnp.concatenate([after(packed[0], one), given], axis=0)
    by_z, by_y = swap(near, 4), swap(near, 2)
    own_parts = [part_sum] + [swap(part_sum, m) for m in near_masks[1:]]
    by_z, by_y = after(by_z, part_sum), after(by_y, part_sum)
    cut = near.shape[0] // 2
    parts = [near, by_z, by_y, swap(by_y[:cut], 4), swap(by_z[cut:], 2)]

    x = pl.pallas_call(
        functools.partial(picked_kernel, steps=steps),
        in_specs=[vmem] * 7,
        out_specs=vmem,
        out_shape=jax.ShapeDtypeStruct((total, full // 2), bf16),
        scratch_shapes=[pltpu.VMEM((n_ex * 8, main), bf16)],
        compiler_params=limit,
        name="picked_rows",
    )(one, rest, *parts)

    x_twin = swap(x, 1)
    own_half = jnp.concatenate(after(own_parts, x), axis=0)
    twin_half = swap(own_half, 1)
    left = pltpu.VMEM((total + classes, full // 2), bf16)
    direct, gram, target = pl.pallas_call(
        functools.partial(half_kernel, classes=classes),
        in_specs=[vmem] * 3,
        out_specs=[vmem] * 3,
        out_shape=[
            jax.ShapeDtypeStruct((total, rows), f32),
            jax.ShapeDtypeStruct((total + classes, total), f32),
            jax.ShapeDtypeStruct((classes, full // 2), f32),
        ],
        scratch_shapes=[left],
        compiler_params=limit,
        name="own_half_products",
    )(feat, own_half, x)

    scores, resid = pl.pallas_call(
        functools.partial(pursuit_kernel, steps=steps, scale=1.0 / math.sqrt(full)),
        in_specs=[vmem] * 8,
        out_specs=[vmem, anywhere],
        out_shape=[
            jax.ShapeDtypeStruct((steps, rows), f32),
            jax.ShapeDtypeStruct((classes, full), f32),
        ],
        scratch_shapes=[pltpu.VMEM((classes, full), f32), left, pltpu.SemaphoreType.DMA((4,))],
        compiler_params=limit,
        name="pursuit",
    )(labels, feat, x, x_twin, direct, gram, target, twin_half)
    return scores, resid


def solution(mesh):
    return jax.shard_map(
        functools.partial(on_device, n_ex=mesh.shape["ex"]),
        mesh=mesh,
        in_specs=(P(("grp", "ex"), None), P(("grp", "ex")), P("grp", None)),
        out_specs=(P(None, ("grp", "ex")), P("grp", None)),
        check_vma=False,
    )
```

```python
import functools
import math

import jax
import jax.numpy as jnp
from jax import lax
from jax.experimental import pallas as pl
from jax.experimental.pallas import tpu as pltpu
from jax.sharding import PartitionSpec as P

ridge = 1.0
slots = 2
f32 = jnp.float32
bf16 = jnp.bfloat16


def nt_dot(a, b):
    return lax.dot_general(a, b, (((1,), (1,)), ((), ())), preferred_element_type=f32)


def column(tile, height, start=0):
    return jnp.concatenate([tile[:, start + q : start + q + 1] for q in range(height // 8)], axis=0)


def spread(values, start=0):
    lane = lax.broadcasted_iota(jnp.int32, (8, 128), 1)
    tile = jnp.zeros((8, 128), f32)
    for q in range(values.shape[0] // 8):
        tile = jnp.where(lane == start + q, values[8 * q : 8 * q + 8], tile)
    return tile


def encode(x, count_tile=None):
    height, width = x.shape
    top = jnp.max(jnp.abs(x), axis=1, keepdims=True)
    power = jnp.ceil(jnp.log2(jnp.maximum(top, 1e-30)) + 0.01)
    whole_x = jnp.round(x * jnp.exp2(15.0 - power))
    mark = spread(power)
    if count_tile is not None:
        mark = mark + count_tile
    chunks = [whole_x[:, j * 128 : (j + 1) * 128] for j in range(width // 128)]
    return jnp.concatenate(chunks + [mark], axis=0).astype(jnp.int32).astype(jnp.int16)


def decode(code, height):
    value = code.astype(jnp.int32).astype(f32)
    count = value.shape[0] // height
    mark = value[count * height :]
    x = jnp.concatenate([value[j * height : (j + 1) * height] for j in range(count)], axis=1)
    return x * jnp.exp2(column(mark, height) - 15.0), mark


def sums_kernel(
    labels_hbm, pick_hbm, feat_hbm, feat_ref, send_ref, keep_ref, held, labels_ref, pick_ref, left, sems, *, n_ex
):
    rows, full = feat_ref.shape
    steps, classes = pick_ref.shape
    width = full // n_ex
    groups = n_ex // 2
    device = lax.axis_index("ex")
    core = device % 2
    small = [
        pltpu.make_async_copy(pick_hbm, pick_ref, sems.at[n_ex]),
        pltpu.make_async_copy(labels_hbm, labels_ref, sems.at[n_ex + 1]),
    ]
    for copy in small:
        copy.start()
    columns = []
    copies = []
    for i in range(n_ex):
        block = (1 - core) * groups + i if i < groups else core * groups + i - groups
        at = pl.ds(pl.multiple_of(block * width, width), width)
        columns.append(at)
        copies.append(pltpu.make_async_copy(feat_hbm.at[:, at], feat_ref.at[:, at], sems.at[i]))
        copies[-1].start()

    for copy in small:
        copy.wait()
    local = pick_ref[...] - device * rows
    mine = (local >= 0) & (local < rows)
    lane = lax.broadcasted_iota(jnp.int32, local.shape, 1)
    first = jnp.min(jnp.where(mine, lane, classes), axis=1, keepdims=True)
    last = jnp.max(jnp.where(mine, lane, -1), axis=1, keepdims=True)
    spot0 = jnp.max(jnp.where(mine & (lane == first), local, -1), axis=1, keepdims=True)
    spot1 = jnp.max(jnp.where(mine & (lane == last) & (last > first), local, -1), axis=1, keepdims=True)
    member = lax.broadcasted_iota(jnp.int32, (classes, rows), 0) == labels_ref[...].reshape(1, rows)
    line = lax.broadcasted_iota(jnp.int32, (steps, rows), 1)
    left[...] = jnp.concatenate(
        [
            jnp.where(member, 1.0, 0.0),
            jnp.where(line == spot0, 1.0, 0.0),
            jnp.where(line == spot1, 1.0, 0.0),
            jnp.zeros((16 - 2 * steps, rows), f32),
        ],
        axis=0,
    ).astype(bf16)
    count = jnp.sum(jnp.where(member, 1.0, 0.0), axis=1, keepdims=True)
    tile = spread(count, classes // 8)
    base = groups * classes
    for ref in (send_ref, keep_ref):
        ref[base : base + 8, :128] = tile
        if width > 128:
            ref[base : base + 8, 128:] = jnp.zeros((8, width - 128), f32)

    for i in range(n_ex):
        copies[i].wait()
        both = jnp.dot(left[...], feat_ref[:, columns[i]], preferred_element_type=f32)
        k = i % groups
        ref = send_ref if i < groups else keep_ref
        ref[k * classes : (k + 1) * classes, :] = both[:classes]
        held[:, columns[i]] = both[classes : classes + 8]


def pack_kernel(held, rows_ref, *, steps):
    half = held.shape[1] // 2
    used = steps * slots
    main = rows_ref.shape[2]
    core = lax.axis_index("ex") % 2
    for part, side in ((0, core), (1, 1 - core)):
        h = held[:, pl.ds(pl.multiple_of(side * half, half), half)]
        lines = [h[:used, :main]]
        for q in range(slots):
            lines.append(jnp.concatenate([h[q * steps + u : q * steps + u + 1, main:] for u in range(steps)], axis=1))
        rows_ref[part] = jnp.concatenate(lines, axis=0).astype(bf16)


def near_id(step, parity):
    first = 1 + parity
    flip = (step % 2) * first + (step // 2) * (3 - first)
    return (lax.axis_index("ex") // 2 % 4) ^ flip


def counts_of(mark, classes):
    lane = lax.broadcasted_iota(jnp.int32, mark.shape, 1)
    return jnp.where(lane < classes // 8, 0.0, mark)


def pair_kernel(keep_ref, got_ref, hold_ref, tile_ref, code_ref, *, classes):
    far = code_ref.shape[0] // 2
    base = 4 * far * classes
    tile = keep_ref[base : base + 8, :128] + got_ref[base : base + 8, :128]
    tile_ref[...] = tile
    core = lax.axis_index("ex") % 2
    for step in (1, 3, 0, 2):
        for j in range(far):
            block = j * 4 + near_id(step, core)
            at = pl.ds(pl.multiple_of(block * classes, classes), classes)
            value = keep_ref[at, :] + got_ref[at, :]
            if step % 2:
                code_ref[step // 2 * far + j] = encode(value, tile)
            else:
                hold_ref[step // 2 * far + j] = value


def halve_kernel(hold_ref, tile_ref, got_ref, rest_ref, count_ref, code_ref, *, classes):
    far = code_ref.shape[0]
    mark = decode(got_ref[0], classes)[1]
    tile = tile_ref[...] + counts_of(mark, classes)
    count_ref[...] = tile
    for j in range(far):
        code_ref[j] = encode(hold_ref[far + j] + decode(got_ref[far + j], classes)[0], tile)
        rest_ref[j] = hold_ref[j] + decode(got_ref[j], classes)[0]


def near_kernel(hold_ref, tile_ref, got_ref, code_ref, *, classes):
    for j in range(code_ref.shape[0]):
        value, mark = decode(got_ref[j], classes)
        code_ref[j] = encode(hold_ref[j] + value, tile_ref[...] + counts_of(mark, classes))


def add_kernel(*refs, classes, last):
    code_ref = refs[-1]
    for j in range(code_ref.shape[0]):
        value, mark = decode(refs[0][j], classes)
        for ref in refs[1:-1]:
            more, more_mark = decode(ref[j], classes)
            value = value + more
            mark = mark + more_mark
        if last:
            code_ref[j] = encode(value / jnp.sqrt(column(mark, classes, classes // 8)))
        else:
            code_ref[j] = encode(value, counts_of(mark, classes))


def diagonal(block):
    n = block.shape[0]
    eye = lax.broadcasted_iota(jnp.int32, (n, n), 0) == lax.broadcasted_iota(jnp.int32, (n, n), 1)
    return jnp.sum(jnp.where(eye, block, 0.0), axis=1, keepdims=True)


def factor_all(gram):
    order = len(gram)
    factor = [[None] * order for _ in range(order)]
    for j in range(order):
        value = gram[j][j]
        for k in range(j):
            value = value - factor[j][k] * factor[j][k]
        root = jnp.sqrt(value)
        factor[j][j] = 1.0 / root
        for i in range(j + 1, order):
            value = gram[i][j]
            for k in range(j):
                value = value - factor[i][k] * factor[j][k]
            factor[i][j] = value * factor[j][j]
    return factor


def solve_all(factor, right):
    order = len(right)
    forward = []
    for i in range(order):
        value = right[i]
        for j in range(i):
            value = value - factor[i][j] * forward[j]
        forward.append(value * factor[i][i])
    result = []
    for size in range(1, order + 1):
        back = [None] * size
        for i in reversed(range(size)):
            value = forward[i]
            for j in range(i + 1, size):
                value = value - factor[j][i] * back[j]
            back[i] = value * factor[i][i]
        result.append(back)
    return result


def select_kernel(pick_ref, one_ref, *, n_ex, rows, tail):
    steps, classes = pick_ref.shape
    lines = one_ref.shape[1]
    device = lax.axis_index("ex")
    pick = pick_ref[...]
    lane = lax.broadcasted_iota(jnp.int32, pick.shape, 1)
    owner = jnp.zeros_like(pick)
    rank = jnp.zeros_like(pick)
    for d in range(n_ex):
        here = (pick >= d * rows) & (pick < (d + 1) * rows)
        first = jnp.min(jnp.where(here, lane, classes), axis=1, keepdims=True)
        owner = jnp.where(here, d, owner)
        rank = jnp.where(here & (lane > first), 1, rank)
    away = owner ^ device
    bits = n_ex.bit_length() - 1
    far = jnp.zeros_like(pick)
    for b in range(3, bits):
        far = far + (((away >> b) & 1) << (bits - 1 - b))
    by_y, by_z = (away >> 1) & 1, (away >> 2) & 1
    near = jnp.where(device % 2 == 0, by_y + 2 * by_z, by_z + 2 * by_y)
    spot = (2 * near + (away & 1)) * (n_ex // 8) + far
    step = lax.broadcasted_iota(jnp.int32, pick.shape, 0)
    line = lax.broadcasted_iota(jnp.int32, (lines, classes), 0)
    where = spot * 8 + (slots * steps + rank if tail else rank * steps + step)
    hits = [jnp.where(line == where[s : s + 1, :], 1.0, 0.0) for s in range(steps)]
    pad = jnp.zeros((lines, 128 - steps * classes), f32)
    one_ref[...] = jnp.transpose(jnp.concatenate(hits + [pad], axis=1))[: steps * classes].astype(bf16)


def picked_kernel(one_ref, rest_ref, *refs, steps):
    parts, (x_ref, rows_ref) = refs[:-2], refs[-2:]
    total, half = x_ref.shape
    classes = total // steps
    main = rows_ref.shape[1]
    tail = half - main
    at = 0
    for part in parts:
        rows_ref[at : at + part.shape[0], :] = part[...]
        at += part.shape[0]
    x_ref[:, :main] = jnp.dot(one_ref[...], rows_ref[...], preferred_element_type=f32).astype(bf16)
    for s in range(steps):
        at = slice(s * classes, (s + 1) * classes)
        rest = jnp.dot(rest_ref[at, :], rows_ref[:, s * tail : (s + 1) * tail], preferred_element_type=f32)
        x_ref[at, main:] = rest.astype(bf16)


def half_target(side, code_ref, x_ref, target_ref, target_at, left_ref, *, classes):
    half = left_ref.shape[1]
    far = code_ref.shape[0] // 4
    width = half // code_ref.shape[0]
    here = pl.ds(pl.multiple_of(side * half, half), half)
    for k in range(4 * far):
        block = k % far * 4 + near_id(k // far, side)
        target = decode(code_ref[k], classes)[0]
        target_ref[:, pl.ds(pl.multiple_of(target_at + block * width, width), width)] = target
        left_ref[:classes, pl.ds(pl.multiple_of(block * width, width), width)] = target.astype(bf16)
    left_ref[classes:, :] = x_ref[...]
    return nt_dot(left_ref[...], x_ref[...]), here


def half_kernel(feat_ref, code_ref, x_ref, direct_ref, gram_ref, target_ref, left_ref, *, classes):
    core = lax.axis_index("ex") % 2
    gram_ref[...], here = half_target(core, code_ref, x_ref, target_ref, 0, left_ref, classes=classes)
    direct_ref[...] = nt_dot(left_ref[: direct_ref.shape[0], :], feat_ref[:, here])


def pursuit_kernel(
    labels_ref, feat_ref, x_own, x_twin, direct_own, gram_own, target_own, code_ref,
    scores_ref, resid_hbm, resid_ref, left_ref, sems, *, steps, scale
):
    classes, full = resid_ref.shape
    half = full // 2
    core = lax.axis_index("ex") % 2
    gram, other = half_target(1 - core, code_ref, x_twin, resid_ref, (1 - core) * half, left_ref, classes=classes)
    gram = gram + gram_own[...]
    blocks = [
        [
            diagonal(gram[(a + 1) * classes : (a + 2) * classes, b * classes : (b + 1) * classes])
            + (ridge if a == b else 0.0)
            for b in range(a + 1)
        ]
        for a in range(steps)
    ]
    rhs = [diagonal(gram[:classes, a * classes : (a + 1) * classes]) for a in range(steps)]
    weights = solve_all(factor_all(blocks), rhs)
    last = weights[steps - 1]
    copies = []
    span = half // 2
    for x_ref, side in ((x_own, core), (x_twin, 1 - core)):
        for q in range(2):
            there = slice(q * span, (q + 1) * span)
            here = pl.ds(pl.multiple_of(side * half + q * span, span), span)
            value = target_own[:, there] if x_ref is x_own else resid_ref[:, here]
            for k in range(steps):
                value = value - last[k] * x_ref[k * classes : (k + 1) * classes, there].astype(f32)
            resid_ref[:, here] = value
            copies.append(pltpu.make_async_copy(resid_ref.at[:, here], resid_hbm.at[:, here], sems.at[len(copies)]))
            copies[-1].start()

    direct = direct_own[...] + nt_dot(left_ref[: direct_own.shape[0], :], feat_ref[:, other])
    member = lax.broadcasted_iota(jnp.int32, (classes, direct.shape[1]), 0) == labels_ref[...].reshape(1, direct.shape[1])
    for s in range(steps):
        value = direct[:classes]
        for k in range(s):
            value = value - weights[s - 1][k] * direct[(k + 1) * classes : (k + 2) * classes]
        scores_ref[s : s + 1, :] = jnp.sum(jnp.where(member, value, 0.0), axis=0, keepdims=True) * scale
    for copy in copies:
        copy.wait()


def on_device(features, labels, pick_index, *, n_ex):
    rows, full = features.shape
    steps, classes = pick_index.shape
    groups = n_ex // 2
    width = full // n_ex
    total = steps * classes
    main = full // 2 * steps * slots // 8
    limit = pltpu.CompilerParams(vmem_limit_bytes=16 << 20)
    vmem = pl.BlockSpec(memory_space=pltpu.VMEM)
    hbm = pl.BlockSpec(memory_space=pltpu.HBM)
    anywhere = pl.BlockSpec(memory_space=pl.ANY)
    half = jax.ShapeDtypeStruct((groups * classes + 8, width), f32)
    code = jax.ShapeDtypeStruct((groups // 4, classes * (width // 128) + 8, 128), jnp.int16)

    def swap(x, mask):
        return lax.ppermute(x, "ex", [(d, d ^ mask) for d in range(n_ex)])

    def cross(x, first):
        masks = (2, 4) if first else (4, 2)
        return lax.ppermute(x, "ex", [(d, d ^ masks[d % 2]) for d in range(n_ex)])

    def after(x, *others):
        return lax.optimization_barrier((x,) + others)[0]

    feat, send, keep, held = pl.pallas_call(
        functools.partial(sums_kernel, n_ex=n_ex),
        in_specs=[hbm] * 3,
        out_specs=[vmem] * 4,
        out_shape=[pltpu.VMEM((rows, full), bf16), half, half, jax.ShapeDtypeStruct((8, full), f32)],
        scratch_shapes=[
            pltpu.VMEM(labels.shape, jnp.int32),
            pltpu.VMEM(pick_index.shape, jnp.int32),
            pltpu.VMEM((classes + 16, rows), bf16),
            pltpu.SemaphoreType.DMA((n_ex + 2,)),
        ],
        compiler_params=limit,
        name="class_sums",
    )(*[pltpu.with_memory_space_constraint(a, pltpu.HBM) for a in (labels, pick_index, features)])

    def add(codes, last):
        return pl.pallas_call(
            functools.partial(add_kernel, classes=classes, last=last),
            in_specs=[vmem] * len(codes),
            out_specs=vmem,
            out_shape=code,
            compiler_params=limit,
            cost_estimate=pl.CostEstimate(flops=10**10, bytes_accessed=10**8, transcendentals=0) if last else None,
            name="add_sums",
        )(*codes)

    far_masks = [8 << b for b in range(n_ex.bit_length() - 4)]
    got = swap(send, 1)
    far = groups // 4

    def call(kernel, name, outs, *args):
        return pl.pallas_call(
            functools.partial(kernel, classes=classes),
            in_specs=[vmem] * len(args),
            out_specs=[vmem] * len(outs),
            out_shape=outs,
            compiler_params=limit,
            name=name,
        )(*args)

    def held_sums(count):
        return [jax.ShapeDtypeStruct((count, classes, width), f32), jax.ShapeDtypeStruct((8, 128), f32)]

    two = jax.ShapeDtypeStruct((2 * far,) + code.shape[1:], jnp.int16)
    hold, tile, pair_code = call(pair_kernel, "pair_sums", held_sums(2 * far) + [two], keep, got)
    packed = pl.pallas_call(
        functools.partial(pack_kernel, steps=steps),
        in_specs=[vmem],
        out_specs=vmem,
        out_shape=jax.ShapeDtypeStruct((2, 8, main), bf16),
        compiler_params=limit,
        name="pack_rows",
    )(held)
    for mask in reversed(far_masks):
        packed = jnp.concatenate([packed, swap(packed, mask)], axis=1)

    got = cross(pair_code, True)
    hold, tile, half_code = call(halve_kernel, "half_sums", held_sums(far) + [code], hold, tile, got)
    got = cross(half_code, False)
    given = swap(after(packed[1], half_code), 1)
    (part_sum,) = call(near_kernel, "near_sums", [code], hold, tile, after(got, packed))

    def select(tail, *others):
        return pl.pallas_call(
            functools.partial(select_kernel, n_ex=n_ex, rows=rows, tail=tail),
            in_specs=[vmem],
            out_specs=vmem,
            out_shape=jax.ShapeDtypeStruct((total, n_ex * 8), bf16),
            compiler_params=limit,
            name="select_tails" if tail else "select_rows",
        )(after(pick_index, *others))

    rest = select(True, pair_code)
    near_sum = after(part_sum, rest, given)
    more = swap(near_sum, far_masks[0])
    one = select(False, near_sum)
    part_sum = add([near_sum, more], len(far_masks) == 1)
    for mask in far_masks[1:]:
        part_sum = add([part_sum, swap(part_sum, mask)], mask == far_masks[-1])
    near = jnp.concatenate([after(packed[0], one), given], axis=0)
    got = cross(part_sum, True)
    pair = jnp.concatenate([part_sum, got], axis=0)
    own_parts = [pair, cross(pair, False)]
    lines = jnp.concatenate([near, after(cross(near, True), got)], axis=0)
    parts = [lines, cross(lines, False)]

    x = pl.pallas_call(
        functools.partial(picked_kernel, steps=steps),
        in_specs=[vmem] * 4,
        out_specs=vmem,
        out_shape=jax.ShapeDtypeStruct((total, full // 2), bf16),
        scratch_shapes=[pltpu.VMEM((n_ex * 8, main), bf16)],
        compiler_params=limit,
        name="picked_rows",
    )(after(one, own_parts[1]), rest, *parts)

    x_twin = swap(x, 1)
    own_half = jnp.concatenate(own_parts, axis=0)
    twin_half = swap(own_half, 1)
    left = pltpu.VMEM((total + classes, full // 2), bf16)
    direct, gram, target = pl.pallas_call(
        functools.partial(half_kernel, classes=classes),
        in_specs=[vmem] * 3,
        out_specs=[vmem] * 3,
        out_shape=[
            jax.ShapeDtypeStruct((total, rows), f32),
            jax.ShapeDtypeStruct((total + classes, total), f32),
            jax.ShapeDtypeStruct((classes, full // 2), f32),
        ],
        scratch_shapes=[left],
        compiler_params=limit,
        name="own_half_products",
    )(feat, own_half, x)

    scores, resid = pl.pallas_call(
        functools.partial(pursuit_kernel, steps=steps, scale=1.0 / math.sqrt(full)),
        in_specs=[vmem] * 8,
        out_specs=[vmem, anywhere],
        out_shape=[
            jax.ShapeDtypeStruct((steps, rows), f32),
            jax.ShapeDtypeStruct((classes, full), f32),
        ],
        scratch_shapes=[pltpu.VMEM((classes, full), f32), left, pltpu.SemaphoreType.DMA((4,))],
        compiler_params=limit,
        name="pursuit",
    )(labels, feat, x, x_twin, direct, gram, target, twin_half)
    return scores, resid


def solution(mesh):
    return jax.shard_map(
        functools.partial(on_device, n_ex=mesh.shape["ex"]),
        mesh=mesh,
        in_specs=(P(("grp", "ex"), None), P(("grp", "ex")), P("grp", None)),
        out_specs=(P(None, ("grp", "ex")), P("grp", None)),
        check_vma=False,
    )
```

```python
import functools
import math

import jax
import jax.numpy as jnp
from jax import lax
from jax.experimental import pallas as pl
from jax.experimental.pallas import tpu as pltpu
from jax.sharding import PartitionSpec as P

ridge = 1.0
slots = 2
f32 = jnp.float32
bf16 = jnp.bfloat16


def nt_dot(a, b):
    return lax.dot_general(a, b, (((1,), (1,)), ((), ())), preferred_element_type=f32)


def column(tile, height, start=0):
    return jnp.concatenate([tile[:, start + q : start + q + 1] for q in range(height // 8)], axis=0)


def spread(values, start=0):
    lane = lax.broadcasted_iota(jnp.int32, (8, 128), 1)
    tile = jnp.zeros((8, 128), f32)
    for q in range(values.shape[0] // 8):
        tile = jnp.where(lane == start + q, values[8 * q : 8 * q + 8], tile)
    return tile


def encode(x, count_tile=None):
    height, width = x.shape
    top = jnp.max(jnp.abs(x), axis=1, keepdims=True)
    power = jnp.ceil(jnp.log2(jnp.maximum(top, 1e-30)) + 0.01)
    whole_x = jnp.round(x * jnp.exp2(15.0 - power))
    mark = spread(power)
    if count_tile is not None:
        mark = mark + count_tile
    chunks = [whole_x[:, j * 128 : (j + 1) * 128] for j in range(width // 128)]
    return jnp.concatenate(chunks + [mark], axis=0).astype(jnp.int32).astype(jnp.int16)


def decode(code, height):
    value = code.astype(jnp.int32).astype(f32)
    count = value.shape[0] // height
    mark = value[count * height :]
    x = jnp.concatenate([value[j * height : (j + 1) * height] for j in range(count)], axis=1)
    return x * jnp.exp2(column(mark, height) - 15.0), mark


def sums_kernel(
    labels_hbm, pick_hbm, feat_hbm, feat_ref, send_ref, keep_ref, labels_ref, pick_ref, left, sems, *, n_ex
):
    rows, full = feat_ref.shape
    steps, classes = pick_ref.shape
    width = full // n_ex
    groups = n_ex // 2
    device = lax.axis_index("ex")
    core = device % 2
    small = [
        pltpu.make_async_copy(pick_hbm, pick_ref, sems.at[n_ex]),
        pltpu.make_async_copy(labels_hbm, labels_ref, sems.at[n_ex + 1]),
    ]
    for copy in small:
        copy.start()
    columns = []
    copies = []
    for i in range(n_ex):
        block = (1 - core) * groups + i if i < groups else core * groups + i - groups
        at = pl.ds(pl.multiple_of(block * width, width), width)
        columns.append(at)
        copies.append(pltpu.make_async_copy(feat_hbm.at[:, at], feat_ref.at[:, at], sems.at[i]))
        copies[-1].start()

    for copy in small:
        copy.wait()
    local = pick_ref[...] - device * rows
    mine = (local >= 0) & (local < rows)
    lane = lax.broadcasted_iota(jnp.int32, local.shape, 1)
    first = jnp.min(jnp.where(mine, lane, classes), axis=1, keepdims=True)
    last = jnp.max(jnp.where(mine, lane, -1), axis=1, keepdims=True)
    spot0 = jnp.max(jnp.where(mine & (lane == first), local, -1), axis=1, keepdims=True)
    spot1 = jnp.max(jnp.where(mine & (lane == last) & (last > first), local, -1), axis=1, keepdims=True)
    member = lax.broadcasted_iota(jnp.int32, (classes, rows), 0) == labels_ref[...].reshape(1, rows)
    line = lax.broadcasted_iota(jnp.int32, (steps, rows), 1)
    left[...] = jnp.concatenate(
        [
            jnp.where(member, 1.0, 0.0),
            jnp.where(line == spot0, 1.0, 0.0),
            jnp.where(line == spot1, 1.0, 0.0),
            jnp.zeros((16 - 2 * steps, rows), f32),
        ],
        axis=0,
    ).astype(bf16)
    count = jnp.sum(jnp.where(member, 1.0, 0.0), axis=1, keepdims=True)
    tile = spread(count, classes // 8)
    base = groups * classes
    for ref in (send_ref, keep_ref):
        ref[base : base + 8, :128] = tile
        if width > 128:
            ref[base : base + 8, 128:] = jnp.zeros((8, width - 128), f32)

    for i in range(n_ex):
        copies[i].wait()
        both = jnp.dot(left[...], feat_ref[:, columns[i]], preferred_element_type=f32)
        k = i % groups
        ref = send_ref if i < groups else keep_ref
        ref[k * classes : (k + 1) * classes, :] = both[:classes]
        ref[base + 8 + 8 * k : base + 16 + 8 * k, :] = both[classes : classes + 8]


def pack_kernel(keep_ref, got_ref, rows_ref, *, steps, start):
    lines, main = rows_ref.shape
    used = steps * slots
    count = (keep_ref.shape[0] - start) // 8
    halves = []
    for ref in (keep_ref, got_ref):
        halves.append(jnp.concatenate([ref[start + 8 * k : start + 8 * k + 8, :] for k in range(count)], axis=1))
    out = [h[:used, :main] for h in halves]
    for h in halves:
        for q in range(slots):
            out.append(jnp.concatenate([h[q * steps + u : q * steps + u + 1, main:] for u in range(steps)], axis=1))
    rows_ref[...] = jnp.concatenate(out, axis=0).astype(bf16)


def near_id(step, parity):
    first = 1 + parity
    flip = (step % 2) * first + (step // 2) * (3 - first)
    return (lax.axis_index("ex") // 2 % 4) ^ flip


def counts_of(mark, classes):
    lane = lax.broadcasted_iota(jnp.int32, mark.shape, 1)
    return jnp.where(lane < classes // 8, 0.0, mark)


def pair_kernel(keep_ref, got_ref, hold_ref, tile_ref, code_ref, *, classes):
    far = code_ref.shape[0] // 2
    base = 4 * far * classes
    tile = keep_ref[base : base + 8, :128] + got_ref[base : base + 8, :128]
    tile_ref[...] = tile
    core = lax.axis_index("ex") % 2
    for step in (1, 3, 0, 2):
        for j in range(far):
            block = j * 4 + near_id(step, core)
            at = pl.ds(pl.multiple_of(block * classes, classes), classes)
            value = keep_ref[at, :] + got_ref[at, :]
            if step % 2:
                code_ref[step // 2 * far + j] = encode(value, tile)
            else:
                hold_ref[step // 2 * far + j] = value


def halve_kernel(hold_ref, tile_ref, got_ref, rest_ref, count_ref, code_ref, *, classes):
    far = code_ref.shape[0]
    mark = decode(got_ref[0], classes)[1]
    tile = tile_ref[...] + counts_of(mark, classes)
    count_ref[...] = tile
    for j in range(far):
        code_ref[j] = encode(hold_ref[far + j] + decode(got_ref[far + j], classes)[0], tile)
        rest_ref[j] = hold_ref[j] + decode(got_ref[j], classes)[0]


def near_kernel(hold_ref, tile_ref, got_ref, code_ref, *, classes):
    for j in range(code_ref.shape[0]):
        value, mark = decode(got_ref[j], classes)
        code_ref[j] = encode(hold_ref[j] + value, tile_ref[...] + counts_of(mark, classes))


def add_kernel(*refs, classes, last):
    code_ref = refs[-1]
    for j in range(code_ref.shape[0]):
        value, mark = decode(refs[0][j], classes)
        for ref in refs[1:-1]:
            more, more_mark = decode(ref[j], classes)
            value = value + more
            mark = mark + more_mark
        if last:
            code_ref[j] = encode(value / jnp.sqrt(column(mark, classes, classes // 8)))
        else:
            code_ref[j] = encode(value, counts_of(mark, classes))


def diagonal(block):
    n = block.shape[0]
    eye = lax.broadcasted_iota(jnp.int32, (n, n), 0) == lax.broadcasted_iota(jnp.int32, (n, n), 1)
    return jnp.sum(jnp.where(eye, block, 0.0), axis=1, keepdims=True)


def factor_all(gram):
    order = len(gram)
    factor = [[None] * order for _ in range(order)]
    for j in range(order):
        value = gram[j][j]
        for k in range(j):
            value = value - factor[j][k] * factor[j][k]
        root = jnp.sqrt(value)
        factor[j][j] = 1.0 / root
        for i in range(j + 1, order):
            value = gram[i][j]
            for k in range(j):
                value = value - factor[i][k] * factor[j][k]
            factor[i][j] = value * factor[j][j]
    return factor


def solve_all(factor, right):
    order = len(right)
    forward = []
    for i in range(order):
        value = right[i]
        for j in range(i):
            value = value - factor[i][j] * forward[j]
        forward.append(value * factor[i][i])
    result = []
    for size in range(1, order + 1):
        back = [None] * size
        for i in reversed(range(size)):
            value = forward[i]
            for j in range(i + 1, size):
                value = value - factor[j][i] * back[j]
            back[i] = value * factor[i][i]
        result.append(back)
    return result


def select_kernel(pick_ref, one_ref, *, n_ex, rows, tail):
    steps, classes = pick_ref.shape
    lines = one_ref.shape[1]
    device = lax.axis_index("ex")
    pick = pick_ref[...]
    lane = lax.broadcasted_iota(jnp.int32, pick.shape, 1)
    owner = jnp.zeros_like(pick)
    rank = jnp.zeros_like(pick)
    for d in range(n_ex):
        here = (pick >= d * rows) & (pick < (d + 1) * rows)
        first = jnp.min(jnp.where(here, lane, classes), axis=1, keepdims=True)
        owner = jnp.where(here, d, owner)
        rank = jnp.where(here & (lane > first), 1, rank)
    away = owner ^ device
    bits = n_ex.bit_length() - 1
    far = jnp.zeros_like(pick)
    for b in range(3, bits):
        far = far + (((away >> b) & 1) << (bits - 1 - b))
    by_y, by_z = (away >> 1) & 1, (away >> 2) & 1
    near = jnp.where(device % 2 == 0, by_y + 2 * by_z, by_z + 2 * by_y)
    others = n_ex // 8 - 1
    spot = jnp.where(far == 0, near, 3 + near * others + far)
    side = away & 1
    used = steps * slots
    step = lax.broadcasted_iota(jnp.int32, pick.shape, 0)
    line = lax.broadcasted_iota(jnp.int32, (lines, classes), 0)
    if tail:
        where = spot * 16 + 2 * used + side * slots + rank
    else:
        where = spot * 16 + side * used + rank * steps + step
    hits = [jnp.where(line == where[s : s + 1, :], 1.0, 0.0) for s in range(steps)]
    pad = jnp.zeros((lines, 128 - steps * classes), f32)
    one_ref[...] = jnp.transpose(jnp.concatenate(hits + [pad], axis=1))[: steps * classes].astype(bf16)


def picked_kernel(one_ref, rest_ref, *refs, steps):
    parts, (x_ref, rows_ref) = refs[:-2], refs[-2:]
    total, half = x_ref.shape
    classes = total // steps
    main = rows_ref.shape[1]
    tail = half - main
    at = 0
    for part in parts:
        rows_ref[at : at + part.shape[0], :] = part[...]
        at += part.shape[0]
    x_ref[:, :main] = jnp.dot(one_ref[...], rows_ref[...], preferred_element_type=f32).astype(bf16)
    for s in range(steps):
        at = slice(s * classes, (s + 1) * classes)
        rest = jnp.dot(rest_ref[at, :], rows_ref[:, s * tail : (s + 1) * tail], preferred_element_type=f32)
        x_ref[at, main:] = rest.astype(bf16)


def half_target(side, code_ref, x_ref, target_ref, target_at, left_ref, *, classes):
    half = left_ref.shape[1]
    far = code_ref.shape[0] // 4
    width = half // code_ref.shape[0]
    here = pl.ds(pl.multiple_of(side * half, half), half)
    for k in range(4 * far):
        block = k % far * 4 + near_id(k // far, side)
        target = decode(code_ref[k], classes)[0]
        target_ref[:, pl.ds(pl.multiple_of(target_at + block * width, width), width)] = target
        left_ref[:classes, pl.ds(pl.multiple_of(block * width, width), width)] = target.astype(bf16)
    left_ref[classes:, :] = x_ref[...]
    return nt_dot(left_ref[...], x_ref[...]), here


def half_kernel(feat_ref, code_ref, x_ref, direct_ref, gram_ref, target_ref, left_ref, *, classes):
    core = lax.axis_index("ex") % 2
    gram_ref[...], here = half_target(core, code_ref, x_ref, target_ref, 0, left_ref, classes=classes)
    direct_ref[...] = nt_dot(left_ref[: direct_ref.shape[0], :], feat_ref[:, here])


def pursuit_kernel(
    labels_ref, feat_ref, x_own, x_twin, direct_own, gram_own, target_own, code_ref,
    scores_ref, resid_hbm, resid_ref, left_ref, sems, *, steps, scale
):
    classes, full = resid_ref.shape
    half = full // 2
    core = lax.axis_index("ex") % 2
    gram, other = half_target(1 - core, code_ref, x_twin, resid_ref, (1 - core) * half, left_ref, classes=classes)
    gram = gram + gram_own[...]
    blocks = [
        [
            diagonal(gram[(a + 1) * classes : (a + 2) * classes, b * classes : (b + 1) * classes])
            + (ridge if a == b else 0.0)
            for b in range(a + 1)
        ]
        for a in range(steps)
    ]
    rhs = [diagonal(gram[:classes, a * classes : (a + 1) * classes]) for a in range(steps)]
    weights = solve_all(factor_all(blocks), rhs)
    last = weights[steps - 1]
    copies = []
    span = half // 2
    for x_ref, side in ((x_own, core), (x_twin, 1 - core)):
        for q in range(2):
            there = slice(q * span, (q + 1) * span)
            here = pl.ds(pl.multiple_of(side * half + q * span, span), span)
            value = target_own[:, there] if x_ref is x_own else resid_ref[:, here]
            for k in range(steps):
                value = value - last[k] * x_ref[k * classes : (k + 1) * classes, there].astype(f32)
            resid_ref[:, here] = value
            copies.append(pltpu.make_async_copy(resid_ref.at[:, here], resid_hbm.at[:, here], sems.at[len(copies)]))
            copies[-1].start()

    direct = direct_own[...] + nt_dot(left_ref[: direct_own.shape[0], :], feat_ref[:, other])
    member = lax.broadcasted_iota(jnp.int32, (classes, direct.shape[1]), 0) == labels_ref[...].reshape(1, direct.shape[1])
    for s in range(steps):
        value = direct[:classes]
        for k in range(s):
            value = value - weights[s - 1][k] * direct[(k + 1) * classes : (k + 2) * classes]
        scores_ref[s : s + 1, :] = jnp.sum(jnp.where(member, value, 0.0), axis=0, keepdims=True) * scale
    for copy in copies:
        copy.wait()


def on_device(features, labels, pick_index, *, n_ex):
    rows, full = features.shape
    steps, classes = pick_index.shape
    groups = n_ex // 2
    width = full // n_ex
    total = steps * classes
    main = full // 2 * steps * slots // 8
    limit = pltpu.CompilerParams(vmem_limit_bytes=16 << 20)
    vmem = pl.BlockSpec(memory_space=pltpu.VMEM)
    hbm = pl.BlockSpec(memory_space=pltpu.HBM)
    anywhere = pl.BlockSpec(memory_space=pl.ANY)
    half = jax.ShapeDtypeStruct((groups * (classes + 8) + 8, width), f32)
    code = jax.ShapeDtypeStruct((groups // 4, classes * (width // 128) + 8, 128), jnp.int16)

    def swap(x, mask):
        return lax.ppermute(x, "ex", [(d, d ^ mask) for d in range(n_ex)])

    def cross(x, first):
        masks = (2, 4) if first else (4, 2)
        return lax.ppermute(x, "ex", [(d, d ^ masks[d % 2]) for d in range(n_ex)])

    def after(x, *others):
        return lax.optimization_barrier((x,) + others)[0]

    feat, send, keep = pl.pallas_call(
        functools.partial(sums_kernel, n_ex=n_ex),
        in_specs=[hbm] * 3,
        out_specs=[vmem] * 3,
        out_shape=[pltpu.VMEM((rows, full), bf16), half, half],
        scratch_shapes=[
            pltpu.VMEM(labels.shape, jnp.int32),
            pltpu.VMEM(pick_index.shape, jnp.int32),
            pltpu.VMEM((classes + 16, rows), bf16),
            pltpu.SemaphoreType.DMA((n_ex + 2,)),
        ],
        compiler_params=limit,
        name="class_sums",
    )(*[pltpu.with_memory_space_constraint(a, pltpu.HBM) for a in (labels, pick_index, features)])

    def add(codes, last):
        return pl.pallas_call(
            functools.partial(add_kernel, classes=classes, last=last),
            in_specs=[vmem] * len(codes),
            out_specs=vmem,
            out_shape=code,
            compiler_params=limit,
            cost_estimate=pl.CostEstimate(flops=10**10, bytes_accessed=10**8, transcendentals=0) if last else None,
            name="add_sums",
        )(*codes)

    far_masks = [8 << b for b in range(n_ex.bit_length() - 4)]
    got = swap(send, 1)
    far = groups // 4

    weight = pl.CostEstimate(flops=10**10, bytes_accessed=10**8, transcendentals=0)

    def call(kernel, name, outs, *args):
        return pl.pallas_call(
            functools.partial(kernel, classes=classes),
            in_specs=[vmem] * len(args),
            out_specs=[vmem] * len(outs),
            out_shape=outs,
            compiler_params=limit,
            cost_estimate=weight,
            name=name,
        )(*args)

    def held_sums(count):
        return [jax.ShapeDtypeStruct((count, classes, width), f32), jax.ShapeDtypeStruct((8, 128), f32)]

    two = jax.ShapeDtypeStruct((2 * far,) + code.shape[1:], jnp.int16)
    hold, tile, pair_code = call(pair_kernel, "pair_sums", held_sums(2 * far) + [two], keep, got)
    here = pl.pallas_call(
        functools.partial(pack_kernel, steps=steps, start=groups * classes + 8),
        in_specs=[vmem] * 2,
        out_specs=vmem,
        out_shape=jax.ShapeDtypeStruct((16, main), bf16),
        compiler_params=limit,
        name="pack_rows",
    )(keep, after(got, pair_code))
    there = []
    for mask in reversed(far_masks):
        so_far = jnp.concatenate([here] + there, axis=0) if there else here
        there.append(swap(so_far, mask))

    got = cross(pair_code, True)
    hold, tile, half_code = call(halve_kernel, "half_sums", held_sums(far) + [code], hold, tile, got)
    here_next = cross(after(here, half_code), True)
    got = cross(half_code, False)
    (part_sum,) = call(near_kernel, "near_sums", [code], hold, tile, after(got, there))

    def select(tail, *others):
        return pl.pallas_call(
            functools.partial(select_kernel, n_ex=n_ex, rows=rows, tail=tail),
            in_specs=[vmem],
            out_specs=vmem,
            out_shape=jax.ShapeDtypeStruct((total, n_ex * 8), bf16),
            compiler_params=limit,
            name="select_tails" if tail else "select_rows",
        )(after(pick_index, *others))

    rest = select(True, pair_code)
    one = select(False, half_code)
    near_sum = after(part_sum, rest, one)
    more = swap(near_sum, far_masks[0])
    here_all = jnp.concatenate([after(here, near_sum), here_next], axis=0)
    here_far = cross(here_all, False)
    part_sum = add([near_sum, more], len(far_masks) == 1)
    for mask in far_masks[1:]:
        part_sum = add([part_sum, swap(part_sum, mask)], mask == far_masks[-1])
    there = after(jnp.concatenate(there, axis=0) if len(there) > 1 else there[0], more)
    got = cross(part_sum, True)
    pair = jnp.concatenate([part_sum, got], axis=0)
    own_parts = [pair, cross(pair, False)]
    there_all = jnp.concatenate([there, cross(there, True)], axis=0)
    parts = [here_all, here_far, there_all, cross(there_all, False)]

    x = pl.pallas_call(
        functools.partial(picked_kernel, steps=steps),
        in_specs=[vmem] * 6,
        out_specs=vmem,
        out_shape=jax.ShapeDtypeStruct((total, full // 2), bf16),
        scratch_shapes=[pltpu.VMEM((n_ex * 8, main), bf16)],
        compiler_params=limit,
        name="picked_rows",
    )(after(one, own_parts[1]), rest, *parts)

    x_twin = swap(x, 1)
    own_half = jnp.concatenate(own_parts, axis=0)
    twin_half = swap(own_half, 1)
    left = pltpu.VMEM((total + classes, full // 2), bf16)
    direct, gram, target = pl.pallas_call(
        functools.partial(half_kernel, classes=classes),
        in_specs=[vmem] * 3,
        out_specs=[vmem] * 3,
        out_shape=[
            jax.ShapeDtypeStruct((total, rows), f32),
            jax.ShapeDtypeStruct((total + classes, total), f32),
            jax.ShapeDtypeStruct((classes, full // 2), f32),
        ],
        scratch_shapes=[left],
        compiler_params=limit,
        name="own_half_products",
    )(feat, own_half, x)

    scores, resid = pl.pallas_call(
        functools.partial(pursuit_kernel, steps=steps, scale=1.0 / math.sqrt(full)),
        in_specs=[vmem] * 8,
        out_specs=[vmem, anywhere],
        out_shape=[
            jax.ShapeDtypeStruct((steps, rows), f32),
            jax.ShapeDtypeStruct((classes, full), f32),
        ],
        scratch_shapes=[pltpu.VMEM((classes, full), f32), left, pltpu.SemaphoreType.DMA((4,))],
        compiler_params=limit,
        name="pursuit",
    )(labels, feat, x, x_twin, direct, gram, target, twin_half)
    return scores, resid


def solution(mesh):
    return jax.shard_map(
        functools.partial(on_device, n_ex=mesh.shape["ex"]),
        mesh=mesh,
        in_specs=(P(("grp", "ex"), None), P(("grp", "ex")), P("grp", None)),
        out_specs=(P(None, ("grp", "ex")), P("grp", None)),
        check_vma=False,
    )
```

```python
import functools
import math

import jax
import jax.numpy as jnp
from jax import lax
from jax.experimental import pallas as pl
from jax.experimental.pallas import tpu as pltpu
from jax.sharding import PartitionSpec as P

ridge = 1.0
slots = 2
near_masks = (0, 4, 2, 6)
f32 = jnp.float32
bf16 = jnp.bfloat16


def nt_dot(a, b):
    return lax.dot_general(a, b, (((1,), (1,)), ((), ())), preferred_element_type=f32)


def column(tile, height, start=0):
    return jnp.concatenate([tile[:, start + q : start + q + 1] for q in range(height // 8)], axis=0)


def spread(values, start=0):
    lane = lax.broadcasted_iota(jnp.int32, (8, 128), 1)
    tile = jnp.zeros((8, 128), f32)
    for q in range(values.shape[0] // 8):
        tile = jnp.where(lane == start + q, values[8 * q : 8 * q + 8], tile)
    return tile


def encode(x, count_tile=None):
    height, width = x.shape
    top = jnp.max(jnp.abs(x), axis=1, keepdims=True)
    power = jnp.ceil(jnp.log2(jnp.maximum(top, 1e-30)) + 0.01)
    whole_x = jnp.round(x * jnp.exp2(15.0 - power))
    mark = spread(power)
    if count_tile is not None:
        mark = mark + count_tile
    chunks = [whole_x[:, j * 128 : (j + 1) * 128] for j in range(width // 128)]
    return jnp.concatenate(chunks + [mark], axis=0).astype(jnp.int32).astype(jnp.int16)


def decode(code, height):
    value = code.astype(jnp.int32).astype(f32)
    count = value.shape[0] // height
    mark = value[count * height :]
    x = jnp.concatenate([value[j * height : (j + 1) * height] for j in range(count)], axis=1)
    return x * jnp.exp2(column(mark, height) - 15.0), mark


def sums_kernel(
    labels_hbm, pick_hbm, feat_hbm, feat_ref, send_ref, keep_ref, held, labels_ref, pick_ref, left, sems, *, n_ex
):
    rows, full = feat_ref.shape
    steps, classes = pick_ref.shape
    width = full // n_ex
    groups = n_ex // 2
    device = lax.axis_index("ex")
    core = device % 2
    small = [
        pltpu.make_async_copy(pick_hbm, pick_ref, sems.at[n_ex]),
        pltpu.make_async_copy(labels_hbm, labels_ref, sems.at[n_ex + 1]),
    ]
    for copy in small:
        copy.start()
    columns = []
    copies = []
    for i in range(n_ex):
        block = (1 - core) * groups + i if i < groups else core * groups + i - groups
        at = pl.ds(pl.multiple_of(block * width, width), width)
        columns.append(at)
        copies.append(pltpu.make_async_copy(feat_hbm.at[:, at], feat_ref.at[:, at], sems.at[i]))
        copies[-1].start()

    for copy in small:
        copy.wait()
    local = pick_ref[...] - device * rows
    mine = (local >= 0) & (local < rows)
    lane = lax.broadcasted_iota(jnp.int32, local.shape, 1)
    first = jnp.min(jnp.where(mine, lane, classes), axis=1, keepdims=True)
    last = jnp.max(jnp.where(mine, lane, -1), axis=1, keepdims=True)
    spot0 = jnp.max(jnp.where(mine & (lane == first), local, -1), axis=1, keepdims=True)
    spot1 = jnp.max(jnp.where(mine & (lane == last) & (last > first), local, -1), axis=1, keepdims=True)
    member = lax.broadcasted_iota(jnp.int32, (classes, rows), 0) == labels_ref[...].reshape(1, rows)
    line = lax.broadcasted_iota(jnp.int32, (steps, rows), 1)
    left[...] = jnp.concatenate(
        [
            jnp.where(member, 1.0, 0.0),
            jnp.where(line == spot0, 1.0, 0.0),
            jnp.where(line == spot1, 1.0, 0.0),
            jnp.zeros((16 - 2 * steps, rows), f32),
        ],
        axis=0,
    ).astype(bf16)
    count = jnp.sum(jnp.where(member, 1.0, 0.0), axis=1, keepdims=True)
    tile = spread(count, classes // 8)
    base = groups * classes
    for ref in (send_ref, keep_ref):
        ref[base : base + 8, :128] = tile
        if width > 128:
            ref[base : base + 8, 128:] = jnp.zeros((8, width - 128), f32)

    for i in range(n_ex):
        copies[i].wait()
        both = jnp.dot(left[...], feat_ref[:, columns[i]], preferred_element_type=f32)
        k = i % groups
        ref = send_ref if i < groups else keep_ref
        ref[k * classes : (k + 1) * classes, :] = both[:classes]
        held[:, columns[i]] = both[classes : classes + 8]


def pack_kernel(held, rows_ref, *, steps):
    half = held.shape[1] // 2
    used = steps * slots
    main = rows_ref.shape[2]
    core = lax.axis_index("ex") % 2
    for part, side in ((0, core), (1, 1 - core)):
        h = held[:, pl.ds(pl.multiple_of(side * half, half), half)]
        lines = [h[:used, :main]]
        for q in range(slots):
            lines.append(jnp.concatenate([h[q * steps + u : q * steps + u + 1, main:] for u in range(steps)], axis=1))
        rows_ref[part] = jnp.concatenate(lines, axis=0).astype(bf16)


def near_id(mask):
    return (lax.axis_index("ex") // 2 % 4) ^ (mask // 2)


def pair_kernel(keep_ref, got_ref, *code_refs, classes):
    far = code_refs[0].shape[0]
    base = 4 * far * classes
    tile = keep_ref[base : base + 8, :128] + got_ref[base : base + 8, :128]
    for mask, code_ref in zip(near_masks, code_refs):
        for j in range(far):
            at = pl.ds(pl.multiple_of((j * 4 + near_id(mask)) * classes, classes), classes)
            code_ref[j] = encode(keep_ref[at, :] + got_ref[at, :], tile)


def add_kernel(*refs, classes, last):
    code_ref = refs[-1]
    for j in range(code_ref.shape[0]):
        value, mark = decode(refs[0][j], classes)
        for ref in refs[1:-1]:
            more, more_mark = decode(ref[j], classes)
            value = value + more
            mark = mark + more_mark
        if last:
            code_ref[j] = encode(value / jnp.sqrt(column(mark, classes, classes // 8)))
        else:
            lane = lax.broadcasted_iota(jnp.int32, mark.shape, 1)
            code_ref[j] = encode(value, jnp.where(lane < classes // 8, 0.0, mark))


def diagonal(block):
    n = block.shape[0]
    eye = lax.broadcasted_iota(jnp.int32, (n, n), 0) == lax.broadcasted_iota(jnp.int32, (n, n), 1)
    return jnp.sum(jnp.where(eye, block, 0.0), axis=1, keepdims=True)


def factor_all(gram):
    order = len(gram)
    factor = [[None] * order for _ in range(order)]
    for j in range(order):
        value = gram[j][j]
        for k in range(j):
            value = value - factor[j][k] * factor[j][k]
        root = jnp.sqrt(value)
        factor[j][j] = 1.0 / root
        for i in range(j + 1, order):
            value = gram[i][j]
            for k in range(j):
                value = value - factor[i][k] * factor[j][k]
            factor[i][j] = value * factor[j][j]
    return factor


def solve_all(factor, right):
    order = len(right)
    forward = []
    for i in range(order):
        value = right[i]
        for j in range(i):
            value = value - factor[i][j] * forward[j]
        forward.append(value * factor[i][i])
    result = []
    for size in range(1, order + 1):
        back = [None] * size
        for i in reversed(range(size)):
            value = forward[i]
            for j in range(i + 1, size):
                value = value - factor[j][i] * back[j]
            back[i] = value * factor[i][i]
        result.append(back)
    return result


def select_kernel(pick_ref, one_ref, *, n_ex, rows, tail):
    steps, classes = pick_ref.shape
    lines = one_ref.shape[1]
    device = lax.axis_index("ex")
    pick = pick_ref[...]
    lane = lax.broadcasted_iota(jnp.int32, pick.shape, 1)
    owner = jnp.zeros_like(pick)
    rank = jnp.zeros_like(pick)
    for d in range(n_ex):
        here = (pick >= d * rows) & (pick < (d + 1) * rows)
        first = jnp.min(jnp.where(here, lane, classes), axis=1, keepdims=True)
        owner = jnp.where(here, d, owner)
        rank = jnp.where(here & (lane > first), 1, rank)
    away = owner ^ device
    bits = n_ex.bit_length() - 1
    far = jnp.zeros_like(pick)
    for b in range(3, bits):
        far = far + (((away >> b) & 1) << (bits - 1 - b))
    near = ((away >> 2) & 1) + 2 * ((away >> 1) & 1)
    spot = (2 * near + (away & 1)) * (n_ex // 8) + far
    step = lax.broadcasted_iota(jnp.int32, pick.shape, 0)
    line = lax.broadcasted_iota(jnp.int32, (lines, classes), 0)
    where = spot * 8 + (slots * steps + rank if tail else rank * steps + step)
    hits = [jnp.where(line == where[s : s + 1, :], 1.0, 0.0) for s in range(steps)]
    pad = jnp.zeros((lines, 128 - steps * classes), f32)
    one_ref[...] = jnp.transpose(jnp.concatenate(hits + [pad], axis=1))[: steps * classes].astype(bf16)


def picked_kernel(one_ref, rest_ref, *refs, steps):
    parts, (x_ref, rows_ref) = refs[:-2], refs[-2:]
    total, half = x_ref.shape
    classes = total // steps
    main = rows_ref.shape[1]
    tail = half - main
    at = 0
    for part in parts:
        rows_ref[at : at + part.shape[0], :] = part[...]
        at += part.shape[0]
    x_ref[:, :main] = jnp.dot(one_ref[...], rows_ref[...], preferred_element_type=f32).astype(bf16)
    for s in range(steps):
        at = slice(s * classes, (s + 1) * classes)
        rest = jnp.dot(rest_ref[at, :], rows_ref[:, s * tail : (s + 1) * tail], preferred_element_type=f32)
        x_ref[at, main:] = rest.astype(bf16)


def half_target(side, code_ref, x_ref, target_ref, target_at, left_ref, *, classes):
    half = left_ref.shape[1]
    far = code_ref.shape[0] // 4
    width = half // code_ref.shape[0]
    here = pl.ds(pl.multiple_of(side * half, half), half)
    for k in range(4 * far):
        block = k % far * 4 + near_id(near_masks[k // far])
        target = decode(code_ref[k], classes)[0]
        target_ref[:, pl.ds(pl.multiple_of(target_at + block * width, width), width)] = target
        left_ref[:classes, pl.ds(pl.multiple_of(block * width, width), width)] = target.astype(bf16)
    left_ref[classes:, :] = x_ref[...]
    return nt_dot(left_ref[...], x_ref[...]), here


def half_kernel(feat_ref, code_ref, x_ref, direct_ref, gram_ref, target_ref, left_ref, *, classes):
    core = lax.axis_index("ex") % 2
    gram_ref[...], here = half_target(core, code_ref, x_ref, target_ref, 0, left_ref, classes=classes)
    direct_ref[...] = nt_dot(left_ref[: direct_ref.shape[0], :], feat_ref[:, here])


def pursuit_kernel(
    labels_ref, feat_ref, x_own, x_twin, direct_own, gram_own, target_own, code_ref,
    scores_ref, resid_hbm, resid_ref, left_ref, sems, *, steps, scale
):
    classes, full = resid_ref.shape
    half = full // 2
    core = lax.axis_index("ex") % 2
    gram, other = half_target(1 - core, code_ref, x_twin, resid_ref, (1 - core) * half, left_ref, classes=classes)
    gram = gram + gram_own[...]
    blocks = [
        [
            diagonal(gram[(a + 1) * classes : (a + 2) * classes, b * classes : (b + 1) * classes])
            + (ridge if a == b else 0.0)
            for b in range(a + 1)
        ]
        for a in range(steps)
    ]
    rhs = [diagonal(gram[:classes, a * classes : (a + 1) * classes]) for a in range(steps)]
    weights = solve_all(factor_all(blocks), rhs)
    last = weights[steps - 1]
    copies = []
    span = half // 2
    for x_ref, side in ((x_own, core), (x_twin, 1 - core)):
        for q in range(2):
            there = slice(q * span, (q + 1) * span)
            here = pl.ds(pl.multiple_of(side * half + q * span, span), span)
            value = target_own[:, there] if x_ref is x_own else resid_ref[:, here]
            for k in range(steps):
                value = value - last[k] * x_ref[k * classes : (k + 1) * classes, there].astype(f32)
            resid_ref[:, here] = value
            copies.append(pltpu.make_async_copy(resid_ref.at[:, here], resid_hbm.at[:, here], sems.at[len(copies)]))
            copies[-1].start()

    direct = direct_own[...] + nt_dot(left_ref[: direct_own.shape[0], :], feat_ref[:, other])
    member = lax.broadcasted_iota(jnp.int32, (classes, direct.shape[1]), 0) == labels_ref[...].reshape(1, direct.shape[1])
    for s in range(steps):
        value = direct[:classes]
        for k in range(s):
            value = value - weights[s - 1][k] * direct[(k + 1) * classes : (k + 2) * classes]
        scores_ref[s : s + 1, :] = jnp.sum(jnp.where(member, value, 0.0), axis=0, keepdims=True) * scale
    for copy in copies:
        copy.wait()


def on_device(features, labels, pick_index, *, n_ex):
    rows, full = features.shape
    steps, classes = pick_index.shape
    groups = n_ex // 2
    width = full // n_ex
    total = steps * classes
    main = full // 2 * steps * slots // 8
    limit = pltpu.CompilerParams(vmem_limit_bytes=16 << 20)
    vmem = pl.BlockSpec(memory_space=pltpu.VMEM)
    hbm = pl.BlockSpec(memory_space=pltpu.HBM)
    anywhere = pl.BlockSpec(memory_space=pl.ANY)
    half = jax.ShapeDtypeStruct((groups * classes + 8, width), f32)
    code = jax.ShapeDtypeStruct((groups // 4, classes * (width // 128) + 8, 128), jnp.int16)

    def near_swaps(x):
        diagonal_part, by_y = swap(x[3], 6), swap(x[2], 2)
        return [swap(x[1], 4), by_y, diagonal_part]

    def swap(x, mask):
        return lax.ppermute(x, "ex", [(d, d ^ mask) for d in range(n_ex)])

    def after(x, *others):
        return lax.optimization_barrier((x,) + others)[0]

    feat, send, keep, held = pl.pallas_call(
        functools.partial(sums_kernel, n_ex=n_ex),
        in_specs=[hbm] * 3,
        out_specs=[vmem] * 4,
        out_shape=[pltpu.VMEM((rows, full), bf16), half, half, jax.ShapeDtypeStruct((8, full), f32)],
        scratch_shapes=[
            pltpu.VMEM(labels.shape, jnp.int32),
            pltpu.VMEM(pick_index.shape, jnp.int32),
            pltpu.VMEM((classes + 16, rows), bf16),
            pltpu.SemaphoreType.DMA((n_ex + 2,)),
        ],
        compiler_params=limit,
        name="class_sums",
    )(*[pltpu.with_memory_space_constraint(a, pltpu.HBM) for a in (labels, pick_index, features)])

    def add(codes, last):
        return pl.pallas_call(
            functools.partial(add_kernel, classes=classes, last=last),
            in_specs=[vmem] * len(codes),
            out_specs=vmem,
            out_shape=code,
            compiler_params=limit,
            name="add_sums",
        )(*codes)

    far_masks = [8 << b for b in range(n_ex.bit_length() - 4)]
    got = swap(send, 1)
    codes = pl.pallas_call(
        functools.partial(pair_kernel, classes=classes),
        in_specs=[vmem] * 2,
        out_specs=[vmem] * 4,
        out_shape=[code] * 4,
        compiler_params=limit,
        name="pair_sums",
    )(keep, got)
    packed = pl.pallas_call(
        functools.partial(pack_kernel, steps=steps),
        in_specs=[vmem],
        out_specs=vmem,
        out_shape=jax.ShapeDtypeStruct((2, 8, main), bf16),
        compiler_params=limit,
        name="pack_rows",
    )(held)
    for mask in reversed(far_masks):
        packed = jnp.concatenate([packed, swap(packed, mask)], axis=1)

    near_codes = near_swaps(codes)
    part_sum = add([codes[0], after(near_codes[2], packed), near_codes[1], near_codes[0]], False)

    def select(tail, *others):
        return pl.pallas_call(
            functools.partial(select_kernel, n_ex=n_ex, rows=rows, tail=tail),
            in_specs=[vmem],
            out_specs=vmem,
            out_shape=jax.ShapeDtypeStruct((total, n_ex * 8), bf16),
            compiler_params=limit,
            name="select_tails" if tail else "select_rows",
        )(after(pick_index, *others))

    one = select(False, codes[0])
    rest = select(True, codes[0])
    given = swap(after(packed[1], part_sum), 1)
    part_sum = after(part_sum, one, rest)
    for mask in far_masks:
        more = swap(part_sum, mask)
        part_sum = add([part_sum, more], mask == far_masks[-1])
    near = jnp.concatenate([after(packed[0], more), given], axis=0)
    parts = [near] + near_swaps([near] * 4)
    own_parts = [part_sum] + near_swaps([None, after(part_sum, parts[1]), part_sum, part_sum])

    x = pl.pallas_call(
        functools.partial(picked_kernel, steps=steps),
        in_specs=[vmem] * 6,
        out_specs=vmem,
        out_shape=jax.ShapeDtypeStruct((total, full // 2), bf16),
        scratch_shapes=[pltpu.VMEM((n_ex * 8, main), bf16)],
        compiler_params=limit,
        name="picked_rows",
    )(one, rest, *parts)

    x_twin = swap(x, 1)
    own_half = jnp.concatenate(after(own_parts, x), axis=0)
    twin_half = swap(own_half, 1)
    left = pltpu.VMEM((total + classes, full // 2), bf16)
    direct, gram, target = pl.pallas_call(
        functools.partial(half_kernel, classes=classes),
        in_specs=[vmem] * 3,
        out_specs=[vmem] * 3,
        out_shape=[
            jax.ShapeDtypeStruct((total, rows), f32),
            jax.ShapeDtypeStruct((total + classes, total), f32),
            jax.ShapeDtypeStruct((classes, full // 2), f32),
        ],
        scratch_shapes=[left],
        compiler_params=limit,
        name="own_half_products",
    )(feat, own_half, x)

    scores, resid = pl.pallas_call(
        functools.partial(pursuit_kernel, steps=steps, scale=1.0 / math.sqrt(full)),
        in_specs=[vmem] * 8,
        out_specs=[vmem, anywhere],
        out_shape=[
            jax.ShapeDtypeStruct((steps, rows), f32),
            jax.ShapeDtypeStruct((classes, full), f32),
        ],
        scratch_shapes=[pltpu.VMEM((classes, full), f32), left, pltpu.SemaphoreType.DMA((4,))],
        compiler_params=limit,
        name="pursuit",
    )(labels, feat, x, x_twin, direct, gram, target, twin_half)
    return scores, resid


def solution(mesh):
    return jax.shard_map(
        functools.partial(on_device, n_ex=mesh.shape["ex"]),
        mesh=mesh,
        in_specs=(P(("grp", "ex"), None), P(("grp", "ex")), P("grp", None)),
        out_specs=(P(None, ("grp", "ex")), P("grp", None)),
        check_vma=False,
    )
```

```python
import functools
import math

import jax
import jax.numpy as jnp
from jax import lax
from jax.experimental import pallas as pl
from jax.experimental.pallas import tpu as pltpu
from jax.sharding import PartitionSpec as P

ridge = 1.0
slots = 2
f32 = jnp.float32
bf16 = jnp.bfloat16


def nt_dot(a, b):
    return lax.dot_general(a, b, (((1,), (1,)), ((), ())), preferred_element_type=f32)


def column(tile, height, start=0):
    return jnp.concatenate([tile[:, start + q : start + q + 1] for q in range(height // 8)], axis=0)


def spread(values, start=0):
    lane = lax.broadcasted_iota(jnp.int32, (8, 128), 1)
    tile = jnp.zeros((8, 128), f32)
    for q in range(values.shape[0] // 8):
        tile = jnp.where(lane == start + q, values[8 * q : 8 * q + 8], tile)
    return tile


def encode(x, count_tile=None):
    height, width = x.shape
    top = jnp.max(jnp.abs(x), axis=1, keepdims=True)
    power = jnp.ceil(jnp.log2(jnp.maximum(top, 1e-30)) + 0.01)
    whole_x = jnp.round(x * jnp.exp2(15.0 - power))
    mark = spread(power)
    if count_tile is not None:
        mark = mark + count_tile
    chunks = [whole_x[:, j * 128 : (j + 1) * 128] for j in range(width // 128)]
    return jnp.concatenate(chunks + [mark], axis=0).astype(jnp.int32).astype(jnp.int16)


def decode(code, height):
    value = code.astype(jnp.int32).astype(f32)
    count = value.shape[0] // height
    mark = value[count * height :]
    x = jnp.concatenate([value[j * height : (j + 1) * height] for j in range(count)], axis=1)
    return x * jnp.exp2(column(mark, height) - 15.0), mark


def sums_kernel(
    labels_hbm, pick_hbm, feat_hbm, feat_ref, send_ref, keep_ref, held, labels_ref, pick_ref, left, sems, *, n_ex
):
    rows, full = feat_ref.shape
    steps, classes = pick_ref.shape
    width = full // n_ex
    groups = n_ex // 2
    device = lax.axis_index("ex")
    core = device % 2
    small = [
        pltpu.make_async_copy(pick_hbm, pick_ref, sems.at[n_ex]),
        pltpu.make_async_copy(labels_hbm, labels_ref, sems.at[n_ex + 1]),
    ]
    for copy in small:
        copy.start()
    columns = []
    copies = []
    for i in range(n_ex):
        block = (1 - core) * groups + i if i < groups else core * groups + i - groups
        at = pl.ds(pl.multiple_of(block * width, width), width)
        columns.append(at)
        copies.append(pltpu.make_async_copy(feat_hbm.at[:, at], feat_ref.at[:, at], sems.at[i]))
        copies[-1].start()

    for copy in small:
        copy.wait()
    local = pick_ref[...] - device * rows
    mine = (local >= 0) & (local < rows)
    lane = lax.broadcasted_iota(jnp.int32, local.shape, 1)
    first = jnp.min(jnp.where(mine, lane, classes), axis=1, keepdims=True)
    last = jnp.max(jnp.where(mine, lane, -1), axis=1, keepdims=True)
    spot0 = jnp.max(jnp.where(mine & (lane == first), local, -1), axis=1, keepdims=True)
    spot1 = jnp.max(jnp.where(mine & (lane == last) & (last > first), local, -1), axis=1, keepdims=True)
    member = lax.broadcasted_iota(jnp.int32, (classes, rows), 0) == labels_ref[...].reshape(1, rows)
    line = lax.broadcasted_iota(jnp.int32, (steps, rows), 1)
    left[...] = jnp.concatenate(
        [
            jnp.where(member, 1.0, 0.0),
            jnp.where(line == spot0, 1.0, 0.0),
            jnp.where(line == spot1, 1.0, 0.0),
            jnp.zeros((16 - 2 * steps, rows), f32),
        ],
        axis=0,
    ).astype(bf16)
    count = jnp.sum(jnp.where(member, 1.0, 0.0), axis=1, keepdims=True)
    tile = spread(count, classes // 8)
    base = groups * classes
    for ref in (send_ref, keep_ref):
        ref[base : base + 8, :128] = tile
        if width > 128:
            ref[base : base + 8, 128:] = jnp.zeros((8, width - 128), f32)

    for i in range(n_ex):
        copies[i].wait()
        both = jnp.dot(left[...], feat_ref[:, columns[i]], preferred_element_type=f32)
        k = i % groups
        ref = send_ref if i < groups else keep_ref
        ref[k * classes : (k + 1) * classes, :] = both[:classes]
        held[:, columns[i]] = both[classes : classes + 8]


def pack_kernel(held, rows_ref, *, steps):
    half = held.shape[1] // 2
    used = steps * slots
    main = rows_ref.shape[2]
    core = lax.axis_index("ex") % 2
    for part, side in ((0, core), (1, 1 - core)):
        h = held[:, pl.ds(pl.multiple_of(side * half, half), half)]
        lines = [h[:used, :main]]
        for q in range(slots):
            lines.append(jnp.concatenate([h[q * steps + u : q * steps + u + 1, main:] for u in range(steps)], axis=1))
        rows_ref[part] = jnp.concatenate(lines, axis=0).astype(bf16)


def near_id(step, parity):
    first = 1 + parity
    flip = (step % 2) * first + (step // 2) * (3 - first)
    return (lax.axis_index("ex") // 2 % 4) ^ flip


def pair_kernel(keep_ref, got_ref, *code_refs, classes):
    far = code_refs[0].shape[0]
    base = 4 * far * classes
    tile = keep_ref[base : base + 8, :128] + got_ref[base : base + 8, :128]
    core = lax.axis_index("ex") % 2
    for step, code_ref in enumerate(code_refs):
        for j in range(far):
            at = pl.ds(pl.multiple_of((j * 4 + near_id(step, core)) * classes, classes), classes)
            code_ref[j] = encode(keep_ref[at, :] + got_ref[at, :], tile)


def add_kernel(*refs, classes, last):
    code_ref = refs[-1]
    for j in range(code_ref.shape[0]):
        value, mark = decode(refs[0][j], classes)
        for ref in refs[1:-1]:
            more, more_mark = decode(ref[j], classes)
            value = value + more
            mark = mark + more_mark
        if last:
            code_ref[j] = encode(value / jnp.sqrt(column(mark, classes, classes // 8)))
        else:
            lane = lax.broadcasted_iota(jnp.int32, mark.shape, 1)
            code_ref[j] = encode(value, jnp.where(lane < classes // 8, 0.0, mark))


def diagonal(block):
    n = block.shape[0]
    eye = lax.broadcasted_iota(jnp.int32, (n, n), 0) == lax.broadcasted_iota(jnp.int32, (n, n), 1)
    return jnp.sum(jnp.where(eye, block, 0.0), axis=1, keepdims=True)


def factor_all(gram):
    order = len(gram)
    factor = [[None] * order for _ in range(order)]
    for j in range(order):
        value = gram[j][j]
        for k in range(j):
            value = value - factor[j][k] * factor[j][k]
        root = jnp.sqrt(value)
        factor[j][j] = 1.0 / root
        for i in range(j + 1, order):
            value = gram[i][j]
            for k in range(j):
                value = value - factor[i][k] * factor[j][k]
            factor[i][j] = value * factor[j][j]
    return factor


def solve_all(factor, right):
    order = len(right)
    forward = []
    for i in range(order):
        value = right[i]
        for j in range(i):
            value = value - factor[i][j] * forward[j]
        forward.append(value * factor[i][i])
    result = []
    for size in range(1, order + 1):
        back = [None] * size
        for i in reversed(range(size)):
            value = forward[i]
            for j in range(i + 1, size):
                value = value - factor[j][i] * back[j]
            back[i] = value * factor[i][i]
        result.append(back)
    return result


def select_kernel(pick_ref, one_ref, *, n_ex, rows, tail):
    steps, classes = pick_ref.shape
    lines = one_ref.shape[1]
    device = lax.axis_index("ex")
    pick = pick_ref[...]
    lane = lax.broadcasted_iota(jnp.int32, pick.shape, 1)
    owner = jnp.zeros_like(pick)
    rank = jnp.zeros_like(pick)
    for d in range(n_ex):
        here = (pick >= d * rows) & (pick < (d + 1) * rows)
        first = jnp.min(jnp.where(here, lane, classes), axis=1, keepdims=True)
        owner = jnp.where(here, d, owner)
        rank = jnp.where(here & (lane > first), 1, rank)
    away = owner ^ device
    bits = n_ex.bit_length() - 1
    far = jnp.zeros_like(pick)
    for b in range(3, bits):
        far = far + (((away >> b) & 1) << (bits - 1 - b))
    by_y, by_z = (away >> 1) & 1, (away >> 2) & 1
    near = jnp.where(device % 2 == 0, by_y + 2 * by_z, by_z + 2 * by_y)
    spot = (2 * near + (away & 1)) * (n_ex // 8) + far
    step = lax.broadcasted_iota(jnp.int32, pick.shape, 0)
    line = lax.broadcasted_iota(jnp.int32, (lines, classes), 0)
    where = spot * 8 + (slots * steps + rank if tail else rank * steps + step)
    hits = [jnp.where(line == where[s : s + 1, :], 1.0, 0.0) for s in range(steps)]
    pad = jnp.zeros((lines, 128 - steps * classes), f32)
    one_ref[...] = jnp.transpose(jnp.concatenate(hits + [pad], axis=1))[: steps * classes].astype(bf16)


def picked_kernel(one_ref, rest_ref, *refs, steps):
    parts, (x_ref, rows_ref) = refs[:-2], refs[-2:]
    total, half = x_ref.shape
    classes = total // steps
    main = rows_ref.shape[1]
    tail = half - main
    at = 0
    for part in parts:
        rows_ref[at : at + part.shape[0], :] = part[...]
        at += part.shape[0]
    x_ref[:, :main] = jnp.dot(one_ref[...], rows_ref[...], preferred_element_type=f32).astype(bf16)
    for s in range(steps):
        at = slice(s * classes, (s + 1) * classes)
        rest = jnp.dot(rest_ref[at, :], rows_ref[:, s * tail : (s + 1) * tail], preferred_element_type=f32)
        x_ref[at, main:] = rest.astype(bf16)


def half_target(side, code_ref, x_ref, target_ref, target_at, left_ref, *, classes):
    half = left_ref.shape[1]
    far = code_ref.shape[0] // 4
    width = half // code_ref.shape[0]
    here = pl.ds(pl.multiple_of(side * half, half), half)
    for k in range(4 * far):
        block = k % far * 4 + near_id(k // far, side)
        target = decode(code_ref[k], classes)[0]
        target_ref[:, pl.ds(pl.multiple_of(target_at + block * width, width), width)] = target
        left_ref[:classes, pl.ds(pl.multiple_of(block * width, width), width)] = target.astype(bf16)
    left_ref[classes:, :] = x_ref[...]
    return nt_dot(left_ref[...], x_ref[...]), here


def half_kernel(feat_ref, code_ref, x_ref, direct_ref, gram_ref, target_ref, left_ref, *, classes):
    core = lax.axis_index("ex") % 2
    gram_ref[...], here = half_target(core, code_ref, x_ref, target_ref, 0, left_ref, classes=classes)
    direct_ref[...] = nt_dot(left_ref[: direct_ref.shape[0], :], feat_ref[:, here])


def pursuit_kernel(
    labels_ref, feat_ref, x_own, x_twin, direct_own, gram_own, target_own, code_ref,
    scores_ref, resid_hbm, resid_ref, left_ref, sems, *, steps, scale
):
    classes, full = resid_ref.shape
    half = full // 2
    core = lax.axis_index("ex") % 2
    gram, other = half_target(1 - core, code_ref, x_twin, resid_ref, (1 - core) * half, left_ref, classes=classes)
    gram = gram + gram_own[...]
    blocks = [
        [
            diagonal(gram[(a + 1) * classes : (a + 2) * classes, b * classes : (b + 1) * classes])
            + (ridge if a == b else 0.0)
            for b in range(a + 1)
        ]
        for a in range(steps)
    ]
    rhs = [diagonal(gram[:classes, a * classes : (a + 1) * classes]) for a in range(steps)]
    weights = solve_all(factor_all(blocks), rhs)
    last = weights[steps - 1]
    copies = []
    span = half // 2
    for x_ref, side in ((x_own, core), (x_twin, 1 - core)):
        for q in range(2):
            there = slice(q * span, (q + 1) * span)
            here = pl.ds(pl.multiple_of(side * half + q * span, span), span)
            value = target_own[:, there] if x_ref is x_own else resid_ref[:, here]
            for k in range(steps):
                value = value - last[k] * x_ref[k * classes : (k + 1) * classes, there].astype(f32)
            resid_ref[:, here] = value
            copies.append(pltpu.make_async_copy(resid_ref.at[:, here], resid_hbm.at[:, here], sems.at[len(copies)]))
            copies[-1].start()

    direct = direct_own[...] + nt_dot(left_ref[: direct_own.shape[0], :], feat_ref[:, other])
    member = lax.broadcasted_iota(jnp.int32, (classes, direct.shape[1]), 0) == labels_ref[...].reshape(1, direct.shape[1])
    for s in range(steps):
        value = direct[:classes]
        for k in range(s):
            value = value - weights[s - 1][k] * direct[(k + 1) * classes : (k + 2) * classes]
        scores_ref[s : s + 1, :] = jnp.sum(jnp.where(member, value, 0.0), axis=0, keepdims=True) * scale
    for copy in copies:
        copy.wait()


def on_device(features, labels, pick_index, *, n_ex):
    rows, full = features.shape
    steps, classes = pick_index.shape
    groups = n_ex // 2
    width = full // n_ex
    total = steps * classes
    main = full // 2 * steps * slots // 8
    limit = pltpu.CompilerParams(vmem_limit_bytes=16 << 20)
    vmem = pl.BlockSpec(memory_space=pltpu.VMEM)
    hbm = pl.BlockSpec(memory_space=pltpu.HBM)
    anywhere = pl.BlockSpec(memory_space=pl.ANY)
    half = jax.ShapeDtypeStruct((groups * classes + 8, width), f32)
    code = jax.ShapeDtypeStruct((groups // 4, classes * (width // 128) + 8, 128), jnp.int16)

    def near_swaps(x):
        diagonal_part, second = swap(x[3], 6), cross(x[2], False)
        return [cross(x[1], True), second, diagonal_part]

    def cross(x, first):
        masks = (2, 4) if first else (4, 2)
        return lax.ppermute(x, "ex", [(d, d ^ masks[d % 2]) for d in range(n_ex)])

    def swap(x, mask):
        return lax.ppermute(x, "ex", [(d, d ^ mask) for d in range(n_ex)])

    def after(x, *others):
        return lax.optimization_barrier((x,) + others)[0]

    feat, send, keep, held = pl.pallas_call(
        functools.partial(sums_kernel, n_ex=n_ex),
        in_specs=[hbm] * 3,
        out_specs=[vmem] * 4,
        out_shape=[pltpu.VMEM((rows, full), bf16), half, half, jax.ShapeDtypeStruct((8, full), f32)],
        scratch_shapes=[
            pltpu.VMEM(labels.shape, jnp.int32),
            pltpu.VMEM(pick_index.shape, jnp.int32),
            pltpu.VMEM((classes + 16, rows), bf16),
            pltpu.SemaphoreType.DMA((n_ex + 2,)),
        ],
        compiler_params=limit,
        name="class_sums",
    )(*[pltpu.with_memory_space_constraint(a, pltpu.HBM) for a in (labels, pick_index, features)])

    def add(codes, last):
        return pl.pallas_call(
            functools.partial(add_kernel, classes=classes, last=last),
            in_specs=[vmem] * len(codes),
            out_specs=vmem,
            out_shape=code,
            compiler_params=limit,
            name="add_sums",
        )(*codes)

    far_masks = [8 << b for b in range(n_ex.bit_length() - 4)]
    got = swap(send, 1)
    codes = pl.pallas_call(
        functools.partial(pair_kernel, classes=classes),
        in_specs=[vmem] * 2,
        out_specs=[vmem] * 4,
        out_shape=[code] * 4,
        compiler_params=limit,
        name="pair_sums",
    )(keep, got)
    packed = pl.pallas_call(
        functools.partial(pack_kernel, steps=steps),
        in_specs=[vmem],
        out_specs=vmem,
        out_shape=jax.ShapeDtypeStruct((2, 8, main), bf16),
        compiler_params=limit,
        name="pack_rows",
    )(held)
    for mask in reversed(far_masks):
        packed = jnp.concatenate([packed, swap(packed, mask)], axis=1)

    near_codes = near_swaps(codes)
    part_sum = add([codes[0], after(near_codes[2], packed), near_codes[1], near_codes[0]], False)

    def select(tail, *others):
        return pl.pallas_call(
            functools.partial(select_kernel, n_ex=n_ex, rows=rows, tail=tail),
            in_specs=[vmem],
            out_specs=vmem,
            out_shape=jax.ShapeDtypeStruct((total, n_ex * 8), bf16),
            compiler_params=limit,
            name="select_tails" if tail else "select_rows",
        )(after(pick_index, *others))

    one = select(False, codes[0])
    rest = select(True, codes[0])
    given = swap(after(packed[1], part_sum), 1)
    part_sum = after(part_sum, one, rest)
    for mask in far_masks:
        more = swap(part_sum, mask)
        part_sum = add([part_sum, more], mask == far_masks[-1])
    near = jnp.concatenate([after(packed[0], more), given], axis=0)
    parts = [near] + near_swaps([near] * 4)
    own_parts = [part_sum] + near_swaps([None, after(part_sum, parts[1]), part_sum, part_sum])

    x = pl.pallas_call(
        functools.partial(picked_kernel, steps=steps),
        in_specs=[vmem] * 6,
        out_specs=vmem,
        out_shape=jax.ShapeDtypeStruct((total, full // 2), bf16),
        scratch_shapes=[pltpu.VMEM((n_ex * 8, main), bf16)],
        compiler_params=limit,
        name="picked_rows",
    )(one, rest, *parts)

    x_twin = swap(x, 1)
    own_half = jnp.concatenate(after(own_parts, x), axis=0)
    twin_half = swap(own_half, 1)
    left = pltpu.VMEM((total + classes, full // 2), bf16)
    direct, gram, target = pl.pallas_call(
        functools.partial(half_kernel, classes=classes),
        in_specs=[vmem] * 3,
        out_specs=[vmem] * 3,
        out_shape=[
            jax.ShapeDtypeStruct((total, rows), f32),
            jax.ShapeDtypeStruct((total + classes, total), f32),
            jax.ShapeDtypeStruct((classes, full // 2), f32),
        ],
        scratch_shapes=[left],
        compiler_params=limit,
        name="own_half_products",
    )(feat, own_half, x)

    scores, resid = pl.pallas_call(
        functools.partial(pursuit_kernel, steps=steps, scale=1.0 / math.sqrt(full)),
        in_specs=[vmem] * 8,
        out_specs=[vmem, anywhere],
        out_shape=[
            jax.ShapeDtypeStruct((steps, rows), f32),
            jax.ShapeDtypeStruct((classes, full), f32),
        ],
        scratch_shapes=[pltpu.VMEM((classes, full), f32), left, pltpu.SemaphoreType.DMA((4,))],
        compiler_params=limit,
        name="pursuit",
    )(labels, feat, x, x_twin, direct, gram, target, twin_half)
    return scores, resid


def solution(mesh):
    return jax.shard_map(
        functools.partial(on_device, n_ex=mesh.shape["ex"]),
        mesh=mesh,
        in_specs=(P(("grp", "ex"), None), P(("grp", "ex")), P("grp", None)),
        out_specs=(P(None, ("grp", "ex")), P("grp", None)),
        check_vma=False,
    )
```

```python
import functools
import math

import jax
import jax.numpy as jnp
from jax import lax
from jax.experimental import pallas as pl
from jax.experimental.pallas import tpu as pltpu
from jax.sharding import PartitionSpec as P

ridge = 1.0
slots = 2
near_masks = (0, 4, 2, 6)
f32 = jnp.float32
bf16 = jnp.bfloat16


def nt_dot(a, b):
    return lax.dot_general(a, b, (((1,), (1,)), ((), ())), preferred_element_type=f32)


def column(tile, height, start=0):
    return jnp.concatenate([tile[:, start + q : start + q + 1] for q in range(height // 8)], axis=0)


def spread(values, start=0):
    lane = lax.broadcasted_iota(jnp.int32, (8, 128), 1)
    tile = jnp.zeros((8, 128), f32)
    for q in range(values.shape[0] // 8):
        tile = jnp.where(lane == start + q, values[8 * q : 8 * q + 8], tile)
    return tile


def encode(x, count_tile=None):
    height, width = x.shape
    top = jnp.max(jnp.abs(x), axis=1, keepdims=True)
    power = jnp.ceil(jnp.log2(jnp.maximum(top, 1e-30)) + 0.01)
    whole_x = jnp.round(x * jnp.exp2(15.0 - power))
    mark = spread(power)
    if count_tile is not None:
        mark = mark + count_tile
    chunks = [whole_x[:, j * 128 : (j + 1) * 128] for j in range(width // 128)]
    return jnp.concatenate(chunks + [mark], axis=0).astype(jnp.int32).astype(jnp.int16)


def decode(code, height):
    value = code.astype(jnp.int32).astype(f32)
    count = value.shape[0] // height
    mark = value[count * height :]
    x = jnp.concatenate([value[j * height : (j + 1) * height] for j in range(count)], axis=1)
    return x * jnp.exp2(column(mark, height) - 15.0), mark


def sums_kernel(
    labels_hbm, pick_hbm, feat_hbm, feat_ref, send_ref, keep_ref, held, labels_ref, pick_ref, left, sems, *, n_ex
):
    rows, full = feat_ref.shape
    steps, classes = pick_ref.shape
    width = full // n_ex
    groups = n_ex // 2
    device = lax.axis_index("ex")
    core = device % 2
    small = [
        pltpu.make_async_copy(pick_hbm, pick_ref, sems.at[n_ex]),
        pltpu.make_async_copy(labels_hbm, labels_ref, sems.at[n_ex + 1]),
    ]
    for copy in small:
        copy.start()
    columns = []
    copies = []
    for i in range(n_ex):
        block = (1 - core) * groups + i if i < groups else core * groups + i - groups
        at = pl.ds(pl.multiple_of(block * width, width), width)
        columns.append(at)
        copies.append(pltpu.make_async_copy(feat_hbm.at[:, at], feat_ref.at[:, at], sems.at[i]))
        copies[-1].start()

    for copy in small:
        copy.wait()
    local = pick_ref[...] - device * rows
    mine = (local >= 0) & (local < rows)
    lane = lax.broadcasted_iota(jnp.int32, local.shape, 1)
    first = jnp.min(jnp.where(mine, lane, classes), axis=1, keepdims=True)
    last = jnp.max(jnp.where(mine, lane, -1), axis=1, keepdims=True)
    spot0 = jnp.max(jnp.where(mine & (lane == first), local, -1), axis=1, keepdims=True)
    spot1 = jnp.max(jnp.where(mine & (lane == last) & (last > first), local, -1), axis=1, keepdims=True)
    member = lax.broadcasted_iota(jnp.int32, (classes, rows), 0) == labels_ref[...].reshape(1, rows)
    line = lax.broadcasted_iota(jnp.int32, (steps, rows), 1)
    left[...] = jnp.concatenate(
        [
            jnp.where(member, 1.0, 0.0),
            jnp.where(line == spot0, 1.0, 0.0),
            jnp.where(line == spot1, 1.0, 0.0),
            jnp.zeros((16 - 2 * steps, rows), f32),
        ],
        axis=0,
    ).astype(bf16)
    count = jnp.sum(jnp.where(member, 1.0, 0.0), axis=1, keepdims=True)
    tile = spread(count, classes // 8)
    base = groups * classes
    for ref in (send_ref, keep_ref):
        ref[base : base + 8, :128] = tile
        if width > 128:
            ref[base : base + 8, 128:] = jnp.zeros((8, width - 128), f32)

    for i in range(n_ex):
        copies[i].wait()
        both = jnp.dot(left[...], feat_ref[:, columns[i]], preferred_element_type=f32)
        k = i % groups
        ref = send_ref if i < groups else keep_ref
        ref[k * classes : (k + 1) * classes, :] = both[:classes]
        held[:, columns[i]] = both[classes : classes + 8]


def pack_kernel(held, rows_ref, *, steps):
    half = held.shape[1] // 2
    used = steps * slots
    main = rows_ref.shape[2]
    core = lax.axis_index("ex") % 2
    for part, side in ((0, core), (1, 1 - core)):
        h = held[:, pl.ds(pl.multiple_of(side * half, half), half)]
        lines = [h[:used, :main]]
        for q in range(slots):
            lines.append(jnp.concatenate([h[q * steps + u : q * steps + u + 1, main:] for u in range(steps)], axis=1))
        rows_ref[part] = jnp.concatenate(lines, axis=0).astype(bf16)


def near_id(mask):
    return (lax.axis_index("ex") // 2 % 4) ^ (mask // 2)


def pair_kernel(keep_ref, got_ref, *code_refs, classes):
    far = code_refs[0].shape[0]
    base = 4 * far * classes
    tile = keep_ref[base : base + 8, :128] + got_ref[base : base + 8, :128]
    for mask, code_ref in zip(near_masks, code_refs):
        for j in range(far):
            at = pl.ds(pl.multiple_of((j * 4 + near_id(mask)) * classes, classes), classes)
            code_ref[j] = encode(keep_ref[at, :] + got_ref[at, :], tile)


def add_kernel(*refs, classes, last):
    code_ref = refs[-1]
    for j in range(code_ref.shape[0]):
        value, mark = decode(refs[0][j], classes)
        for ref in refs[1:-1]:
            more, more_mark = decode(ref[j], classes)
            value = value + more
            mark = mark + more_mark
        if last:
            code_ref[j] = encode(value / jnp.sqrt(column(mark, classes, classes // 8)))
        else:
            lane = lax.broadcasted_iota(jnp.int32, mark.shape, 1)
            code_ref[j] = encode(value, jnp.where(lane < classes // 8, 0.0, mark))


def diagonal(block):
    n = block.shape[0]
    eye = lax.broadcasted_iota(jnp.int32, (n, n), 0) == lax.broadcasted_iota(jnp.int32, (n, n), 1)
    return jnp.sum(jnp.where(eye, block, 0.0), axis=1, keepdims=True)


def factor_all(gram):
    order = len(gram)
    factor = [[None] * order for _ in range(order)]
    for j in range(order):
        value = gram[j][j]
        for k in range(j):
            value = value - factor[j][k] * factor[j][k]
        root = jnp.sqrt(value)
        factor[j][j] = 1.0 / root
        for i in range(j + 1, order):
            value = gram[i][j]
            for k in range(j):
                value = value - factor[i][k] * factor[j][k]
            factor[i][j] = value * factor[j][j]
    return factor


def solve_all(factor, right):
    order = len(right)
    forward = []
    for i in range(order):
        value = right[i]
        for j in range(i):
            value = value - factor[i][j] * forward[j]
        forward.append(value * factor[i][i])
    result = []
    for size in range(1, order + 1):
        back = [None] * size
        for i in reversed(range(size)):
            value = forward[i]
            for j in range(i + 1, size):
                value = value - factor[j][i] * back[j]
            back[i] = value * factor[i][i]
        result.append(back)
    return result


def select_kernel(pick_ref, one_ref, *, n_ex, rows, tail):
    steps, classes = pick_ref.shape
    lines = one_ref.shape[1]
    device = lax.axis_index("ex")
    pick = pick_ref[...]
    lane = lax.broadcasted_iota(jnp.int32, pick.shape, 1)
    owner = jnp.zeros_like(pick)
    rank = jnp.zeros_like(pick)
    for d in range(n_ex):
        here = (pick >= d * rows) & (pick < (d + 1) * rows)
        first = jnp.min(jnp.where(here, lane, classes), axis=1, keepdims=True)
        owner = jnp.where(here, d, owner)
        rank = jnp.where(here & (lane > first), 1, rank)
    away = owner ^ device
    bits = n_ex.bit_length() - 1
    far = jnp.zeros_like(pick)
    for b in range(3, bits):
        far = far + (((away >> b) & 1) << (bits - 1 - b))
    near = ((away >> 2) & 1) + 2 * ((away >> 1) & 1)
    spot = (2 * near + (away & 1)) * (n_ex // 8) + far
    step = lax.broadcasted_iota(jnp.int32, pick.shape, 0)
    line = lax.broadcasted_iota(jnp.int32, (lines, classes), 0)
    where = spot * 8 + (slots * steps + rank if tail else rank * steps + step)
    hits = [jnp.where(line == where[s : s + 1, :], 1.0, 0.0) for s in range(steps)]
    pad = jnp.zeros((lines, 128 - steps * classes), f32)
    one_ref[...] = jnp.transpose(jnp.concatenate(hits + [pad], axis=1))[: steps * classes].astype(bf16)


def picked_kernel(one_ref, rest_ref, *refs, steps):
    parts, (x_ref, rows_ref) = refs[:-2], refs[-2:]
    total, half = x_ref.shape
    classes = total // steps
    main = rows_ref.shape[1]
    tail = half - main
    at = 0
    for part in parts:
        rows_ref[at : at + part.shape[0], :] = part[...]
        at += part.shape[0]
    x_ref[:, :main] = jnp.dot(one_ref[...], rows_ref[...], preferred_element_type=f32).astype(bf16)
    for s in range(steps):
        at = slice(s * classes, (s + 1) * classes)
        rest = jnp.dot(rest_ref[at, :], rows_ref[:, s * tail : (s + 1) * tail], preferred_element_type=f32)
        x_ref[at, main:] = rest.astype(bf16)


def prepare(j, side, code_ref, x_ref, target_ref, target_at, left_ref, *, classes):
    far = code_ref.shape[0] // 4
    width = left_ref.shape[1] // code_ref.shape[0]
    for k, mask in enumerate(near_masks):
        block = j * 4 + near_id(mask)
        target = decode(code_ref[k * far + j], classes)[0]
        target_ref[:, pl.ds(pl.multiple_of(target_at + block * width, width), width)] = target
        left_ref[:classes, pl.ds(pl.multiple_of(block * width, width), width)] = target.astype(bf16)
    cols = slice(j * 4 * width, (j + 1) * 4 * width)
    left_ref[classes:, cols] = x_ref[:, cols]
    return cols


def half_kernel(feat_ref, code_ref, x_ref, direct_ref, gram_ref, target_ref, left_ref, *, classes):
    core = lax.axis_index("ex") % 2
    half = left_ref.shape[1]
    far = code_ref.shape[0] // 4
    gram = direct = 0.0
    cols = prepare(0, core, code_ref, x_ref, target_ref, 0, left_ref, classes=classes)
    for j in range(far):
        now = cols
        if j + 1 < far:
            cols = prepare(j + 1, core, code_ref, x_ref, target_ref, 0, left_ref, classes=classes)
        span = half // far
        here = pl.ds(pl.multiple_of(core * half + j * span, span), span)
        direct = direct + nt_dot(left_ref[: direct_ref.shape[0], now], feat_ref[:, here])
        gram = gram + nt_dot(left_ref[:, now], x_ref[:, now])
    direct_ref[...] = direct
    gram_ref[...] = gram


def pursuit_kernel(
    labels_ref, feat_ref, x_own, x_twin, direct_own, gram_own, target_own, code_ref,
    scores_ref, resid_hbm, resid_ref, left_ref, sems, *, steps, scale
):
    classes, full = resid_ref.shape
    half = full // 2
    core = lax.axis_index("ex") % 2
    gram = gram_own[...]
    for j in range(code_ref.shape[0] // 4):
        cols = prepare(j, 1 - core, code_ref, x_twin, resid_ref, (1 - core) * half, left_ref, classes=classes)
        gram = gram + nt_dot(left_ref[:, cols], x_twin[:, cols])
    blocks = [
        [
            diagonal(gram[(a + 1) * classes : (a + 2) * classes, b * classes : (b + 1) * classes])
            + (ridge if a == b else 0.0)
            for b in range(a + 1)
        ]
        for a in range(steps)
    ]
    rhs = [diagonal(gram[:classes, a * classes : (a + 1) * classes]) for a in range(steps)]
    weights = solve_all(factor_all(blocks), rhs)
    last = weights[steps - 1]
    copies = []
    direct = direct_own[...]
    span = half // 2
    for x_ref, side in ((x_own, core), (x_twin, 1 - core)):
        for q in range(2):
            there = slice(q * span, (q + 1) * span)
            here = pl.ds(pl.multiple_of(side * half + q * span, span), span)
            value = target_own[:, there] if x_ref is x_own else resid_ref[:, here]
            for k in range(steps):
                value = value - last[k] * x_ref[k * classes : (k + 1) * classes, there].astype(f32)
            resid_ref[:, here] = value
            copies.append(pltpu.make_async_copy(resid_ref.at[:, here], resid_hbm.at[:, here], sems.at[len(copies)]))
            copies[-1].start()
            step = half // 4
            at = (len(copies) - 1) * step
            other = pl.ds(pl.multiple_of((1 - core) * half + at, step), step)
            direct = direct + nt_dot(left_ref[: direct.shape[0], at : at + step], feat_ref[:, other])

    member = lax.broadcasted_iota(jnp.int32, (classes, direct.shape[1]), 0) == labels_ref[...].reshape(1, direct.shape[1])
    for s in range(steps):
        value = direct[:classes]
        for k in range(s):
            value = value - weights[s - 1][k] * direct[(k + 1) * classes : (k + 2) * classes]
        scores_ref[s : s + 1, :] = jnp.sum(jnp.where(member, value, 0.0), axis=0, keepdims=True) * scale
    for copy in copies:
        copy.wait()


def on_device(features, labels, pick_index, *, n_ex):
    rows, full = features.shape
    steps, classes = pick_index.shape
    groups = n_ex // 2
    width = full // n_ex
    total = steps * classes
    main = full // 2 * steps * slots // 8
    limit = pltpu.CompilerParams(vmem_limit_bytes=16 << 20)
    vmem = pl.BlockSpec(memory_space=pltpu.VMEM)
    hbm = pl.BlockSpec(memory_space=pltpu.HBM)
    anywhere = pl.BlockSpec(memory_space=pl.ANY)
    half = jax.ShapeDtypeStruct((groups * classes + 8, width), f32)
    code = jax.ShapeDtypeStruct((groups // 4, classes * (width // 128) + 8, 128), jnp.int16)

    def swap(x, mask):
        return lax.ppermute(x, "ex", [(d, d ^ mask) for d in range(n_ex)])

    def after(x, *others):
        return lax.optimization_barrier((x,) + others)[0]

    feat, send, keep, held = pl.pallas_call(
        functools.partial(sums_kernel, n_ex=n_ex),
        in_specs=[hbm] * 3,
        out_specs=[vmem] * 4,
        out_shape=[pltpu.VMEM((rows, full), bf16), half, half, jax.ShapeDtypeStruct((8, full), f32)],
        scratch_shapes=[
            pltpu.VMEM(labels.shape, jnp.int32),
            pltpu.VMEM(pick_index.shape, jnp.int32),
            pltpu.VMEM((classes + 16, rows), bf16),
            pltpu.SemaphoreType.DMA((n_ex + 2,)),
        ],
        compiler_params=limit,
        name="class_sums",
    )(*[pltpu.with_memory_space_constraint(a, pltpu.HBM) for a in (labels, pick_index, features)])

    def add(codes, last):
        return pl.pallas_call(
            functools.partial(add_kernel, classes=classes, last=last),
            in_specs=[vmem] * len(codes),
            out_specs=vmem,
            out_shape=code,
            compiler_params=limit,
            name="add_sums",
        )(*codes)

    far_masks = [8 << b for b in range(n_ex.bit_length() - 4)]
    got = swap(send, 1)
    codes = pl.pallas_call(
        functools.partial(pair_kernel, classes=classes),
        in_specs=[vmem] * 2,
        out_specs=[vmem] * 4,
        out_shape=[code] * 4,
        compiler_params=limit,
        name="pair_sums",
    )(keep, got)
    packed = pl.pallas_call(
        functools.partial(pack_kernel, steps=steps),
        in_specs=[vmem],
        out_specs=vmem,
        out_shape=jax.ShapeDtypeStruct((2, 8, main), bf16),
        compiler_params=limit,
        name="pack_rows",
    )(held)
    for mask in reversed(far_masks):
        packed = jnp.concatenate([packed, swap(packed, mask)], axis=1)

    near_codes = [swap(c, m) for c, m in zip(codes[1:], near_masks[1:])]
    part_sum = add([codes[0], after(near_codes[0], packed)] + near_codes[1:], False)

    def select(tail, *others):
        return pl.pallas_call(
            functools.partial(select_kernel, n_ex=n_ex, rows=rows, tail=tail),
            in_specs=[vmem],
            out_specs=vmem,
            out_shape=jax.ShapeDtypeStruct((total, n_ex * 8), bf16),
            compiler_params=limit,
            name="select_tails" if tail else "select_rows",
        )(after(pick_index, *others))

    one = select(False, codes[0])
    rest = select(True, codes[0])
    given = swap(after(packed[1], part_sum), 1)
    part_sum = after(part_sum, one, rest)
    for mask in far_masks:
        more = swap(part_sum, mask)
        part_sum = add([part_sum, more], mask == far_masks[-1])
    near = jnp.concatenate([after(packed[0], more), given], axis=0)
    parts = [near] + [swap(near, m) for m in near_masks[1:]]
    own_parts = [part_sum] + [swap(part_sum, m) for m in near_masks[1:3]]
    own_parts.append(swap(after(part_sum, parts[1]), near_masks[3]))

    x = pl.pallas_call(
        functools.partial(picked_kernel, steps=steps),
        in_specs=[vmem] * 6,
        out_specs=vmem,
        out_shape=jax.ShapeDtypeStruct((total, full // 2), bf16),
        scratch_shapes=[pltpu.VMEM((n_ex * 8, main), bf16)],
        compiler_params=limit,
        name="picked_rows",
    )(one, rest, *parts)

    x_twin = swap(x, 1)
    own_half = jnp.concatenate(after(own_parts, x), axis=0)
    twin_half = swap(own_half, 1)
    left = pltpu.VMEM((total + classes, full // 2), bf16)
    direct, gram, target = pl.pallas_call(
        functools.partial(half_kernel, classes=classes),
        in_specs=[vmem] * 3,
        out_specs=[vmem] * 3,
        out_shape=[
            jax.ShapeDtypeStruct((total, rows), f32),
            jax.ShapeDtypeStruct((total + classes, total), f32),
            jax.ShapeDtypeStruct((classes, full // 2), f32),
        ],
        scratch_shapes=[left],
        compiler_params=limit,
        name="own_half_products",
    )(feat, own_half, x)

    scores, resid = pl.pallas_call(
        functools.partial(pursuit_kernel, steps=steps, scale=1.0 / math.sqrt(full)),
        in_specs=[vmem] * 8,
        out_specs=[vmem, anywhere],
        out_shape=[
            jax.ShapeDtypeStruct((steps, rows), f32),
            jax.ShapeDtypeStruct((classes, full), f32),
        ],
        scratch_shapes=[pltpu.VMEM((classes, full), f32), left, pltpu.SemaphoreType.DMA((4,))],
        compiler_params=limit,
        name="pursuit",
    )(labels, feat, x, x_twin, direct, gram, target, twin_half)
    return scores, resid


def solution(mesh):
    return jax.shard_map(
        functools.partial(on_device, n_ex=mesh.shape["ex"]),
        mesh=mesh,
        in_specs=(P(("grp", "ex"), None), P(("grp", "ex")), P("grp", None)),
        out_specs=(P(None, ("grp", "ex")), P("grp", None)),
        check_vma=False,
    )
```

```python
import functools
import math

import jax
import jax.numpy as jnp
from jax import lax
from jax.experimental import pallas as pl
from jax.experimental.pallas import tpu as pltpu
from jax.sharding import PartitionSpec as P

ridge = 1.0
slots = 2
near_masks = (0, 4, 2, 6)
f32 = jnp.float32
bf16 = jnp.bfloat16


def nt_dot(a, b):
    return lax.dot_general(a, b, (((1,), (1,)), ((), ())), preferred_element_type=f32)


def column(tile, height, start=0):
    return jnp.concatenate([tile[:, start + q : start + q + 1] for q in range(height // 8)], axis=0)


def spread(values, start=0):
    lane = lax.broadcasted_iota(jnp.int32, (8, 128), 1)
    tile = jnp.zeros((8, 128), f32)
    for q in range(values.shape[0] // 8):
        tile = jnp.where(lane == start + q, values[8 * q : 8 * q + 8], tile)
    return tile


def encode(x, count_tile=None):
    height, width = x.shape
    top = jnp.max(jnp.abs(x), axis=1, keepdims=True)
    power = jnp.ceil(jnp.log2(jnp.maximum(top, 1e-30)) + 0.01)
    whole_x = jnp.round(x * jnp.exp2(15.0 - power))
    mark = spread(power)
    if count_tile is not None:
        mark = mark + count_tile
    chunks = [whole_x[:, j * 128 : (j + 1) * 128] for j in range(width // 128)]
    return jnp.concatenate(chunks + [mark], axis=0).astype(jnp.int32).astype(jnp.int16)


def decode(code, height):
    value = code.astype(jnp.int32).astype(f32)
    count = value.shape[0] // height
    mark = value[count * height :]
    x = jnp.concatenate([value[j * height : (j + 1) * height] for j in range(count)], axis=1)
    return x * jnp.exp2(column(mark, height) - 15.0), mark


def sums_kernel(
    labels_hbm, pick_hbm, feat_hbm, feat_ref, send_ref, keep_ref, held, labels_ref, pick_ref, left, sems, *, n_ex
):
    rows, full = feat_ref.shape
    steps, classes = pick_ref.shape
    width = full // n_ex
    groups = n_ex // 2
    device = lax.axis_index("ex")
    core = device % 2
    small = [
        pltpu.make_async_copy(pick_hbm, pick_ref, sems.at[n_ex]),
        pltpu.make_async_copy(labels_hbm, labels_ref, sems.at[n_ex + 1]),
    ]
    for copy in small:
        copy.start()
    columns = []
    copies = []
    for i in range(n_ex):
        block = (1 - core) * groups + i if i < groups else core * groups + i - groups
        at = pl.ds(pl.multiple_of(block * width, width), width)
        columns.append(at)
        copies.append(pltpu.make_async_copy(feat_hbm.at[:, at], feat_ref.at[:, at], sems.at[i]))
        copies[-1].start()

    for copy in small:
        copy.wait()
    local = pick_ref[...] - device * rows
    mine = (local >= 0) & (local < rows)
    lane = lax.broadcasted_iota(jnp.int32, local.shape, 1)
    first = jnp.min(jnp.where(mine, lane, classes), axis=1, keepdims=True)
    last = jnp.max(jnp.where(mine, lane, -1), axis=1, keepdims=True)
    spot0 = jnp.max(jnp.where(mine & (lane == first), local, -1), axis=1, keepdims=True)
    spot1 = jnp.max(jnp.where(mine & (lane == last) & (last > first), local, -1), axis=1, keepdims=True)
    member = lax.broadcasted_iota(jnp.int32, (classes, rows), 0) == labels_ref[...].reshape(1, rows)
    line = lax.broadcasted_iota(jnp.int32, (steps, rows), 1)
    left[...] = jnp.concatenate(
        [
            jnp.where(member, 1.0, 0.0),
            jnp.where(line == spot0, 1.0, 0.0),
            jnp.where(line == spot1, 1.0, 0.0),
            jnp.zeros((16 - 2 * steps, rows), f32),
        ],
        axis=0,
    ).astype(bf16)
    count = jnp.sum(jnp.where(member, 1.0, 0.0), axis=1, keepdims=True)
    tile = spread(count, classes // 8)
    base = groups * classes
    for ref in (send_ref, keep_ref):
        ref[base : base + 8, :128] = tile
        if width > 128:
            ref[base : base + 8, 128:] = jnp.zeros((8, width - 128), f32)

    for i in range(n_ex):
        copies[i].wait()
        both = jnp.dot(left[...], feat_ref[:, columns[i]], preferred_element_type=f32)
        k = i % groups
        ref = send_ref if i < groups else keep_ref
        ref[k * classes : (k + 1) * classes, :] = both[:classes]
        held[:, columns[i]] = both[classes : classes + 8]


def pack_kernel(held, rows_ref, *, steps):
    half = held.shape[1] // 2
    used = steps * slots
    main = rows_ref.shape[2]
    core = lax.axis_index("ex") % 2
    for part, side in ((0, core), (1, 1 - core)):
        h = held[:, pl.ds(pl.multiple_of(side * half, half), half)]
        lines = [h[:used, :main]]
        for q in range(slots):
            lines.append(jnp.concatenate([h[q * steps + u : q * steps + u + 1, main:] for u in range(steps)], axis=1))
        rows_ref[part] = jnp.concatenate(lines, axis=0).astype(bf16)


def near_id(mask):
    return (lax.axis_index("ex") // 2 % 4) ^ (mask // 2)


def pair_kernel(keep_ref, got_ref, *code_refs, classes):
    far = code_refs[0].shape[0]
    base = 4 * far * classes
    tile = keep_ref[base : base + 8, :128] + got_ref[base : base + 8, :128]
    for mask, code_ref in zip(near_masks, code_refs):
        for j in range(far):
            at = pl.ds(pl.multiple_of((j * 4 + near_id(mask)) * classes, classes), classes)
            code_ref[j] = encode(keep_ref[at, :] + got_ref[at, :], tile)


def add_kernel(*refs, classes, last):
    code_ref = refs[-1]
    for j in range(code_ref.shape[0]):
        value, mark = decode(refs[0][j], classes)
        for ref in refs[1:-1]:
            more, more_mark = decode(ref[j], classes)
            value = value + more
            mark = mark + more_mark
        if last:
            code_ref[j] = encode(value / jnp.sqrt(column(mark, classes, classes // 8)))
        else:
            lane = lax.broadcasted_iota(jnp.int32, mark.shape, 1)
            code_ref[j] = encode(value, jnp.where(lane < classes // 8, 0.0, mark))


def diagonal(block):
    n = block.shape[0]
    eye = lax.broadcasted_iota(jnp.int32, (n, n), 0) == lax.broadcasted_iota(jnp.int32, (n, n), 1)
    return jnp.sum(jnp.where(eye, block, 0.0), axis=1, keepdims=True)


def factor_all(gram):
    order = len(gram)
    factor = [[None] * order for _ in range(order)]
    for j in range(order):
        value = gram[j][j]
        for k in range(j):
            value = value - factor[j][k] * factor[j][k]
        root = jnp.sqrt(value)
        factor[j][j] = 1.0 / root
        for i in range(j + 1, order):
            value = gram[i][j]
            for k in range(j):
                value = value - factor[i][k] * factor[j][k]
            factor[i][j] = value * factor[j][j]
    return factor


def solve_all(factor, right):
    order = len(right)
    forward = []
    for i in range(order):
        value = right[i]
        for j in range(i):
            value = value - factor[i][j] * forward[j]
        forward.append(value * factor[i][i])
    result = []
    for size in range(1, order + 1):
        back = [None] * size
        for i in reversed(range(size)):
            value = forward[i]
            for j in range(i + 1, size):
                value = value - factor[j][i] * back[j]
            back[i] = value * factor[i][i]
        result.append(back)
    return result


def select_kernel(pick_ref, one_ref, *, n_ex, rows, tail):
    steps, classes = pick_ref.shape
    lines = one_ref.shape[1]
    device = lax.axis_index("ex")
    pick = pick_ref[...]
    lane = lax.broadcasted_iota(jnp.int32, pick.shape, 1)
    owner = jnp.zeros_like(pick)
    rank = jnp.zeros_like(pick)
    for d in range(n_ex):
        here = (pick >= d * rows) & (pick < (d + 1) * rows)
        first = jnp.min(jnp.where(here, lane, classes), axis=1, keepdims=True)
        owner = jnp.where(here, d, owner)
        rank = jnp.where(here & (lane > first), 1, rank)
    away = owner ^ device
    bits = n_ex.bit_length() - 1
    far = jnp.zeros_like(pick)
    for b in range(3, bits):
        far = far + (((away >> b) & 1) << (bits - 1 - b))
    by_y, by_z = (away >> 1) & 1, (away >> 2) & 1
    near = 3 * by_z + 2 * by_y - 4 * by_z * by_y
    spot = (2 * near + (away & 1)) * (n_ex // 8) + far
    step = lax.broadcasted_iota(jnp.int32, pick.shape, 0)
    line = lax.broadcasted_iota(jnp.int32, (lines, classes), 0)
    where = spot * 8 + (slots * steps + rank if tail else rank * steps + step)
    hits = [jnp.where(line == where[s : s + 1, :], 1.0, 0.0) for s in range(steps)]
    pad = jnp.zeros((lines, 128 - steps * classes), f32)
    one_ref[...] = jnp.transpose(jnp.concatenate(hits + [pad], axis=1))[: steps * classes].astype(bf16)


def picked_kernel(one_ref, rest_ref, *refs, steps):
    parts, (x_ref, rows_ref) = refs[:-2], refs[-2:]
    total, half = x_ref.shape
    classes = total // steps
    main = rows_ref.shape[1]
    tail = half - main
    at = 0
    for part in parts:
        rows_ref[at : at + part.shape[0], :] = part[...]
        at += part.shape[0]
    x_ref[:, :main] = jnp.dot(one_ref[...], rows_ref[...], preferred_element_type=f32).astype(bf16)
    for s in range(steps):
        at = slice(s * classes, (s + 1) * classes)
        rest = jnp.dot(rest_ref[at, :], rows_ref[:, s * tail : (s + 1) * tail], preferred_element_type=f32)
        x_ref[at, main:] = rest.astype(bf16)


def half_target(side, code_ref, x_ref, target_ref, target_at, left_ref, *, classes):
    half = left_ref.shape[1]
    far = code_ref.shape[0] // 4
    width = half // code_ref.shape[0]
    here = pl.ds(pl.multiple_of(side * half, half), half)
    for k in range(4 * far):
        block = k % far * 4 + near_id(near_masks[k // far])
        target = decode(code_ref[k], classes)[0]
        target_ref[:, pl.ds(pl.multiple_of(target_at + block * width, width), width)] = target
        left_ref[:classes, pl.ds(pl.multiple_of(block * width, width), width)] = target.astype(bf16)
    left_ref[classes:, :] = x_ref[...]
    return nt_dot(left_ref[...], x_ref[...]), here


def half_kernel(feat_ref, code_ref, x_ref, direct_ref, gram_ref, target_ref, left_ref, *, classes):
    core = lax.axis_index("ex") % 2
    gram_ref[...], here = half_target(core, code_ref, x_ref, target_ref, 0, left_ref, classes=classes)
    direct_ref[...] = nt_dot(left_ref[: direct_ref.shape[0], :], feat_ref[:, here])


def pursuit_kernel(
    labels_ref, feat_ref, x_own, x_twin, direct_own, gram_own, target_own, code_ref,
    scores_ref, resid_hbm, resid_ref, left_ref, sems, *, steps, scale
):
    classes, full = resid_ref.shape
    half = full // 2
    core = lax.axis_index("ex") % 2
    gram, other = half_target(1 - core, code_ref, x_twin, resid_ref, (1 - core) * half, left_ref, classes=classes)
    gram = gram + gram_own[...]
    blocks = [
        [
            diagonal(gram[(a + 1) * classes : (a + 2) * classes, b * classes : (b + 1) * classes])
            + (ridge if a == b else 0.0)
            for b in range(a + 1)
        ]
        for a in range(steps)
    ]
    rhs = [diagonal(gram[:classes, a * classes : (a + 1) * classes]) for a in range(steps)]
    weights = solve_all(factor_all(blocks), rhs)
    last = weights[steps - 1]
    copies = []
    span = half // 2
    for x_ref, side in ((x_own, core), (x_twin, 1 - core)):
        for q in range(2):
            there = slice(q * span, (q + 1) * span)
            here = pl.ds(pl.multiple_of(side * half + q * span, span), span)
            value = target_own[:, there] if x_ref is x_own else resid_ref[:, here]
            for k in range(steps):
                value = value - last[k] * x_ref[k * classes : (k + 1) * classes, there].astype(f32)
            resid_ref[:, here] = value
            copies.append(pltpu.make_async_copy(resid_ref.at[:, here], resid_hbm.at[:, here], sems.at[len(copies)]))
            copies[-1].start()

    direct = direct_own[...] + nt_dot(left_ref[: direct_own.shape[0], :], feat_ref[:, other])
    member = lax.broadcasted_iota(jnp.int32, (classes, direct.shape[1]), 0) == labels_ref[...].reshape(1, direct.shape[1])
    for s in range(steps):
        value = direct[:classes]
        for k in range(s):
            value = value - weights[s - 1][k] * direct[(k + 1) * classes : (k + 2) * classes]
        scores_ref[s : s + 1, :] = jnp.sum(jnp.where(member, value, 0.0), axis=0, keepdims=True) * scale
    for copy in copies:
        copy.wait()


def on_device(features, labels, pick_index, *, n_ex):
    rows, full = features.shape
    steps, classes = pick_index.shape
    groups = n_ex // 2
    width = full // n_ex
    total = steps * classes
    main = full // 2 * steps * slots // 8
    limit = pltpu.CompilerParams(vmem_limit_bytes=16 << 20)
    vmem = pl.BlockSpec(memory_space=pltpu.VMEM)
    hbm = pl.BlockSpec(memory_space=pltpu.HBM)
    anywhere = pl.BlockSpec(memory_space=pl.ANY)
    half = jax.ShapeDtypeStruct((groups * classes + 8, width), f32)
    code = jax.ShapeDtypeStruct((groups // 4, classes * (width // 128) + 8, 128), jnp.int16)

    def near_swaps(x):
        diagonal_part, by_y = swap(x[3], 6), swap(x[2], 2)
        return [swap(x[1], 4), by_y, diagonal_part]

    def swap(x, mask):
        return lax.ppermute(x, "ex", [(d, d ^ mask) for d in range(n_ex)])

    def after(x, *others):
        return lax.optimization_barrier((x,) + others)[0]

    feat, send, keep, held = pl.pallas_call(
        functools.partial(sums_kernel, n_ex=n_ex),
        in_specs=[hbm] * 3,
        out_specs=[vmem] * 4,
        out_shape=[pltpu.VMEM((rows, full), bf16), half, half, jax.ShapeDtypeStruct((8, full), f32)],
        scratch_shapes=[
            pltpu.VMEM(labels.shape, jnp.int32),
            pltpu.VMEM(pick_index.shape, jnp.int32),
            pltpu.VMEM((classes + 16, rows), bf16),
            pltpu.SemaphoreType.DMA((n_ex + 2,)),
        ],
        compiler_params=limit,
        name="class_sums",
    )(*[pltpu.with_memory_space_constraint(a, pltpu.HBM) for a in (labels, pick_index, features)])

    def add(codes, last):
        return pl.pallas_call(
            functools.partial(add_kernel, classes=classes, last=last),
            in_specs=[vmem] * len(codes),
            out_specs=vmem,
            out_shape=code,
            compiler_params=limit,
            name="add_sums",
        )(*codes)

    far_masks = [8 << b for b in range(n_ex.bit_length() - 4)]
    got = swap(send, 1)
    codes = pl.pallas_call(
        functools.partial(pair_kernel, classes=classes),
        in_specs=[vmem] * 2,
        out_specs=[vmem] * 4,
        out_shape=[code] * 4,
        compiler_params=limit,
        name="pair_sums",
    )(keep, got)
    packed = pl.pallas_call(
        functools.partial(pack_kernel, steps=steps),
        in_specs=[vmem],
        out_specs=vmem,
        out_shape=jax.ShapeDtypeStruct((2, 8, main), bf16),
        compiler_params=limit,
        name="pack_rows",
    )(held)
    for mask in reversed(far_masks):
        packed = jnp.concatenate([packed, swap(packed, mask)], axis=1)

    near_codes = near_swaps(codes)
    part_sum = add([codes[0], after(near_codes[2], packed), near_codes[1], near_codes[0]], False)

    def select(tail, *others):
        return pl.pallas_call(
            functools.partial(select_kernel, n_ex=n_ex, rows=rows, tail=tail),
            in_specs=[vmem],
            out_specs=vmem,
            out_shape=jax.ShapeDtypeStruct((total, n_ex * 8), bf16),
            compiler_params=limit,
            name="select_tails" if tail else "select_rows",
        )(after(pick_index, *others))

    one = select(False, codes[0])
    rest = select(True, codes[0])
    given = swap(after(packed[1], part_sum), 1)
    part_sum = after(part_sum, one, rest)
    for mask in far_masks:
        more = swap(part_sum, mask)
        part_sum = add([part_sum, more], mask == far_masks[-1])
    near = jnp.concatenate([after(packed[0], more), given], axis=0)
    parts = [near] + near_swaps([near] * 4)
    own_parts = [part_sum] + near_swaps([None, after(part_sum, parts[3]), part_sum, part_sum])

    x = pl.pallas_call(
        functools.partial(picked_kernel, steps=steps),
        in_specs=[vmem] * 6,
        out_specs=vmem,
        out_shape=jax.ShapeDtypeStruct((total, full // 2), bf16),
        scratch_shapes=[pltpu.VMEM((n_ex * 8, main), bf16)],
        compiler_params=limit,
        name="picked_rows",
    )(one, rest, parts[0], *parts[:0:-1])

    x_twin = swap(x, 1)
    own_half = jnp.concatenate(after(own_parts, x), axis=0)
    twin_half = swap(own_half, 1)
    left = pltpu.VMEM((total + classes, full // 2), bf16)
    direct, gram, target = pl.pallas_call(
        functools.partial(half_kernel, classes=classes),
        in_specs=[vmem] * 3,
        out_specs=[vmem] * 3,
        out_shape=[
            jax.ShapeDtypeStruct((total, rows), f32),
            jax.ShapeDtypeStruct((total + classes, total), f32),
            jax.ShapeDtypeStruct((classes, full // 2), f32),
        ],
        scratch_shapes=[left],
        compiler_params=limit,
        name="own_half_products",
    )(feat, own_half, x)

    scores, resid = pl.pallas_call(
        functools.partial(pursuit_kernel, steps=steps, scale=1.0 / math.sqrt(full)),
        in_specs=[vmem] * 8,
        out_specs=[vmem, anywhere],
        out_shape=[
            jax.ShapeDtypeStruct((steps, rows), f32),
            jax.ShapeDtypeStruct((classes, full), f32),
        ],
        scratch_shapes=[pltpu.VMEM((classes, full), f32), left, pltpu.SemaphoreType.DMA((4,))],
        compiler_params=limit,
        name="pursuit",
    )(labels, feat, x, x_twin, direct, gram, target, twin_half)
    return scores, resid


def solution(mesh):
    return jax.shard_map(
        functools.partial(on_device, n_ex=mesh.shape["ex"]),
        mesh=mesh,
        in_specs=(P(("grp", "ex"), None), P(("grp", "ex")), P("grp", None)),
        out_specs=(P(None, ("grp", "ex")), P("grp", None)),
        check_vma=False,
    )
```

```python
import functools
import math

import jax
import jax.numpy as jnp
from jax import lax
from jax.experimental import pallas as pl
from jax.experimental.pallas import tpu as pltpu
from jax.sharding import PartitionSpec as P

ridge = 1.0
slots = 2
near_masks = (0, 4, 2, 6)
gather_masks = (0, 2, 4, 6)
f32 = jnp.float32
bf16 = jnp.bfloat16


def nt_dot(a, b):
    return lax.dot_general(a, b, (((1,), (1,)), ((), ())), preferred_element_type=f32)


def column(tile, height, start=0):
    return jnp.concatenate([tile[:, start + q : start + q + 1] for q in range(height // 8)], axis=0)


def spread(values, start=0):
    lane = lax.broadcasted_iota(jnp.int32, (8, 128), 1)
    tile = jnp.zeros((8, 128), f32)
    for q in range(values.shape[0] // 8):
        tile = jnp.where(lane == start + q, values[8 * q : 8 * q + 8], tile)
    return tile


def encode(x, count_tile=None):
    height, width = x.shape
    top = jnp.max(jnp.abs(x), axis=1, keepdims=True)
    power = jnp.ceil(jnp.log2(jnp.maximum(top, 1e-30)) + 0.01)
    whole_x = jnp.round(x * jnp.exp2(15.0 - power))
    mark = spread(power)
    if count_tile is not None:
        mark = mark + count_tile
    chunks = [whole_x[:, j * 128 : (j + 1) * 128] for j in range(width // 128)]
    return jnp.concatenate(chunks + [mark], axis=0).astype(jnp.int32).astype(jnp.int16)


def decode(code, height):
    value = code.astype(jnp.int32).astype(f32)
    count = value.shape[0] // height
    mark = value[count * height :]
    x = jnp.concatenate([value[j * height : (j + 1) * height] for j in range(count)], axis=1)
    return x * jnp.exp2(column(mark, height) - 15.0), mark


def sums_kernel(
    labels_hbm, pick_hbm, feat_hbm, feat_ref, send_ref, keep_ref, held, labels_ref, pick_ref, left, sems, *, n_ex
):
    rows, full = feat_ref.shape
    steps, classes = pick_ref.shape
    width = full // n_ex
    groups = n_ex // 2
    device = lax.axis_index("ex")
    core = device % 2
    small = [
        pltpu.make_async_copy(pick_hbm, pick_ref, sems.at[n_ex]),
        pltpu.make_async_copy(labels_hbm, labels_ref, sems.at[n_ex + 1]),
    ]
    for copy in small:
        copy.start()
    columns = []
    copies = []
    for i in range(n_ex):
        block = (1 - core) * groups + i if i < groups else core * groups + i - groups
        at = pl.ds(pl.multiple_of(block * width, width), width)
        columns.append(at)
        copies.append(pltpu.make_async_copy(feat_hbm.at[:, at], feat_ref.at[:, at], sems.at[i]))
        copies[-1].start()

    for copy in small:
        copy.wait()
    local = pick_ref[...] - device * rows
    mine = (local >= 0) & (local < rows)
    lane = lax.broadcasted_iota(jnp.int32, local.shape, 1)
    first = jnp.min(jnp.where(mine, lane, classes), axis=1, keepdims=True)
    last = jnp.max(jnp.where(mine, lane, -1), axis=1, keepdims=True)
    spot0 = jnp.max(jnp.where(mine & (lane == first), local, -1), axis=1, keepdims=True)
    spot1 = jnp.max(jnp.where(mine & (lane == last) & (last > first), local, -1), axis=1, keepdims=True)
    member = lax.broadcasted_iota(jnp.int32, (classes, rows), 0) == labels_ref[...].reshape(1, rows)
    line = lax.broadcasted_iota(jnp.int32, (steps, rows), 1)
    left[...] = jnp.concatenate(
        [
            jnp.where(member, 1.0, 0.0),
            jnp.where(line == spot0, 1.0, 0.0),
            jnp.where(line == spot1, 1.0, 0.0),
            jnp.zeros((16 - 2 * steps, rows), f32),
        ],
        axis=0,
    ).astype(bf16)
    count = jnp.sum(jnp.where(member, 1.0, 0.0), axis=1, keepdims=True)
    tile = spread(count, classes // 8)
    base = groups * classes
    for ref in (send_ref, keep_ref):
        ref[base : base + 8, :128] = tile
        if width > 128:
            ref[base : base + 8, 128:] = jnp.zeros((8, width - 128), f32)

    for i in range(n_ex):
        copies[i].wait()
        both = jnp.dot(left[...], feat_ref[:, columns[i]], preferred_element_type=f32)
        k = i % groups
        ref = send_ref if i < groups else keep_ref
        ref[k * classes : (k + 1) * classes, :] = both[:classes]
        held[:, columns[i]] = both[classes : classes + 8]


def pack_kernel(held, rows_ref, *, steps):
    half = held.shape[1] // 2
    used = steps * slots
    main = rows_ref.shape[2]
    core = lax.axis_index("ex") % 2
    for part, side in ((0, core), (1, 1 - core)):
        h = held[:, pl.ds(pl.multiple_of(side * half, half), half)]
        lines = [h[:used, :main]]
        for q in range(slots):
            lines.append(jnp.concatenate([h[q * steps + u : q * steps + u + 1, main:] for u in range(steps)], axis=1))
        rows_ref[part] = jnp.concatenate(lines, axis=0).astype(bf16)


def near_id(mask):
    return (lax.axis_index("ex") // 2 % 4) ^ (mask // 2)


def pair_kernel(keep_ref, got_ref, *code_refs, classes):
    far = code_refs[0].shape[0]
    base = 4 * far * classes
    tile = keep_ref[base : base + 8, :128] + got_ref[base : base + 8, :128]
    for mask, code_ref in zip(near_masks, code_refs):
        for j in range(far):
            at = pl.ds(pl.multiple_of((j * 4 + near_id(mask)) * classes, classes), classes)
            code_ref[j] = encode(keep_ref[at, :] + got_ref[at, :], tile)


def add_kernel(*refs, classes, last):
    code_ref = refs[-1]
    for j in range(code_ref.shape[0]):
        value, mark = decode(refs[0][j], classes)
        for ref in refs[1:-1]:
            more, more_mark = decode(ref[j], classes)
            value = value + more
            mark = mark + more_mark
        if last:
            code_ref[j] = encode(value / jnp.sqrt(column(mark, classes, classes // 8)))
        else:
            lane = lax.broadcasted_iota(jnp.int32, mark.shape, 1)
            code_ref[j] = encode(value, jnp.where(lane < classes // 8, 0.0, mark))


def diagonal(block):
    n = block.shape[0]
    eye = lax.broadcasted_iota(jnp.int32, (n, n), 0) == lax.broadcasted_iota(jnp.int32, (n, n), 1)
    return jnp.sum(jnp.where(eye, block, 0.0), axis=1, keepdims=True)


def factor_all(gram):
    order = len(gram)
    factor = [[None] * order for _ in range(order)]
    for j in range(order):
        value = gram[j][j]
        for k in range(j):
            value = value - factor[j][k] * factor[j][k]
        root = jnp.sqrt(value)
        factor[j][j] = 1.0 / root
        for i in range(j + 1, order):
            value = gram[i][j]
            for k in range(j):
                value = value - factor[i][k] * factor[j][k]
            factor[i][j] = value * factor[j][j]
    return factor


def solve_all(factor, right):
    order = len(right)
    forward = []
    for i in range(order):
        value = right[i]
        for j in range(i):
            value = value - factor[i][j] * forward[j]
        forward.append(value * factor[i][i])
    result = []
    for size in range(1, order + 1):
        back = [None] * size
        for i in reversed(range(size)):
            value = forward[i]
            for j in range(i + 1, size):
                value = value - factor[j][i] * back[j]
            back[i] = value * factor[i][i]
        result.append(back)
    return result


def select_kernel(pick_ref, one_ref, *, n_ex, rows, tail):
    steps, classes = pick_ref.shape
    lines = one_ref.shape[1]
    device = lax.axis_index("ex")
    pick = pick_ref[...]
    lane = lax.broadcasted_iota(jnp.int32, pick.shape, 1)
    owner = jnp.zeros_like(pick)
    rank = jnp.zeros_like(pick)
    for d in range(n_ex):
        here = (pick >= d * rows) & (pick < (d + 1) * rows)
        first = jnp.min(jnp.where(here, lane, classes), axis=1, keepdims=True)
        owner = jnp.where(here, d, owner)
        rank = jnp.where(here & (lane > first), 1, rank)
    away = owner ^ device
    bits = n_ex.bit_length() - 1
    far = jnp.zeros_like(pick)
    for b in range(3, bits):
        far = far + (((away >> b) & 1) << (bits - 1 - b))
    by_y, by_z = (away >> 1) & 1, (away >> 2) & 1
    near = 3 * by_z + 2 * by_y - 4 * by_z * by_y
    spot = (2 * near + (away & 1)) * (n_ex // 8) + far
    step = lax.broadcasted_iota(jnp.int32, pick.shape, 0)
    line = lax.broadcasted_iota(jnp.int32, (lines, classes), 0)
    where = spot * 8 + (slots * steps + rank if tail else rank * steps + step)
    hits = [jnp.where(line == where[s : s + 1, :], 1.0, 0.0) for s in range(steps)]
    pad = jnp.zeros((lines, 128 - steps * classes), f32)
    one_ref[...] = jnp.transpose(jnp.concatenate(hits + [pad], axis=1))[: steps * classes].astype(bf16)


def picked_kernel(one_ref, rest_ref, *refs, steps):
    parts, (x_ref, rows_ref) = refs[:-2], refs[-2:]
    total, half = x_ref.shape
    classes = total // steps
    main = rows_ref.shape[1]
    tail = half - main
    at = 0
    for part in parts:
        rows_ref[at : at + part.shape[0], :] = part[...]
        at += part.shape[0]
    x_ref[:, :main] = jnp.dot(one_ref[...], rows_ref[...], preferred_element_type=f32).astype(bf16)
    for s in range(steps):
        at = slice(s * classes, (s + 1) * classes)
        rest = jnp.dot(rest_ref[at, :], rows_ref[:, s * tail : (s + 1) * tail], preferred_element_type=f32)
        x_ref[at, main:] = rest.astype(bf16)


def half_target(side, code_ref, x_ref, target_ref, target_at, left_ref, *, classes):
    half = left_ref.shape[1]
    far = code_ref.shape[0] // 4
    width = half // code_ref.shape[0]
    here = pl.ds(pl.multiple_of(side * half, half), half)
    for k in range(4 * far):
        block = k % far * 4 + near_id(gather_masks[k // far])
        target = decode(code_ref[k], classes)[0]
        target_ref[:, pl.ds(pl.multiple_of(target_at + block * width, width), width)] = target
        left_ref[:classes, pl.ds(pl.multiple_of(block * width, width), width)] = target.astype(bf16)
    left_ref[classes:, :] = x_ref[...]
    return nt_dot(left_ref[...], x_ref[...]), here


def half_kernel(feat_ref, code_ref, x_ref, direct_ref, gram_ref, target_ref, left_ref, *, classes):
    core = lax.axis_index("ex") % 2
    gram_ref[...], here = half_target(core, code_ref, x_ref, target_ref, 0, left_ref, classes=classes)
    direct_ref[...] = nt_dot(left_ref[: direct_ref.shape[0], :], feat_ref[:, here])


def pursuit_kernel(
    labels_ref, feat_ref, x_own, x_twin, direct_own, gram_own, target_own, code_ref,
    scores_ref, resid_hbm, resid_ref, left_ref, sems, *, steps, scale
):
    classes, full = resid_ref.shape
    half = full // 2
    core = lax.axis_index("ex") % 2
    gram, other = half_target(1 - core, code_ref, x_twin, resid_ref, (1 - core) * half, left_ref, classes=classes)
    gram = gram + gram_own[...]
    blocks = [
        [
            diagonal(gram[(a + 1) * classes : (a + 2) * classes, b * classes : (b + 1) * classes])
            + (ridge if a == b else 0.0)
            for b in range(a + 1)
        ]
        for a in range(steps)
    ]
    rhs = [diagonal(gram[:classes, a * classes : (a + 1) * classes]) for a in range(steps)]
    weights = solve_all(factor_all(blocks), rhs)
    last = weights[steps - 1]
    copies = []
    span = half // 2
    for x_ref, side in ((x_own, core), (x_twin, 1 - core)):
        for q in range(2):
            there = slice(q * span, (q + 1) * span)
            here = pl.ds(pl.multiple_of(side * half + q * span, span), span)
            value = target_own[:, there] if x_ref is x_own else resid_ref[:, here]
            for k in range(steps):
                value = value - last[k] * x_ref[k * classes : (k + 1) * classes, there].astype(f32)
            resid_ref[:, here] = value
            copies.append(pltpu.make_async_copy(resid_ref.at[:, here], resid_hbm.at[:, here], sems.at[len(copies)]))
            copies[-1].start()

    direct = direct_own[...] + nt_dot(left_ref[: direct_own.shape[0], :], feat_ref[:, other])
    member = lax.broadcasted_iota(jnp.int32, (classes, direct.shape[1]), 0) == labels_ref[...].reshape(1, direct.shape[1])
    for s in range(steps):
        value = direct[:classes]
        for k in range(s):
            value = value - weights[s - 1][k] * direct[(k + 1) * classes : (k + 2) * classes]
        scores_ref[s : s + 1, :] = jnp.sum(jnp.where(member, value, 0.0), axis=0, keepdims=True) * scale
    for copy in copies:
        copy.wait()


def on_device(features, labels, pick_index, *, n_ex):
    rows, full = features.shape
    steps, classes = pick_index.shape
    groups = n_ex // 2
    width = full // n_ex
    total = steps * classes
    main = full // 2 * steps * slots // 8
    limit = pltpu.CompilerParams(vmem_limit_bytes=16 << 20)
    vmem = pl.BlockSpec(memory_space=pltpu.VMEM)
    hbm = pl.BlockSpec(memory_space=pltpu.HBM)
    anywhere = pl.BlockSpec(memory_space=pl.ANY)
    half = jax.ShapeDtypeStruct((groups * classes + 8, width), f32)
    code = jax.ShapeDtypeStruct((groups // 4, classes * (width // 128) + 8, 128), jnp.int16)

    def near_swaps(x):
        diagonal_part, by_y = swap(x[3], 6), swap(x[2], 2)
        return [swap(x[1], 4), by_y, diagonal_part]

    def swap(x, mask):
        return lax.ppermute(x, "ex", [(d, d ^ mask) for d in range(n_ex)])

    def after(x, *others):
        return lax.optimization_barrier((x,) + others)[0]

    feat, send, keep, held = pl.pallas_call(
        functools.partial(sums_kernel, n_ex=n_ex),
        in_specs=[hbm] * 3,
        out_specs=[vmem] * 4,
        out_shape=[pltpu.VMEM((rows, full), bf16), half, half, jax.ShapeDtypeStruct((8, full), f32)],
        scratch_shapes=[
            pltpu.VMEM(labels.shape, jnp.int32),
            pltpu.VMEM(pick_index.shape, jnp.int32),
            pltpu.VMEM((classes + 16, rows), bf16),
            pltpu.SemaphoreType.DMA((n_ex + 2,)),
        ],
        compiler_params=limit,
        name="class_sums",
    )(*[pltpu.with_memory_space_constraint(a, pltpu.HBM) for a in (labels, pick_index, features)])

    def add(codes, last):
        return pl.pallas_call(
            functools.partial(add_kernel, classes=classes, last=last),
            in_specs=[vmem] * len(codes),
            out_specs=vmem,
            out_shape=code,
            compiler_params=limit,
            name="add_sums",
        )(*codes)

    far_masks = [8 << b for b in range(n_ex.bit_length() - 4)]
    got = swap(send, 1)
    codes = pl.pallas_call(
        functools.partial(pair_kernel, classes=classes),
        in_specs=[vmem] * 2,
        out_specs=[vmem] * 4,
        out_shape=[code] * 4,
        compiler_params=limit,
        name="pair_sums",
    )(keep, got)
    packed = pl.pallas_call(
        functools.partial(pack_kernel, steps=steps),
        in_specs=[vmem],
        out_specs=vmem,
        out_shape=jax.ShapeDtypeStruct((2, 8, main), bf16),
        compiler_params=limit,
        name="pack_rows",
    )(held)
    for mask in reversed(far_masks):
        packed = jnp.concatenate([packed, swap(packed, mask)], axis=1)

    near_codes = near_swaps(codes)
    part_sum = add([codes[0], after(near_codes[2], packed), near_codes[1], near_codes[0]], False)

    def select(tail, *others):
        return pl.pallas_call(
            functools.partial(select_kernel, n_ex=n_ex, rows=rows, tail=tail),
            in_specs=[vmem],
            out_specs=vmem,
            out_shape=jax.ShapeDtypeStruct((total, n_ex * 8), bf16),
            compiler_params=limit,
            name="select_tails" if tail else "select_rows",
        )(after(pick_index, *others))

    one = select(False, codes[0])
    rest = select(True, codes[0])
    given = swap(after(packed[1], part_sum), 1)
    part_sum = after(part_sum, one, rest)
    for mask in far_masks:
        more = swap(part_sum, mask)
        part_sum = add([part_sum, more], mask == far_masks[-1])
    near = jnp.concatenate([after(packed[0], more), given], axis=0)
    parts = [near] + near_swaps([near] * 4)
    pair = jnp.concatenate([after(part_sum, parts[3]), swap(part_sum, 2)], axis=0)
    own_parts = [pair, swap(pair, 4)]

    x = pl.pallas_call(
        functools.partial(picked_kernel, steps=steps),
        in_specs=[vmem] * 6,
        out_specs=vmem,
        out_shape=jax.ShapeDtypeStruct((total, full // 2), bf16),
        scratch_shapes=[pltpu.VMEM((n_ex * 8, main), bf16)],
        compiler_params=limit,
        name="picked_rows",
    )(after(one, own_parts[1]), rest, parts[0], *parts[:0:-1])

    x_twin = swap(x, 1)
    own_half = jnp.concatenate(own_parts, axis=0)
    twin_half = swap(own_half, 1)
    left = pltpu.VMEM((total + classes, full // 2), bf16)
    direct, gram, target = pl.pallas_call(
        functools.partial(half_kernel, classes=classes),
        in_specs=[vmem] * 3,
        out_specs=[vmem] * 3,
        out_shape=[
            jax.ShapeDtypeStruct((total, rows), f32),
            jax.ShapeDtypeStruct((total + classes, total), f32),
            jax.ShapeDtypeStruct((classes, full // 2), f32),
        ],
        scratch_shapes=[left],
        compiler_params=limit,
        name="own_half_products",
    )(feat, own_half, x)

    scores, resid = pl.pallas_call(
        functools.partial(pursuit_kernel, steps=steps, scale=1.0 / math.sqrt(full)),
        in_specs=[vmem] * 8,
        out_specs=[vmem, anywhere],
        out_shape=[
            jax.ShapeDtypeStruct((steps, rows), f32),
            jax.ShapeDtypeStruct((classes, full), f32),
        ],
        scratch_shapes=[pltpu.VMEM((classes, full), f32), left, pltpu.SemaphoreType.DMA((4,))],
        compiler_params=limit,
        name="pursuit",
    )(labels, feat, x, x_twin, direct, gram, target, twin_half)
    return scores, resid


def solution(mesh):
    return jax.shard_map(
        functools.partial(on_device, n_ex=mesh.shape["ex"]),
        mesh=mesh,
        in_specs=(P(("grp", "ex"), None), P(("grp", "ex")), P("grp", None)),
        out_specs=(P(None, ("grp", "ex")), P("grp", None)),
        check_vma=False,
    )
```

```python
import functools
import math

import jax
import jax.numpy as jnp
from jax import lax
from jax.experimental import pallas as pl
from jax.experimental.pallas import tpu as pltpu
from jax.sharding import PartitionSpec as P

ridge = 1.0
slots = 2
near_masks = (0, 4, 2, 6)
f32 = jnp.float32
bf16 = jnp.bfloat16


def nt_dot(a, b):
    return lax.dot_general(a, b, (((1,), (1,)), ((), ())), preferred_element_type=f32)


def column(tile, height, start=0):
    return jnp.concatenate([tile[:, start + q : start + q + 1] for q in range(height // 8)], axis=0)


def spread(values, start=0):
    lane = lax.broadcasted_iota(jnp.int32, (8, 128), 1)
    tile = jnp.zeros((8, 128), f32)
    for q in range(values.shape[0] // 8):
        tile = jnp.where(lane == start + q, values[8 * q : 8 * q + 8], tile)
    return tile


def encode(x, count_tile=None):
    height, width = x.shape
    top = jnp.max(jnp.abs(x), axis=1, keepdims=True)
    power = jnp.ceil(jnp.log2(jnp.maximum(top, 1e-30)) + 0.01)
    whole_x = jnp.round(x * jnp.exp2(15.0 - power))
    mark = spread(power)
    if count_tile is not None:
        mark = mark + count_tile
    chunks = [whole_x[:, j * 128 : (j + 1) * 128] for j in range(width // 128)]
    return jnp.concatenate(chunks + [mark], axis=0).astype(jnp.int32).astype(jnp.int16)


def decode(code, height):
    value = code.astype(jnp.int32).astype(f32)
    count = value.shape[0] // height
    mark = value[count * height :]
    x = jnp.concatenate([value[j * height : (j + 1) * height] for j in range(count)], axis=1)
    return x * jnp.exp2(column(mark, height) - 15.0), mark


def sums_kernel(
    labels_hbm, pick_hbm, feat_hbm, feat_ref, send_ref, keep_ref, held, labels_ref, pick_ref, left, sems, *, n_ex
):
    rows, full = feat_ref.shape
    steps, classes = pick_ref.shape
    width = full // n_ex
    groups = n_ex // 2
    device = lax.axis_index("ex")
    core = device % 2
    small = [
        pltpu.make_async_copy(pick_hbm, pick_ref, sems.at[n_ex]),
        pltpu.make_async_copy(labels_hbm, labels_ref, sems.at[n_ex + 1]),
    ]
    for copy in small:
        copy.start()
    columns = []
    copies = []
    for i in range(n_ex):
        block = (1 - core) * groups + i if i < groups else core * groups + i - groups
        at = pl.ds(pl.multiple_of(block * width, width), width)
        columns.append(at)
        copies.append(pltpu.make_async_copy(feat_hbm.at[:, at], feat_ref.at[:, at], sems.at[i]))
        copies[-1].start()

    for copy in small:
        copy.wait()
    local = pick_ref[...] - device * rows
    mine = (local >= 0) & (local < rows)
    lane = lax.broadcasted_iota(jnp.int32, local.shape, 1)
    first = jnp.min(jnp.where(mine, lane, classes), axis=1, keepdims=True)
    last = jnp.max(jnp.where(mine, lane, -1), axis=1, keepdims=True)
    spot0 = jnp.max(jnp.where(mine & (lane == first), local, -1), axis=1, keepdims=True)
    spot1 = jnp.max(jnp.where(mine & (lane == last) & (last > first), local, -1), axis=1, keepdims=True)
    member = lax.broadcasted_iota(jnp.int32, (classes, rows), 0) == labels_ref[...].reshape(1, rows)
    line = lax.broadcasted_iota(jnp.int32, (steps, rows), 1)
    left[...] = jnp.concatenate(
        [
            jnp.where(member, 1.0, 0.0),
            jnp.where(line == spot0, 1.0, 0.0),
            jnp.where(line == spot1, 1.0, 0.0),
            jnp.zeros((16 - 2 * steps, rows), f32),
        ],
        axis=0,
    ).astype(bf16)
    count = jnp.sum(jnp.where(member, 1.0, 0.0), axis=1, keepdims=True)
    tile = spread(count, classes // 8)
    base = groups * classes
    for ref in (send_ref, keep_ref):
        ref[base : base + 8, :128] = tile
        if width > 128:
            ref[base : base + 8, 128:] = jnp.zeros((8, width - 128), f32)

    for i in range(n_ex):
        copies[i].wait()
        both = jnp.dot(left[...], feat_ref[:, columns[i]], preferred_element_type=f32)
        k = i % groups
        ref = send_ref if i < groups else keep_ref
        ref[k * classes : (k + 1) * classes, :] = both[:classes]
        held[:, columns[i]] = both[classes : classes + 8]


def pack_kernel(held, rows_ref, *, steps):
    half = held.shape[1] // 2
    used = steps * slots
    main = rows_ref.shape[2]
    core = lax.axis_index("ex") % 2
    for part, side in ((0, core), (1, 1 - core)):
        h = held[:, pl.ds(pl.multiple_of(side * half, half), half)]
        lines = [h[:used, :main]]
        for q in range(slots):
            lines.append(jnp.concatenate([h[q * steps + u : q * steps + u + 1, main:] for u in range(steps)], axis=1))
        rows_ref[part] = jnp.concatenate(lines, axis=0).astype(bf16)


def near_id(mask):
    return (lax.axis_index("ex") // 2 % 4) ^ (mask // 2)


def pair_kernel(keep_ref, got_ref, *code_refs, classes):
    far = code_refs[0].shape[0]
    base = 4 * far * classes
    tile = keep_ref[base : base + 8, :128] + got_ref[base : base + 8, :128]
    for mask, code_ref in zip(near_masks, code_refs):
        for j in range(far):
            at = pl.ds(pl.multiple_of((j * 4 + near_id(mask)) * classes, classes), classes)
            code_ref[j] = encode(keep_ref[at, :] + got_ref[at, :], tile)


def add_kernel(*refs, classes, last):
    code_ref = refs[-1]
    for j in range(code_ref.shape[0]):
        value, mark = decode(refs[0][j], classes)
        for ref in refs[1:-1]:
            more, more_mark = decode(ref[j], classes)
            value = value + more
            mark = mark + more_mark
        if last:
            code_ref[j] = encode(value / jnp.sqrt(column(mark, classes, classes // 8)))
        else:
            lane = lax.broadcasted_iota(jnp.int32, mark.shape, 1)
            code_ref[j] = encode(value, jnp.where(lane < classes // 8, 0.0, mark))


def diagonal(block):
    n = block.shape[0]
    eye = lax.broadcasted_iota(jnp.int32, (n, n), 0) == lax.broadcasted_iota(jnp.int32, (n, n), 1)
    return jnp.sum(jnp.where(eye, block, 0.0), axis=1, keepdims=True)


def factor_all(gram):
    order = len(gram)
    factor = [[None] * order for _ in range(order)]
    for j in range(order):
        value = gram[j][j]
        for k in range(j):
            value = value - factor[j][k] * factor[j][k]
        root = jnp.sqrt(value)
        factor[j][j] = 1.0 / root
        for i in range(j + 1, order):
            value = gram[i][j]
            for k in range(j):
                value = value - factor[i][k] * factor[j][k]
            factor[i][j] = value * factor[j][j]
    return factor


def solve_all(factor, right):
    order = len(right)
    forward = []
    for i in range(order):
        value = right[i]
        for j in range(i):
            value = value - factor[i][j] * forward[j]
        forward.append(value * factor[i][i])
    result = []
    for size in range(1, order + 1):
        back = [None] * size
        for i in reversed(range(size)):
            value = forward[i]
            for j in range(i + 1, size):
                value = value - factor[j][i] * back[j]
            back[i] = value * factor[i][i]
        result.append(back)
    return result


def select_kernel(pick_ref, one_ref, *, n_ex, rows, tail):
    steps, classes = pick_ref.shape
    lines = one_ref.shape[1]
    device = lax.axis_index("ex")
    pick = pick_ref[...]
    lane = lax.broadcasted_iota(jnp.int32, pick.shape, 1)
    owner = jnp.zeros_like(pick)
    rank = jnp.zeros_like(pick)
    for d in range(n_ex):
        here = (pick >= d * rows) & (pick < (d + 1) * rows)
        first = jnp.min(jnp.where(here, lane, classes), axis=1, keepdims=True)
        owner = jnp.where(here, d, owner)
        rank = jnp.where(here & (lane > first), 1, rank)
    away = owner ^ device
    bits = n_ex.bit_length() - 1
    far = jnp.zeros_like(pick)
    for b in range(3, bits):
        far = far + (((away >> b) & 1) << (bits - 1 - b))
    by_y, by_z = (away >> 1) & 1, (away >> 2) & 1
    near = 3 * by_y + 2 * by_z - 4 * by_z * by_y
    spot = (2 * near + (away & 1)) * (n_ex // 8) + far
    step = lax.broadcasted_iota(jnp.int32, pick.shape, 0)
    line = lax.broadcasted_iota(jnp.int32, (lines, classes), 0)
    where = spot * 8 + (slots * steps + rank if tail else rank * steps + step)
    hits = [jnp.where(line == where[s : s + 1, :], 1.0, 0.0) for s in range(steps)]
    pad = jnp.zeros((lines, 128 - steps * classes), f32)
    one_ref[...] = jnp.transpose(jnp.concatenate(hits + [pad], axis=1))[: steps * classes].astype(bf16)


def picked_kernel(one_ref, rest_ref, *refs, steps):
    parts, (x_ref, rows_ref) = refs[:-2], refs[-2:]
    total, half = x_ref.shape
    classes = total // steps
    main = rows_ref.shape[1]
    tail = half - main
    at = 0
    for part in parts:
        rows_ref[at : at + part.shape[0], :] = part[...]
        at += part.shape[0]
    x_ref[:, :main] = jnp.dot(one_ref[...], rows_ref[...], preferred_element_type=f32).astype(bf16)
    for s in range(steps):
        at = slice(s * classes, (s + 1) * classes)
        rest = jnp.dot(rest_ref[at, :], rows_ref[:, s * tail : (s + 1) * tail], preferred_element_type=f32)
        x_ref[at, main:] = rest.astype(bf16)


def half_target(side, code_ref, x_ref, target_ref, target_at, left_ref, *, classes):
    half = left_ref.shape[1]
    far = code_ref.shape[0] // 4
    width = half // code_ref.shape[0]
    here = pl.ds(pl.multiple_of(side * half, half), half)
    for k in range(4 * far):
        block = k % far * 4 + near_id(near_masks[k // far])
        target = decode(code_ref[k], classes)[0]
        target_ref[:, pl.ds(pl.multiple_of(target_at + block * width, width), width)] = target
        left_ref[:classes, pl.ds(pl.multiple_of(block * width, width), width)] = target.astype(bf16)
    left_ref[classes:, :] = x_ref[...]
    return nt_dot(left_ref[...], x_ref[...]), here


def half_kernel(feat_ref, code_ref, x_ref, direct_ref, gram_ref, target_ref, left_ref, *, classes):
    core = lax.axis_index("ex") % 2
    gram_ref[...], here = half_target(core, code_ref, x_ref, target_ref, 0, left_ref, classes=classes)
    direct_ref[...] = nt_dot(left_ref[: direct_ref.shape[0], :], feat_ref[:, here])


def pursuit_kernel(
    labels_ref, feat_ref, x_own, x_twin, direct_own, gram_own, target_own, code_ref,
    scores_ref, resid_hbm, resid_ref, left_ref, sems, *, steps, scale
):
    classes, full = resid_ref.shape
    half = full // 2
    core = lax.axis_index("ex") % 2
    gram, other = half_target(1 - core, code_ref, x_twin, resid_ref, (1 - core) * half, left_ref, classes=classes)
    gram = gram + gram_own[...]
    blocks = [
        [
            diagonal(gram[(a + 1) * classes : (a + 2) * classes, b * classes : (b + 1) * classes])
            + (ridge if a == b else 0.0)
            for b in range(a + 1)
        ]
        for a in range(steps)
    ]
    rhs = [diagonal(gram[:classes, a * classes : (a + 1) * classes]) for a in range(steps)]
    weights = solve_all(factor_all(blocks), rhs)
    last = weights[steps - 1]
    copies = []
    span = half // 2
    for x_ref, side in ((x_own, core), (x_twin, 1 - core)):
        for q in range(2):
            there = slice(q * span, (q + 1) * span)
            here = pl.ds(pl.multiple_of(side * half + q * span, span), span)
            value = target_own[:, there] if x_ref is x_own else resid_ref[:, here]
            for k in range(steps):
                value = value - last[k] * x_ref[k * classes : (k + 1) * classes, there].astype(f32)
            resid_ref[:, here] = value
            copies.append(pltpu.make_async_copy(resid_ref.at[:, here], resid_hbm.at[:, here], sems.at[len(copies)]))
            copies[-1].start()

    direct = direct_own[...] + nt_dot(left_ref[: direct_own.shape[0], :], feat_ref[:, other])
    member = lax.broadcasted_iota(jnp.int32, (classes, direct.shape[1]), 0) == labels_ref[...].reshape(1, direct.shape[1])
    for s in range(steps):
        value = direct[:classes]
        for k in range(s):
            value = value - weights[s - 1][k] * direct[(k + 1) * classes : (k + 2) * classes]
        scores_ref[s : s + 1, :] = jnp.sum(jnp.where(member, value, 0.0), axis=0, keepdims=True) * scale
    for copy in copies:
        copy.wait()


def on_device(features, labels, pick_index, *, n_ex):
    rows, full = features.shape
    steps, classes = pick_index.shape
    groups = n_ex // 2
    width = full // n_ex
    total = steps * classes
    main = full // 2 * steps * slots // 8
    limit = pltpu.CompilerParams(vmem_limit_bytes=16 << 20)
    vmem = pl.BlockSpec(memory_space=pltpu.VMEM)
    hbm = pl.BlockSpec(memory_space=pltpu.HBM)
    anywhere = pl.BlockSpec(memory_space=pl.ANY)
    half = jax.ShapeDtypeStruct((groups * classes + 8, width), f32)
    code = jax.ShapeDtypeStruct((groups // 4, classes * (width // 128) + 8, 128), jnp.int16)

    def near_swaps(x):
        diagonal_part, by_y = swap(x[3], 6), swap(x[2], 2)
        return [swap(x[1], 4), by_y, diagonal_part]

    def swap(x, mask):
        return lax.ppermute(x, "ex", [(d, d ^ mask) for d in range(n_ex)])

    def after(x, *others):
        return lax.optimization_barrier((x,) + others)[0]

    feat, send, keep, held = pl.pallas_call(
        functools.partial(sums_kernel, n_ex=n_ex),
        in_specs=[hbm] * 3,
        out_specs=[vmem] * 4,
        out_shape=[pltpu.VMEM((rows, full), bf16), half, half, jax.ShapeDtypeStruct((8, full), f32)],
        scratch_shapes=[
            pltpu.VMEM(labels.shape, jnp.int32),
            pltpu.VMEM(pick_index.shape, jnp.int32),
            pltpu.VMEM((classes + 16, rows), bf16),
            pltpu.SemaphoreType.DMA((n_ex + 2,)),
        ],
        compiler_params=limit,
        name="class_sums",
    )(*[pltpu.with_memory_space_constraint(a, pltpu.HBM) for a in (labels, pick_index, features)])

    def add(codes, last):
        return pl.pallas_call(
            functools.partial(add_kernel, classes=classes, last=last),
            in_specs=[vmem] * len(codes),
            out_specs=vmem,
            out_shape=code,
            compiler_params=limit,
            name="add_sums",
        )(*codes)

    far_masks = [8 << b for b in range(n_ex.bit_length() - 4)]
    got = swap(send, 1)
    codes = pl.pallas_call(
        functools.partial(pair_kernel, classes=classes),
        in_specs=[vmem] * 2,
        out_specs=[vmem] * 4,
        out_shape=[code] * 4,
        compiler_params=limit,
        name="pair_sums",
    )(keep, got)
    packed = pl.pallas_call(
        functools.partial(pack_kernel, steps=steps),
        in_specs=[vmem],
        out_specs=vmem,
        out_shape=jax.ShapeDtypeStruct((2, 8, main), bf16),
        compiler_params=limit,
        name="pack_rows",
    )(held)
    for mask in reversed(far_masks):
        packed = jnp.concatenate([packed, swap(packed, mask)], axis=1)

    near_codes = near_swaps(codes)
    part_sum = add([codes[0], after(near_codes[2], packed), near_codes[1], near_codes[0]], False)

    def select(tail, *others):
        return pl.pallas_call(
            functools.partial(select_kernel, n_ex=n_ex, rows=rows, tail=tail),
            in_specs=[vmem],
            out_specs=vmem,
            out_shape=jax.ShapeDtypeStruct((total, n_ex * 8), bf16),
            compiler_params=limit,
            name="select_tails" if tail else "select_rows",
        )(after(pick_index, *others))

    one = select(False, codes[0])
    rest = select(True, codes[0])
    given = swap(after(packed[1], part_sum), 1)
    part_sum = after(part_sum, one, rest)
    for mask in far_masks:
        more = swap(part_sum, mask)
        part_sum = add([part_sum, more], mask == far_masks[-1])
    near = jnp.concatenate([after(packed[0], more), given], axis=0)
    parts = [near] + near_swaps([near] * 4)
    own_parts = [part_sum] + near_swaps([None, after(part_sum, parts[3]), part_sum, part_sum])

    x = pl.pallas_call(
        functools.partial(picked_kernel, steps=steps),
        in_specs=[vmem] * 6,
        out_specs=vmem,
        out_shape=jax.ShapeDtypeStruct((total, full // 2), bf16),
        scratch_shapes=[pltpu.VMEM((n_ex * 8, main), bf16)],
        compiler_params=limit,
        name="picked_rows",
    )(one, rest, parts[0], parts[3], parts[1], parts[2])

    x_twin = swap(x, 1)
    own_half = jnp.concatenate(after(own_parts, x), axis=0)
    twin_half = swap(own_half, 1)
    left = pltpu.VMEM((total + classes, full // 2), bf16)
    direct, gram, target = pl.pallas_call(
        functools.partial(half_kernel, classes=classes),
        in_specs=[vmem] * 3,
        out_specs=[vmem] * 3,
        out_shape=[
            jax.ShapeDtypeStruct((total, rows), f32),
            jax.ShapeDtypeStruct((total + classes, total), f32),
            jax.ShapeDtypeStruct((classes, full // 2), f32),
        ],
        scratch_shapes=[left],
        compiler_params=limit,
        name="own_half_products",
    )(feat, own_half, x)

    scores, resid = pl.pallas_call(
        functools.partial(pursuit_kernel, steps=steps, scale=1.0 / math.sqrt(full)),
        in_specs=[vmem] * 8,
        out_specs=[vmem, anywhere],
        out_shape=[
            jax.ShapeDtypeStruct((steps, rows), f32),
            jax.ShapeDtypeStruct((classes, full), f32),
        ],
        scratch_shapes=[pltpu.VMEM((classes, full), f32), left, pltpu.SemaphoreType.DMA((4,))],
        compiler_params=limit,
        name="pursuit",
    )(labels, feat, x, x_twin, direct, gram, target, twin_half)
    return scores, resid


def solution(mesh):
    return jax.shard_map(
        functools.partial(on_device, n_ex=mesh.shape["ex"]),
        mesh=mesh,
        in_specs=(P(("grp", "ex"), None), P(("grp", "ex")), P("grp", None)),
        out_specs=(P(None, ("grp", "ex")), P("grp", None)),
        check_vma=False,
    )
```

```python
import functools
import math

import jax
import jax.numpy as jnp
from jax import lax
from jax.experimental import pallas as pl
from jax.experimental.pallas import tpu as pltpu
from jax.sharding import PartitionSpec as P

ridge = 1.0
slots = 2
near_masks = (0, 4, 2, 6)
f32 = jnp.float32
bf16 = jnp.bfloat16


def nt_dot(a, b):
    return lax.dot_general(a, b, (((1,), (1,)), ((), ())), preferred_element_type=f32)


def column(tile, height, start=0):
    return jnp.concatenate([tile[:, start + q : start + q + 1] for q in range(height // 8)], axis=0)


def spread(values, start=0):
    lane = lax.broadcasted_iota(jnp.int32, (8, 128), 1)
    tile = jnp.zeros((8, 128), f32)
    for q in range(values.shape[0] // 8):
        tile = jnp.where(lane == start + q, values[8 * q : 8 * q + 8], tile)
    return tile


def encode(x, count_tile=None):
    height, width = x.shape
    top = jnp.max(jnp.abs(x), axis=1, keepdims=True)
    power = jnp.ceil(jnp.log2(jnp.maximum(top, 1e-30)) + 0.01)
    whole_x = jnp.round(x * jnp.exp2(15.0 - power))
    mark = spread(power)
    if count_tile is not None:
        mark = mark + count_tile
    chunks = [whole_x[:, j * 128 : (j + 1) * 128] for j in range(width // 128)]
    return jnp.concatenate(chunks + [mark], axis=0).astype(jnp.int32).astype(jnp.int16)


def decode(code, height):
    value = code.astype(jnp.int32).astype(f32)
    count = value.shape[0] // height
    mark = value[count * height :]
    x = jnp.concatenate([value[j * height : (j + 1) * height] for j in range(count)], axis=1)
    return x * jnp.exp2(column(mark, height) - 15.0), mark


def sums_kernel(
    labels_hbm, pick_hbm, feat_hbm, feat_ref, send_ref, keep_ref, held, labels_ref, pick_ref, left, sems, *, n_ex
):
    rows, full = feat_ref.shape
    steps, classes = pick_ref.shape
    width = full // n_ex
    groups = n_ex // 2
    device = lax.axis_index("ex")
    core = device % 2
    small = [
        pltpu.make_async_copy(pick_hbm, pick_ref, sems.at[n_ex]),
        pltpu.make_async_copy(labels_hbm, labels_ref, sems.at[n_ex + 1]),
    ]
    for copy in small:
        copy.start()
    columns = []
    copies = []
    for i in range(n_ex):
        block = (1 - core) * groups + i if i < groups else core * groups + i - groups
        at = pl.ds(pl.multiple_of(block * width, width), width)
        columns.append(at)
        copies.append(pltpu.make_async_copy(feat_hbm.at[:, at], feat_ref.at[:, at], sems.at[i]))
        copies[-1].start()

    for copy in small:
        copy.wait()
    local = pick_ref[...] - device * rows
    mine = (local >= 0) & (local < rows)
    lane = lax.broadcasted_iota(jnp.int32, local.shape, 1)
    first = jnp.min(jnp.where(mine, lane, classes), axis=1, keepdims=True)
    last = jnp.max(jnp.where(mine, lane, -1), axis=1, keepdims=True)
    spot0 = jnp.max(jnp.where(mine & (lane == first), local, -1), axis=1, keepdims=True)
    spot1 = jnp.max(jnp.where(mine & (lane == last) & (last > first), local, -1), axis=1, keepdims=True)
    member = lax.broadcasted_iota(jnp.int32, (classes, rows), 0) == labels_ref[...].reshape(1, rows)
    line = lax.broadcasted_iota(jnp.int32, (steps, rows), 1)
    left[...] = jnp.concatenate(
        [
            jnp.where(member, 1.0, 0.0),
            jnp.where(line == spot0, 1.0, 0.0),
            jnp.where(line == spot1, 1.0, 0.0),
            jnp.zeros((16 - 2 * steps, rows), f32),
        ],
        axis=0,
    ).astype(bf16)
    count = jnp.sum(jnp.where(member, 1.0, 0.0), axis=1, keepdims=True)
    tile = spread(count, classes // 8)
    base = groups * classes
    for ref in (send_ref, keep_ref):
        ref[base : base + 8, :128] = tile
        if width > 128:
            ref[base : base + 8, 128:] = jnp.zeros((8, width - 128), f32)

    for i in range(n_ex):
        copies[i].wait()
        both = jnp.dot(left[...], feat_ref[:, columns[i]], preferred_element_type=f32)
        k = i % groups
        ref = send_ref if i < groups else keep_ref
        ref[k * classes : (k + 1) * classes, :] = both[:classes]
        held[:, columns[i]] = both[classes : classes + 8]


def pack_kernel(held, rows_ref, *, steps):
    half = held.shape[1] // 2
    used = steps * slots
    main = rows_ref.shape[2]
    core = lax.axis_index("ex") % 2
    for part, side in ((0, core), (1, 1 - core)):
        h = held[:, pl.ds(pl.multiple_of(side * half, half), half)]
        lines = [h[:used, :main]]
        for q in range(slots):
            lines.append(jnp.concatenate([h[q * steps + u : q * steps + u + 1, main:] for u in range(steps)], axis=1))
        rows_ref[part] = jnp.concatenate(lines, axis=0).astype(bf16)


def near_id(mask):
    return (lax.axis_index("ex") // 2 % 4) ^ (mask // 2)


def pair_kernel(keep_ref, got_ref, *code_refs, classes):
    far = code_refs[0].shape[0]
    base = 4 * far * classes
    tile = keep_ref[base : base + 8, :128] + got_ref[base : base + 8, :128]
    for mask, code_ref in zip(near_masks, code_refs):
        for j in range(far):
            at = pl.ds(pl.multiple_of((j * 4 + near_id(mask)) * classes, classes), classes)
            code_ref[j] = encode(keep_ref[at, :] + got_ref[at, :], tile)


def add_kernel(*refs, classes, last):
    code_ref = refs[-1]
    for j in range(code_ref.shape[0]):
        value, mark = decode(refs[0][j], classes)
        for ref in refs[1:-1]:
            more, more_mark = decode(ref[j], classes)
            value = value + more
            mark = mark + more_mark
        if last:
            code_ref[j] = encode(value / jnp.sqrt(column(mark, classes, classes // 8)))
        else:
            lane = lax.broadcasted_iota(jnp.int32, mark.shape, 1)
            code_ref[j] = encode(value, jnp.where(lane < classes // 8, 0.0, mark))


def diagonal(block):
    n = block.shape[0]
    eye = lax.broadcasted_iota(jnp.int32, (n, n), 0) == lax.broadcasted_iota(jnp.int32, (n, n), 1)
    return jnp.sum(jnp.where(eye, block, 0.0), axis=1, keepdims=True)


def factor_all(gram):
    order = len(gram)
    factor = [[None] * order for _ in range(order)]
    for j in range(order):
        value = gram[j][j]
        for k in range(j):
            value = value - factor[j][k] * factor[j][k]
        root = jnp.sqrt(value)
        factor[j][j] = 1.0 / root
        for i in range(j + 1, order):
            value = gram[i][j]
            for k in range(j):
                value = value - factor[i][k] * factor[j][k]
            factor[i][j] = value * factor[j][j]
    return factor


def solve_all(factor, right):
    order = len(right)
    forward = []
    for i in range(order):
        value = right[i]
        for j in range(i):
            value = value - factor[i][j] * forward[j]
        forward.append(value * factor[i][i])
    result = []
    for size in range(1, order + 1):
        back = [None] * size
        for i in reversed(range(size)):
            value = forward[i]
            for j in range(i + 1, size):
                value = value - factor[j][i] * back[j]
            back[i] = value * factor[i][i]
        result.append(back)
    return result


def select_kernel(pick_ref, one_ref, *, n_ex, rows, tail):
    steps, classes = pick_ref.shape
    lines = one_ref.shape[1]
    device = lax.axis_index("ex")
    pick = pick_ref[...]
    lane = lax.broadcasted_iota(jnp.int32, pick.shape, 1)
    owner = jnp.zeros_like(pick)
    rank = jnp.zeros_like(pick)
    for d in range(n_ex):
        here = (pick >= d * rows) & (pick < (d + 1) * rows)
        first = jnp.min(jnp.where(here, lane, classes), axis=1, keepdims=True)
        owner = jnp.where(here, d, owner)
        rank = jnp.where(here & (lane > first), 1, rank)
    away = owner ^ device
    bits = n_ex.bit_length() - 1
    far = jnp.zeros_like(pick)
    for b in range(3, bits):
        far = far + (((away >> b) & 1) << (bits - 1 - b))
    by_y, by_z = (away >> 1) & 1, (away >> 2) & 1
    near = 3 * by_z + 2 * by_y - 4 * by_z * by_y
    spot = (2 * near + (away & 1)) * (n_ex // 8) + far
    step = lax.broadcasted_iota(jnp.int32, pick.shape, 0)
    line = lax.broadcasted_iota(jnp.int32, (lines, classes), 0)
    where = spot * 8 + (slots * steps + rank if tail else rank * steps + step)
    hits = [jnp.where(line == where[s : s + 1, :], 1.0, 0.0) for s in range(steps)]
    pad = jnp.zeros((lines, 128 - steps * classes), f32)
    one_ref[...] = jnp.transpose(jnp.concatenate(hits + [pad], axis=1))[: steps * classes].astype(bf16)


def picked_kernel(one_ref, rest_ref, *refs, steps):
    parts, (x_ref, rows_ref) = refs[:-2], refs[-2:]
    total, half = x_ref.shape
    classes = total // steps
    main = rows_ref.shape[1]
    tail = half - main
    at = 0
    for part in parts:
        rows_ref[at : at + part.shape[0], :] = part[...]
        at += part.shape[0]
    x_ref[:, :main] = jnp.dot(one_ref[...], rows_ref[...], preferred_element_type=f32).astype(bf16)
    for s in range(steps):
        at = slice(s * classes, (s + 1) * classes)
        rest = jnp.dot(rest_ref[at, :], rows_ref[:, s * tail : (s + 1) * tail], preferred_element_type=f32)
        x_ref[at, main:] = rest.astype(bf16)


def half_target(side, code_ref, x_ref, target_ref, target_at, left_ref, *, classes):
    half = left_ref.shape[1]
    far = code_ref.shape[0] // 4
    width = half // code_ref.shape[0]
    here = pl.ds(pl.multiple_of(side * half, half), half)
    for k in range(4 * far):
        block = k % far * 4 + near_id(near_masks[k // far])
        target = decode(code_ref[k], classes)[0]
        target_ref[:, pl.ds(pl.multiple_of(target_at + block * width, width), width)] = target
        left_ref[:classes, pl.ds(pl.multiple_of(block * width, width), width)] = target.astype(bf16)
    left_ref[classes:, :] = x_ref[...]
    return nt_dot(left_ref[...], x_ref[...]), here


def half_kernel(feat_ref, code_ref, x_ref, direct_ref, gram_ref, target_ref, left_ref, *, classes):
    core = lax.axis_index("ex") % 2
    gram_ref[...], here = half_target(core, code_ref, x_ref, target_ref, 0, left_ref, classes=classes)
    direct_ref[...] = nt_dot(left_ref[: direct_ref.shape[0], :], feat_ref[:, here])


def pursuit_kernel(
    labels_ref, feat_ref, x_own, x_twin, direct_own, gram_own, target_own, code_ref,
    scores_ref, resid_hbm, resid_ref, left_ref, sems, *, steps, scale
):
    classes, full = resid_ref.shape
    half = full // 2
    core = lax.axis_index("ex") % 2
    gram, other = half_target(1 - core, code_ref, x_twin, resid_ref, (1 - core) * half, left_ref, classes=classes)
    gram = gram + gram_own[...]
    blocks = [
        [
            diagonal(gram[(a + 1) * classes : (a + 2) * classes, b * classes : (b + 1) * classes])
            + (ridge if a == b else 0.0)
            for b in range(a + 1)
        ]
        for a in range(steps)
    ]
    rhs = [diagonal(gram[:classes, a * classes : (a + 1) * classes]) for a in range(steps)]
    weights = solve_all(factor_all(blocks), rhs)
    last = weights[steps - 1]
    copies = []
    span = half // 2
    for x_ref, side in ((x_own, core), (x_twin, 1 - core)):
        for q in range(2):
            there = slice(q * span, (q + 1) * span)
            here = pl.ds(pl.multiple_of(side * half + q * span, span), span)
            value = target_own[:, there] if x_ref is x_own else resid_ref[:, here]
            for k in range(steps):
                value = value - last[k] * x_ref[k * classes : (k + 1) * classes, there].astype(f32)
            resid_ref[:, here] = value
            copies.append(pltpu.make_async_copy(resid_ref.at[:, here], resid_hbm.at[:, here], sems.at[len(copies)]))
            copies[-1].start()

    direct = direct_own[...] + nt_dot(left_ref[: direct_own.shape[0], :], feat_ref[:, other])
    member = lax.broadcasted_iota(jnp.int32, (classes, direct.shape[1]), 0) == labels_ref[...].reshape(1, direct.shape[1])
    for s in range(steps):
        value = direct[:classes]
        for k in range(s):
            value = value - weights[s - 1][k] * direct[(k + 1) * classes : (k + 2) * classes]
        scores_ref[s : s + 1, :] = jnp.sum(jnp.where(member, value, 0.0), axis=0, keepdims=True) * scale
    for copy in copies:
        copy.wait()


def on_device(features, labels, pick_index, *, n_ex):
    rows, full = features.shape
    steps, classes = pick_index.shape
    groups = n_ex // 2
    width = full // n_ex
    total = steps * classes
    main = full // 2 * steps * slots // 8
    limit = pltpu.CompilerParams(vmem_limit_bytes=16 << 20)
    vmem = pl.BlockSpec(memory_space=pltpu.VMEM)
    hbm = pl.BlockSpec(memory_space=pltpu.HBM)
    anywhere = pl.BlockSpec(memory_space=pl.ANY)
    half = jax.ShapeDtypeStruct((groups * classes + 8, width), f32)
    code = jax.ShapeDtypeStruct((groups // 4, classes * (width // 128) + 8, 128), jnp.int16)

    def near_swaps(x):
        diagonal_part, by_y = swap(x[3], 6), swap(x[2], 2)
        return [swap(x[1], 4), by_y, diagonal_part]

    def swap(x, mask):
        return lax.ppermute(x, "ex", [(d, d ^ mask) for d in range(n_ex)])

    def after(x, *others):
        return lax.optimization_barrier((x,) + others)[0]

    feat, send, keep, held = pl.pallas_call(
        functools.partial(sums_kernel, n_ex=n_ex),
        in_specs=[hbm] * 3,
        out_specs=[vmem] * 4,
        out_shape=[pltpu.VMEM((rows, full), bf16), half, half, jax.ShapeDtypeStruct((8, full), f32)],
        scratch_shapes=[
            pltpu.VMEM(labels.shape, jnp.int32),
            pltpu.VMEM(pick_index.shape, jnp.int32),
            pltpu.VMEM((classes + 16, rows), bf16),
            pltpu.SemaphoreType.DMA((n_ex + 2,)),
        ],
        compiler_params=limit,
        name="class_sums",
    )(*[pltpu.with_memory_space_constraint(a, pltpu.HBM) for a in (labels, pick_index, features)])

    def add(codes, last):
        return pl.pallas_call(
            functools.partial(add_kernel, classes=classes, last=last),
            in_specs=[vmem] * len(codes),
            out_specs=vmem,
            out_shape=code,
            compiler_params=limit,
            cost_estimate=pl.CostEstimate(flops=10**10, bytes_accessed=10**8, transcendentals=0) if last else None,
            name="add_sums",
        )(*codes)

    far_masks = [8 << b for b in range(n_ex.bit_length() - 4)]
    got = swap(send, 1)
    codes = pl.pallas_call(
        functools.partial(pair_kernel, classes=classes),
        in_specs=[vmem] * 2,
        out_specs=[vmem] * 4,
        out_shape=[code] * 4,
        compiler_params=limit,
        name="pair_sums",
    )(keep, got)
    packed = pl.pallas_call(
        functools.partial(pack_kernel, steps=steps),
        in_specs=[vmem],
        out_specs=vmem,
        out_shape=jax.ShapeDtypeStruct((2, 8, main), bf16),
        compiler_params=limit,
        name="pack_rows",
    )(held)
    for mask in reversed(far_masks):
        packed = jnp.concatenate([packed, swap(packed, mask)], axis=1)

    near_codes = near_swaps(codes)
    part_sum = add([codes[0], after(near_codes[2], packed), near_codes[1], near_codes[0]], False)

    def select(tail, *others):
        return pl.pallas_call(
            functools.partial(select_kernel, n_ex=n_ex, rows=rows, tail=tail),
            in_specs=[vmem],
            out_specs=vmem,
            out_shape=jax.ShapeDtypeStruct((total, n_ex * 8), bf16),
            compiler_params=limit,
            name="select_tails" if tail else "select_rows",
        )(after(pick_index, *others))

    rest = select(True, codes[0])
    near_sum = after(part_sum, rest)
    more = swap(near_sum, far_masks[0])
    one = select(False, near_sum)
    part_sum = add([near_sum, more], len(far_masks) == 1)
    for mask in far_masks[1:]:
        part_sum = add([part_sum, swap(part_sum, mask)], mask == far_masks[-1])
    given = swap(after(packed[1], near_sum), 1)
    near = jnp.concatenate([after(packed[0], one), given], axis=0)
    parts = [near] + near_swaps([near] * 4)
    own_parts = [part_sum] + near_swaps([None, after(part_sum, parts[1]), part_sum, part_sum])

    x = pl.pallas_call(
        functools.partial(picked_kernel, steps=steps),
        in_specs=[vmem] * 6,
        out_specs=vmem,
        out_shape=jax.ShapeDtypeStruct((total, full // 2), bf16),
        scratch_shapes=[pltpu.VMEM((n_ex * 8, main), bf16)],
        compiler_params=limit,
        name="picked_rows",
    )(one, rest, parts[0], *parts[:0:-1])

    x_twin = swap(x, 1)
    own_half = jnp.concatenate(after(own_parts, x), axis=0)
    twin_half = swap(own_half, 1)
    left = pltpu.VMEM((total + classes, full // 2), bf16)
    direct, gram, target = pl.pallas_call(
        functools.partial(half_kernel, classes=classes),
        in_specs=[vmem] * 3,
        out_specs=[vmem] * 3,
        out_shape=[
            jax.ShapeDtypeStruct((total, rows), f32),
            jax.ShapeDtypeStruct((total + classes, total), f32),
            jax.ShapeDtypeStruct((classes, full // 2), f32),
        ],
        scratch_shapes=[left],
        compiler_params=limit,
        name="own_half_products",
    )(feat, own_half, x)

    scores, resid = pl.pallas_call(
        functools.partial(pursuit_kernel, steps=steps, scale=1.0 / math.sqrt(full)),
        in_specs=[vmem] * 8,
        out_specs=[vmem, anywhere],
        out_shape=[
            jax.ShapeDtypeStruct((steps, rows), f32),
            jax.ShapeDtypeStruct((classes, full), f32),
        ],
        scratch_shapes=[pltpu.VMEM((classes, full), f32), left, pltpu.SemaphoreType.DMA((4,))],
        compiler_params=limit,
        name="pursuit",
    )(labels, feat, x, x_twin, direct, gram, target, twin_half)
    return scores, resid


def solution(mesh):
    return jax.shard_map(
        functools.partial(on_device, n_ex=mesh.shape["ex"]),
        mesh=mesh,
        in_specs=(P(("grp", "ex"), None), P(("grp", "ex")), P("grp", None)),
        out_specs=(P(None, ("grp", "ex")), P("grp", None)),
        check_vma=False,
    )
```

```python
import functools
import math

import jax
import jax.numpy as jnp
from jax import lax
from jax.experimental import pallas as pl
from jax.experimental.pallas import tpu as pltpu
from jax.sharding import PartitionSpec as P

ridge = 1.0
slots = 2
near_masks = (0, 4, 2, 6)
f32 = jnp.float32
bf16 = jnp.bfloat16


def nt_dot(a, b):
    return lax.dot_general(a, b, (((1,), (1,)), ((), ())), preferred_element_type=f32)


def column(tile, height, start=0):
    return jnp.concatenate([tile[:, start + q : start + q + 1] for q in range(height // 8)], axis=0)


def spread(values, start=0):
    lane = lax.broadcasted_iota(jnp.int32, (8, 128), 1)
    tile = jnp.zeros((8, 128), f32)
    for q in range(values.shape[0] // 8):
        tile = jnp.where(lane == start + q, values[8 * q : 8 * q + 8], tile)
    return tile


def encode(x, count_tile=None):
    height, width = x.shape
    top = jnp.max(jnp.abs(x), axis=1, keepdims=True)
    power = jnp.ceil(jnp.log2(jnp.maximum(top, 1e-30)) + 0.01)
    whole_x = jnp.round(x * jnp.exp2(15.0 - power))
    mark = spread(power)
    if count_tile is not None:
        mark = mark + count_tile
    chunks = [whole_x[:, j * 128 : (j + 1) * 128] for j in range(width // 128)]
    return jnp.concatenate(chunks + [mark], axis=0).astype(jnp.int32).astype(jnp.int16)


def decode(code, height):
    value = code.astype(jnp.int32).astype(f32)
    count = value.shape[0] // height
    mark = value[count * height :]
    x = jnp.concatenate([value[j * height : (j + 1) * height] for j in range(count)], axis=1)
    return x * jnp.exp2(column(mark, height) - 15.0), mark


def sums_kernel(
    labels_hbm, pick_hbm, feat_hbm, feat_ref, send_ref, keep_ref, held, labels_ref, pick_ref, left, sems, *, n_ex
):
    rows, full = feat_ref.shape
    steps, classes = pick_ref.shape
    width = full // n_ex
    groups = n_ex // 2
    device = lax.axis_index("ex")
    core = device % 2
    small = [
        pltpu.make_async_copy(pick_hbm, pick_ref, sems.at[n_ex]),
        pltpu.make_async_copy(labels_hbm, labels_ref, sems.at[n_ex + 1]),
    ]
    for copy in small:
        copy.start()
    columns = []
    copies = []
    for i in range(n_ex):
        block = (1 - core) * groups + i if i < groups else core * groups + i - groups
        at = pl.ds(pl.multiple_of(block * width, width), width)
        columns.append(at)
        copies.append(pltpu.make_async_copy(feat_hbm.at[:, at], feat_ref.at[:, at], sems.at[i]))
        copies[-1].start()

    for copy in small:
        copy.wait()
    local = pick_ref[...] - device * rows
    mine = (local >= 0) & (local < rows)
    lane = lax.broadcasted_iota(jnp.int32, local.shape, 1)
    first = jnp.min(jnp.where(mine, lane, classes), axis=1, keepdims=True)
    last = jnp.max(jnp.where(mine, lane, -1), axis=1, keepdims=True)
    spot0 = jnp.max(jnp.where(mine & (lane == first), local, -1), axis=1, keepdims=True)
    spot1 = jnp.max(jnp.where(mine & (lane == last) & (last > first), local, -1), axis=1, keepdims=True)
    member = lax.broadcasted_iota(jnp.int32, (classes, rows), 0) == labels_ref[...].reshape(1, rows)
    line = lax.broadcasted_iota(jnp.int32, (steps, rows), 1)
    left[...] = jnp.concatenate(
        [
            jnp.where(member, 1.0, 0.0),
            jnp.where(line == spot0, 1.0, 0.0),
            jnp.where(line == spot1, 1.0, 0.0),
            jnp.zeros((16 - 2 * steps, rows), f32),
        ],
        axis=0,
    ).astype(bf16)
    count = jnp.sum(jnp.where(member, 1.0, 0.0), axis=1, keepdims=True)
    tile = spread(count, classes // 8)
    base = groups * classes
    for ref in (send_ref, keep_ref):
        ref[base : base + 8, :128] = tile
        if width > 128:
            ref[base : base + 8, 128:] = jnp.zeros((8, width - 128), f32)

    for i in range(n_ex):
        copies[i].wait()
        both = jnp.dot(left[...], feat_ref[:, columns[i]], preferred_element_type=f32)
        k = i % groups
        ref = send_ref if i < groups else keep_ref
        ref[k * classes : (k + 1) * classes, :] = both[:classes]
        held[:, columns[i]] = both[classes : classes + 8]


def pack_kernel(held, rows_ref, *, steps):
    half = held.shape[1] // 2
    used = steps * slots
    main = rows_ref.shape[2]
    core = lax.axis_index("ex") % 2
    for part, side in ((0, core), (1, 1 - core)):
        h = held[:, pl.ds(pl.multiple_of(side * half, half), half)]
        lines = [h[:used, :main]]
        for q in range(slots):
            lines.append(jnp.concatenate([h[q * steps + u : q * steps + u + 1, main:] for u in range(steps)], axis=1))
        rows_ref[part] = jnp.concatenate(lines, axis=0).astype(bf16)


def near_id(mask):
    return (lax.axis_index("ex") // 2 % 4) ^ (mask // 2)


def pair_kernel(keep_ref, got_ref, *code_refs, classes):
    far = code_refs[0].shape[0]
    base = 4 * far * classes
    tile = keep_ref[base : base + 8, :128] + got_ref[base : base + 8, :128]
    for mask, code_ref in zip(near_masks, code_refs):
        for j in range(far):
            at = pl.ds(pl.multiple_of((j * 4 + near_id(mask)) * classes, classes), classes)
            code_ref[j] = encode(keep_ref[at, :] + got_ref[at, :], tile)


def add_kernel(*refs, classes, last):
    code_ref = refs[-1]
    for j in range(code_ref.shape[0]):
        value, mark = decode(refs[0][j], classes)
        for ref in refs[1:-1]:
            more, more_mark = decode(ref[j], classes)
            value = value + more
            mark = mark + more_mark
        if last:
            code_ref[j] = encode(value / jnp.sqrt(column(mark, classes, classes // 8)))
        else:
            lane = lax.broadcasted_iota(jnp.int32, mark.shape, 1)
            code_ref[j] = encode(value, jnp.where(lane < classes // 8, 0.0, mark))


def diagonal(block):
    n = block.shape[0]
    eye = lax.broadcasted_iota(jnp.int32, (n, n), 0) == lax.broadcasted_iota(jnp.int32, (n, n), 1)
    return jnp.sum(jnp.where(eye, block, 0.0), axis=1, keepdims=True)


def factor_all(gram):
    order = len(gram)
    factor = [[None] * order for _ in range(order)]
    for j in range(order):
        value = gram[j][j]
        for k in range(j):
            value = value - factor[j][k] * factor[j][k]
        root = jnp.sqrt(value)
        factor[j][j] = 1.0 / root
        for i in range(j + 1, order):
            value = gram[i][j]
            for k in range(j):
                value = value - factor[i][k] * factor[j][k]
            factor[i][j] = value * factor[j][j]
    return factor


def solve_all(factor, right):
    order = len(right)
    forward = []
    for i in range(order):
        value = right[i]
        for j in range(i):
            value = value - factor[i][j] * forward[j]
        forward.append(value * factor[i][i])
    result = []
    for size in range(1, order + 1):
        back = [None] * size
        for i in reversed(range(size)):
            value = forward[i]
            for j in range(i + 1, size):
                value = value - factor[j][i] * back[j]
            back[i] = value * factor[i][i]
        result.append(back)
    return result


def select_kernel(pick_ref, one_ref, *, n_ex, rows, tail):
    steps, classes = pick_ref.shape
    lines = one_ref.shape[1]
    device = lax.axis_index("ex")
    pick = pick_ref[...]
    lane = lax.broadcasted_iota(jnp.int32, pick.shape, 1)
    owner = jnp.zeros_like(pick)
    rank = jnp.zeros_like(pick)
    for d in range(n_ex):
        here = (pick >= d * rows) & (pick < (d + 1) * rows)
        first = jnp.min(jnp.where(here, lane, classes), axis=1, keepdims=True)
        owner = jnp.where(here, d, owner)
        rank = jnp.where(here & (lane > first), 1, rank)
    away = owner ^ device
    bits = n_ex.bit_length() - 1
    far = jnp.zeros_like(pick)
    for b in range(3, bits):
        far = far + (((away >> b) & 1) << (bits - 1 - b))
    by_y, by_z = (away >> 1) & 1, (away >> 2) & 1
    near = 3 * by_y + 2 * by_z - 4 * by_z * by_y
    spot = (2 * near + (away & 1)) * (n_ex // 8) + far
    step = lax.broadcasted_iota(jnp.int32, pick.shape, 0)
    line = lax.broadcasted_iota(jnp.int32, (lines, classes), 0)
    where = spot * 8 + (slots * steps + rank if tail else rank * steps + step)
    hits = [jnp.where(line == where[s : s + 1, :], 1.0, 0.0) for s in range(steps)]
    pad = jnp.zeros((lines, 128 - steps * classes), f32)
    one_ref[...] = jnp.transpose(jnp.concatenate(hits + [pad], axis=1))[: steps * classes].astype(bf16)


def picked_kernel(one_ref, rest_ref, *refs, steps):
    parts, (x_ref, rows_ref) = refs[:-2], refs[-2:]
    total, half = x_ref.shape
    classes = total // steps
    main = rows_ref.shape[1]
    tail = half - main
    at = 0
    for part in parts:
        rows_ref[at : at + part.shape[0], :] = part[...]
        at += part.shape[0]
    x_ref[:, :main] = jnp.dot(one_ref[...], rows_ref[...], preferred_element_type=f32).astype(bf16)
    for s in range(steps):
        at = slice(s * classes, (s + 1) * classes)
        rest = jnp.dot(rest_ref[at, :], rows_ref[:, s * tail : (s + 1) * tail], preferred_element_type=f32)
        x_ref[at, main:] = rest.astype(bf16)


def half_target(side, code_ref, x_ref, target_ref, target_at, left_ref, *, classes):
    half = left_ref.shape[1]
    far = code_ref.shape[0] // 4
    width = half // code_ref.shape[0]
    here = pl.ds(pl.multiple_of(side * half, half), half)
    for k in range(4 * far):
        block = k % far * 4 + near_id(near_masks[k // far])
        target = decode(code_ref[k], classes)[0]
        target_ref[:, pl.ds(pl.multiple_of(target_at + block * width, width), width)] = target
        left_ref[:classes, pl.ds(pl.multiple_of(block * width, width), width)] = target.astype(bf16)
    left_ref[classes:, :] = x_ref[...]
    return nt_dot(left_ref[...], x_ref[...]), here


def half_kernel(feat_ref, code_ref, x_ref, direct_ref, gram_ref, target_ref, left_ref, *, classes):
    core = lax.axis_index("ex") % 2
    gram_ref[...], here = half_target(core, code_ref, x_ref, target_ref, 0, left_ref, classes=classes)
    direct_ref[...] = nt_dot(left_ref[: direct_ref.shape[0], :], feat_ref[:, here])


def pursuit_kernel(
    labels_ref, feat_ref, x_own, x_twin, direct_own, gram_own, target_own, code_ref,
    scores_ref, resid_hbm, resid_ref, left_ref, sems, *, steps, scale
):
    classes, full = resid_ref.shape
    half = full // 2
    core = lax.axis_index("ex") % 2
    gram, other = half_target(1 - core, code_ref, x_twin, resid_ref, (1 - core) * half, left_ref, classes=classes)
    gram = gram + gram_own[...]
    blocks = [
        [
            diagonal(gram[(a + 1) * classes : (a + 2) * classes, b * classes : (b + 1) * classes])
            + (ridge if a == b else 0.0)
            for b in range(a + 1)
        ]
        for a in range(steps)
    ]
    rhs = [diagonal(gram[:classes, a * classes : (a + 1) * classes]) for a in range(steps)]
    weights = solve_all(factor_all(blocks), rhs)
    last = weights[steps - 1]
    copies = []
    span = half // 2
    for x_ref, side in ((x_own, core), (x_twin, 1 - core)):
        for q in range(2):
            there = slice(q * span, (q + 1) * span)
            here = pl.ds(pl.multiple_of(side * half + q * span, span), span)
            value = target_own[:, there] if x_ref is x_own else resid_ref[:, here]
            for k in range(steps):
                value = value - last[k] * x_ref[k * classes : (k + 1) * classes, there].astype(f32)
            resid_ref[:, here] = value
            copies.append(pltpu.make_async_copy(resid_ref.at[:, here], resid_hbm.at[:, here], sems.at[len(copies)]))
            copies[-1].start()

    direct = direct_own[...] + nt_dot(left_ref[: direct_own.shape[0], :], feat_ref[:, other])
    member = lax.broadcasted_iota(jnp.int32, (classes, direct.shape[1]), 0) == labels_ref[...].reshape(1, direct.shape[1])
    for s in range(steps):
        value = direct[:classes]
        for k in range(s):
            value = value - weights[s - 1][k] * direct[(k + 1) * classes : (k + 2) * classes]
        scores_ref[s : s + 1, :] = jnp.sum(jnp.where(member, value, 0.0), axis=0, keepdims=True) * scale
    for copy in copies:
        copy.wait()


def on_device(features, labels, pick_index, *, n_ex):
    rows, full = features.shape
    steps, classes = pick_index.shape
    groups = n_ex // 2
    width = full // n_ex
    total = steps * classes
    main = full // 2 * steps * slots // 8
    limit = pltpu.CompilerParams(vmem_limit_bytes=16 << 20)
    vmem = pl.BlockSpec(memory_space=pltpu.VMEM)
    hbm = pl.BlockSpec(memory_space=pltpu.HBM)
    anywhere = pl.BlockSpec(memory_space=pl.ANY)
    half = jax.ShapeDtypeStruct((groups * classes + 8, width), f32)
    code = jax.ShapeDtypeStruct((groups // 4, classes * (width // 128) + 8, 128), jnp.int16)

    def near_swaps(x):
        diagonal_part, by_y = swap(x[3], 6), swap(x[2], 2)
        return [swap(x[1], 4), by_y, diagonal_part]

    def swap(x, mask):
        return lax.ppermute(x, "ex", [(d, d ^ mask) for d in range(n_ex)])

    def after(x, *others):
        return lax.optimization_barrier((x,) + others)[0]

    feat, send, keep, held = pl.pallas_call(
        functools.partial(sums_kernel, n_ex=n_ex),
        in_specs=[hbm] * 3,
        out_specs=[vmem] * 4,
        out_shape=[pltpu.VMEM((rows, full), bf16), half, half, jax.ShapeDtypeStruct((8, full), f32)],
        scratch_shapes=[
            pltpu.VMEM(labels.shape, jnp.int32),
            pltpu.VMEM(pick_index.shape, jnp.int32),
            pltpu.VMEM((classes + 16, rows), bf16),
            pltpu.SemaphoreType.DMA((n_ex + 2,)),
        ],
        compiler_params=limit,
        name="class_sums",
    )(*[pltpu.with_memory_space_constraint(a, pltpu.HBM) for a in (labels, pick_index, features)])

    def add(codes, last):
        return pl.pallas_call(
            functools.partial(add_kernel, classes=classes, last=last),
            in_specs=[vmem] * len(codes),
            out_specs=vmem,
            out_shape=code,
            compiler_params=limit,
            name="add_sums",
        )(*codes)

    far_masks = [8 << b for b in range(n_ex.bit_length() - 4)]
    got = swap(send, 1)
    codes = pl.pallas_call(
        functools.partial(pair_kernel, classes=classes),
        in_specs=[vmem] * 2,
        out_specs=[vmem] * 4,
        out_shape=[code] * 4,
        compiler_params=limit,
        name="pair_sums",
    )(keep, got)
    packed = pl.pallas_call(
        functools.partial(pack_kernel, steps=steps),
        in_specs=[vmem],
        out_specs=vmem,
        out_shape=jax.ShapeDtypeStruct((2, 8, main), bf16),
        compiler_params=limit,
        name="pack_rows",
    )(held)
    for mask in reversed(far_masks):
        packed = jnp.concatenate([packed, swap(packed, mask)], axis=1)

    near_codes = near_swaps(codes)
    part_sum = add([codes[0], after(near_codes[2], packed), near_codes[1], near_codes[0]], False)

    def select(tail, *others):
        return pl.pallas_call(
            functools.partial(select_kernel, n_ex=n_ex, rows=rows, tail=tail),
            in_specs=[vmem],
            out_specs=vmem,
            out_shape=jax.ShapeDtypeStruct((total, n_ex * 8), bf16),
            compiler_params=limit,
            name="select_tails" if tail else "select_rows",
        )(after(pick_index, *others))

    one = select(False, codes[0])
    rest = select(True, codes[0])
    given = swap(after(packed[1], part_sum), 1)
    part_sum = after(part_sum, one, rest)
    for mask in far_masks:
        more = swap(part_sum, mask)
        part_sum = add([part_sum, more], mask == far_masks[-1])
    near = jnp.concatenate([after(packed[0], more), given], axis=0)
    parts = [near] + near_swaps([near] * 4)
    own_parts = [part_sum] + near_swaps([None, part_sum, after(part_sum, parts[3]), part_sum])

    x = pl.pallas_call(
        functools.partial(picked_kernel, steps=steps),
        in_specs=[vmem] * 6,
        out_specs=vmem,
        out_shape=jax.ShapeDtypeStruct((total, full // 2), bf16),
        scratch_shapes=[pltpu.VMEM((n_ex * 8, main), bf16)],
        compiler_params=limit,
        name="picked_rows",
    )(one, rest, parts[0], parts[3], parts[1], parts[2])

    x_twin = swap(x, 1)
    own_half = jnp.concatenate(after(own_parts, x), axis=0)
    twin_half = swap(own_half, 1)
    left = pltpu.VMEM((total + classes, full // 2), bf16)
    direct, gram, target = pl.pallas_call(
        functools.partial(half_kernel, classes=classes),
        in_specs=[vmem] * 3,
        out_specs=[vmem] * 3,
        out_shape=[
            jax.ShapeDtypeStruct((total, rows), f32),
            jax.ShapeDtypeStruct((total + classes, total), f32),
            jax.ShapeDtypeStruct((classes, full // 2), f32),
        ],
        scratch_shapes=[left],
        compiler_params=limit,
        name="own_half_products",
    )(feat, own_half, x)

    scores, resid = pl.pallas_call(
        functools.partial(pursuit_kernel, steps=steps, scale=1.0 / math.sqrt(full)),
        in_specs=[vmem] * 8,
        out_specs=[vmem, anywhere],
        out_shape=[
            jax.ShapeDtypeStruct((steps, rows), f32),
            jax.ShapeDtypeStruct((classes, full), f32),
        ],
        scratch_shapes=[pltpu.VMEM((classes, full), f32), left, pltpu.SemaphoreType.DMA((4,))],
        compiler_params=limit,
        name="pursuit",
    )(labels, feat, x, x_twin, direct, gram, target, twin_half)
    return scores, resid


def solution(mesh):
    return jax.shard_map(
        functools.partial(on_device, n_ex=mesh.shape["ex"]),
        mesh=mesh,
        in_specs=(P(("grp", "ex"), None), P(("grp", "ex")), P("grp", None)),
        out_specs=(P(None, ("grp", "ex")), P("grp", None)),
        check_vma=False,
    )
```

```python
import functools
import math

import jax
import jax.numpy as jnp
from jax import lax
from jax.experimental import pallas as pl
from jax.experimental.pallas import tpu as pltpu
from jax.sharding import PartitionSpec as P

ridge = 1.0
slots = 2
near_masks = (0, 4, 2, 6)
f32 = jnp.float32
bf16 = jnp.bfloat16


def nt_dot(a, b):
    return lax.dot_general(a, b, (((1,), (1,)), ((), ())), preferred_element_type=f32)


def column(tile, height, start=0):
    return jnp.concatenate([tile[:, start + q : start + q + 1] for q in range(height // 8)], axis=0)


def spread(values, start=0):
    lane = lax.broadcasted_iota(jnp.int32, (8, 128), 1)
    tile = jnp.zeros((8, 128), f32)
    for q in range(values.shape[0] // 8):
        tile = jnp.where(lane == start + q, values[8 * q : 8 * q + 8], tile)
    return tile


def encode(x, count_tile=None):
    height, width = x.shape
    top = jnp.max(jnp.abs(x), axis=1, keepdims=True)
    power = jnp.ceil(jnp.log2(jnp.maximum(top, 1e-30)) + 0.01)
    whole_x = jnp.round(x * jnp.exp2(15.0 - power))
    mark = spread(power)
    if count_tile is not None:
        mark = mark + count_tile
    chunks = [whole_x[:, j * 128 : (j + 1) * 128] for j in range(width // 128)]
    return jnp.concatenate(chunks + [mark], axis=0).astype(jnp.int32).astype(jnp.int16)


def decode(code, height):
    value = code.astype(jnp.int32).astype(f32)
    count = value.shape[0] // height
    mark = value[count * height :]
    x = jnp.concatenate([value[j * height : (j + 1) * height] for j in range(count)], axis=1)
    return x * jnp.exp2(column(mark, height) - 15.0), mark


def sums_kernel(
    labels_hbm, pick_hbm, feat_hbm, feat_ref, send_ref, keep_ref, held, labels_ref, pick_ref, left, sems, *, n_ex
):
    rows, full = feat_ref.shape
    steps, classes = pick_ref.shape
    width = full // n_ex
    groups = n_ex // 2
    device = lax.axis_index("ex")
    core = device % 2
    small = [
        pltpu.make_async_copy(pick_hbm, pick_ref, sems.at[n_ex]),
        pltpu.make_async_copy(labels_hbm, labels_ref, sems.at[n_ex + 1]),
    ]
    for copy in small:
        copy.start()
    columns = []
    copies = []
    for i in range(n_ex):
        block = (1 - core) * groups + i if i < groups else core * groups + i - groups
        at = pl.ds(pl.multiple_of(block * width, width), width)
        columns.append(at)
        copies.append(pltpu.make_async_copy(feat_hbm.at[:, at], feat_ref.at[:, at], sems.at[i]))
        copies[-1].start()

    for copy in small:
        copy.wait()
    local = pick_ref[...] - device * rows
    mine = (local >= 0) & (local < rows)
    lane = lax.broadcasted_iota(jnp.int32, local.shape, 1)
    first = jnp.min(jnp.where(mine, lane, classes), axis=1, keepdims=True)
    last = jnp.max(jnp.where(mine, lane, -1), axis=1, keepdims=True)
    spot0 = jnp.max(jnp.where(mine & (lane == first), local, -1), axis=1, keepdims=True)
    spot1 = jnp.max(jnp.where(mine & (lane == last) & (last > first), local, -1), axis=1, keepdims=True)
    member = lax.broadcasted_iota(jnp.int32, (classes, rows), 0) == labels_ref[...].reshape(1, rows)
    line = lax.broadcasted_iota(jnp.int32, (steps, rows), 1)
    left[...] = jnp.concatenate(
        [
            jnp.where(member, 1.0, 0.0),
            jnp.where(line == spot0, 1.0, 0.0),
            jnp.where(line == spot1, 1.0, 0.0),
            jnp.zeros((16 - 2 * steps, rows), f32),
        ],
        axis=0,
    ).astype(bf16)
    count = jnp.sum(jnp.where(member, 1.0, 0.0), axis=1, keepdims=True)
    tile = spread(count, classes // 8)
    base = groups * classes
    for ref in (send_ref, keep_ref):
        ref[base : base + 8, :128] = tile
        if width > 128:
            ref[base : base + 8, 128:] = jnp.zeros((8, width - 128), f32)

    for i in range(n_ex):
        copies[i].wait()
        both = jnp.dot(left[...], feat_ref[:, columns[i]], preferred_element_type=f32)
        k = i % groups
        ref = send_ref if i < groups else keep_ref
        ref[k * classes : (k + 1) * classes, :] = both[:classes]
        held[:, columns[i]] = both[classes : classes + 8]


def pack_kernel(held, rows_ref, *, steps):
    half = held.shape[1] // 2
    used = steps * slots
    main = rows_ref.shape[2]
    core = lax.axis_index("ex") % 2
    for part, side in ((0, core), (1, 1 - core)):
        h = held[:, pl.ds(pl.multiple_of(side * half, half), half)]
        lines = [h[:used, :main]]
        for q in range(slots):
            lines.append(jnp.concatenate([h[q * steps + u : q * steps + u + 1, main:] for u in range(steps)], axis=1))
        rows_ref[part] = jnp.concatenate(lines, axis=0).astype(bf16)


def near_id(mask):
    return (lax.axis_index("ex") // 2 % 4) ^ (mask // 2)


def pair_kernel(keep_ref, got_ref, *code_refs, classes):
    far = code_refs[0].shape[0]
    base = 4 * far * classes
    tile = keep_ref[base : base + 8, :128] + got_ref[base : base + 8, :128]
    for mask, code_ref in zip(near_masks, code_refs):
        for j in range(far):
            at = pl.ds(pl.multiple_of((j * 4 + near_id(mask)) * classes, classes), classes)
            code_ref[j] = encode(keep_ref[at, :] + got_ref[at, :], tile)


def add_kernel(*refs, classes, last):
    code_ref = refs[-1]
    for j in range(code_ref.shape[0]):
        value, mark = decode(refs[0][j], classes)
        for ref in refs[1:-1]:
            more, more_mark = decode(ref[j], classes)
            value = value + more
            mark = mark + more_mark
        if last:
            code_ref[j] = encode(value / jnp.sqrt(column(mark, classes, classes // 8)))
        else:
            lane = lax.broadcasted_iota(jnp.int32, mark.shape, 1)
            code_ref[j] = encode(value, jnp.where(lane < classes // 8, 0.0, mark))


def diagonal(block):
    n = block.shape[0]
    eye = lax.broadcasted_iota(jnp.int32, (n, n), 0) == lax.broadcasted_iota(jnp.int32, (n, n), 1)
    return jnp.sum(jnp.where(eye, block, 0.0), axis=1, keepdims=True)


def factor_all(gram):
    order = len(gram)
    factor = [[None] * order for _ in range(order)]
    for j in range(order):
        value = gram[j][j]
        for k in range(j):
            value = value - factor[j][k] * factor[j][k]
        root = jnp.sqrt(value)
        factor[j][j] = 1.0 / root
        for i in range(j + 1, order):
            value = gram[i][j]
            for k in range(j):
                value = value - factor[i][k] * factor[j][k]
            factor[i][j] = value * factor[j][j]
    return factor


def solve_all(factor, right):
    order = len(right)
    forward = []
    for i in range(order):
        value = right[i]
        for j in range(i):
            value = value - factor[i][j] * forward[j]
        forward.append(value * factor[i][i])
    result = []
    for size in range(1, order + 1):
        back = [None] * size
        for i in reversed(range(size)):
            value = forward[i]
            for j in range(i + 1, size):
                value = value - factor[j][i] * back[j]
            back[i] = value * factor[i][i]
        result.append(back)
    return result


def select_kernel(pick_ref, one_ref, *, n_ex, rows, tail):
    steps, classes = pick_ref.shape
    lines = one_ref.shape[1]
    device = lax.axis_index("ex")
    pick = pick_ref[...]
    lane = lax.broadcasted_iota(jnp.int32, pick.shape, 1)
    owner = jnp.zeros_like(pick)
    rank = jnp.zeros_like(pick)
    for d in range(n_ex):
        here = (pick >= d * rows) & (pick < (d + 1) * rows)
        first = jnp.min(jnp.where(here, lane, classes), axis=1, keepdims=True)
        owner = jnp.where(here, d, owner)
        rank = jnp.where(here & (lane > first), 1, rank)
    away = owner ^ device
    bits = n_ex.bit_length() - 1
    far = jnp.zeros_like(pick)
    for b in range(3, bits):
        far = far + (((away >> b) & 1) << (bits - 1 - b))
    by_y, by_z = (away >> 1) & 1, (away >> 2) & 1
    near = 3 * by_z + 2 * by_y - 4 * by_z * by_y
    spot = (2 * near + (away & 1)) * (n_ex // 8) + far
    step = lax.broadcasted_iota(jnp.int32, pick.shape, 0)
    line = lax.broadcasted_iota(jnp.int32, (lines, classes), 0)
    where = spot * 8 + (slots * steps + rank if tail else rank * steps + step)
    hits = [jnp.where(line == where[s : s + 1, :], 1.0, 0.0) for s in range(steps)]
    pad = jnp.zeros((lines, 128 - steps * classes), f32)
    one_ref[...] = jnp.transpose(jnp.concatenate(hits + [pad], axis=1))[: steps * classes].astype(bf16)


def picked_kernel(one_ref, rest_ref, *refs, steps):
    parts, (x_ref, rows_ref) = refs[:-2], refs[-2:]
    total, half = x_ref.shape
    classes = total // steps
    main = rows_ref.shape[1]
    tail = half - main
    at = 0
    for part in parts:
        rows_ref[at : at + part.shape[0], :] = part[...]
        at += part.shape[0]
    x_ref[:, :main] = jnp.dot(one_ref[...], rows_ref[...], preferred_element_type=f32).astype(bf16)
    for s in range(steps):
        at = slice(s * classes, (s + 1) * classes)
        rest = jnp.dot(rest_ref[at, :], rows_ref[:, s * tail : (s + 1) * tail], preferred_element_type=f32)
        x_ref[at, main:] = rest.astype(bf16)


def half_target(side, code_ref, x_ref, target_ref, target_at, left_ref, *, classes):
    half = left_ref.shape[1]
    far = code_ref.shape[0] // 4
    width = half // code_ref.shape[0]
    here = pl.ds(pl.multiple_of(side * half, half), half)
    for k in range(4 * far):
        block = k % far * 4 + near_id(near_masks[k // far])
        target = decode(code_ref[k], classes)[0]
        target_ref[:, pl.ds(pl.multiple_of(target_at + block * width, width), width)] = target
        left_ref[:classes, pl.ds(pl.multiple_of(block * width, width), width)] = target.astype(bf16)
    left_ref[classes:, :] = x_ref[...]
    return nt_dot(left_ref[...], x_ref[...]), here


def half_kernel(feat_ref, code_ref, x_ref, direct_ref, gram_ref, target_ref, left_ref, *, classes):
    core = lax.axis_index("ex") % 2
    gram_ref[...], here = half_target(core, code_ref, x_ref, target_ref, 0, left_ref, classes=classes)
    direct_ref[...] = nt_dot(left_ref[: direct_ref.shape[0], :], feat_ref[:, here])


def pursuit_kernel(
    labels_ref, feat_ref, x_own, x_twin, direct_own, gram_own, target_own, code_ref,
    scores_ref, resid_hbm, resid_ref, left_ref, sems, *, steps, scale
):
    classes, full = resid_ref.shape
    half = full // 2
    core = lax.axis_index("ex") % 2
    gram, other = half_target(1 - core, code_ref, x_twin, resid_ref, (1 - core) * half, left_ref, classes=classes)
    gram = gram + gram_own[...]
    blocks = [
        [
            diagonal(gram[(a + 1) * classes : (a + 2) * classes, b * classes : (b + 1) * classes])
            + (ridge if a == b else 0.0)
            for b in range(a + 1)
        ]
        for a in range(steps)
    ]
    rhs = [diagonal(gram[:classes, a * classes : (a + 1) * classes]) for a in range(steps)]
    weights = solve_all(factor_all(blocks), rhs)
    last = weights[steps - 1]
    copies = []
    span = half
    for x_ref, side in ((x_own, core), (x_twin, 1 - core)):
        for q in range(1):
            there = slice(q * span, (q + 1) * span)
            here = pl.ds(pl.multiple_of(side * half + q * span, span), span)
            value = target_own[:, there] if x_ref is x_own else resid_ref[:, here]
            for k in range(steps):
                value = value - last[k] * x_ref[k * classes : (k + 1) * classes, there].astype(f32)
            resid_ref[:, here] = value
            copies.append(pltpu.make_async_copy(resid_ref.at[:, here], resid_hbm.at[:, here], sems.at[len(copies)]))
            copies[-1].start()

    direct = direct_own[...] + nt_dot(left_ref[: direct_own.shape[0], :], feat_ref[:, other])
    member = lax.broadcasted_iota(jnp.int32, (classes, direct.shape[1]), 0) == labels_ref[...].reshape(1, direct.shape[1])
    for s in range(steps):
        value = direct[:classes]
        for k in range(s):
            value = value - weights[s - 1][k] * direct[(k + 1) * classes : (k + 2) * classes]
        scores_ref[s : s + 1, :] = jnp.sum(jnp.where(member, value, 0.0), axis=0, keepdims=True) * scale
    for copy in copies:
        copy.wait()


def on_device(features, labels, pick_index, *, n_ex):
    rows, full = features.shape
    steps, classes = pick_index.shape
    groups = n_ex // 2
    width = full // n_ex
    total = steps * classes
    main = full // 2 * steps * slots // 8
    limit = pltpu.CompilerParams(vmem_limit_bytes=16 << 20)
    vmem = pl.BlockSpec(memory_space=pltpu.VMEM)
    hbm = pl.BlockSpec(memory_space=pltpu.HBM)
    anywhere = pl.BlockSpec(memory_space=pl.ANY)
    half = jax.ShapeDtypeStruct((groups * classes + 8, width), f32)
    code = jax.ShapeDtypeStruct((groups // 4, classes * (width // 128) + 8, 128), jnp.int16)

    def near_swaps(x):
        diagonal_part, by_y = swap(x[3], 6), swap(x[2], 2)
        return [swap(x[1], 4), by_y, diagonal_part]

    def swap(x, mask):
        return lax.ppermute(x, "ex", [(d, d ^ mask) for d in range(n_ex)])

    def after(x, *others):
        return lax.optimization_barrier((x,) + others)[0]

    feat, send, keep, held = pl.pallas_call(
        functools.partial(sums_kernel, n_ex=n_ex),
        in_specs=[hbm] * 3,
        out_specs=[vmem] * 4,
        out_shape=[pltpu.VMEM((rows, full), bf16), half, half, jax.ShapeDtypeStruct((8, full), f32)],
        scratch_shapes=[
            pltpu.VMEM(labels.shape, jnp.int32),
            pltpu.VMEM(pick_index.shape, jnp.int32),
            pltpu.VMEM((classes + 16, rows), bf16),
            pltpu.SemaphoreType.DMA((n_ex + 2,)),
        ],
        compiler_params=limit,
        name="class_sums",
    )(*[pltpu.with_memory_space_constraint(a, pltpu.HBM) for a in (labels, pick_index, features)])

    def add(codes, last):
        return pl.pallas_call(
            functools.partial(add_kernel, classes=classes, last=last),
            in_specs=[vmem] * len(codes),
            out_specs=vmem,
            out_shape=code,
            compiler_params=limit,
            name="add_sums",
        )(*codes)

    far_masks = [8 << b for b in range(n_ex.bit_length() - 4)]
    got = swap(send, 1)
    codes = pl.pallas_call(
        functools.partial(pair_kernel, classes=classes),
        in_specs=[vmem] * 2,
        out_specs=[vmem] * 4,
        out_shape=[code] * 4,
        compiler_params=limit,
        name="pair_sums",
    )(keep, got)
    packed = pl.pallas_call(
        functools.partial(pack_kernel, steps=steps),
        in_specs=[vmem],
        out_specs=vmem,
        out_shape=jax.ShapeDtypeStruct((2, 8, main), bf16),
        compiler_params=limit,
        name="pack_rows",
    )(held)
    for mask in reversed(far_masks):
        packed = jnp.concatenate([packed, swap(packed, mask)], axis=1)

    near_codes = near_swaps(codes)
    part_sum = add([codes[0], after(near_codes[2], packed), near_codes[1], near_codes[0]], False)

    def select(tail, *others):
        return pl.pallas_call(
            functools.partial(select_kernel, n_ex=n_ex, rows=rows, tail=tail),
            in_specs=[vmem],
            out_specs=vmem,
            out_shape=jax.ShapeDtypeStruct((total, n_ex * 8), bf16),
            compiler_params=limit,
            name="select_tails" if tail else "select_rows",
        )(after(pick_index, *others))

    one = select(False, codes[0])
    rest = select(True, codes[0])
    given = swap(after(packed[1], part_sum), 1)
    part_sum = after(part_sum, one, rest)
    for mask in far_masks:
        more = swap(part_sum, mask)
        part_sum = add([part_sum, more], mask == far_masks[-1])
    near = jnp.concatenate([after(packed[0], more), given], axis=0)
    parts = [near] + near_swaps([near] * 4)
    own_parts = [part_sum] + near_swaps([None, after(part_sum, parts[3]), part_sum, part_sum])

    x = pl.pallas_call(
        functools.partial(picked_kernel, steps=steps),
        in_specs=[vmem] * 6,
        out_specs=vmem,
        out_shape=jax.ShapeDtypeStruct((total, full // 2), bf16),
        scratch_shapes=[pltpu.VMEM((n_ex * 8, main), bf16)],
        compiler_params=limit,
        name="picked_rows",
    )(one, rest, parts[0], *parts[:0:-1])

    x_twin = swap(x, 1)
    own_half = jnp.concatenate(after(own_parts, x), axis=0)
    twin_half = swap(own_half, 1)
    left = pltpu.VMEM((total + classes, full // 2), bf16)
    direct, gram, target = pl.pallas_call(
        functools.partial(half_kernel, classes=classes),
        in_specs=[vmem] * 3,
        out_specs=[vmem] * 3,
        out_shape=[
            jax.ShapeDtypeStruct((total, rows), f32),
            jax.ShapeDtypeStruct((total + classes, total), f32),
            jax.ShapeDtypeStruct((classes, full // 2), f32),
        ],
        scratch_shapes=[left],
        compiler_params=limit,
        name="own_half_products",
    )(feat, own_half, x)

    scores, resid = pl.pallas_call(
        functools.partial(pursuit_kernel, steps=steps, scale=1.0 / math.sqrt(full)),
        in_specs=[vmem] * 8,
        out_specs=[vmem, anywhere],
        out_shape=[
            jax.ShapeDtypeStruct((steps, rows), f32),
            jax.ShapeDtypeStruct((classes, full), f32),
        ],
        scratch_shapes=[pltpu.VMEM((classes, full), f32), left, pltpu.SemaphoreType.DMA((4,))],
        compiler_params=limit,
        name="pursuit",
    )(labels, feat, x, x_twin, direct, gram, target, twin_half)
    return scores, resid


def solution(mesh):
    return jax.shard_map(
        functools.partial(on_device, n_ex=mesh.shape["ex"]),
        mesh=mesh,
        in_specs=(P(("grp", "ex"), None), P(("grp", "ex")), P("grp", None)),
        out_specs=(P(None, ("grp", "ex")), P("grp", None)),
        check_vma=False,
    )
```
